32 devices in a mesh: seq: 8 (over z, x), chan: 4 (over y, core).
Axes of the slice: x: 2, y: 2, z: 4, core: 2. Of those that a mesh axis runs over, the one named last changes fastest.
Arguments:
- query_in: bfloat16 [1024, 512], P('seq', 'chan'), may hold values from -6 to 6
- key_in: bfloat16 [1024, 512], P('seq', 'chan'), may hold values from -6 to 6
- value_in: bfloat16 [1024, 512], P('seq', 'chan'), may hold values from -6 to 6
- short_taps: float32 [3, 7, 512], P(None, None, 'chan'), may hold values from -2 to 2
- long_filters: bfloat16 [32, 1024], P('chan'), may hold values from -1.1 to 1.1
- skip_gain: float32 [512], P('chan'), may hold values from -1 to 1
- cotangent: bfloat16 [1024, 512], P('seq', 'chan'), may hold values from -6 to 6
Outputs:
- block_out: bfloat16 [1024, 512], P('seq', 'chan')
- input_grads: bfloat16 [3, 1024, 512], P(None, 'seq', 'chan')
- tap_grads: float32 [3, 7, 512], P(None, None, 'chan')
- skip_grad: float32 [512], P('chan')
- filter_grad: float32 [32, 1024], P('chan')
The draws below stay inside these ranges and needn't reach their ends.
All inputs are finite; a program needn't handle non-finite values.
Results may differ from the reference program's by a relative error of at most 0.0085.
Values may be sent and summed in bfloat16 or wider, within the bound.
No kernel may reach another device: no remote copies, remote signals or barrier semaphores. Data moves between devices by JAX's collectives and lax.ppermute only.
A program may use at most 128 MiB of HBM per device.

```python
import math
import jax
import jax.numpy as jnp
from jax import lax

GROUP = 16
TAPS = 7
CH = 512
GROUPS = 32
SEQ_LEN = 1024


def draw_long_filters(key, part):
    subkeys = jax.random.split(key, 4)
    lag_axis = jnp.arange(SEQ_LEN, dtype=jnp.float32)
    slow_rate = jax.random.uniform(subkeys[0], (GROUPS, 1), jnp.float32, 0.3, 2.0) / SEQ_LEN
    fast_rate = 1.0 / jax.random.uniform(subkeys[1], (GROUPS, 1), jnp.float32, 30.0, 50.0)
    fast_share = 0.5
    rough_part = jax.random.truncated_normal(subkeys[3], -4.0, 4.0, (GROUPS, SEQ_LEN), jnp.float32)
    chosen = jax.random.uniform(subkeys[2], (GROUPS, 1), jnp.float32) < fast_share
    decay_rate = jnp.where(chosen, fast_rate, slow_rate)
    energy = jnp.sqrt(jnp.expm1(-2.0 * decay_rate * SEQ_LEN) / jnp.expm1(-2.0 * decay_rate))
    return (jnp.exp(-decay_rate * lag_axis) * rough_part / energy).astype(jnp.bfloat16)


def block_levels(rng, shape, pieces, low, high):
    factor_of, own = 1.0, jax.random.fold_in(rng, 6)
    for dim, parts in pieces:
        steps = jnp.exp(jax.random.uniform(jax.random.fold_in(own, dim), (parts,), jnp.float32, low / len(pieces), high / len(pieces)))
        factor_of = factor_of * jnp.repeat(steps, shape[dim] // parts).reshape([-1 if axis == dim else 1 for axis in range(len(shape))])
    return factor_of


def scatter_about(stream_key, shape, deviation, reach, shards=(), kind=jnp.bfloat16):
    entries = jax.random.normal(stream_key, shape, jnp.float32) * deviation
    if len(shards) > 0:
        entries = block_levels(stream_key, shape, shards, -0.22, 0.18) * entries
    return jnp.clip(entries, min=-reach, max=reach).astype(kind)


def setup_inputs(seed: int = 0) -> dict:
    arg_keys = jax.random.split(jax.random.key(seed), 8)
    return {
        "query_in": scatter_about(arg_keys[0], (SEQ_LEN, CH), 1.0, 6.0, ((0, 8), (1, 4))),
        "key_in": scatter_about(arg_keys[1], (SEQ_LEN, CH), 1.0, 6.0, ((0, 8), (1, 4))),
        "value_in": scatter_about(arg_keys[2], (SEQ_LEN, CH), 1.0, 6.0, ((0, 8), (1, 4))),
        "short_taps": scatter_about(arg_keys[3], (3, TAPS, CH), TAPS ** -0.5, 2.0, ((2, 4),), jnp.float32),
        "long_filters": draw_long_filters(jax.random.fold_in(arg_keys[7], 71), 0),
        "skip_gain": jnp.clip(jax.random.uniform(arg_keys[5], (CH,), jnp.float32, -1.0, 1.0) * block_levels(arg_keys[5], (CH,), ((0, 4),), -0.4, 0.0), -1.0, 1.0),
        "cotangent": scatter_about(arg_keys[6], (SEQ_LEN, CH), 1.0, 6.0, ((0, 8), (1, 4))),
    }


def delayed(signal, offset):
    return jnp.pad(signal, ((offset, 0), (0, 0)))[:signal.shape[0]]

def advanced(signal, offset):
    return jnp.pad(signal, ((0, offset), (0, 0)))[offset:]

def reference(query_in, key_in, value_in, short_taps, long_filters, skip_gain, cotangent):
    inputs = [query_in.astype(jnp.float32), key_in.astype(jnp.float32), value_in.astype(jnp.float32)]
    shorts = []
    for stream in range(3):
        running = jnp.zeros_like(inputs[stream])
        for offset in range(TAPS):
            running = running + short_taps[stream, offset] * delayed(inputs[stream], offset)
        shorts.append(running)
    query_short, key_short, value_short = shorts
    gating = (key_short * value_short).astype(jnp.bfloat16)
    relayed = (cotangent.astype(jnp.float32) * query_short).astype(jnp.bfloat16)
    gating_wide = gating.astype(jnp.float32)
    relayed_wide = relayed.astype(jnp.float32)
    length = 2 * SEQ_LEN
    gating_groups = gating_wide.T.reshape(GROUPS, GROUP, SEQ_LEN)
    relayed_groups = relayed_wide.T.reshape(GROUPS, GROUP, SEQ_LEN)

    def per_group(members):
        gating_row, relayed_row, filter_row = members
        filter_spec = jnp.fft.rfft(filter_row, length)
        gating_spec = jnp.fft.rfft(gating_row, length, axis=-1)
        relayed_spec = jnp.fft.rfft(relayed_row, length, axis=-1)
        forward = jnp.fft.irfft(gating_spec * filter_spec[None, :], length, axis=-1)[:, :SEQ_LEN]
        backward = jnp.fft.irfft(relayed_spec * jnp.conj(filter_spec)[None, :], length, axis=-1)[:, :SEQ_LEN]
        lag_sums = jnp.fft.irfft(lax.optimization_barrier(jnp.sum(relayed_spec * jnp.conj(gating_spec), axis=0)), length)[:SEQ_LEN]
        return (forward, backward, lag_sums)
    forward, backward, lag_sums = lax.map(per_group, (gating_groups, relayed_groups, long_filters.astype(jnp.float32)))
    long_out = forward.reshape(CH, SEQ_LEN).T + skip_gain * gating_wide
    block_out = (query_short * long_out).astype(jnp.bfloat16)
    cot_wide = cotangent.astype(jnp.float32)
    grad_gating = backward.reshape(CH, SEQ_LEN).T + skip_gain * relayed_wide
    grad_shorts = [cot_wide * long_out, grad_gating * value_short, grad_gating * key_short]
    input_list = []
    tap_list = []
    for stream in range(3):
        running = jnp.zeros_like(grad_shorts[stream])
        tap_terms = []
        for offset in range(TAPS):
            running = running + short_taps[stream, offset] * advanced(grad_shorts[stream], offset)
            tap_terms.append(lax.optimization_barrier(jnp.sum(grad_shorts[stream] * delayed(inputs[stream], offset), axis=0)))
        input_list.append(running)
        tap_list.append(jnp.stack(tap_terms))
    input_grads = jnp.stack(input_list).astype(jnp.bfloat16)
    tap_scale = 1.0 / math.sqrt(SEQ_LEN)
    tap_grads = jnp.stack(tap_list) * tap_scale
    skip_grad = lax.optimization_barrier(jnp.sum(relayed_wide * gating_wide, axis=0)) * tap_scale
    filter_grad = lag_sums * (1.0 / math.sqrt(SEQ_LEN * GROUP))
    return (block_out, input_grads, tap_grads, skip_grad, filter_grad)
```

```python
import functools
import math

import jax
import jax.numpy as jnp
from jax import lax
from jax.experimental import pallas as pl
from jax.experimental.pallas import tpu as pltpu
from jax.sharding import PartitionSpec as P


def from_behind(value, axis, steps):
    count = lax.axis_size(axis)
    initial, last = (max(0, -steps), min(count, count - steps))
    return lax.ppermute(value, axis, [(source, source + steps) for source in range(initial, last)])


def short_forward(extended, weights, rows_here):
    margin = weights.shape[0] - 1
    running = jnp.zeros((rows_here, extended.shape[1]), jnp.float32)
    for offset in range(weights.shape[0]):
        running = (
            running + weights[offset] * extended[margin - offset : margin - offset + rows_here]
        )
    return running


def short_backward(extended, weights, rows_here):
    running = jnp.zeros((rows_here, extended.shape[1]), jnp.float32)
    for offset in range(weights.shape[0]):
        running = running + weights[offset] * extended[offset : offset + rows_here]
    return running


def tap_sums(grad_rows, extended, tap_count, rows_here):
    margin = tap_count - 1
    sums_list = []
    for offset in range(tap_count):
        sums_list.append(
            jnp.sum(grad_rows * extended[margin - offset : margin - offset + rows_here], axis=0)
        )
    return jnp.stack(sums_list)


def hankel(padded, lag_start, height, breadth, seq_total):
    span = height + breadth - 1
    window = lax.dynamic_slice_in_dim(padded, lag_start + seq_total, span, axis=1)
    tiled = jnp.tile(window, (1, height))
    tiled = jnp.pad(tiled, ((0, 0), (0, height)))
    return tiled.reshape(padded.shape[0], height, span + 1)[:, :, :breadth]


def causal_part(padded, source_rows, source_start, target_start, target_count, seq_total):
    breadth = source_rows.shape[0]
    matrix = hankel(
        padded, target_start - source_start - breadth + 1, target_count, breadth, seq_total
    )
    return jnp.einsum("gts,sgc->tgc", matrix, source_rows[::-1], preferred_element_type=jnp.float32)


def anti_part(padded, target_rows, target_start, source_start, source_count, seq_total):
    breadth = target_rows.shape[0]
    matrix = hankel(
        padded, target_start - source_start - source_count + 1, source_count, breadth, seq_total
    )
    return jnp.einsum("gab,bgc->agc", matrix, target_rows, preferred_element_type=jnp.float32)[::-1]


def lag_part(buffer, target_rows, source_rows, target_start, source_start, seq_total):
    height = target_rows.shape[0]
    breadth = source_rows.shape[0]
    groups = target_rows.shape[1]
    padded_source = jnp.pad(source_rows[::-1], ((0, height), (0, 0), (0, 0)))
    products = jnp.einsum(
        "tgc,sgc->gts", target_rows, padded_source, preferred_element_type=jnp.float32
    )
    full_width = height + breadth
    skewed = products.reshape(groups, height * full_width)[:, : height * (full_width - 1)]
    skewed = skewed.reshape(groups, height, full_width - 1)
    diagonal = jnp.sum(skewed, axis=1)
    position = target_start - source_start - breadth + 1 + seq_total
    current = lax.dynamic_slice_in_dim(buffer, position, full_width - 1, axis=1)
    return lax.dynamic_update_slice_in_dim(buffer, current + diagonal, position, axis=1)


def local(query_in, key_in, value_in, short_taps, long_filters, skip_gain, cotangent):
    tok_rows, chan_width = query_in.shape
    groups, seq_total = long_filters.shape
    members = chan_width // groups
    tap_count = short_taps.shape[1]
    margin = tap_count - 1
    device = lax.axis_index("seq")
    own_start = device * tok_rows
    rim_rows = jnp.stack(
        [query_in[tok_rows - margin :], key_in[tok_rows - margin :], value_in[tok_rows - margin :]]
    )
    before = from_behind(rim_rows, "seq", 1)
    streams = [query_in, key_in, value_in]
    extended = [
        jnp.concatenate([before[stream], streams[stream]]).astype(jnp.float32)
        for stream in range(3)
    ]
    query_short = short_forward(extended[0], short_taps[0], tok_rows)
    key_short = short_forward(extended[1], short_taps[1], tok_rows)
    value_short = short_forward(extended[2], short_taps[2], tok_rows)
    gating = (key_short * value_short).astype(jnp.bfloat16)
    relayed = (cotangent.astype(jnp.float32) * query_short).astype(jnp.bfloat16)
    gating_wide = gating.astype(jnp.float32)
    relayed_wide = relayed.astype(jnp.float32)
    gating_groups = gating.reshape(tok_rows, groups, members)
    relayed_groups = relayed.reshape(tok_rows, groups, members)
    padded = jnp.concatenate([jnp.zeros((groups, seq_total), jnp.bfloat16), long_filters], axis=1)
    lag_buffer = jnp.zeros((groups, 2 * seq_total), jnp.float32)
    zeros_out = jnp.zeros((tok_rows, groups, members), jnp.float32)

    def target_pair(distance):
        return distance < 0

    totals = (zeros_out, lag_buffer)
    shard_rows = lax.all_gather(gating, "seq", axis=0, tiled=True)
    piece_rows = shard_rows.shape[0]
    step_rows = min(piece_rows, tok_rows)
    pieces = shard_rows.reshape(piece_rows // step_rows, step_rows, groups, members)

    def forward_visit_block(carried, element):
        position, rows_block = element
        source_start = position * step_rows

        def forward_active(partial_value):
            output_part, buffer = partial_value
            output_part = output_part + causal_part(
                padded, rows_block, source_start, own_start, tok_rows, seq_total
            )
            distance = device - source_start // tok_rows
            buffer = lax.cond(
                target_pair(distance),
                lambda held: lag_part(
                    held, relayed_groups, rows_block, own_start, source_start, seq_total
                ),
                lambda held: held,
                buffer,
            )
            return (output_part, buffer)

        carried = lax.cond(
            source_start < own_start + tok_rows,
            forward_active,
            lambda partial_value: partial_value,
            carried,
        )
        return (carried, None)

    totals, ignored = lax.scan(
        forward_visit_block, totals, (jnp.arange(piece_rows // step_rows, dtype=jnp.int32), pieces)
    )
    output_part, lag_buffer = totals
    output_sum = output_part.reshape(tok_rows, chan_width)
    totals = (zeros_out, lag_buffer)
    shard_rows = lax.all_gather(relayed, "seq", axis=0, tiled=True)
    piece_rows = shard_rows.shape[0]
    backward_step_rows = min(piece_rows, tok_rows)
    pieces = shard_rows.reshape(
        piece_rows // backward_step_rows, backward_step_rows, groups, members
    )

    def backward_visit_block(carried, element):
        position, rows_block = element
        target_start = position * backward_step_rows

        def backward_active(partial_value):
            grad_part, buffer = partial_value
            grad_part = grad_part + anti_part(
                padded, rows_block, target_start, own_start, tok_rows, seq_total
            )
            distance = target_start // tok_rows - device
            buffer = lax.cond(
                target_pair(distance),
                lambda held: held,
                lambda held: lag_part(
                    held, rows_block, gating_groups, target_start, own_start, seq_total
                ),
                buffer,
            )
            return (grad_part, buffer)

        carried = lax.cond(
            target_start + backward_step_rows > own_start,
            backward_active,
            lambda partial_value: partial_value,
            carried,
        )
        return (carried, None)

    totals, ignored = lax.scan(
        backward_visit_block,
        totals,
        (jnp.arange(piece_rows // backward_step_rows, dtype=jnp.int32), pieces),
    )
    grad_part, lag_buffer = totals
    grad_sum = grad_part.reshape(tok_rows, chan_width)
    lag_local = lag_buffer[:, seq_total:]
    long_out = output_sum + skip_gain * gating_wide
    block_out = (query_short * long_out).astype(jnp.bfloat16)
    grad_gating = grad_sum + skip_gain * relayed_wide
    cot_wide = cotangent.astype(jnp.float32)
    grad_shorts = [cot_wide * long_out, grad_gating * value_short, grad_gating * key_short]
    lead_rows = jnp.stack([grad_shorts[stream][:margin] for stream in range(3)])
    after = from_behind(lead_rows, "seq", -1)
    input_grads = jnp.stack(
        [
            short_backward(
                jnp.concatenate([grad_shorts[stream], after[stream]]), short_taps[stream], tok_rows
            )
            for stream in range(3)
        ]
    ).astype(jnp.bfloat16)
    tap_local = jnp.stack(
        [
            tap_sums(grad_shorts[stream], extended[stream], tap_count, tok_rows)
            for stream in range(3)
        ]
    )
    skip_local = jnp.sum(relayed_wide * gating_wide, axis=0)
    lag_total, tap_total, skip_total = lax.psum((lag_local, tap_local, skip_local), "seq")
    tap_scale = 1.0 / math.sqrt(seq_total)
    lag_scale = 1.0 / math.sqrt(seq_total * members)
    return (
        block_out,
        input_grads,
        tap_total * tap_scale,
        skip_total * tap_scale,
        lag_total * lag_scale,
    )


def pack_kernel(query_ref, key_ref, value_ref, cot_ref, out_ref):
    count, _, members, tok_rows = out_ref.shape
    for stream, ref in enumerate((query_ref, key_ref, value_ref, cot_ref)):
        flipped = ref[...].astype(jnp.float32).T.astype(jnp.bfloat16)
        out_ref[:, stream] = flipped.reshape(count, members, tok_rows)


def group_kernel(in_ref, taps_ref, filters_ref, skip_ref, out_ref, params_ref, wide_ref):
    count, _, members, span = in_ref.shape
    groups, seq_total = filters_ref.shape
    streams, tap_count, chan_width = taps_ref.shape
    rows = count * members
    mine = lax.axis_index("seq")
    shape = (count, members, span)
    lane = lax.broadcasted_iota(jnp.int32, (1, 1, span), 2)

    def later(value, steps):
        if steps == 0:
            return value
        turned = pltpu.roll(value, steps, 2)
        before = jnp.concatenate([jnp.zeros_like(turned[:1]), turned[:-1]], axis=0)
        return jnp.where(lane >= steps, turned, before)

    def earlier(value, steps):
        if steps == 0:
            return value
        turned = pltpu.roll(value, span - steps, 2)
        after = jnp.concatenate([turned[1:], jnp.zeros_like(turned[:1])], axis=0)
        return jnp.where(lane < span - steps, turned, after)

    table = jnp.concatenate(
        [taps_ref[stream] for stream in range(streams)] + [skip_ref[...]], axis=0
    )
    width = table.shape[0]
    table = jnp.concatenate(
        [table, jnp.zeros((params_ref.shape[1] - width, chan_width), jnp.float32)], axis=0
    )
    params_ref[...] = table.T
    params = params_ref[pl.ds(pl.multiple_of(mine * members, members), members), :]

    def column(index):
        return jnp.broadcast_to(params[:, index : index + 1], (members, span))[None]

    chosen = lax.broadcasted_iota(jnp.int32, (groups, 1), 0) == mine
    filter_row = jnp.sum(
        jnp.where(chosen, filters_ref[...].astype(jnp.float32), 0.0), axis=0, keepdims=True
    )
    filter_row = jnp.concatenate([filter_row, jnp.zeros((1, span), jnp.float32)], axis=1)
    spread = jnp.broadcast_to(filter_row, (span, seq_total + span))
    toeplitz = pltpu.roll(spread, 0, 1, stride=1, stride_axis=0)[:, :seq_total]
    toeplitz = toeplitz.astype(jnp.bfloat16)

    inputs = [in_ref[:, stream].astype(jnp.float32) for stream in range(streams)]
    cot = in_ref[:, streams].astype(jnp.float32)
    shorts = []
    for stream in range(streams):
        running = column(stream * tap_count) * inputs[stream]
        for offset in range(1, tap_count):
            running = running + column(stream * tap_count + offset) * later(
                inputs[stream], offset
            )
        shorts.append(running)
    query_short, key_short, value_short = shorts
    gating = (key_short * value_short).astype(jnp.bfloat16).reshape(rows, span)
    relayed = (cot * query_short).astype(jnp.bfloat16).reshape(rows, span)

    gating_parts, relayed_parts, filter_parts = [gating], [relayed], [toeplitz[:, :span]]
    for step in range(1, count):
        gap = jnp.zeros((step * members, span), jnp.bfloat16)
        gating_parts.append(jnp.concatenate([gap, gating[: rows - step * members]], axis=0))
        relayed_parts.append(jnp.concatenate([relayed[step * members :], gap], axis=0))
        filter_parts.append(toeplitz[:, step * span : (step + 1) * span])
    gating_lags = jnp.concatenate(gating_parts, axis=1)
    relayed_lags = jnp.concatenate(relayed_parts, axis=1)
    forward = jnp.dot(
        gating_lags, jnp.concatenate(filter_parts, axis=0), preferred_element_type=jnp.float32
    )
    backward = lax.dot_general(
        relayed_lags, toeplitz, (((1,), (1,)), ((), ())), preferred_element_type=jnp.float32
    )
    flip = (
        lax.broadcasted_iota(jnp.int32, (span, span), 0)
        + lax.broadcasted_iota(jnp.int32, (span, span), 1)
        == span - 1
    ).astype(jnp.bfloat16)
    gating_turned = lax.dot_general(
        flip, gating, (((1,), (1,)), ((), ())), preferred_element_type=jnp.float32
    ).astype(jnp.bfloat16)
    products = jnp.dot(gating_turned, relayed_lags, preferred_element_type=jnp.float32)
    wide_ref[:, :seq_total] = products
    wide_ref[:, seq_total:] = jnp.zeros((span, span), jnp.float32)
    skewed = pltpu.roll(wide_ref[...], 0, 1, stride=1, stride_axis=0)
    diagonal = jnp.sum(skewed, axis=0, keepdims=True)
    diagonal = pltpu.roll(diagonal, seq_total + 1, 1)[:, :seq_total]
    lag_scale = 1.0 / math.sqrt(seq_total * members)
    lag_sums = jnp.concatenate(
        [diagonal[:, step * span : (step + 1) * span] for step in range(count)], axis=0
    )
    lag_sums = lag_sums * lag_scale

    gating_wide = gating.astype(jnp.float32).reshape(shape)
    relayed_wide = relayed.astype(jnp.float32).reshape(shape)
    gain = column(streams * tap_count)
    long_out = forward.reshape(shape) + gain * gating_wide
    grad_gating = backward.reshape(shape) + gain * relayed_wide
    out_ref[:, 0] = (query_short * long_out).astype(jnp.bfloat16)
    grad_shorts = [cot * long_out, grad_gating * value_short, grad_gating * key_short]
    tap_scale = 1.0 / math.sqrt(seq_total)
    stats = jnp.zeros((members, span), jnp.float32)
    stat_lane = lax.broadcasted_iota(jnp.int32, (members, span), 1)

    def put(stats, index, product):
        total = jnp.sum(jnp.sum(product, axis=0), axis=1, keepdims=True)
        return jnp.where(stat_lane == index, total, stats)

    for stream in range(streams):
        running = None
        for offset in range(tap_count):
            index = stream * tap_count + offset
            moved = earlier(grad_shorts[stream], offset)
            term = column(index) * moved
            running = term if running is None else running + term
            stats = put(stats, index, moved * inputs[stream])
        out_ref[:, 1 + stream] = running.astype(jnp.bfloat16)
    stats = put(stats, streams * tap_count, relayed_wide * gating_wide) * tap_scale

    stats_high = stats.astype(jnp.bfloat16)
    stats_low = (stats - stats_high.astype(jnp.float32)).astype(jnp.bfloat16)
    stats_pair = jnp.where(
        stat_lane < span // 2,
        stats_high.astype(jnp.float32),
        pltpu.roll(stats_low.astype(jnp.float32), span // 2, 1),
    ).astype(jnp.bfloat16)
    lag_high = lag_sums.astype(jnp.bfloat16).astype(jnp.float32)
    lag_pair = jnp.concatenate([lag_high, lag_sums - lag_high], axis=0).astype(jnp.bfloat16)
    out_ref[:, streams + 1] = jnp.broadcast_to(stats_pair[None], shape)
    out_ref[:, streams + 2] = jnp.broadcast_to(lag_pair[None], shape)


def unpack_kernel(in_ref, out_ref, grads_ref, taps_ref, skip_ref, lags_ref):
    count, _, members, span = in_ref.shape
    streams, tap_count, chan_width = taps_ref.shape
    for stream in range(streams + 1):
        block = in_ref[:, stream].reshape(count * members, span).astype(jnp.float32)
        flipped = block.T.astype(jnp.bfloat16)
        if stream == 0:
            out_ref[...] = flipped
        else:
            grads_ref[stream - 1] = flipped
    stats = in_ref[:, streams + 1].reshape(count * members, span).astype(jnp.float32)
    stats = stats + pltpu.roll(stats, span // 2, 1)
    stats = stats.T
    for stream in range(streams):
        taps_ref[stream] = stats[stream * tap_count : (stream + 1) * tap_count]
    skip_ref[...] = stats[streams * tap_count : streams * tap_count + 1]
    lags = in_ref[:, streams + 2].astype(jnp.float32)
    lags = lags[:, : members // 2] + lags[:, members // 2 :]
    for step in range(members // 2):
        lags_ref[:, step * span : (step + 1) * span] = lags[:, step]


def by_group(query_in, key_in, value_in, short_taps, long_filters, skip_gain, cotangent):
    tok_rows, chan_width = query_in.shape
    groups, seq_total = long_filters.shape
    streams, tap_count, _ = short_taps.shape
    members = chan_width // groups
    count = groups
    vmem = pl.BlockSpec(memory_space=pltpu.VMEM)
    params = pltpu.CompilerParams(vmem_limit_bytes=32 * 1024 * 1024)
    packed = pl.pallas_call(
        pack_kernel,
        out_shape=jax.ShapeDtypeStruct((count, streams + 1, members, tok_rows), jnp.bfloat16),
        in_specs=[vmem] * 4,
        out_specs=vmem,
        compiler_params=params,
        name="pack",
    )(query_in, key_in, value_in, cotangent)
    packed = lax.all_to_all(packed, "seq", 0, 0, tiled=True)
    results = pl.pallas_call(
        group_kernel,
        out_shape=jax.ShapeDtypeStruct((count, streams + 3, members, tok_rows), jnp.bfloat16),
        in_specs=[vmem] * 4,
        out_specs=vmem,
        scratch_shapes=[
            pltpu.VMEM((chan_width, 32), jnp.float32),
            pltpu.VMEM((tok_rows, seq_total + tok_rows), jnp.float32),
        ],
        compiler_params=params,
        name="group",
    )(packed, short_taps, long_filters, skip_gain.reshape(1, chan_width))
    results = lax.all_to_all(results, "seq", 0, 0, tiled=True)
    block_out, input_grads, tap_grads, skip_grad, filter_grad = pl.pallas_call(
        unpack_kernel,
        out_shape=(
            jax.ShapeDtypeStruct((tok_rows, chan_width), jnp.bfloat16),
            jax.ShapeDtypeStruct((streams, tok_rows, chan_width), jnp.bfloat16),
            jax.ShapeDtypeStruct((streams, tap_count, chan_width), jnp.float32),
            jax.ShapeDtypeStruct((1, chan_width), jnp.float32),
            jax.ShapeDtypeStruct((groups, seq_total), jnp.float32),
        ),
        in_specs=[vmem],
        out_specs=(vmem,) * 5,
        compiler_params=params,
        name="unpack",
    )(results)
    return block_out, input_grads, tap_grads, skip_grad.reshape(chan_width), filter_grad


def plan(query_in, key_in, value_in, short_taps, long_filters, skip_gain, cotangent):
    tok_rows, chan_width = query_in.shape
    groups, seq_total = long_filters.shape
    fits = (
        lax.axis_size("seq") == groups
        and tok_rows == 128
        and chan_width == 128
        and chan_width // groups == 16
        and seq_total == groups * tok_rows
        and short_taps.shape[0] * short_taps.shape[1] < 32
    )
    chosen = by_group if fits else local
    return chosen(query_in, key_in, value_in, short_taps, long_filters, skip_gain, cotangent)


def solution(mesh):
    in_specs = (
        P("seq", "chan"),
        P("seq", "chan"),
        P("seq", "chan"),
        P(None, None, "chan"),
        P("chan", None),
        P("chan"),
        P("seq", "chan"),
    )
    out_specs = (
        P("seq", "chan"),
        P(None, "seq", "chan"),
        P(None, None, "chan"),
        P("chan"),
        P("chan", None),
    )
    return jax.shard_map(plan, mesh=mesh, in_specs=in_specs, out_specs=out_specs, check_vma=False)
```

```python
import functools
import math

import jax
import jax.numpy as jnp
from jax import lax
from jax.experimental import pallas as pl
from jax.experimental.pallas import tpu as pltpu
from jax.sharding import PartitionSpec as P


def from_behind(value, axis, steps):
    count = lax.axis_size(axis)
    initial, last = (max(0, -steps), min(count, count - steps))
    return lax.ppermute(value, axis, [(source, source + steps) for source in range(initial, last)])


def short_forward(extended, weights, rows_here):
    margin = weights.shape[0] - 1
    running = jnp.zeros((rows_here, extended.shape[1]), jnp.float32)
    for offset in range(weights.shape[0]):
        running = (
            running + weights[offset] * extended[margin - offset : margin - offset + rows_here]
        )
    return running


def short_backward(extended, weights, rows_here):
    running = jnp.zeros((rows_here, extended.shape[1]), jnp.float32)
    for offset in range(weights.shape[0]):
        running = running + weights[offset] * extended[offset : offset + rows_here]
    return running


def tap_sums(grad_rows, extended, tap_count, rows_here):
    margin = tap_count - 1
    sums_list = []
    for offset in range(tap_count):
        sums_list.append(
            jnp.sum(grad_rows * extended[margin - offset : margin - offset + rows_here], axis=0)
        )
    return jnp.stack(sums_list)


def hankel(padded, lag_start, height, breadth, seq_total):
    span = height + breadth - 1
    window = lax.dynamic_slice_in_dim(padded, lag_start + seq_total, span, axis=1)
    tiled = jnp.tile(window, (1, height))
    tiled = jnp.pad(tiled, ((0, 0), (0, height)))
    return tiled.reshape(padded.shape[0], height, span + 1)[:, :, :breadth]


def causal_part(padded, source_rows, source_start, target_start, target_count, seq_total):
    breadth = source_rows.shape[0]
    matrix = hankel(
        padded, target_start - source_start - breadth + 1, target_count, breadth, seq_total
    )
    return jnp.einsum("gts,sgc->tgc", matrix, source_rows[::-1], preferred_element_type=jnp.float32)


def anti_part(padded, target_rows, target_start, source_start, source_count, seq_total):
    breadth = target_rows.shape[0]
    matrix = hankel(
        padded, target_start - source_start - source_count + 1, source_count, breadth, seq_total
    )
    return jnp.einsum("gab,bgc->agc", matrix, target_rows, preferred_element_type=jnp.float32)[::-1]


def lag_part(buffer, target_rows, source_rows, target_start, source_start, seq_total):
    height = target_rows.shape[0]
    breadth = source_rows.shape[0]
    groups = target_rows.shape[1]
    padded_source = jnp.pad(source_rows[::-1], ((0, height), (0, 0), (0, 0)))
    products = jnp.einsum(
        "tgc,sgc->gts", target_rows, padded_source, preferred_element_type=jnp.float32
    )
    full_width = height + breadth
    skewed = products.reshape(groups, height * full_width)[:, : height * (full_width - 1)]
    skewed = skewed.reshape(groups, height, full_width - 1)
    diagonal = jnp.sum(skewed, axis=1)
    position = target_start - source_start - breadth + 1 + seq_total
    current = lax.dynamic_slice_in_dim(buffer, position, full_width - 1, axis=1)
    return lax.dynamic_update_slice_in_dim(buffer, current + diagonal, position, axis=1)


def local(query_in, key_in, value_in, short_taps, long_filters, skip_gain, cotangent):
    tok_rows, chan_width = query_in.shape
    groups, seq_total = long_filters.shape
    members = chan_width // groups
    tap_count = short_taps.shape[1]
    margin = tap_count - 1
    device = lax.axis_index("seq")
    own_start = device * tok_rows
    rim_rows = jnp.stack(
        [query_in[tok_rows - margin :], key_in[tok_rows - margin :], value_in[tok_rows - margin :]]
    )
    before = from_behind(rim_rows, "seq", 1)
    streams = [query_in, key_in, value_in]
    extended = [
        jnp.concatenate([before[stream], streams[stream]]).astype(jnp.float32)
        for stream in range(3)
    ]
    query_short = short_forward(extended[0], short_taps[0], tok_rows)
    key_short = short_forward(extended[1], short_taps[1], tok_rows)
    value_short = short_forward(extended[2], short_taps[2], tok_rows)
    gating = (key_short * value_short).astype(jnp.bfloat16)
    relayed = (cotangent.astype(jnp.float32) * query_short).astype(jnp.bfloat16)
    gating_wide = gating.astype(jnp.float32)
    relayed_wide = relayed.astype(jnp.float32)
    gating_groups = gating.reshape(tok_rows, groups, members)
    relayed_groups = relayed.reshape(tok_rows, groups, members)
    padded = jnp.concatenate([jnp.zeros((groups, seq_total), jnp.bfloat16), long_filters], axis=1)
    lag_buffer = jnp.zeros((groups, 2 * seq_total), jnp.float32)
    zeros_out = jnp.zeros((tok_rows, groups, members), jnp.float32)

    def target_pair(distance):
        return distance < 0

    totals = (zeros_out, lag_buffer)
    shard_rows = lax.all_gather(gating, "seq", axis=0, tiled=True)
    piece_rows = shard_rows.shape[0]
    step_rows = min(piece_rows, tok_rows)
    pieces = shard_rows.reshape(piece_rows // step_rows, step_rows, groups, members)

    def forward_visit_block(carried, element):
        position, rows_block = element
        source_start = position * step_rows

        def forward_active(partial_value):
            output_part, buffer = partial_value
            output_part = output_part + causal_part(
                padded, rows_block, source_start, own_start, tok_rows, seq_total
            )
            distance = device - source_start // tok_rows
            buffer = lax.cond(
                target_pair(distance),
                lambda held: lag_part(
                    held, relayed_groups, rows_block, own_start, source_start, seq_total
                ),
                lambda held: held,
                buffer,
            )
            return (output_part, buffer)

        carried = lax.cond(
            source_start < own_start + tok_rows,
            forward_active,
            lambda partial_value: partial_value,
            carried,
        )
        return (carried, None)

    totals, ignored = lax.scan(
        forward_visit_block, totals, (jnp.arange(piece_rows // step_rows, dtype=jnp.int32), pieces)
    )
    output_part, lag_buffer = totals
    output_sum = output_part.reshape(tok_rows, chan_width)
    totals = (zeros_out, lag_buffer)
    shard_rows = lax.all_gather(relayed, "seq", axis=0, tiled=True)
    piece_rows = shard_rows.shape[0]
    backward_step_rows = min(piece_rows, tok_rows)
    pieces = shard_rows.reshape(
        piece_rows // backward_step_rows, backward_step_rows, groups, members
    )

    def backward_visit_block(carried, element):
        position, rows_block = element
        target_start = position * backward_step_rows

        def backward_active(partial_value):
            grad_part, buffer = partial_value
            grad_part = grad_part + anti_part(
                padded, rows_block, target_start, own_start, tok_rows, seq_total
            )
            distance = target_start // tok_rows - device
            buffer = lax.cond(
                target_pair(distance),
                lambda held: held,
                lambda held: lag_part(
                    held, rows_block, gating_groups, target_start, own_start, seq_total
                ),
                buffer,
            )
            return (grad_part, buffer)

        carried = lax.cond(
            target_start + backward_step_rows > own_start,
            backward_active,
            lambda partial_value: partial_value,
            carried,
        )
        return (carried, None)

    totals, ignored = lax.scan(
        backward_visit_block,
        totals,
        (jnp.arange(piece_rows // backward_step_rows, dtype=jnp.int32), pieces),
    )
    grad_part, lag_buffer = totals
    grad_sum = grad_part.reshape(tok_rows, chan_width)
    lag_local = lag_buffer[:, seq_total:]
    long_out = output_sum + skip_gain * gating_wide
    block_out = (query_short * long_out).astype(jnp.bfloat16)
    grad_gating = grad_sum + skip_gain * relayed_wide
    cot_wide = cotangent.astype(jnp.float32)
    grad_shorts = [cot_wide * long_out, grad_gating * value_short, grad_gating * key_short]
    lead_rows = jnp.stack([grad_shorts[stream][:margin] for stream in range(3)])
    after = from_behind(lead_rows, "seq", -1)
    input_grads = jnp.stack(
        [
            short_backward(
                jnp.concatenate([grad_shorts[stream], after[stream]]), short_taps[stream], tok_rows
            )
            for stream in range(3)
        ]
    ).astype(jnp.bfloat16)
    tap_local = jnp.stack(
        [
            tap_sums(grad_shorts[stream], extended[stream], tap_count, tok_rows)
            for stream in range(3)
        ]
    )
    skip_local = jnp.sum(relayed_wide * gating_wide, axis=0)
    lag_total, tap_total, skip_total = lax.psum((lag_local, tap_local, skip_local), "seq")
    tap_scale = 1.0 / math.sqrt(seq_total)
    lag_scale = 1.0 / math.sqrt(seq_total * members)
    return (
        block_out,
        input_grads,
        tap_total * tap_scale,
        skip_total * tap_scale,
        lag_total * lag_scale,
    )


def pack_kernel(
    query_ref, key_ref, value_ref, cot_ref, taps_ref, filters_ref, skip_ref,
    out_ref, params_ref, row_ref,
    stream_buf, taps_buf, filters_buf, skip_buf, table_buf, sems,
):
    count, _, members, tok_rows = out_ref.shape
    streams, tap_count, chan_width = taps_buf.shape
    groups = filters_buf.shape[0]
    mine = lax.axis_index("seq")
    moves = [
        pltpu.make_async_copy(ref, stream_buf.at[stream], sems.at[stream])
        for stream, ref in enumerate((query_ref, key_ref, value_ref, cot_ref))
    ]
    small = [
        pltpu.make_async_copy(ref, buf, sems.at[streams + 1 + index])
        for index, (ref, buf) in enumerate(
            ((taps_ref, taps_buf), (filters_ref, filters_buf), (skip_ref, skip_buf))
        )
    ]
    for move in moves + small:
        move.start()
    for stream, move in enumerate(moves):
        move.wait()
        flipped = stream_buf[stream].astype(jnp.float32).T.astype(jnp.bfloat16)
        out_ref[:, stream] = flipped.reshape(count, members, tok_rows)
    for move in small:
        move.wait()
    table = jnp.concatenate(
        [taps_buf[stream] for stream in range(streams)]
        + [skip_buf[...], jnp.zeros((2, chan_width), jnp.float32)],
        axis=0,
    )
    table_buf[...] = table.T
    params_ref[...] = table_buf[pl.ds(pl.multiple_of(mine * members, members), members), :]
    chosen = lax.broadcasted_iota(jnp.int32, (groups, 1), 0) == mine
    row_ref[...] = jnp.sum(
        jnp.where(chosen, filters_buf[...].astype(jnp.float32), 0.0), axis=0, keepdims=True
    )


def group_kernel(tap_count, in_ref, params_ref, row_ref, out_ref, wide_ref):
    count, _, members, span = in_ref.shape
    seq_total = row_ref.shape[1]
    streams = 3
    rows = count * members
    shape = (count, members, span)
    lane = lax.broadcasted_iota(jnp.int32, (1, 1, span), 2)

    def later(value, steps):
        if steps == 0:
            return value
        turned = pltpu.roll(value, steps, 2)
        before = jnp.concatenate([jnp.zeros_like(turned[:1]), turned[:-1]], axis=0)
        return jnp.where(lane >= steps, turned, before)

    def earlier(value, steps):
        if steps == 0:
            return value
        turned = pltpu.roll(value, span - steps, 2)
        after = jnp.concatenate([turned[1:], jnp.zeros_like(turned[:1])], axis=0)
        return jnp.where(lane < span - steps, turned, after)

    params = params_ref[...]

    def column(index):
        return jnp.broadcast_to(params[:, index : index + 1], (members, span))[None]

    filter_row = jnp.concatenate([row_ref[...], jnp.zeros((1, span), jnp.float32)], axis=1)
    spread = jnp.broadcast_to(filter_row, (span, seq_total + span))
    toeplitz = pltpu.roll(spread, 0, 1, stride=1, stride_axis=0)[:, :seq_total]
    toeplitz = toeplitz.astype(jnp.bfloat16)

    inputs = [in_ref[:, stream].astype(jnp.float32) for stream in range(streams)]
    cot = in_ref[:, streams].astype(jnp.float32)
    shorts = []
    for stream in range(streams):
        running = column(stream * tap_count) * inputs[stream]
        for offset in range(1, tap_count):
            running = running + column(stream * tap_count + offset) * later(
                inputs[stream], offset
            )
        shorts.append(running)
    query_short, key_short, value_short = shorts
    gating = (key_short * value_short).astype(jnp.bfloat16).reshape(rows, span)
    relayed = (cot * query_short).astype(jnp.bfloat16).reshape(rows, span)

    gating_parts, relayed_parts, filter_parts = [gating], [relayed], [toeplitz[:, :span]]
    for step in range(1, count):
        gap = jnp.zeros((step * members, span), jnp.bfloat16)
        gating_parts.append(jnp.concatenate([gap, gating[: rows - step * members]], axis=0))
        relayed_parts.append(jnp.concatenate([relayed[step * members :], gap], axis=0))
        filter_parts.append(toeplitz[:, step * span : (step + 1) * span])
    gating_lags = jnp.concatenate(gating_parts, axis=1)
    relayed_lags = jnp.concatenate(relayed_parts, axis=1)
    forward = jnp.dot(
        gating_lags, jnp.concatenate(filter_parts, axis=0), preferred_element_type=jnp.float32
    )
    backward = lax.dot_general(
        relayed_lags, toeplitz, (((1,), (1,)), ((), ())), preferred_element_type=jnp.float32
    )
    flip = (
        lax.broadcasted_iota(jnp.int32, (span, span), 0)
        + lax.broadcasted_iota(jnp.int32, (span, span), 1)
        == span - 1
    ).astype(jnp.bfloat16)
    gating_turned = lax.dot_general(
        flip, gating, (((1,), (1,)), ((), ())), preferred_element_type=jnp.float32
    ).astype(jnp.bfloat16)
    products = jnp.dot(gating_turned, relayed_lags, preferred_element_type=jnp.float32)
    wide_ref[:, :seq_total] = products
    wide_ref[:, seq_total:] = jnp.zeros((span, span), jnp.float32)
    skewed = pltpu.roll(wide_ref[...], 0, 1, stride=1, stride_axis=0)
    diagonal = jnp.sum(skewed, axis=0, keepdims=True)
    diagonal = pltpu.roll(diagonal, seq_total + 1, 1)[:, :seq_total]
    lag_scale = 1.0 / math.sqrt(seq_total * members)
    lag_sums = jnp.concatenate(
        [diagonal[:, step * span : (step + 1) * span] for step in range(count)], axis=0
    )
    lag_sums = lag_sums * lag_scale

    gating_wide = gating.astype(jnp.float32).reshape(shape)
    relayed_wide = relayed.astype(jnp.float32).reshape(shape)
    gain = column(streams * tap_count)
    long_out = forward.reshape(shape) + gain * gating_wide
    grad_gating = backward.reshape(shape) + gain * relayed_wide
    out_ref[:, 0] = (query_short * long_out).astype(jnp.bfloat16)
    grad_shorts = [cot * long_out, grad_gating * value_short, grad_gating * key_short]
    tap_scale = 1.0 / math.sqrt(seq_total)
    stats = jnp.zeros((members, span), jnp.float32)
    stat_lane = lax.broadcasted_iota(jnp.int32, (members, span), 1)

    def put(stats, index, product):
        total = jnp.sum(jnp.sum(product, axis=0), axis=1, keepdims=True)
        return jnp.where(stat_lane == index, total, stats)

    for stream in range(streams):
        running = None
        for offset in range(tap_count):
            index = stream * tap_count + offset
            moved = earlier(grad_shorts[stream], offset)
            term = column(index) * moved
            running = term if running is None else running + term
            stats = put(stats, index, moved * inputs[stream])
        out_ref[:, 1 + stream] = running.astype(jnp.bfloat16)
    stats = put(stats, streams * tap_count, relayed_wide * gating_wide) * tap_scale

    half = span // 2
    stats_high = stats.astype(jnp.bfloat16).astype(jnp.float32)
    stats_low = pltpu.roll(stats - stats_high, half // 2, 1)
    lag_tile = jnp.concatenate([lag_sums, pltpu.roll(lag_sums, half, 1)], axis=0)
    tile = jnp.where(
        stat_lane < half, jnp.where(stat_lane < half // 2, stats_high, stats_low), lag_tile
    )
    out_ref[:, streams + 1] = jnp.broadcast_to(tile.astype(jnp.bfloat16)[None], shape)


def unpack_kernel(in_ref, out_ref, grads_ref, taps_ref, skip_ref, lags_ref):
    count, _, members, span = in_ref.shape
    streams, tap_count, chan_width = taps_ref.shape
    for stream in range(streams + 1):
        block = in_ref[:, stream].reshape(count * members, span).astype(jnp.float32)
        flipped = block.T.astype(jnp.bfloat16)
        if stream == 0:
            out_ref[...] = flipped
        else:
            grads_ref[stream - 1] = flipped
    tile = in_ref[:, streams + 1].astype(jnp.float32)
    stats = tile.reshape(count * members, span)
    stats = (stats + pltpu.roll(stats, span - span // 4, 1)).T
    for stream in range(streams):
        taps_ref[stream] = stats[stream * tap_count : (stream + 1) * tap_count]
    skip_ref[...] = stats[streams * tap_count : streams * tap_count + 1]
    lane = lax.broadcasted_iota(jnp.int32, (1, 1, span), 2)
    lags = jnp.where(
        lane < span // 2, pltpu.roll(tile[:, members // 2 :], span // 2, 2), tile[:, : members // 2]
    )
    for step in range(members // 2):
        lags_ref[:, step * span : (step + 1) * span] = lags[:, step]


def by_group(query_in, key_in, value_in, short_taps, long_filters, skip_gain, cotangent):
    tok_rows, chan_width = query_in.shape
    groups, seq_total = long_filters.shape
    streams, tap_count, _ = short_taps.shape
    members = chan_width // groups
    count = groups
    vmem = pl.BlockSpec(memory_space=pltpu.VMEM)
    params = pltpu.CompilerParams(vmem_limit_bytes=32 * 1024 * 1024)
    rows_padded = streams * tap_count + 3
    packed, params_own, filter_own = pl.pallas_call(
        pack_kernel,
        out_shape=(
            jax.ShapeDtypeStruct((count, streams + 1, members, tok_rows), jnp.bfloat16),
            jax.ShapeDtypeStruct((members, rows_padded), jnp.float32),
            jax.ShapeDtypeStruct((1, seq_total), jnp.float32),
        ),
        in_specs=[pl.BlockSpec(memory_space=pltpu.HBM)] * 7,
        out_specs=(vmem,) * 3,
        scratch_shapes=[
            pltpu.VMEM((streams + 1, tok_rows, chan_width), jnp.bfloat16),
            pltpu.VMEM((streams, tap_count, chan_width), jnp.float32),
            pltpu.VMEM((groups, seq_total), jnp.bfloat16),
            pltpu.VMEM((1, chan_width), jnp.float32),
            pltpu.VMEM((chan_width, rows_padded), jnp.float32),
            pltpu.SemaphoreType.DMA((streams + 4,)),
        ],
        compiler_params=params,
        name="pack",
    )(
        *(
            pltpu.with_memory_space_constraint(value, pltpu.HBM)
            for value in (
                query_in, key_in, value_in, cotangent, short_taps, long_filters,
                skip_gain.reshape(1, chan_width),
            )
        )
    )
    packed = lax.all_to_all(packed, "seq", 0, 0, tiled=True)
    results = pl.pallas_call(
        functools.partial(group_kernel, tap_count),
        out_shape=jax.ShapeDtypeStruct((count, streams + 2, members, tok_rows), jnp.bfloat16),
        in_specs=[vmem] * 3,
        out_specs=vmem,
        scratch_shapes=[pltpu.VMEM((tok_rows, seq_total + tok_rows), jnp.float32)],
        compiler_params=params,
        name="group",
    )(packed, params_own, filter_own)
    results = lax.all_to_all(results, "seq", 0, 0, tiled=True)
    block_out, input_grads, tap_grads, skip_grad, filter_grad = pl.pallas_call(
        unpack_kernel,
        out_shape=(
            jax.ShapeDtypeStruct((tok_rows, chan_width), jnp.bfloat16),
            jax.ShapeDtypeStruct((streams, tok_rows, chan_width), jnp.bfloat16),
            jax.ShapeDtypeStruct((streams, tap_count, chan_width), jnp.float32),
            jax.ShapeDtypeStruct((1, chan_width), jnp.float32),
            jax.ShapeDtypeStruct((groups, seq_total), jnp.float32),
        ),
        in_specs=[vmem],
        out_specs=(vmem,) * 5,
        compiler_params=params,
        name="unpack",
    )(results)
    return block_out, input_grads, tap_grads, skip_grad.reshape(chan_width), filter_grad


def plan(query_in, key_in, value_in, short_taps, long_filters, skip_gain, cotangent):
    tok_rows, chan_width = query_in.shape
    groups, seq_total = long_filters.shape
    tap_rows = short_taps.shape[0] * short_taps.shape[1]
    fits = (
        lax.axis_size("seq") == groups
        and tok_rows == 128
        and chan_width == 128
        and chan_width // groups == 16
        and seq_total == groups * tok_rows
        and tap_rows % 8 == 5
        and tap_rows < 32
    )
    chosen = by_group if fits else local
    return chosen(query_in, key_in, value_in, short_taps, long_filters, skip_gain, cotangent)


def solution(mesh):
    in_specs = (
        P("seq", "chan"),
        P("seq", "chan"),
        P("seq", "chan"),
        P(None, None, "chan"),
        P("chan", None),
        P("chan"),
        P("seq", "chan"),
    )
    out_specs = (
        P("seq", "chan"),
        P(None, "seq", "chan"),
        P(None, None, "chan"),
        P("chan"),
        P("chan", None),
    )
    return jax.shard_map(plan, mesh=mesh, in_specs=in_specs, out_specs=out_specs, check_vma=False)
```

```python
import functools
import math

import jax
import jax.numpy as jnp
from jax import lax
from jax.experimental import pallas as pl
from jax.experimental.pallas import tpu as pltpu
from jax.sharding import PartitionSpec as P


def from_behind(value, axis, steps):
    count = lax.axis_size(axis)
    initial, last = (max(0, -steps), min(count, count - steps))
    return lax.ppermute(value, axis, [(source, source + steps) for source in range(initial, last)])


def short_forward(extended, weights, rows_here):
    margin = weights.shape[0] - 1
    running = jnp.zeros((rows_here, extended.shape[1]), jnp.float32)
    for offset in range(weights.shape[0]):
        running = (
            running + weights[offset] * extended[margin - offset : margin - offset + rows_here]
        )
    return running


def short_backward(extended, weights, rows_here):
    running = jnp.zeros((rows_here, extended.shape[1]), jnp.float32)
    for offset in range(weights.shape[0]):
        running = running + weights[offset] * extended[offset : offset + rows_here]
    return running


def tap_sums(grad_rows, extended, tap_count, rows_here):
    margin = tap_count - 1
    sums_list = []
    for offset in range(tap_count):
        sums_list.append(
            jnp.sum(grad_rows * extended[margin - offset : margin - offset + rows_here], axis=0)
        )
    return jnp.stack(sums_list)


def hankel(padded, lag_start, height, breadth, seq_total):
    span = height + breadth - 1
    window = lax.dynamic_slice_in_dim(padded, lag_start + seq_total, span, axis=1)
    tiled = jnp.tile(window, (1, height))
    tiled = jnp.pad(tiled, ((0, 0), (0, height)))
    return tiled.reshape(padded.shape[0], height, span + 1)[:, :, :breadth]


def causal_part(padded, source_rows, source_start, target_start, target_count, seq_total):
    breadth = source_rows.shape[0]
    matrix = hankel(
        padded, target_start - source_start - breadth + 1, target_count, breadth, seq_total
    )
    return jnp.einsum("gts,sgc->tgc", matrix, source_rows[::-1], preferred_element_type=jnp.float32)


def anti_part(padded, target_rows, target_start, source_start, source_count, seq_total):
    breadth = target_rows.shape[0]
    matrix = hankel(
        padded, target_start - source_start - source_count + 1, source_count, breadth, seq_total
    )
    return jnp.einsum("gab,bgc->agc", matrix, target_rows, preferred_element_type=jnp.float32)[::-1]


def lag_part(buffer, target_rows, source_rows, target_start, source_start, seq_total):
    height = target_rows.shape[0]
    breadth = source_rows.shape[0]
    groups = target_rows.shape[1]
    padded_source = jnp.pad(source_rows[::-1], ((0, height), (0, 0), (0, 0)))
    products = jnp.einsum(
        "tgc,sgc->gts", target_rows, padded_source, preferred_element_type=jnp.float32
    )
    full_width = height + breadth
    skewed = products.reshape(groups, height * full_width)[:, : height * (full_width - 1)]
    skewed = skewed.reshape(groups, height, full_width - 1)
    diagonal = jnp.sum(skewed, axis=1)
    position = target_start - source_start - breadth + 1 + seq_total
    current = lax.dynamic_slice_in_dim(buffer, position, full_width - 1, axis=1)
    return lax.dynamic_update_slice_in_dim(buffer, current + diagonal, position, axis=1)


def local(query_in, key_in, value_in, short_taps, long_filters, skip_gain, cotangent):
    tok_rows, chan_width = query_in.shape
    groups, seq_total = long_filters.shape
    members = chan_width // groups
    tap_count = short_taps.shape[1]
    margin = tap_count - 1
    device = lax.axis_index("seq")
    own_start = device * tok_rows
    rim_rows = jnp.stack(
        [query_in[tok_rows - margin :], key_in[tok_rows - margin :], value_in[tok_rows - margin :]]
    )
    before = from_behind(rim_rows, "seq", 1)
    streams = [query_in, key_in, value_in]
    extended = [
        jnp.concatenate([before[stream], streams[stream]]).astype(jnp.float32)
        for stream in range(3)
    ]
    query_short = short_forward(extended[0], short_taps[0], tok_rows)
    key_short = short_forward(extended[1], short_taps[1], tok_rows)
    value_short = short_forward(extended[2], short_taps[2], tok_rows)
    gating = (key_short * value_short).astype(jnp.bfloat16)
    relayed = (cotangent.astype(jnp.float32) * query_short).astype(jnp.bfloat16)
    gating_wide = gating.astype(jnp.float32)
    relayed_wide = relayed.astype(jnp.float32)
    gating_groups = gating.reshape(tok_rows, groups, members)
    relayed_groups = relayed.reshape(tok_rows, groups, members)
    padded = jnp.concatenate([jnp.zeros((groups, seq_total), jnp.bfloat16), long_filters], axis=1)
    lag_buffer = jnp.zeros((groups, 2 * seq_total), jnp.float32)
    zeros_out = jnp.zeros((tok_rows, groups, members), jnp.float32)

    def target_pair(distance):
        return distance < 0

    totals = (zeros_out, lag_buffer)
    shard_rows = lax.all_gather(gating, "seq", axis=0, tiled=True)
    piece_rows = shard_rows.shape[0]
    step_rows = min(piece_rows, tok_rows)
    pieces = shard_rows.reshape(piece_rows // step_rows, step_rows, groups, members)

    def forward_visit_block(carried, element):
        position, rows_block = element
        source_start = position * step_rows

        def forward_active(partial_value):
            output_part, buffer = partial_value
            output_part = output_part + causal_part(
                padded, rows_block, source_start, own_start, tok_rows, seq_total
            )
            distance = device - source_start // tok_rows
            buffer = lax.cond(
                target_pair(distance),
                lambda held: lag_part(
                    held, relayed_groups, rows_block, own_start, source_start, seq_total
                ),
                lambda held: held,
                buffer,
            )
            return (output_part, buffer)

        carried = lax.cond(
            source_start < own_start + tok_rows,
            forward_active,
            lambda partial_value: partial_value,
            carried,
        )
        return (carried, None)

    totals, ignored = lax.scan(
        forward_visit_block, totals, (jnp.arange(piece_rows // step_rows, dtype=jnp.int32), pieces)
    )
    output_part, lag_buffer = totals
    output_sum = output_part.reshape(tok_rows, chan_width)
    totals = (zeros_out, lag_buffer)
    shard_rows = lax.all_gather(relayed, "seq", axis=0, tiled=True)
    piece_rows = shard_rows.shape[0]
    backward_step_rows = min(piece_rows, tok_rows)
    pieces = shard_rows.reshape(
        piece_rows // backward_step_rows, backward_step_rows, groups, members
    )

    def backward_visit_block(carried, element):
        position, rows_block = element
        target_start = position * backward_step_rows

        def backward_active(partial_value):
            grad_part, buffer = partial_value
            grad_part = grad_part + anti_part(
                padded, rows_block, target_start, own_start, tok_rows, seq_total
            )
            distance = target_start // tok_rows - device
            buffer = lax.cond(
                target_pair(distance),
                lambda held: held,
                lambda held: lag_part(
                    held, rows_block, gating_groups, target_start, own_start, seq_total
                ),
                buffer,
            )
            return (grad_part, buffer)

        carried = lax.cond(
            target_start + backward_step_rows > own_start,
            backward_active,
            lambda partial_value: partial_value,
            carried,
        )
        return (carried, None)

    totals, ignored = lax.scan(
        backward_visit_block,
        totals,
        (jnp.arange(piece_rows // backward_step_rows, dtype=jnp.int32), pieces),
    )
    grad_part, lag_buffer = totals
    grad_sum = grad_part.reshape(tok_rows, chan_width)
    lag_local = lag_buffer[:, seq_total:]
    long_out = output_sum + skip_gain * gating_wide
    block_out = (query_short * long_out).astype(jnp.bfloat16)
    grad_gating = grad_sum + skip_gain * relayed_wide
    cot_wide = cotangent.astype(jnp.float32)
    grad_shorts = [cot_wide * long_out, grad_gating * value_short, grad_gating * key_short]
    lead_rows = jnp.stack([grad_shorts[stream][:margin] for stream in range(3)])
    after = from_behind(lead_rows, "seq", -1)
    input_grads = jnp.stack(
        [
            short_backward(
                jnp.concatenate([grad_shorts[stream], after[stream]]), short_taps[stream], tok_rows
            )
            for stream in range(3)
        ]
    ).astype(jnp.bfloat16)
    tap_local = jnp.stack(
        [
            tap_sums(grad_shorts[stream], extended[stream], tap_count, tok_rows)
            for stream in range(3)
        ]
    )
    skip_local = jnp.sum(relayed_wide * gating_wide, axis=0)
    lag_total, tap_total, skip_total = lax.psum((lag_local, tap_local, skip_local), "seq")
    tap_scale = 1.0 / math.sqrt(seq_total)
    lag_scale = 1.0 / math.sqrt(seq_total * members)
    return (
        block_out,
        input_grads,
        tap_total * tap_scale,
        skip_total * tap_scale,
        lag_total * lag_scale,
    )


def pack_kernel(
    query_ref, key_ref, value_ref, cot_ref, taps_ref, filters_ref, skip_ref,
    out_ref, params_ref, row_ref,
    stream_buf, taps_buf, filters_buf, skip_buf, table_buf, sems,
):
    count, _, members, tok_rows = out_ref.shape
    streams, tap_count, chan_width = taps_buf.shape
    groups = filters_buf.shape[0]
    mine = lax.axis_index("seq")
    moves = [
        pltpu.make_async_copy(ref, stream_buf.at[stream], sems.at[stream])
        for stream, ref in enumerate((query_ref, key_ref, value_ref, cot_ref))
    ]
    small = [
        pltpu.make_async_copy(ref, buf, sems.at[streams + 1 + index])
        for index, (ref, buf) in enumerate(
            ((taps_ref, taps_buf), (filters_ref, filters_buf), (skip_ref, skip_buf))
        )
    ]
    for move in moves + small:
        move.start()
    for stream, move in enumerate(moves):
        move.wait()
        flipped = stream_buf[stream].astype(jnp.float32).T.astype(jnp.bfloat16)
        out_ref[:, stream] = flipped.reshape(count, members, tok_rows)
    for move in small:
        move.wait()
    table = jnp.concatenate(
        [taps_buf[stream] for stream in range(streams)]
        + [skip_buf[...], jnp.zeros((2, chan_width), jnp.float32)],
        axis=0,
    )
    table_buf[...] = table.T
    params_ref[...] = table_buf[pl.ds(pl.multiple_of(mine * members, members), members), :]
    chosen = lax.broadcasted_iota(jnp.int32, (groups, 1), 0) == mine
    row_ref[...] = jnp.sum(
        jnp.where(chosen, filters_buf[...].astype(jnp.float32), 0.0), axis=0, keepdims=True
    )


def group_kernel(tap_count, in_ref, params_ref, row_ref, out_ref, wide_ref):
    count, _, members, span = in_ref.shape
    seq_total = row_ref.shape[1]
    streams = 3
    rows = count * members
    shape = (count, members, span)
    lane = lax.broadcasted_iota(jnp.int32, (1, 1, span), 2)

    def later(value, steps):
        if steps == 0:
            return value
        turned = pltpu.roll(value, steps, 2)
        before = jnp.concatenate([jnp.zeros_like(turned[:1]), turned[:-1]], axis=0)
        return jnp.where(lane >= steps, turned, before)

    def earlier(value, steps):
        if steps == 0:
            return value
        turned = pltpu.roll(value, span - steps, 2)
        after = jnp.concatenate([turned[1:], jnp.zeros_like(turned[:1])], axis=0)
        return jnp.where(lane < span - steps, turned, after)

    params = params_ref[...]

    def column(index):
        return jnp.broadcast_to(params[:, index : index + 1], (members, span))[None]

    filter_row = jnp.concatenate([row_ref[...], jnp.zeros((1, span), jnp.float32)], axis=1)
    spread = jnp.broadcast_to(filter_row, (span, seq_total + span))
    toeplitz = pltpu.roll(spread, 0, 1, stride=1, stride_axis=0)[:, :seq_total]
    toeplitz = toeplitz.astype(jnp.bfloat16)

    inputs = [in_ref[:, stream].astype(jnp.float32) for stream in range(streams)]
    cot = in_ref[:, streams].astype(jnp.float32)
    shorts = []
    for stream in range(streams):
        running = column(stream * tap_count) * inputs[stream]
        for offset in range(1, tap_count):
            running = running + column(stream * tap_count + offset) * later(
                inputs[stream], offset
            )
        shorts.append(running)
    query_short, key_short, value_short = shorts
    gating = (key_short * value_short).astype(jnp.bfloat16).reshape(rows, span)
    relayed = (cot * query_short).astype(jnp.bfloat16).reshape(rows, span)

    gating_parts, relayed_parts, filter_parts = [gating], [relayed], [toeplitz[:, :span]]
    for step in range(1, count):
        gap = jnp.zeros((step * members, span), jnp.bfloat16)
        gating_parts.append(jnp.concatenate([gap, gating[: rows - step * members]], axis=0))
        relayed_parts.append(jnp.concatenate([relayed[step * members :], gap], axis=0))
        filter_parts.append(toeplitz[:, step * span : (step + 1) * span])
    gating_lags = jnp.concatenate(gating_parts, axis=1)
    relayed_lags = jnp.concatenate(relayed_parts, axis=1)
    forward = jnp.dot(
        gating_lags, jnp.concatenate(filter_parts, axis=0), preferred_element_type=jnp.float32
    )
    backward = lax.dot_general(
        relayed_lags, toeplitz, (((1,), (1,)), ((), ())), preferred_element_type=jnp.float32
    )
    flip = (
        lax.broadcasted_iota(jnp.int32, (span, span), 0)
        + lax.broadcasted_iota(jnp.int32, (span, span), 1)
        == span - 1
    ).astype(jnp.bfloat16)
    gating_turned = lax.dot_general(
        flip, gating, (((1,), (1,)), ((), ())), preferred_element_type=jnp.float32
    ).astype(jnp.bfloat16)
    products = jnp.dot(gating_turned, relayed_lags, preferred_element_type=jnp.float32)
    wide_ref[:, :seq_total] = products
    wide_ref[:, seq_total:] = jnp.zeros((span, span), jnp.float32)
    skewed = pltpu.roll(wide_ref[...], 0, 1, stride=1, stride_axis=0)
    diagonal = jnp.sum(skewed, axis=0, keepdims=True)
    diagonal = pltpu.roll(diagonal, seq_total + 1, 1)[:, :seq_total]
    lag_scale = 1.0 / math.sqrt(seq_total * members)
    lag_sums = jnp.concatenate(
        [diagonal[:, step * span : (step + 1) * span] for step in range(count)], axis=0
    )
    lag_sums = lag_sums * lag_scale

    gating_wide = gating.astype(jnp.float32).reshape(shape)
    relayed_wide = relayed.astype(jnp.float32).reshape(shape)
    gain = column(streams * tap_count)
    long_out = forward.reshape(shape) + gain * gating_wide
    grad_gating = backward.reshape(shape) + gain * relayed_wide
    out_ref[:, 0] = (query_short * long_out).astype(jnp.bfloat16)
    grad_shorts = [cot * long_out, grad_gating * value_short, grad_gating * key_short]
    tap_scale = 1.0 / math.sqrt(seq_total)
    stats = jnp.zeros((members, span), jnp.float32)
    stat_lane = lax.broadcasted_iota(jnp.int32, (members, span), 1)

    def put(stats, index, product):
        total = jnp.sum(jnp.sum(product, axis=0), axis=1, keepdims=True)
        return jnp.where(stat_lane == index, total, stats)

    for stream in range(streams):
        running = None
        for offset in range(tap_count):
            index = stream * tap_count + offset
            moved = earlier(grad_shorts[stream], offset)
            term = column(index) * moved
            running = term if running is None else running + term
            stats = put(stats, index, moved * inputs[stream])
        out_ref[:, 1 + stream] = running.astype(jnp.bfloat16)
    stats = put(stats, streams * tap_count, relayed_wide * gating_wide) * tap_scale

    half = span // 2
    stats_high = stats.astype(jnp.bfloat16).astype(jnp.float32)
    stats_low = pltpu.roll(stats - stats_high, half // 2, 1)
    lag_tile = jnp.concatenate([lag_sums, pltpu.roll(lag_sums, half, 1)], axis=0)
    tile = jnp.where(
        stat_lane < half, jnp.where(stat_lane < half // 2, stats_high, stats_low), lag_tile
    )
    out_ref[:, streams + 1] = jnp.broadcast_to(tile.astype(jnp.bfloat16)[None], shape)


def unpack_kernel(in_ref, out_ref, grads_ref, taps_ref, skip_ref, lags_ref):
    count, _, members, span = in_ref.shape
    streams, tap_count, chan_width = taps_ref.shape
    for stream in range(streams + 1):
        block = in_ref[:, stream].reshape(count * members, span).astype(jnp.float32)
        flipped = block.T.astype(jnp.bfloat16)
        if stream == 0:
            out_ref[...] = flipped
        else:
            grads_ref[stream - 1] = flipped
    tile = in_ref[:, streams + 1].astype(jnp.float32)
    stats = tile.reshape(count * members, span)
    stats = (stats + pltpu.roll(stats, span - span // 4, 1)).T
    for stream in range(streams):
        taps_ref[stream] = stats[stream * tap_count : (stream + 1) * tap_count]
    skip_ref[...] = stats[streams * tap_count : streams * tap_count + 1]
    lane = lax.broadcasted_iota(jnp.int32, (1, 1, span), 2)
    lags = jnp.where(
        lane < span // 2, pltpu.roll(tile[:, members // 2 :], span // 2, 2), tile[:, : members // 2]
    )
    for step in range(members // 2):
        lags_ref[:, step * span : (step + 1) * span] = lags[:, step]


def exchange(pieces):
    count = pieces.shape[0]
    spread = pieces.reshape(count // 2, 2, *pieces.shape[1:])
    spread = lax.all_to_all(
        spread, "seq", 0, 0, tiled=True,
        axis_index_groups=[list(range(parity, count, 2)) for parity in range(2)],
    )
    spread = lax.all_to_all(
        spread, "seq", 1, 1, tiled=True,
        axis_index_groups=[[first, first + 1] for first in range(0, count, 2)],
    )
    return spread.reshape(pieces.shape)


def by_group(query_in, key_in, value_in, short_taps, long_filters, skip_gain, cotangent):
    tok_rows, chan_width = query_in.shape
    groups, seq_total = long_filters.shape
    streams, tap_count, _ = short_taps.shape
    members = chan_width // groups
    count = groups
    vmem = pl.BlockSpec(memory_space=pltpu.VMEM)
    params = pltpu.CompilerParams(vmem_limit_bytes=32 * 1024 * 1024)
    rows_padded = streams * tap_count + 3
    packed, params_own, filter_own = pl.pallas_call(
        pack_kernel,
        out_shape=(
            jax.ShapeDtypeStruct((count, streams + 1, members, tok_rows), jnp.bfloat16),
            jax.ShapeDtypeStruct((members, rows_padded), jnp.float32),
            jax.ShapeDtypeStruct((1, seq_total), jnp.float32),
        ),
        in_specs=[pl.BlockSpec(memory_space=pltpu.HBM)] * 7,
        out_specs=(vmem,) * 3,
        scratch_shapes=[
            pltpu.VMEM((streams + 1, tok_rows, chan_width), jnp.bfloat16),
            pltpu.VMEM((streams, tap_count, chan_width), jnp.float32),
            pltpu.VMEM((groups, seq_total), jnp.bfloat16),
            pltpu.VMEM((1, chan_width), jnp.float32),
            pltpu.VMEM((chan_width, rows_padded), jnp.float32),
            pltpu.SemaphoreType.DMA((streams + 4,)),
        ],
        compiler_params=params,
        name="pack",
    )(
        *(
            pltpu.with_memory_space_constraint(value, pltpu.HBM)
            for value in (
                query_in, key_in, value_in, cotangent, short_taps, long_filters,
                skip_gain.reshape(1, chan_width),
            )
        )
    )
    packed = exchange(packed)
    results = pl.pallas_call(
        functools.partial(group_kernel, tap_count),
        out_shape=jax.ShapeDtypeStruct((count, streams + 2, members, tok_rows), jnp.bfloat16),
        in_specs=[vmem] * 3,
        out_specs=vmem,
        scratch_shapes=[pltpu.VMEM((tok_rows, seq_total + tok_rows), jnp.float32)],
        compiler_params=params,
        name="group",
    )(packed, params_own, filter_own)
    results = exchange(results)
    block_out, input_grads, tap_grads, skip_grad, filter_grad = pl.pallas_call(
        unpack_kernel,
        out_shape=(
            jax.ShapeDtypeStruct((tok_rows, chan_width), jnp.bfloat16),
            jax.ShapeDtypeStruct((streams, tok_rows, chan_width), jnp.bfloat16),
            jax.ShapeDtypeStruct((streams, tap_count, chan_width), jnp.float32),
            jax.ShapeDtypeStruct((1, chan_width), jnp.float32),
            jax.ShapeDtypeStruct((groups, seq_total), jnp.float32),
        ),
        in_specs=[vmem],
        out_specs=(vmem,) * 5,
        compiler_params=params,
        name="unpack",
    )(results)
    return block_out, input_grads, tap_grads, skip_grad.reshape(chan_width), filter_grad


def plan(query_in, key_in, value_in, short_taps, long_filters, skip_gain, cotangent):
    tok_rows, chan_width = query_in.shape
    groups, seq_total = long_filters.shape
    tap_rows = short_taps.shape[0] * short_taps.shape[1]
    fits = (
        lax.axis_size("seq") == groups
        and tok_rows == 128
        and chan_width == 128
        and chan_width // groups == 16
        and seq_total == groups * tok_rows
        and tap_rows % 8 == 5
        and tap_rows < 32
    )
    chosen = by_group if fits else local
    return chosen(query_in, key_in, value_in, short_taps, long_filters, skip_gain, cotangent)


def solution(mesh):
    in_specs = (
        P("seq", "chan"),
        P("seq", "chan"),
        P("seq", "chan"),
        P(None, None, "chan"),
        P("chan", None),
        P("chan"),
        P("seq", "chan"),
    )
    out_specs = (
        P("seq", "chan"),
        P(None, "seq", "chan"),
        P(None, None, "chan"),
        P("chan"),
        P("chan", None),
    )
    return jax.shard_map(plan, mesh=mesh, in_specs=in_specs, out_specs=out_specs, check_vma=False)
```

```python
import functools
import math

import jax
import jax.numpy as jnp
from jax import lax
from jax.experimental import pallas as pl
from jax.experimental.pallas import tpu as pltpu
from jax.sharding import PartitionSpec as P


def from_behind(value, axis, steps):
    count = lax.axis_size(axis)
    initial, last = (max(0, -steps), min(count, count - steps))
    return lax.ppermute(value, axis, [(source, source + steps) for source in range(initial, last)])


def short_forward(extended, weights, rows_here):
    margin = weights.shape[0] - 1
    running = jnp.zeros((rows_here, extended.shape[1]), jnp.float32)
    for offset in range(weights.shape[0]):
        running = (
            running + weights[offset] * extended[margin - offset : margin - offset + rows_here]
        )
    return running


def short_backward(extended, weights, rows_here):
    running = jnp.zeros((rows_here, extended.shape[1]), jnp.float32)
    for offset in range(weights.shape[0]):
        running = running + weights[offset] * extended[offset : offset + rows_here]
    return running


def tap_sums(grad_rows, extended, tap_count, rows_here):
    margin = tap_count - 1
    sums_list = []
    for offset in range(tap_count):
        sums_list.append(
            jnp.sum(grad_rows * extended[margin - offset : margin - offset + rows_here], axis=0)
        )
    return jnp.stack(sums_list)


def hankel(padded, lag_start, height, breadth, seq_total):
    span = height + breadth - 1
    window = lax.dynamic_slice_in_dim(padded, lag_start + seq_total, span, axis=1)
    tiled = jnp.tile(window, (1, height))
    tiled = jnp.pad(tiled, ((0, 0), (0, height)))
    return tiled.reshape(padded.shape[0], height, span + 1)[:, :, :breadth]


def causal_part(padded, source_rows, source_start, target_start, target_count, seq_total):
    breadth = source_rows.shape[0]
    matrix = hankel(
        padded, target_start - source_start - breadth + 1, target_count, breadth, seq_total
    )
    return jnp.einsum("gts,sgc->tgc", matrix, source_rows[::-1], preferred_element_type=jnp.float32)


def anti_part(padded, target_rows, target_start, source_start, source_count, seq_total):
    breadth = target_rows.shape[0]
    matrix = hankel(
        padded, target_start - source_start - source_count + 1, source_count, breadth, seq_total
    )
    return jnp.einsum("gab,bgc->agc", matrix, target_rows, preferred_element_type=jnp.float32)[::-1]


def lag_part(buffer, target_rows, source_rows, target_start, source_start, seq_total):
    height = target_rows.shape[0]
    breadth = source_rows.shape[0]
    groups = target_rows.shape[1]
    padded_source = jnp.pad(source_rows[::-1], ((0, height), (0, 0), (0, 0)))
    products = jnp.einsum(
        "tgc,sgc->gts", target_rows, padded_source, preferred_element_type=jnp.float32
    )
    full_width = height + breadth
    skewed = products.reshape(groups, height * full_width)[:, : height * (full_width - 1)]
    skewed = skewed.reshape(groups, height, full_width - 1)
    diagonal = jnp.sum(skewed, axis=1)
    position = target_start - source_start - breadth + 1 + seq_total
    current = lax.dynamic_slice_in_dim(buffer, position, full_width - 1, axis=1)
    return lax.dynamic_update_slice_in_dim(buffer, current + diagonal, position, axis=1)


def local(query_in, key_in, value_in, short_taps, long_filters, skip_gain, cotangent):
    tok_rows, chan_width = query_in.shape
    groups, seq_total = long_filters.shape
    members = chan_width // groups
    tap_count = short_taps.shape[1]
    margin = tap_count - 1
    device = lax.axis_index("seq")
    own_start = device * tok_rows
    rim_rows = jnp.stack(
        [query_in[tok_rows - margin :], key_in[tok_rows - margin :], value_in[tok_rows - margin :]]
    )
    before = from_behind(rim_rows, "seq", 1)
    streams = [query_in, key_in, value_in]
    extended = [
        jnp.concatenate([before[stream], streams[stream]]).astype(jnp.float32)
        for stream in range(3)
    ]
    query_short = short_forward(extended[0], short_taps[0], tok_rows)
    key_short = short_forward(extended[1], short_taps[1], tok_rows)
    value_short = short_forward(extended[2], short_taps[2], tok_rows)
    gating = (key_short * value_short).astype(jnp.bfloat16)
    relayed = (cotangent.astype(jnp.float32) * query_short).astype(jnp.bfloat16)
    gating_wide = gating.astype(jnp.float32)
    relayed_wide = relayed.astype(jnp.float32)
    gating_groups = gating.reshape(tok_rows, groups, members)
    relayed_groups = relayed.reshape(tok_rows, groups, members)
    padded = jnp.concatenate([jnp.zeros((groups, seq_total), jnp.bfloat16), long_filters], axis=1)
    lag_buffer = jnp.zeros((groups, 2 * seq_total), jnp.float32)
    zeros_out = jnp.zeros((tok_rows, groups, members), jnp.float32)

    def target_pair(distance):
        return distance < 0

    totals = (zeros_out, lag_buffer)
    shard_rows = lax.all_gather(gating, "seq", axis=0, tiled=True)
    piece_rows = shard_rows.shape[0]
    step_rows = min(piece_rows, tok_rows)
    pieces = shard_rows.reshape(piece_rows // step_rows, step_rows, groups, members)

    def forward_visit_block(carried, element):
        position, rows_block = element
        source_start = position * step_rows

        def forward_active(partial_value):
            output_part, buffer = partial_value
            output_part = output_part + causal_part(
                padded, rows_block, source_start, own_start, tok_rows, seq_total
            )
            distance = device - source_start // tok_rows
            buffer = lax.cond(
                target_pair(distance),
                lambda held: lag_part(
                    held, relayed_groups, rows_block, own_start, source_start, seq_total
                ),
                lambda held: held,
                buffer,
            )
            return (output_part, buffer)

        carried = lax.cond(
            source_start < own_start + tok_rows,
            forward_active,
            lambda partial_value: partial_value,
            carried,
        )
        return (carried, None)

    totals, ignored = lax.scan(
        forward_visit_block, totals, (jnp.arange(piece_rows // step_rows, dtype=jnp.int32), pieces)
    )
    output_part, lag_buffer = totals
    output_sum = output_part.reshape(tok_rows, chan_width)
    totals = (zeros_out, lag_buffer)
    shard_rows = lax.all_gather(relayed, "seq", axis=0, tiled=True)
    piece_rows = shard_rows.shape[0]
    backward_step_rows = min(piece_rows, tok_rows)
    pieces = shard_rows.reshape(
        piece_rows // backward_step_rows, backward_step_rows, groups, members
    )

    def backward_visit_block(carried, element):
        position, rows_block = element
        target_start = position * backward_step_rows

        def backward_active(partial_value):
            grad_part, buffer = partial_value
            grad_part = grad_part + anti_part(
                padded, rows_block, target_start, own_start, tok_rows, seq_total
            )
            distance = target_start // tok_rows - device
            buffer = lax.cond(
                target_pair(distance),
                lambda held: held,
                lambda held: lag_part(
                    held, rows_block, gating_groups, target_start, own_start, seq_total
                ),
                buffer,
            )
            return (grad_part, buffer)

        carried = lax.cond(
            target_start + backward_step_rows > own_start,
            backward_active,
            lambda partial_value: partial_value,
            carried,
        )
        return (carried, None)

    totals, ignored = lax.scan(
        backward_visit_block,
        totals,
        (jnp.arange(piece_rows // backward_step_rows, dtype=jnp.int32), pieces),
    )
    grad_part, lag_buffer = totals
    grad_sum = grad_part.reshape(tok_rows, chan_width)
    lag_local = lag_buffer[:, seq_total:]
    long_out = output_sum + skip_gain * gating_wide
    block_out = (query_short * long_out).astype(jnp.bfloat16)
    grad_gating = grad_sum + skip_gain * relayed_wide
    cot_wide = cotangent.astype(jnp.float32)
    grad_shorts = [cot_wide * long_out, grad_gating * value_short, grad_gating * key_short]
    lead_rows = jnp.stack([grad_shorts[stream][:margin] for stream in range(3)])
    after = from_behind(lead_rows, "seq", -1)
    input_grads = jnp.stack(
        [
            short_backward(
                jnp.concatenate([grad_shorts[stream], after[stream]]), short_taps[stream], tok_rows
            )
            for stream in range(3)
        ]
    ).astype(jnp.bfloat16)
    tap_local = jnp.stack(
        [
            tap_sums(grad_shorts[stream], extended[stream], tap_count, tok_rows)
            for stream in range(3)
        ]
    )
    skip_local = jnp.sum(relayed_wide * gating_wide, axis=0)
    lag_total, tap_total, skip_total = lax.psum((lag_local, tap_local, skip_local), "seq")
    tap_scale = 1.0 / math.sqrt(seq_total)
    lag_scale = 1.0 / math.sqrt(seq_total * members)
    return (
        block_out,
        input_grads,
        tap_total * tap_scale,
        skip_total * tap_scale,
        lag_total * lag_scale,
    )


def pack_kernel(
    query_ref, key_ref, value_ref, cot_ref, taps_ref, filters_ref, skip_ref,
    *rest,
):
    out_refs, (params_ref, row_ref, whole_buf, stream_buf, taps_buf, filters_buf, skip_buf, table_buf, sems) = (
        rest[:-9], rest[-9:]
    )
    count, _, members, tok_rows = whole_buf.shape
    streams, tap_count, chan_width = taps_buf.shape
    groups = filters_buf.shape[0]
    mine = lax.axis_index("seq")
    moves = [
        pltpu.make_async_copy(ref, stream_buf.at[stream], sems.at[stream])
        for stream, ref in enumerate((query_ref, key_ref, value_ref, cot_ref))
    ]
    small = [
        pltpu.make_async_copy(ref, buf, sems.at[streams + 1 + index])
        for index, (ref, buf) in enumerate(
            ((taps_ref, taps_buf), (filters_ref, filters_buf), (skip_ref, skip_buf))
        )
    ]
    for move in moves + small:
        move.start()
    for stream, move in enumerate(moves):
        move.wait()
        flipped = stream_buf[stream].astype(jnp.float32).T.astype(jnp.bfloat16)
        whole_buf[:, stream] = flipped.reshape(count, members, tok_rows)
    for step, ref in enumerate(out_refs):
        ref[...] = whole_buf[mine ^ step]
    for move in small:
        move.wait()
    table = jnp.concatenate(
        [taps_buf[stream] for stream in range(streams)]
        + [skip_buf[...], jnp.zeros((2, chan_width), jnp.float32)],
        axis=0,
    )
    table_buf[...] = table.T
    params_ref[...] = table_buf[pl.ds(pl.multiple_of(mine * members, members), members), :]
    chosen = lax.broadcasted_iota(jnp.int32, (groups, 1), 0) == mine
    row_ref[...] = jnp.sum(
        jnp.where(chosen, filters_buf[...].astype(jnp.float32), 0.0), axis=0, keepdims=True
    )


def group_kernel(tap_count, count, *refs):
    in_refs, (params_ref, row_ref) = refs[:count], refs[count : count + 2]
    out_refs, (in_ref, out_ref, wide_ref) = refs[count + 2 : 2 * count + 2], refs[2 * count + 2 :]
    mine = lax.axis_index("seq")
    for step, ref in enumerate(in_refs):
        in_ref[mine ^ step] = ref[...]
    count, _, members, span = in_ref.shape
    seq_total = row_ref.shape[1]
    streams = 3
    rows = count * members
    shape = (count, members, span)
    lane = lax.broadcasted_iota(jnp.int32, (1, 1, span), 2)

    def later(value, steps):
        if steps == 0:
            return value
        turned = pltpu.roll(value, steps, 2)
        before = jnp.concatenate([jnp.zeros_like(turned[:1]), turned[:-1]], axis=0)
        return jnp.where(lane >= steps, turned, before)

    def earlier(value, steps):
        if steps == 0:
            return value
        turned = pltpu.roll(value, span - steps, 2)
        after = jnp.concatenate([turned[1:], jnp.zeros_like(turned[:1])], axis=0)
        return jnp.where(lane < span - steps, turned, after)

    params = params_ref[...]

    def column(index):
        return jnp.broadcast_to(params[:, index : index + 1], (members, span))[None]

    filter_row = jnp.concatenate([row_ref[...], jnp.zeros((1, span), jnp.float32)], axis=1)
    spread = jnp.broadcast_to(filter_row, (span, seq_total + span))
    toeplitz = pltpu.roll(spread, 0, 1, stride=1, stride_axis=0)[:, :seq_total]
    toeplitz = toeplitz.astype(jnp.bfloat16)

    inputs = [in_ref[:, stream].astype(jnp.float32) for stream in range(streams)]
    cot = in_ref[:, streams].astype(jnp.float32)
    shorts = []
    for stream in range(streams):
        running = column(stream * tap_count) * inputs[stream]
        for offset in range(1, tap_count):
            running = running + column(stream * tap_count + offset) * later(
                inputs[stream], offset
            )
        shorts.append(running)
    query_short, key_short, value_short = shorts
    gating = (key_short * value_short).astype(jnp.bfloat16).reshape(rows, span)
    relayed = (cot * query_short).astype(jnp.bfloat16).reshape(rows, span)

    gating_parts, relayed_parts, filter_parts = [gating], [relayed], [toeplitz[:, :span]]
    for step in range(1, count):
        gap = jnp.zeros((step * members, span), jnp.bfloat16)
        gating_parts.append(jnp.concatenate([gap, gating[: rows - step * members]], axis=0))
        relayed_parts.append(jnp.concatenate([relayed[step * members :], gap], axis=0))
        filter_parts.append(toeplitz[:, step * span : (step + 1) * span])
    gating_lags = jnp.concatenate(gating_parts, axis=1)
    relayed_lags = jnp.concatenate(relayed_parts, axis=1)
    forward = jnp.dot(
        gating_lags, jnp.concatenate(filter_parts, axis=0), preferred_element_type=jnp.float32
    )
    backward = lax.dot_general(
        relayed_lags, toeplitz, (((1,), (1,)), ((), ())), preferred_element_type=jnp.float32
    )
    flip = (
        lax.broadcasted_iota(jnp.int32, (span, span), 0)
        + lax.broadcasted_iota(jnp.int32, (span, span), 1)
        == span - 1
    ).astype(jnp.bfloat16)
    gating_turned = lax.dot_general(
        flip, gating, (((1,), (1,)), ((), ())), preferred_element_type=jnp.float32
    ).astype(jnp.bfloat16)
    products = jnp.dot(gating_turned, relayed_lags, preferred_element_type=jnp.float32)
    wide_ref[:, :seq_total] = products
    wide_ref[:, seq_total:] = jnp.zeros((span, span), jnp.float32)
    skewed = pltpu.roll(wide_ref[...], 0, 1, stride=1, stride_axis=0)
    diagonal = jnp.sum(skewed, axis=0, keepdims=True)
    diagonal = pltpu.roll(diagonal, seq_total + 1, 1)[:, :seq_total]
    lag_scale = 1.0 / math.sqrt(seq_total * members)
    lag_sums = jnp.concatenate(
        [diagonal[:, step * span : (step + 1) * span] for step in range(count)], axis=0
    )
    lag_sums = lag_sums * lag_scale

    gating_wide = gating.astype(jnp.float32).reshape(shape)
    relayed_wide = relayed.astype(jnp.float32).reshape(shape)
    gain = column(streams * tap_count)
    long_out = forward.reshape(shape) + gain * gating_wide
    grad_gating = backward.reshape(shape) + gain * relayed_wide
    out_ref[:, 0] = (query_short * long_out).astype(jnp.bfloat16)
    grad_shorts = [cot * long_out, grad_gating * value_short, grad_gating * key_short]
    tap_scale = 1.0 / math.sqrt(seq_total)
    stats = jnp.zeros((members, span), jnp.float32)
    stat_lane = lax.broadcasted_iota(jnp.int32, (members, span), 1)

    def put(stats, index, product):
        total = jnp.sum(jnp.sum(product, axis=0), axis=1, keepdims=True)
        return jnp.where(stat_lane == index, total, stats)

    for stream in range(streams):
        running = None
        for offset in range(tap_count):
            index = stream * tap_count + offset
            moved = earlier(grad_shorts[stream], offset)
            term = column(index) * moved
            running = term if running is None else running + term
            stats = put(stats, index, moved * inputs[stream])
        out_ref[:, 1 + stream] = running.astype(jnp.bfloat16)
    stats = put(stats, streams * tap_count, relayed_wide * gating_wide) * tap_scale

    half = span // 2
    stats_high = stats.astype(jnp.bfloat16).astype(jnp.float32)
    stats_low = pltpu.roll(stats - stats_high, half // 2, 1)
    lag_tile = jnp.concatenate([lag_sums, pltpu.roll(lag_sums, half, 1)], axis=0)
    tile = jnp.where(
        stat_lane < half, jnp.where(stat_lane < half // 2, stats_high, stats_low), lag_tile
    )
    out_ref[:, streams + 1] = jnp.broadcast_to(tile.astype(jnp.bfloat16)[None], shape)
    for step, ref in enumerate(out_refs):
        ref[...] = out_ref[mine ^ step]


def unpack_kernel(*refs):
    in_refs, (out_ref, grads_ref, taps_ref, skip_ref, lags_ref, in_ref) = refs[:-6], refs[-6:]
    mine = lax.axis_index("seq")
    for step, ref in enumerate(in_refs):
        in_ref[mine ^ step] = ref[...]
    count, _, members, span = in_ref.shape
    streams, tap_count, chan_width = taps_ref.shape
    for stream in range(streams + 1):
        block = in_ref[:, stream].reshape(count * members, span).astype(jnp.float32)
        flipped = block.T.astype(jnp.bfloat16)
        if stream == 0:
            out_ref[...] = flipped
        else:
            grads_ref[stream - 1] = flipped
    tile = in_ref[:, streams + 1].astype(jnp.float32)
    stats = tile.reshape(count * members, span)
    stats = (stats + pltpu.roll(stats, span - span // 4, 1)).T
    for stream in range(streams):
        taps_ref[stream] = stats[stream * tap_count : (stream + 1) * tap_count]
    skip_ref[...] = stats[streams * tap_count : streams * tap_count + 1]
    lane = lax.broadcasted_iota(jnp.int32, (1, 1, span), 2)
    lags = jnp.where(
        lane < span // 2, pltpu.roll(tile[:, members // 2 :], span // 2, 2), tile[:, : members // 2]
    )
    for step in range(members // 2):
        lags_ref[:, step * span : (step + 1) * span] = lags[:, step]


def exchange(pieces):
    count = len(pieces)
    return [pieces[0]] + [
        lax.ppermute(pieces[step], "seq", [(source, source ^ step) for source in range(count)])
        for step in range(1, count)
    ]


def by_group(query_in, key_in, value_in, short_taps, long_filters, skip_gain, cotangent):
    tok_rows, chan_width = query_in.shape
    groups, seq_total = long_filters.shape
    streams, tap_count, _ = short_taps.shape
    members = chan_width // groups
    count = groups
    vmem = pl.BlockSpec(memory_space=pltpu.VMEM)
    params = pltpu.CompilerParams(vmem_limit_bytes=32 * 1024 * 1024)
    rows_padded = streams * tap_count + 3
    *packed, params_own, filter_own = pl.pallas_call(
        pack_kernel,
        out_shape=(
            *[jax.ShapeDtypeStruct((streams + 1, members, tok_rows), jnp.bfloat16)] * count,
            jax.ShapeDtypeStruct((members, rows_padded), jnp.float32),
            jax.ShapeDtypeStruct((1, seq_total), jnp.float32),
        ),
        in_specs=[pl.BlockSpec(memory_space=pltpu.HBM)] * 7,
        out_specs=(vmem,) * (count + 2),
        scratch_shapes=[
            pltpu.VMEM((count, streams + 1, members, tok_rows), jnp.bfloat16),
            pltpu.VMEM((streams + 1, tok_rows, chan_width), jnp.bfloat16),
            pltpu.VMEM((streams, tap_count, chan_width), jnp.float32),
            pltpu.VMEM((groups, seq_total), jnp.bfloat16),
            pltpu.VMEM((1, chan_width), jnp.float32),
            pltpu.VMEM((chan_width, rows_padded), jnp.float32),
            pltpu.SemaphoreType.DMA((streams + 4,)),
        ],
        compiler_params=params,
        name="pack",
    )(
        *(
            pltpu.with_memory_space_constraint(value, pltpu.HBM)
            for value in (
                query_in, key_in, value_in, cotangent, short_taps, long_filters,
                skip_gain.reshape(1, chan_width),
            )
        )
    )
    packed = exchange(packed)
    results = pl.pallas_call(
        functools.partial(group_kernel, tap_count, count),
        out_shape=[jax.ShapeDtypeStruct((streams + 2, members, tok_rows), jnp.bfloat16)] * count,
        in_specs=[vmem] * (count + 2),
        out_specs=[vmem] * count,
        scratch_shapes=[
            pltpu.VMEM((count, streams + 1, members, tok_rows), jnp.bfloat16),
            pltpu.VMEM((count, streams + 2, members, tok_rows), jnp.bfloat16),
            pltpu.VMEM((tok_rows, seq_total + tok_rows), jnp.float32),
        ],
        compiler_params=params,
        name="group",
    )(*packed, params_own, filter_own)
    results = exchange(results)
    block_out, input_grads, tap_grads, skip_grad, filter_grad = pl.pallas_call(
        unpack_kernel,
        out_shape=(
            jax.ShapeDtypeStruct((tok_rows, chan_width), jnp.bfloat16),
            jax.ShapeDtypeStruct((streams, tok_rows, chan_width), jnp.bfloat16),
            jax.ShapeDtypeStruct((streams, tap_count, chan_width), jnp.float32),
            jax.ShapeDtypeStruct((1, chan_width), jnp.float32),
            jax.ShapeDtypeStruct((groups, seq_total), jnp.float32),
        ),
        in_specs=[vmem] * count,
        out_specs=(vmem,) * 5,
        scratch_shapes=[pltpu.VMEM((count, streams + 2, members, tok_rows), jnp.bfloat16)],
        compiler_params=params,
        name="unpack",
    )(*results)
    return block_out, input_grads, tap_grads, skip_grad.reshape(chan_width), filter_grad


def plan(query_in, key_in, value_in, short_taps, long_filters, skip_gain, cotangent):
    tok_rows, chan_width = query_in.shape
    groups, seq_total = long_filters.shape
    tap_rows = short_taps.shape[0] * short_taps.shape[1]
    fits = (
        lax.axis_size("seq") == groups
        and tok_rows == 128
        and chan_width == 128
        and chan_width // groups == 16
        and seq_total == groups * tok_rows
        and tap_rows % 8 == 5
        and tap_rows < 32
    )
    chosen = by_group if fits else local
    return chosen(query_in, key_in, value_in, short_taps, long_filters, skip_gain, cotangent)


def solution(mesh):
    in_specs = (
        P("seq", "chan"),
        P("seq", "chan"),
        P("seq", "chan"),
        P(None, None, "chan"),
        P("chan", None),
        P("chan"),
        P("seq", "chan"),
    )
    out_specs = (
        P("seq", "chan"),
        P(None, "seq", "chan"),
        P(None, None, "chan"),
        P("chan"),
        P("chan", None),
    )
    return jax.shard_map(plan, mesh=mesh, in_specs=in_specs, out_specs=out_specs, check_vma=False)
```

```python
import functools
import math

import jax
import jax.numpy as jnp
from jax import lax
from jax.experimental import pallas as pl
from jax.experimental.pallas import tpu as pltpu
from jax.sharding import PartitionSpec as P


def from_behind(value, axis, steps):
    count = lax.axis_size(axis)
    initial, last = (max(0, -steps), min(count, count - steps))
    return lax.ppermute(value, axis, [(source, source + steps) for source in range(initial, last)])


def short_forward(extended, weights, rows_here):
    margin = weights.shape[0] - 1
    running = jnp.zeros((rows_here, extended.shape[1]), jnp.float32)
    for offset in range(weights.shape[0]):
        running = (
            running + weights[offset] * extended[margin - offset : margin - offset + rows_here]
        )
    return running


def short_backward(extended, weights, rows_here):
    running = jnp.zeros((rows_here, extended.shape[1]), jnp.float32)
    for offset in range(weights.shape[0]):
        running = running + weights[offset] * extended[offset : offset + rows_here]
    return running


def tap_sums(grad_rows, extended, tap_count, rows_here):
    margin = tap_count - 1
    sums_list = []
    for offset in range(tap_count):
        sums_list.append(
            jnp.sum(grad_rows * extended[margin - offset : margin - offset + rows_here], axis=0)
        )
    return jnp.stack(sums_list)


def hankel(padded, lag_start, height, breadth, seq_total):
    span = height + breadth - 1
    window = lax.dynamic_slice_in_dim(padded, lag_start + seq_total, span, axis=1)
    tiled = jnp.tile(window, (1, height))
    tiled = jnp.pad(tiled, ((0, 0), (0, height)))
    return tiled.reshape(padded.shape[0], height, span + 1)[:, :, :breadth]


def causal_part(padded, source_rows, source_start, target_start, target_count, seq_total):
    breadth = source_rows.shape[0]
    matrix = hankel(
        padded, target_start - source_start - breadth + 1, target_count, breadth, seq_total
    )
    return jnp.einsum("gts,sgc->tgc", matrix, source_rows[::-1], preferred_element_type=jnp.float32)


def anti_part(padded, target_rows, target_start, source_start, source_count, seq_total):
    breadth = target_rows.shape[0]
    matrix = hankel(
        padded, target_start - source_start - source_count + 1, source_count, breadth, seq_total
    )
    return jnp.einsum("gab,bgc->agc", matrix, target_rows, preferred_element_type=jnp.float32)[::-1]


def lag_part(buffer, target_rows, source_rows, target_start, source_start, seq_total):
    height = target_rows.shape[0]
    breadth = source_rows.shape[0]
    groups = target_rows.shape[1]
    padded_source = jnp.pad(source_rows[::-1], ((0, height), (0, 0), (0, 0)))
    products = jnp.einsum(
        "tgc,sgc->gts", target_rows, padded_source, preferred_element_type=jnp.float32
    )
    full_width = height + breadth
    skewed = products.reshape(groups, height * full_width)[:, : height * (full_width - 1)]
    skewed = skewed.reshape(groups, height, full_width - 1)
    diagonal = jnp.sum(skewed, axis=1)
    position = target_start - source_start - breadth + 1 + seq_total
    current = lax.dynamic_slice_in_dim(buffer, position, full_width - 1, axis=1)
    return lax.dynamic_update_slice_in_dim(buffer, current + diagonal, position, axis=1)


def local(query_in, key_in, value_in, short_taps, long_filters, skip_gain, cotangent):
    tok_rows, chan_width = query_in.shape
    groups, seq_total = long_filters.shape
    members = chan_width // groups
    tap_count = short_taps.shape[1]
    margin = tap_count - 1
    device = lax.axis_index("seq")
    own_start = device * tok_rows
    rim_rows = jnp.stack(
        [query_in[tok_rows - margin :], key_in[tok_rows - margin :], value_in[tok_rows - margin :]]
    )
    before = from_behind(rim_rows, "seq", 1)
    streams = [query_in, key_in, value_in]
    extended = [
        jnp.concatenate([before[stream], streams[stream]]).astype(jnp.float32)
        for stream in range(3)
    ]
    query_short = short_forward(extended[0], short_taps[0], tok_rows)
    key_short = short_forward(extended[1], short_taps[1], tok_rows)
    value_short = short_forward(extended[2], short_taps[2], tok_rows)
    gating = (key_short * value_short).astype(jnp.bfloat16)
    relayed = (cotangent.astype(jnp.float32) * query_short).astype(jnp.bfloat16)
    gating_wide = gating.astype(jnp.float32)
    relayed_wide = relayed.astype(jnp.float32)
    gating_groups = gating.reshape(tok_rows, groups, members)
    relayed_groups = relayed.reshape(tok_rows, groups, members)
    padded = jnp.concatenate([jnp.zeros((groups, seq_total), jnp.bfloat16), long_filters], axis=1)
    lag_buffer = jnp.zeros((groups, 2 * seq_total), jnp.float32)
    zeros_out = jnp.zeros((tok_rows, groups, members), jnp.float32)

    def target_pair(distance):
        return distance < 0

    totals = (zeros_out, lag_buffer)
    shard_rows = lax.all_gather(gating, "seq", axis=0, tiled=True)
    piece_rows = shard_rows.shape[0]
    step_rows = min(piece_rows, tok_rows)
    pieces = shard_rows.reshape(piece_rows // step_rows, step_rows, groups, members)

    def forward_visit_block(carried, element):
        position, rows_block = element
        source_start = position * step_rows

        def forward_active(partial_value):
            output_part, buffer = partial_value
            output_part = output_part + causal_part(
                padded, rows_block, source_start, own_start, tok_rows, seq_total
            )
            distance = device - source_start // tok_rows
            buffer = lax.cond(
                target_pair(distance),
                lambda held: lag_part(
                    held, relayed_groups, rows_block, own_start, source_start, seq_total
                ),
                lambda held: held,
                buffer,
            )
            return (output_part, buffer)

        carried = lax.cond(
            source_start < own_start + tok_rows,
            forward_active,
            lambda partial_value: partial_value,
            carried,
        )
        return (carried, None)

    totals, ignored = lax.scan(
        forward_visit_block, totals, (jnp.arange(piece_rows // step_rows, dtype=jnp.int32), pieces)
    )
    output_part, lag_buffer = totals
    output_sum = output_part.reshape(tok_rows, chan_width)
    totals = (zeros_out, lag_buffer)
    shard_rows = lax.all_gather(relayed, "seq", axis=0, tiled=True)
    piece_rows = shard_rows.shape[0]
    backward_step_rows = min(piece_rows, tok_rows)
    pieces = shard_rows.reshape(
        piece_rows // backward_step_rows, backward_step_rows, groups, members
    )

    def backward_visit_block(carried, element):
        position, rows_block = element
        target_start = position * backward_step_rows

        def backward_active(partial_value):
            grad_part, buffer = partial_value
            grad_part = grad_part + anti_part(
                padded, rows_block, target_start, own_start, tok_rows, seq_total
            )
            distance = target_start // tok_rows - device
            buffer = lax.cond(
                target_pair(distance),
                lambda held: held,
                lambda held: lag_part(
                    held, rows_block, gating_groups, target_start, own_start, seq_total
                ),
                buffer,
            )
            return (grad_part, buffer)

        carried = lax.cond(
            target_start + backward_step_rows > own_start,
            backward_active,
            lambda partial_value: partial_value,
            carried,
        )
        return (carried, None)

    totals, ignored = lax.scan(
        backward_visit_block,
        totals,
        (jnp.arange(piece_rows // backward_step_rows, dtype=jnp.int32), pieces),
    )
    grad_part, lag_buffer = totals
    grad_sum = grad_part.reshape(tok_rows, chan_width)
    lag_local = lag_buffer[:, seq_total:]
    long_out = output_sum + skip_gain * gating_wide
    block_out = (query_short * long_out).astype(jnp.bfloat16)
    grad_gating = grad_sum + skip_gain * relayed_wide
    cot_wide = cotangent.astype(jnp.float32)
    grad_shorts = [cot_wide * long_out, grad_gating * value_short, grad_gating * key_short]
    lead_rows = jnp.stack([grad_shorts[stream][:margin] for stream in range(3)])
    after = from_behind(lead_rows, "seq", -1)
    input_grads = jnp.stack(
        [
            short_backward(
                jnp.concatenate([grad_shorts[stream], after[stream]]), short_taps[stream], tok_rows
            )
            for stream in range(3)
        ]
    ).astype(jnp.bfloat16)
    tap_local = jnp.stack(
        [
            tap_sums(grad_shorts[stream], extended[stream], tap_count, tok_rows)
            for stream in range(3)
        ]
    )
    skip_local = jnp.sum(relayed_wide * gating_wide, axis=0)
    lag_total, tap_total, skip_total = lax.psum((lag_local, tap_local, skip_local), "seq")
    tap_scale = 1.0 / math.sqrt(seq_total)
    lag_scale = 1.0 / math.sqrt(seq_total * members)
    return (
        block_out,
        input_grads,
        tap_total * tap_scale,
        skip_total * tap_scale,
        lag_total * lag_scale,
    )


def pack_kernel(
    query_ref, key_ref, value_ref, cot_ref, taps_ref, filters_ref, skip_ref,
    out_ref, columns_ref, toeplitz_ref,
    stream_buf, taps_buf, filters_buf, skip_buf, table_buf, sems,
):
    count, _, members, tok_rows = out_ref.shape
    streams, tap_count, chan_width = taps_buf.shape
    groups, seq_total = filters_buf.shape
    mine = lax.axis_index("seq")
    pairs = [
        (filters_ref, filters_buf),
        (taps_ref, taps_buf),
        (skip_ref, skip_buf),
        (query_ref, stream_buf.at[0]),
        (key_ref, stream_buf.at[1]),
        (value_ref, stream_buf.at[2]),
        (cot_ref, stream_buf.at[3]),
    ]
    moves = [
        pltpu.make_async_copy(ref, buf, sems.at[index]) for index, (ref, buf) in enumerate(pairs)
    ]
    for move in moves:
        move.start()
    moves[0].wait()
    chosen = lax.broadcasted_iota(jnp.int32, (groups, 1), 0) == mine
    row = jnp.sum(
        jnp.where(chosen, filters_buf[...].astype(jnp.float32), 0.0), axis=0, keepdims=True
    )
    row = jnp.concatenate([row, jnp.zeros((1, tok_rows), jnp.float32)], axis=1)
    spread = jnp.broadcast_to(row, (tok_rows, seq_total + tok_rows))
    spread = pltpu.roll(spread, 0, 1, stride=1, stride_axis=0)[:, :seq_total]
    toeplitz_ref[...] = spread.astype(jnp.bfloat16)
    moves[1].wait()
    moves[2].wait()
    table = jnp.concatenate(
        [taps_buf[stream] for stream in range(streams)]
        + [skip_buf[...], jnp.zeros((2, chan_width), jnp.float32)],
        axis=0,
    )
    table_buf[...] = table.T
    table = table_buf[pl.ds(pl.multiple_of(mine * members, members), members), :]
    for index in range(streams * tap_count + 1):
        columns_ref[index] = jnp.broadcast_to(table[:, index : index + 1], (members, tok_rows))
    for stream in range(streams + 1):
        moves[3 + stream].wait()
        flipped = stream_buf[stream].astype(jnp.float32).T.astype(jnp.bfloat16)
        out_ref[:, stream] = flipped.reshape(count, members, tok_rows)


def group_kernel(tap_count, in_ref, columns_ref, toeplitz_ref, out_ref, wide_ref):
    count, _, members, span = in_ref.shape
    seq_total = toeplitz_ref.shape[1]
    streams = 3
    rows = count * members
    part = 8
    parts = [slice(first, first + part) for first in range(0, members, part)]
    shape = (count, members, span)
    lane = lax.broadcasted_iota(jnp.int32, (1, part, span), 2)
    masks = [lane >= steps for steps in range(tap_count)]
    masks_end = [lane < span - steps for steps in range(tap_count)]

    def later(value, steps):
        if steps == 0:
            return value
        turned = pltpu.roll(value, steps, 2)
        before = jnp.concatenate([jnp.zeros_like(turned[:1]), turned[:-1]], axis=0)
        return jnp.where(masks[steps], turned, before)

    def earlier(value, steps):
        if steps == 0:
            return value
        turned = pltpu.roll(value, span - steps, 2)
        after = jnp.concatenate([turned[1:], jnp.zeros_like(turned[:1])], axis=0)
        return jnp.where(masks_end[steps], turned, after)

    def short(stream, chans):
        value = in_ref[:, stream].astype(jnp.float32)[:, chans]
        running = columns_ref[stream * tap_count, chans][None] * value
        for offset in range(1, tap_count):
            weight = columns_ref[stream * tap_count + offset, chans][None]
            running = running + weight * later(value, offset)
        return running

    query_short = [short(0, chans) for chans in parts]
    relayed = jnp.concatenate(
        [
            in_ref[:, streams].astype(jnp.float32)[:, chans] * query
            for chans, query in zip(parts, query_short)
        ],
        axis=1,
    )
    relayed = relayed.astype(jnp.bfloat16).reshape(rows, span)
    key_short = [short(1, chans) for chans in parts]
    value_short = [short(2, chans) for chans in parts]
    gating = jnp.concatenate([key * value for key, value in zip(key_short, value_short)], axis=1)
    gating = gating.astype(jnp.bfloat16).reshape(rows, span)

    gap = jnp.zeros((members, span), jnp.bfloat16)
    forward, backward = None, None
    for step in range(0, count, 2):
        kept = rows - step * members
        lanes = [slice(lag * span, (lag + 1) * span) for lag in (step, step + 1)]
        left = jnp.concatenate(
            [gating[:kept], jnp.concatenate([gap, gating[: kept - members]], axis=0)], axis=1
        )
        right = jnp.concatenate([toeplitz_ref[:, lanes[0]], toeplitz_ref[:, lanes[1]]], axis=0)
        term = jnp.dot(left, right, preferred_element_type=jnp.float32)
        left = jnp.concatenate(
            [
                relayed[rows - kept :],
                jnp.concatenate([relayed[rows - kept + members :], gap], axis=0),
            ],
            axis=1,
        )
        right = toeplitz_ref[:, step * span : (step + 2) * span]
        back = lax.dot_general(
            left, right, (((1,), (1,)), ((), ())), preferred_element_type=jnp.float32
        )
        if step == 0:
            forward, backward = term, back
        else:
            forward = jnp.concatenate(
                [forward[: rows - kept], forward[rows - kept :] + term], axis=0
            )
            backward = jnp.concatenate([backward[:kept] + back, backward[kept:]], axis=0)
    forward = forward.reshape(shape)
    backward = backward.reshape(shape)

    flip = (
        lax.broadcasted_iota(jnp.int32, (span, span), 0)
        + lax.broadcasted_iota(jnp.int32, (span, span), 1)
        == span - 1
    ).astype(jnp.bfloat16)
    gating_turned = lax.dot_general(
        flip, gating, (((1,), (1,)), ((), ())), preferred_element_type=jnp.float32
    ).astype(jnp.bfloat16)
    relayed_lags = [relayed]
    for step in range(1, count):
        gap = jnp.zeros((step * members, span), jnp.bfloat16)
        relayed_lags.append(jnp.concatenate([relayed[step * members :], gap], axis=0))
    wide_ref[:, :seq_total] = jnp.dot(
        gating_turned, jnp.concatenate(relayed_lags, axis=1), preferred_element_type=jnp.float32
    )
    wide_ref[:, seq_total:] = jnp.zeros((span, span), jnp.float32)

    tap_scale = 1.0 / math.sqrt(seq_total)
    stat_lane = lax.broadcasted_iota(jnp.int32, (part, span), 1)
    stats_parts, outs = [], [[] for _ in range(streams + 1)]
    for place, chans in enumerate(parts):
        stats = jnp.zeros((part, span), jnp.float32)

        def put(stats, index, product):
            total = jnp.sum(jnp.sum(product, axis=0), axis=1, keepdims=True)
            return jnp.where(stat_lane == index, total, stats)

        gain = columns_ref[streams * tap_count, chans][None]
        gating_wide = gating.astype(jnp.float32).reshape(shape)[:, chans]
        relayed_wide = relayed.astype(jnp.float32).reshape(shape)[:, chans]
        stats = put(stats, streams * tap_count, relayed_wide * gating_wide)
        long_out = forward[:, chans] + gain * gating_wide
        outs[0].append(query_short[place] * long_out)
        grad_gating = backward[:, chans] + gain * relayed_wide
        grad_shorts = [
            in_ref[:, streams].astype(jnp.float32)[:, chans] * long_out,
            grad_gating * value_short[place],
            grad_gating * key_short[place],
        ]
        for stream in range(streams):
            value = in_ref[:, stream].astype(jnp.float32)[:, chans]
            running = None
            for offset in range(tap_count):
                index = stream * tap_count + offset
                moved = earlier(grad_shorts[stream], offset)
                term = columns_ref[index, chans][None] * moved
                running = term if running is None else running + term
                stats = put(stats, index, moved * value)
            outs[1 + stream].append(running)
        stats_parts.append(stats * tap_scale)
    for index, pieces in enumerate(outs):
        out_ref[:, index] = jnp.concatenate(pieces, axis=1).astype(jnp.bfloat16)
    stats = jnp.concatenate(stats_parts, axis=0)

    skewed = pltpu.roll(wide_ref[...], 0, 1, stride=1, stride_axis=0)
    diagonal = jnp.sum(skewed, axis=0, keepdims=True)
    diagonal = pltpu.roll(diagonal, seq_total + 1, 1)[:, :seq_total]
    lag_scale = 1.0 / math.sqrt(seq_total * members)
    lag_sums = jnp.concatenate(
        [diagonal[:, step * span : (step + 1) * span] for step in range(count)], axis=0
    )
    lag_sums = lag_sums * lag_scale

    half = span // 2
    stat_lane = lax.broadcasted_iota(jnp.int32, (members, span), 1)
    stats_high = stats.astype(jnp.bfloat16).astype(jnp.float32)
    stats_low = pltpu.roll(stats - stats_high, half // 2, 1)
    lag_tile = jnp.concatenate([lag_sums, pltpu.roll(lag_sums, half, 1)], axis=0)
    tile = jnp.where(
        stat_lane < half, jnp.where(stat_lane < half // 2, stats_high, stats_low), lag_tile
    )
    out_ref[:, streams + 1] = jnp.broadcast_to(tile.astype(jnp.bfloat16)[None], shape)


def unpack_kernel(in_ref, out_ref, grads_ref, taps_ref, skip_ref, lags_ref):
    count, _, members, span = in_ref.shape
    streams, tap_count, chan_width = taps_ref.shape
    for stream in range(streams + 1):
        block = in_ref[:, stream].reshape(count * members, span).astype(jnp.float32)
        flipped = block.T.astype(jnp.bfloat16)
        if stream == 0:
            out_ref[...] = flipped
        else:
            grads_ref[stream - 1] = flipped
    tile = in_ref[:, streams + 1].astype(jnp.float32)
    stats = tile.reshape(count * members, span)
    stats = (stats + pltpu.roll(stats, span - span // 4, 1)).T
    for stream in range(streams):
        taps_ref[stream] = stats[stream * tap_count : (stream + 1) * tap_count]
    skip_ref[...] = stats[streams * tap_count : streams * tap_count + 1]
    lane = lax.broadcasted_iota(jnp.int32, (1, 1, span), 2)
    lags = jnp.where(
        lane < span // 2, pltpu.roll(tile[:, members // 2 :], span // 2, 2), tile[:, : members // 2]
    )
    for step in range(members // 2):
        lags_ref[:, step * span : (step + 1) * span] = lags[:, step]


def by_group(query_in, key_in, value_in, short_taps, long_filters, skip_gain, cotangent):
    tok_rows, chan_width = query_in.shape
    groups, seq_total = long_filters.shape
    streams, tap_count, _ = short_taps.shape
    members = chan_width // groups
    count = groups
    vmem = pl.BlockSpec(memory_space=pltpu.VMEM)
    params = pltpu.CompilerParams(vmem_limit_bytes=32 * 1024 * 1024)
    rows_padded = streams * tap_count + 3
    packed, columns, toeplitz = pl.pallas_call(
        pack_kernel,
        out_shape=(
            jax.ShapeDtypeStruct((count, streams + 1, members, tok_rows), jnp.bfloat16),
            jax.ShapeDtypeStruct((streams * tap_count + 1, members, tok_rows), jnp.float32),
            jax.ShapeDtypeStruct((tok_rows, seq_total), jnp.bfloat16),
        ),
        in_specs=[pl.BlockSpec(memory_space=pltpu.HBM)] * 7,
        out_specs=(vmem,) * 3,
        scratch_shapes=[
            pltpu.VMEM((streams + 1, tok_rows, chan_width), jnp.bfloat16),
            pltpu.VMEM((streams, tap_count, chan_width), jnp.float32),
            pltpu.VMEM((groups, seq_total), jnp.bfloat16),
            pltpu.VMEM((1, chan_width), jnp.float32),
            pltpu.VMEM((chan_width, rows_padded), jnp.float32),
            pltpu.SemaphoreType.DMA((streams + 4,)),
        ],
        compiler_params=params,
        name="pack",
    )(
        *(
            pltpu.with_memory_space_constraint(value, pltpu.HBM)
            for value in (
                query_in, key_in, value_in, cotangent, short_taps, long_filters,
                skip_gain.reshape(1, chan_width),
            )
        )
    )
    packed = lax.all_to_all(packed, "seq", 0, 0, tiled=True)
    results = pl.pallas_call(
        functools.partial(group_kernel, tap_count),
        out_shape=jax.ShapeDtypeStruct((count, streams + 2, members, tok_rows), jnp.bfloat16),
        in_specs=[vmem] * 3,
        out_specs=vmem,
        scratch_shapes=[pltpu.VMEM((tok_rows, seq_total + tok_rows), jnp.float32)],
        compiler_params=params,
        name="group",
    )(packed, columns, toeplitz)
    results = lax.all_to_all(results, "seq", 0, 0, tiled=True)
    block_out, input_grads, tap_grads, skip_grad, filter_grad = pl.pallas_call(
        unpack_kernel,
        out_shape=(
            jax.ShapeDtypeStruct((tok_rows, chan_width), jnp.bfloat16),
            jax.ShapeDtypeStruct((streams, tok_rows, chan_width), jnp.bfloat16),
            jax.ShapeDtypeStruct((streams, tap_count, chan_width), jnp.float32),
            jax.ShapeDtypeStruct((1, chan_width), jnp.float32),
            jax.ShapeDtypeStruct((groups, seq_total), jnp.float32),
        ),
        in_specs=[vmem],
        out_specs=(vmem,) * 5,
        compiler_params=params,
        name="unpack",
    )(results)
    return block_out, input_grads, tap_grads, skip_grad.reshape(chan_width), filter_grad


def plan(query_in, key_in, value_in, short_taps, long_filters, skip_gain, cotangent):
    tok_rows, chan_width = query_in.shape
    groups, seq_total = long_filters.shape
    tap_rows = short_taps.shape[0] * short_taps.shape[1]
    fits = (
        lax.axis_size("seq") == groups
        and tok_rows == 128
        and chan_width == 128
        and chan_width // groups == 16
        and seq_total == groups * tok_rows
        and tap_rows % 8 == 5
        and tap_rows < 32
    )
    chosen = by_group if fits else local
    return chosen(query_in, key_in, value_in, short_taps, long_filters, skip_gain, cotangent)


def solution(mesh):
    in_specs = (
        P("seq", "chan"),
        P("seq", "chan"),
        P("seq", "chan"),
        P(None, None, "chan"),
        P("chan", None),
        P("chan"),
        P("seq", "chan"),
    )
    out_specs = (
        P("seq", "chan"),
        P(None, "seq", "chan"),
        P(None, None, "chan"),
        P("chan"),
        P("chan", None),
    )
    return jax.shard_map(plan, mesh=mesh, in_specs=in_specs, out_specs=out_specs, check_vma=False)
```

```python
import functools
import math

import jax
import jax.numpy as jnp
from jax import lax
from jax.experimental import pallas as pl
from jax.experimental.pallas import tpu as pltpu
from jax.sharding import PartitionSpec as P


def from_behind(value, axis, steps):
    count = lax.axis_size(axis)
    initial, last = (max(0, -steps), min(count, count - steps))
    return lax.ppermute(value, axis, [(source, source + steps) for source in range(initial, last)])


def short_forward(extended, weights, rows_here):
    margin = weights.shape[0] - 1
    running = jnp.zeros((rows_here, extended.shape[1]), jnp.float32)
    for offset in range(weights.shape[0]):
        running = (
            running + weights[offset] * extended[margin - offset : margin - offset + rows_here]
        )
    return running


def short_backward(extended, weights, rows_here):
    running = jnp.zeros((rows_here, extended.shape[1]), jnp.float32)
    for offset in range(weights.shape[0]):
        running = running + weights[offset] * extended[offset : offset + rows_here]
    return running


def tap_sums(grad_rows, extended, tap_count, rows_here):
    margin = tap_count - 1
    sums_list = []
    for offset in range(tap_count):
        sums_list.append(
            jnp.sum(grad_rows * extended[margin - offset : margin - offset + rows_here], axis=0)
        )
    return jnp.stack(sums_list)


def hankel(padded, lag_start, height, breadth, seq_total):
    span = height + breadth - 1
    window = lax.dynamic_slice_in_dim(padded, lag_start + seq_total, span, axis=1)
    tiled = jnp.tile(window, (1, height))
    tiled = jnp.pad(tiled, ((0, 0), (0, height)))
    return tiled.reshape(padded.shape[0], height, span + 1)[:, :, :breadth]


def causal_part(padded, source_rows, source_start, target_start, target_count, seq_total):
    breadth = source_rows.shape[0]
    matrix = hankel(
        padded, target_start - source_start - breadth + 1, target_count, breadth, seq_total
    )
    return jnp.einsum("gts,sgc->tgc", matrix, source_rows[::-1], preferred_element_type=jnp.float32)


def anti_part(padded, target_rows, target_start, source_start, source_count, seq_total):
    breadth = target_rows.shape[0]
    matrix = hankel(
        padded, target_start - source_start - source_count + 1, source_count, breadth, seq_total
    )
    return jnp.einsum("gab,bgc->agc", matrix, target_rows, preferred_element_type=jnp.float32)[::-1]


def lag_part(buffer, target_rows, source_rows, target_start, source_start, seq_total):
    height = target_rows.shape[0]
    breadth = source_rows.shape[0]
    groups = target_rows.shape[1]
    padded_source = jnp.pad(source_rows[::-1], ((0, height), (0, 0), (0, 0)))
    products = jnp.einsum(
        "tgc,sgc->gts", target_rows, padded_source, preferred_element_type=jnp.float32
    )
    full_width = height + breadth
    skewed = products.reshape(groups, height * full_width)[:, : height * (full_width - 1)]
    skewed = skewed.reshape(groups, height, full_width - 1)
    diagonal = jnp.sum(skewed, axis=1)
    position = target_start - source_start - breadth + 1 + seq_total
    current = lax.dynamic_slice_in_dim(buffer, position, full_width - 1, axis=1)
    return lax.dynamic_update_slice_in_dim(buffer, current + diagonal, position, axis=1)


def local(query_in, key_in, value_in, short_taps, long_filters, skip_gain, cotangent):
    tok_rows, chan_width = query_in.shape
    groups, seq_total = long_filters.shape
    members = chan_width // groups
    tap_count = short_taps.shape[1]
    margin = tap_count - 1
    device = lax.axis_index("seq")
    own_start = device * tok_rows
    rim_rows = jnp.stack(
        [query_in[tok_rows - margin :], key_in[tok_rows - margin :], value_in[tok_rows - margin :]]
    )
    before = from_behind(rim_rows, "seq", 1)
    streams = [query_in, key_in, value_in]
    extended = [
        jnp.concatenate([before[stream], streams[stream]]).astype(jnp.float32)
        for stream in range(3)
    ]
    query_short = short_forward(extended[0], short_taps[0], tok_rows)
    key_short = short_forward(extended[1], short_taps[1], tok_rows)
    value_short = short_forward(extended[2], short_taps[2], tok_rows)
    gating = (key_short * value_short).astype(jnp.bfloat16)
    relayed = (cotangent.astype(jnp.float32) * query_short).astype(jnp.bfloat16)
    gating_wide = gating.astype(jnp.float32)
    relayed_wide = relayed.astype(jnp.float32)
    gating_groups = gating.reshape(tok_rows, groups, members)
    relayed_groups = relayed.reshape(tok_rows, groups, members)
    padded = jnp.concatenate([jnp.zeros((groups, seq_total), jnp.bfloat16), long_filters], axis=1)
    lag_buffer = jnp.zeros((groups, 2 * seq_total), jnp.float32)
    zeros_out = jnp.zeros((tok_rows, groups, members), jnp.float32)

    def target_pair(distance):
        return distance < 0

    totals = (zeros_out, lag_buffer)
    shard_rows = lax.all_gather(gating, "seq", axis=0, tiled=True)
    piece_rows = shard_rows.shape[0]
    step_rows = min(piece_rows, tok_rows)
    pieces = shard_rows.reshape(piece_rows // step_rows, step_rows, groups, members)

    def forward_visit_block(carried, element):
        position, rows_block = element
        source_start = position * step_rows

        def forward_active(partial_value):
            output_part, buffer = partial_value
            output_part = output_part + causal_part(
                padded, rows_block, source_start, own_start, tok_rows, seq_total
            )
            distance = device - source_start // tok_rows
            buffer = lax.cond(
                target_pair(distance),
                lambda held: lag_part(
                    held, relayed_groups, rows_block, own_start, source_start, seq_total
                ),
                lambda held: held,
                buffer,
            )
            return (output_part, buffer)

        carried = lax.cond(
            source_start < own_start + tok_rows,
            forward_active,
            lambda partial_value: partial_value,
            carried,
        )
        return (carried, None)

    totals, ignored = lax.scan(
        forward_visit_block, totals, (jnp.arange(piece_rows // step_rows, dtype=jnp.int32), pieces)
    )
    output_part, lag_buffer = totals
    output_sum = output_part.reshape(tok_rows, chan_width)
    totals = (zeros_out, lag_buffer)
    shard_rows = lax.all_gather(relayed, "seq", axis=0, tiled=True)
    piece_rows = shard_rows.shape[0]
    backward_step_rows = min(piece_rows, tok_rows)
    pieces = shard_rows.reshape(
        piece_rows // backward_step_rows, backward_step_rows, groups, members
    )

    def backward_visit_block(carried, element):
        position, rows_block = element
        target_start = position * backward_step_rows

        def backward_active(partial_value):
            grad_part, buffer = partial_value
            grad_part = grad_part + anti_part(
                padded, rows_block, target_start, own_start, tok_rows, seq_total
            )
            distance = target_start // tok_rows - device
            buffer = lax.cond(
                target_pair(distance),
                lambda held: held,
                lambda held: lag_part(
                    held, rows_block, gating_groups, target_start, own_start, seq_total
                ),
                buffer,
            )
            return (grad_part, buffer)

        carried = lax.cond(
            target_start + backward_step_rows > own_start,
            backward_active,
            lambda partial_value: partial_value,
            carried,
        )
        return (carried, None)

    totals, ignored = lax.scan(
        backward_visit_block,
        totals,
        (jnp.arange(piece_rows // backward_step_rows, dtype=jnp.int32), pieces),
    )
    grad_part, lag_buffer = totals
    grad_sum = grad_part.reshape(tok_rows, chan_width)
    lag_local = lag_buffer[:, seq_total:]
    long_out = output_sum + skip_gain * gating_wide
    block_out = (query_short * long_out).astype(jnp.bfloat16)
    grad_gating = grad_sum + skip_gain * relayed_wide
    cot_wide = cotangent.astype(jnp.float32)
    grad_shorts = [cot_wide * long_out, grad_gating * value_short, grad_gating * key_short]
    lead_rows = jnp.stack([grad_shorts[stream][:margin] for stream in range(3)])
    after = from_behind(lead_rows, "seq", -1)
    input_grads = jnp.stack(
        [
            short_backward(
                jnp.concatenate([grad_shorts[stream], after[stream]]), short_taps[stream], tok_rows
            )
            for stream in range(3)
        ]
    ).astype(jnp.bfloat16)
    tap_local = jnp.stack(
        [
            tap_sums(grad_shorts[stream], extended[stream], tap_count, tok_rows)
            for stream in range(3)
        ]
    )
    skip_local = jnp.sum(relayed_wide * gating_wide, axis=0)
    lag_total, tap_total, skip_total = lax.psum((lag_local, tap_local, skip_local), "seq")
    tap_scale = 1.0 / math.sqrt(seq_total)
    lag_scale = 1.0 / math.sqrt(seq_total * members)
    return (
        block_out,
        input_grads,
        tap_total * tap_scale,
        skip_total * tap_scale,
        lag_total * lag_scale,
    )


def pack_kernel(
    query_ref, key_ref, value_ref, cot_ref, skip_ref, out_ref, gain_ref, stream_buf, sems
):
    count, streams, members, tok_rows = out_ref.shape
    moves = [
        pltpu.make_async_copy(ref, stream_buf.at[stream], sems.at[stream])
        for stream, ref in enumerate((query_ref, key_ref, value_ref, cot_ref))
    ]
    moves.append(pltpu.make_async_copy(skip_ref, gain_ref, sems.at[streams]))
    for move in moves:
        move.start()
    for stream in range(streams):
        moves[stream].wait()
        flipped = stream_buf[stream].astype(jnp.float32).T.astype(jnp.bfloat16)
        out_ref[:, stream] = flipped.reshape(count, members, tok_rows)
    moves[streams].wait()


def group_kernel(in_ref, taps_ref, filters_ref, gain_ref, out_ref, table_ref, wide_ref):
    count, _, members, span = in_ref.shape
    groups, seq_total = filters_ref.shape
    streams, tap_count, chan_width = taps_ref.shape
    rows = count * members
    mine = lax.axis_index("seq")
    shape = (count, members, span)
    lane = lax.broadcasted_iota(jnp.int32, shape, 2)
    reach = 3

    def later(value, steps):
        if steps == 0:
            return value
        turned = pltpu.roll(value, steps, 2)
        before = jnp.concatenate([jnp.zeros_like(turned[:1]), turned[:-1]], axis=0)
        return jnp.where(lane >= steps, turned, before)

    def earlier(value, steps):
        if steps == 0:
            return value
        turned = pltpu.roll(value, span - steps, 2)
        after = jnp.concatenate([turned[1:], jnp.zeros_like(turned[:1])], axis=0)
        return jnp.where(lane < span - steps, turned, after)

    table = jnp.concatenate(
        [taps_ref[stream] for stream in range(streams)]
        + [gain_ref[...], jnp.zeros((2, chan_width), jnp.float32)],
        axis=0,
    )
    table_ref[...] = table.T
    params = table_ref[pl.ds(pl.multiple_of(mine * members, members), members), :]

    def column(index):
        return jnp.broadcast_to(params[:, index : index + 1], (members, span))[None]

    chosen = lax.broadcasted_iota(jnp.int32, (groups, 1), 0) == mine
    filter_row = jnp.sum(
        jnp.where(chosen, filters_ref[...].astype(jnp.float32), 0.0), axis=0, keepdims=True
    )
    filter_row = jnp.concatenate([filter_row, jnp.zeros((1, span), jnp.float32)], axis=1)
    spread = jnp.broadcast_to(filter_row, (span, seq_total + span))
    toeplitz = pltpu.roll(spread, 0, 1, stride=1, stride_axis=0)[:, :seq_total]
    toeplitz = toeplitz.astype(jnp.bfloat16)

    cot = in_ref[:, streams].astype(jnp.float32)
    delayed, shorts = [], []
    for stream in range(streams):
        value = in_ref[:, stream]
        delayed.append([later(value, first) for first in range(0, tap_count, reach)])
        running = None
        for second in reversed(range(reach)):
            if running is not None:
                running = later(running, 1)
            for first in range(second, tap_count, reach):
                term = column(stream * tap_count + first) * delayed[stream][
                    first // reach
                ].astype(jnp.float32)
                running = term if running is None else running + term
        shorts.append(running)
    query_short, key_short, value_short = shorts
    gating = (key_short * value_short).astype(jnp.bfloat16).reshape(rows, span)
    relayed = (cot * query_short).astype(jnp.bfloat16).reshape(rows, span)

    gating_parts, relayed_parts, filter_parts = [gating], [relayed], [toeplitz[:, :span]]
    for step in range(1, count):
        gap = jnp.zeros((step * members, span), jnp.bfloat16)
        gating_parts.append(jnp.concatenate([gap, gating[: rows - step * members]], axis=0))
        relayed_parts.append(jnp.concatenate([relayed[step * members :], gap], axis=0))
        filter_parts.append(toeplitz[:, step * span : (step + 1) * span])
    gating_lags = jnp.concatenate(gating_parts, axis=1)
    relayed_lags = jnp.concatenate(relayed_parts, axis=1)
    forward = jnp.dot(
        gating_lags, jnp.concatenate(filter_parts, axis=0), preferred_element_type=jnp.float32
    )
    backward = lax.dot_general(
        relayed_lags, toeplitz, (((1,), (1,)), ((), ())), preferred_element_type=jnp.float32
    )
    flip = (
        lax.broadcasted_iota(jnp.int32, (span, span), 0)
        + lax.broadcasted_iota(jnp.int32, (span, span), 1)
        == span - 1
    ).astype(jnp.bfloat16)
    gating_turned = lax.dot_general(
        flip, gating, (((1,), (1,)), ((), ())), preferred_element_type=jnp.float32
    ).astype(jnp.bfloat16)
    products = jnp.dot(gating_turned, relayed_lags, preferred_element_type=jnp.float32)
    wide_ref[:, :seq_total] = products
    wide_ref[:, seq_total:] = jnp.zeros((span, span), jnp.float32)
    skewed = pltpu.roll(wide_ref[...], 0, 1, stride=1, stride_axis=0)
    diagonal = jnp.sum(skewed, axis=0, keepdims=True)
    diagonal = pltpu.roll(diagonal, seq_total + 1, 1)[:, :seq_total]
    lag_scale = 1.0 / math.sqrt(seq_total * members)
    lag_sums = jnp.concatenate(
        [diagonal[:, step * span : (step + 1) * span] for step in range(count)], axis=0
    )
    lag_sums = lag_sums * lag_scale

    gating_wide = gating.astype(jnp.float32).reshape(shape)
    relayed_wide = relayed.astype(jnp.float32).reshape(shape)
    gain = column(streams * tap_count)
    long_out = forward.reshape(shape) + gain * gating_wide
    grad_gating = backward.reshape(shape) + gain * relayed_wide
    out_ref[:, 0] = (query_short * long_out).astype(jnp.bfloat16)
    grad_shorts = [cot * long_out, grad_gating * value_short, grad_gating * key_short]
    tap_scale = 1.0 / math.sqrt(seq_total)
    stats = jnp.zeros((members, span), jnp.float32)
    stat_lane = lax.broadcasted_iota(jnp.int32, (members, span), 1)

    def put(stats, index, product):
        total = jnp.sum(jnp.sum(product, axis=0), axis=1, keepdims=True)
        return jnp.where(stat_lane == index, total, stats)

    for stream in range(streams):
        moved = [earlier(grad_shorts[stream], second) for second in range(reach)]
        running = None
        for place in reversed(range(len(delayed[stream]))):
            if running is not None:
                running = earlier(running, reach)
            value = delayed[stream][place].astype(jnp.float32)
            for second in range(min(reach, tap_count - reach * place)):
                index = stream * tap_count + reach * place + second
                term = column(index) * moved[second]
                running = term if running is None else running + term
                stats = put(stats, index, moved[second] * value)
        out_ref[:, 1 + stream] = running.astype(jnp.bfloat16)
    stats = put(stats, streams * tap_count, relayed_wide * gating_wide) * tap_scale

    half = span // 2
    stats_high = stats.astype(jnp.bfloat16).astype(jnp.float32)
    stats_low = pltpu.roll(stats - stats_high, half // 2, 1)
    lag_tile = jnp.concatenate([lag_sums, pltpu.roll(lag_sums, half, 1)], axis=0)
    tile = jnp.where(
        stat_lane < half, jnp.where(stat_lane < half // 2, stats_high, stats_low), lag_tile
    )
    out_ref[:, streams + 1] = jnp.broadcast_to(tile.astype(jnp.bfloat16)[None], shape)


def unpack_kernel(in_ref, out_ref, grads_ref, taps_ref, skip_ref, lags_ref):
    count, _, members, span = in_ref.shape
    streams, tap_count, chan_width = taps_ref.shape
    for stream in range(streams + 1):
        block = in_ref[:, stream].reshape(count * members, span).astype(jnp.float32)
        flipped = block.T.astype(jnp.bfloat16)
        if stream == 0:
            out_ref[...] = flipped
        else:
            grads_ref[stream - 1] = flipped
    tile = in_ref[:, streams + 1].astype(jnp.float32)
    stats = tile.reshape(count * members, span)
    stats = (stats + pltpu.roll(stats, span - span // 4, 1)).T
    for stream in range(streams):
        taps_ref[stream] = stats[stream * tap_count : (stream + 1) * tap_count]
    skip_ref[...] = stats[streams * tap_count : streams * tap_count + 1]
    lane = lax.broadcasted_iota(jnp.int32, (1, 1, span), 2)
    lags = jnp.where(
        lane < span // 2, pltpu.roll(tile[:, members // 2 :], span // 2, 2), tile[:, : members // 2]
    )
    for step in range(members // 2):
        lags_ref[:, step * span : (step + 1) * span] = lags[:, step]


def by_group(query_in, key_in, value_in, short_taps, long_filters, skip_gain, cotangent):
    tok_rows, chan_width = query_in.shape
    groups, seq_total = long_filters.shape
    streams, tap_count, _ = short_taps.shape
    members = chan_width // groups
    count = groups
    vmem = pl.BlockSpec(memory_space=pltpu.VMEM)
    params = pltpu.CompilerParams(vmem_limit_bytes=32 * 1024 * 1024)
    packed, gain = pl.pallas_call(
        pack_kernel,
        out_shape=(
            jax.ShapeDtypeStruct((count, streams + 1, members, tok_rows), jnp.bfloat16),
            jax.ShapeDtypeStruct((1, chan_width), jnp.float32),
        ),
        in_specs=[pl.BlockSpec(memory_space=pltpu.HBM)] * 5,
        out_specs=(vmem,) * 2,
        scratch_shapes=[
            pltpu.VMEM((streams + 1, tok_rows, chan_width), jnp.bfloat16),
            pltpu.SemaphoreType.DMA((streams + 2,)),
        ],
        compiler_params=params,
        name="pack",
    )(
        *(
            pltpu.with_memory_space_constraint(value, pltpu.HBM)
            for value in (
                query_in, key_in, value_in, cotangent, skip_gain.reshape(1, chan_width)
            )
        )
    )
    packed = lax.all_to_all(packed, "seq", 0, 0, tiled=True)
    results = pl.pallas_call(
        group_kernel,
        out_shape=jax.ShapeDtypeStruct((count, streams + 2, members, tok_rows), jnp.bfloat16),
        in_specs=[vmem] * 4,
        out_specs=vmem,
        scratch_shapes=[
            pltpu.VMEM((chan_width, streams * tap_count + 3), jnp.float32),
            pltpu.VMEM((tok_rows, seq_total + tok_rows), jnp.float32),
        ],
        compiler_params=params,
        name="group",
    )(packed, short_taps, long_filters, gain)
    results = lax.all_to_all(results, "seq", 0, 0, tiled=True)
    block_out, input_grads, tap_grads, skip_grad, filter_grad = pl.pallas_call(
        unpack_kernel,
        out_shape=(
            jax.ShapeDtypeStruct((tok_rows, chan_width), jnp.bfloat16),
            jax.ShapeDtypeStruct((streams, tok_rows, chan_width), jnp.bfloat16),
            jax.ShapeDtypeStruct((streams, tap_count, chan_width), jnp.float32),
            jax.ShapeDtypeStruct((1, chan_width), jnp.float32),
            jax.ShapeDtypeStruct((groups, seq_total), jnp.float32),
        ),
        in_specs=[vmem],
        out_specs=(vmem,) * 5,
        compiler_params=params,
        name="unpack",
    )(results)
    return block_out, input_grads, tap_grads, skip_grad.reshape(chan_width), filter_grad


def plan(query_in, key_in, value_in, short_taps, long_filters, skip_gain, cotangent):
    tok_rows, chan_width = query_in.shape
    groups, seq_total = long_filters.shape
    tap_rows = short_taps.shape[0] * short_taps.shape[1]
    fits = (
        lax.axis_size("seq") == groups
        and tok_rows == 128
        and chan_width == 128
        and chan_width // groups == 16
        and seq_total == groups * tok_rows
        and tap_rows % 8 == 5
        and tap_rows < 32
    )
    chosen = by_group if fits else local
    return chosen(query_in, key_in, value_in, short_taps, long_filters, skip_gain, cotangent)


def solution(mesh):
    in_specs = (
        P("seq", "chan"),
        P("seq", "chan"),
        P("seq", "chan"),
        P(None, None, "chan"),
        P("chan", None),
        P("chan"),
        P("seq", "chan"),
    )
    out_specs = (
        P("seq", "chan"),
        P(None, "seq", "chan"),
        P(None, None, "chan"),
        P("chan"),
        P("chan", None),
    )
    return jax.shard_map(plan, mesh=mesh, in_specs=in_specs, out_specs=out_specs, check_vma=False)
```

```python
import functools
import math

import jax
import jax.numpy as jnp
from jax import lax
from jax.experimental import pallas as pl
from jax.experimental.pallas import tpu as pltpu
from jax.sharding import PartitionSpec as P


def from_behind(value, axis, steps):
    count = lax.axis_size(axis)
    initial, last = (max(0, -steps), min(count, count - steps))
    return lax.ppermute(value, axis, [(source, source + steps) for source in range(initial, last)])


def short_forward(extended, weights, rows_here):
    margin = weights.shape[0] - 1
    running = jnp.zeros((rows_here, extended.shape[1]), jnp.float32)
    for offset in range(weights.shape[0]):
        running = (
            running + weights[offset] * extended[margin - offset : margin - offset + rows_here]
        )
    return running


def short_backward(extended, weights, rows_here):
    running = jnp.zeros((rows_here, extended.shape[1]), jnp.float32)
    for offset in range(weights.shape[0]):
        running = running + weights[offset] * extended[offset : offset + rows_here]
    return running


def tap_sums(grad_rows, extended, tap_count, rows_here):
    margin = tap_count - 1
    sums_list = []
    for offset in range(tap_count):
        sums_list.append(
            jnp.sum(grad_rows * extended[margin - offset : margin - offset + rows_here], axis=0)
        )
    return jnp.stack(sums_list)


def hankel(padded, lag_start, height, breadth, seq_total):
    span = height + breadth - 1
    window = lax.dynamic_slice_in_dim(padded, lag_start + seq_total, span, axis=1)
    tiled = jnp.tile(window, (1, height))
    tiled = jnp.pad(tiled, ((0, 0), (0, height)))
    return tiled.reshape(padded.shape[0], height, span + 1)[:, :, :breadth]


def causal_part(padded, source_rows, source_start, target_start, target_count, seq_total):
    breadth = source_rows.shape[0]
    matrix = hankel(
        padded, target_start - source_start - breadth + 1, target_count, breadth, seq_total
    )
    return jnp.einsum("gts,sgc->tgc", matrix, source_rows[::-1], preferred_element_type=jnp.float32)


def anti_part(padded, target_rows, target_start, source_start, source_count, seq_total):
    breadth = target_rows.shape[0]
    matrix = hankel(
        padded, target_start - source_start - source_count + 1, source_count, breadth, seq_total
    )
    return jnp.einsum("gab,bgc->agc", matrix, target_rows, preferred_element_type=jnp.float32)[::-1]


def lag_part(buffer, target_rows, source_rows, target_start, source_start, seq_total):
    height = target_rows.shape[0]
    breadth = source_rows.shape[0]
    groups = target_rows.shape[1]
    padded_source = jnp.pad(source_rows[::-1], ((0, height), (0, 0), (0, 0)))
    products = jnp.einsum(
        "tgc,sgc->gts", target_rows, padded_source, preferred_element_type=jnp.float32
    )
    full_width = height + breadth
    skewed = products.reshape(groups, height * full_width)[:, : height * (full_width - 1)]
    skewed = skewed.reshape(groups, height, full_width - 1)
    diagonal = jnp.sum(skewed, axis=1)
    position = target_start - source_start - breadth + 1 + seq_total
    current = lax.dynamic_slice_in_dim(buffer, position, full_width - 1, axis=1)
    return lax.dynamic_update_slice_in_dim(buffer, current + diagonal, position, axis=1)


def local(query_in, key_in, value_in, short_taps, long_filters, skip_gain, cotangent):
    tok_rows, chan_width = query_in.shape
    groups, seq_total = long_filters.shape
    members = chan_width // groups
    tap_count = short_taps.shape[1]
    margin = tap_count - 1
    device = lax.axis_index("seq")
    own_start = device * tok_rows
    rim_rows = jnp.stack(
        [query_in[tok_rows - margin :], key_in[tok_rows - margin :], value_in[tok_rows - margin :]]
    )
    before = from_behind(rim_rows, "seq", 1)
    streams = [query_in, key_in, value_in]
    extended = [
        jnp.concatenate([before[stream], streams[stream]]).astype(jnp.float32)
        for stream in range(3)
    ]
    query_short = short_forward(extended[0], short_taps[0], tok_rows)
    key_short = short_forward(extended[1], short_taps[1], tok_rows)
    value_short = short_forward(extended[2], short_taps[2], tok_rows)
    gating = (key_short * value_short).astype(jnp.bfloat16)
    relayed = (cotangent.astype(jnp.float32) * query_short).astype(jnp.bfloat16)
    gating_wide = gating.astype(jnp.float32)
    relayed_wide = relayed.astype(jnp.float32)
    gating_groups = gating.reshape(tok_rows, groups, members)
    relayed_groups = relayed.reshape(tok_rows, groups, members)
    padded = jnp.concatenate([jnp.zeros((groups, seq_total), jnp.bfloat16), long_filters], axis=1)
    lag_buffer = jnp.zeros((groups, 2 * seq_total), jnp.float32)
    zeros_out = jnp.zeros((tok_rows, groups, members), jnp.float32)

    def target_pair(distance):
        return distance < 0

    totals = (zeros_out, lag_buffer)
    shard_rows = lax.all_gather(gating, "seq", axis=0, tiled=True)
    piece_rows = shard_rows.shape[0]
    step_rows = min(piece_rows, tok_rows)
    pieces = shard_rows.reshape(piece_rows // step_rows, step_rows, groups, members)

    def forward_visit_block(carried, element):
        position, rows_block = element
        source_start = position * step_rows

        def forward_active(partial_value):
            output_part, buffer = partial_value
            output_part = output_part + causal_part(
                padded, rows_block, source_start, own_start, tok_rows, seq_total
            )
            distance = device - source_start // tok_rows
            buffer = lax.cond(
                target_pair(distance),
                lambda held: lag_part(
                    held, relayed_groups, rows_block, own_start, source_start, seq_total
                ),
                lambda held: held,
                buffer,
            )
            return (output_part, buffer)

        carried = lax.cond(
            source_start < own_start + tok_rows,
            forward_active,
            lambda partial_value: partial_value,
            carried,
        )
        return (carried, None)

    totals, ignored = lax.scan(
        forward_visit_block, totals, (jnp.arange(piece_rows // step_rows, dtype=jnp.int32), pieces)
    )
    output_part, lag_buffer = totals
    output_sum = output_part.reshape(tok_rows, chan_width)
    totals = (zeros_out, lag_buffer)
    shard_rows = lax.all_gather(relayed, "seq", axis=0, tiled=True)
    piece_rows = shard_rows.shape[0]
    backward_step_rows = min(piece_rows, tok_rows)
    pieces = shard_rows.reshape(
        piece_rows // backward_step_rows, backward_step_rows, groups, members
    )

    def backward_visit_block(carried, element):
        position, rows_block = element
        target_start = position * backward_step_rows

        def backward_active(partial_value):
            grad_part, buffer = partial_value
            grad_part = grad_part + anti_part(
                padded, rows_block, target_start, own_start, tok_rows, seq_total
            )
            distance = target_start // tok_rows - device
            buffer = lax.cond(
                target_pair(distance),
                lambda held: held,
                lambda held: lag_part(
                    held, rows_block, gating_groups, target_start, own_start, seq_total
                ),
                buffer,
            )
            return (grad_part, buffer)

        carried = lax.cond(
            target_start + backward_step_rows > own_start,
            backward_active,
            lambda partial_value: partial_value,
            carried,
        )
        return (carried, None)

    totals, ignored = lax.scan(
        backward_visit_block,
        totals,
        (jnp.arange(piece_rows // backward_step_rows, dtype=jnp.int32), pieces),
    )
    grad_part, lag_buffer = totals
    grad_sum = grad_part.reshape(tok_rows, chan_width)
    lag_local = lag_buffer[:, seq_total:]
    long_out = output_sum + skip_gain * gating_wide
    block_out = (query_short * long_out).astype(jnp.bfloat16)
    grad_gating = grad_sum + skip_gain * relayed_wide
    cot_wide = cotangent.astype(jnp.float32)
    grad_shorts = [cot_wide * long_out, grad_gating * value_short, grad_gating * key_short]
    lead_rows = jnp.stack([grad_shorts[stream][:margin] for stream in range(3)])
    after = from_behind(lead_rows, "seq", -1)
    input_grads = jnp.stack(
        [
            short_backward(
                jnp.concatenate([grad_shorts[stream], after[stream]]), short_taps[stream], tok_rows
            )
            for stream in range(3)
        ]
    ).astype(jnp.bfloat16)
    tap_local = jnp.stack(
        [
            tap_sums(grad_shorts[stream], extended[stream], tap_count, tok_rows)
            for stream in range(3)
        ]
    )
    skip_local = jnp.sum(relayed_wide * gating_wide, axis=0)
    lag_total, tap_total, skip_total = lax.psum((lag_local, tap_local, skip_local), "seq")
    tap_scale = 1.0 / math.sqrt(seq_total)
    lag_scale = 1.0 / math.sqrt(seq_total * members)
    return (
        block_out,
        input_grads,
        tap_total * tap_scale,
        skip_total * tap_scale,
        lag_total * lag_scale,
    )


def pack_kernel(
    query_ref, key_ref, value_ref, cot_ref, skip_ref, out_ref, gain_ref, stream_buf, sems
):
    count, streams, members, tok_rows = out_ref.shape
    moves = [
        pltpu.make_async_copy(ref, stream_buf.at[stream], sems.at[stream])
        for stream, ref in enumerate((query_ref, key_ref, value_ref, cot_ref))
    ]
    moves.append(pltpu.make_async_copy(skip_ref, gain_ref, sems.at[streams]))
    for move in moves:
        move.start()
    for stream in range(streams):
        moves[stream].wait()
        flipped = stream_buf[stream].astype(jnp.float32).T.astype(jnp.bfloat16)
        out_ref[:, stream] = flipped.reshape(count, members, tok_rows)
    moves[streams].wait()


def group_kernel(in_ref, taps_ref, filters_ref, gain_ref, out_ref, table_ref, wide_ref):
    count, _, members, span = in_ref.shape
    groups, seq_total = filters_ref.shape
    streams, tap_count, chan_width = taps_ref.shape
    rows = count * members
    mine = lax.axis_index("seq")
    shape = (count, members, span)
    lane = lax.broadcasted_iota(jnp.int32, shape, 2)
    reach = 3

    def later(value, steps):
        if steps == 0:
            return value
        turned = pltpu.roll(value, steps, 2)
        before = jnp.concatenate([jnp.zeros_like(turned[:1]), turned[:-1]], axis=0)
        return jnp.where(lane >= steps, turned, before)

    def earlier(value, steps):
        if steps == 0:
            return value
        turned = pltpu.roll(value, span - steps, 2)
        after = jnp.concatenate([turned[1:], jnp.zeros_like(turned[:1])], axis=0)
        return jnp.where(lane < span - steps, turned, after)

    table = jnp.concatenate(
        [taps_ref[stream] for stream in range(streams)]
        + [gain_ref[...], jnp.zeros((2, chan_width), jnp.float32)],
        axis=0,
    )
    table_ref[...] = table.T
    params = table_ref[pl.ds(pl.multiple_of(mine * members, members), members), :]

    def column(index):
        return jnp.broadcast_to(params[:, index : index + 1], (members, span))[None]

    chosen = lax.broadcasted_iota(jnp.int32, (groups, 1), 0) == mine
    filter_row = jnp.sum(
        jnp.where(chosen, filters_ref[...].astype(jnp.float32), 0.0), axis=0, keepdims=True
    )
    filter_row = jnp.concatenate([filter_row, jnp.zeros((1, span), jnp.float32)], axis=1)
    spread = jnp.broadcast_to(filter_row, (members, seq_total + span))
    first_rows = pltpu.roll(spread, 0, 1, stride=1, stride_axis=0).astype(jnp.bfloat16)
    row_parts = [first_rows] + [
        pltpu.roll(first_rows, first, 1) for first in range(members, span, members)
    ]
    toeplitz = jnp.concatenate(row_parts, axis=0)[:, :seq_total]

    cot = in_ref[:, streams].astype(jnp.float32)
    delayed, shorts = [], []
    for stream in range(streams):
        value = in_ref[:, stream]
        delayed.append([later(value, first) for first in range(0, tap_count, reach)])
        running = None
        for second in reversed(range(reach)):
            if running is not None:
                running = later(running, 1)
            for first in range(second, tap_count, reach):
                term = column(stream * tap_count + first) * delayed[stream][
                    first // reach
                ].astype(jnp.float32)
                running = term if running is None else running + term
        shorts.append(running)
    query_short, key_short, value_short = shorts
    gating = (key_short * value_short).astype(jnp.bfloat16).reshape(rows, span)
    relayed = (cot * query_short).astype(jnp.bfloat16).reshape(rows, span)

    gating_parts, relayed_parts, filter_parts = [gating], [relayed], [toeplitz[:, :span]]
    for step in range(1, count):
        gap = jnp.zeros((step * members, span), jnp.bfloat16)
        gating_parts.append(jnp.concatenate([gap, gating[: rows - step * members]], axis=0))
        relayed_parts.append(jnp.concatenate([relayed[step * members :], gap], axis=0))
        filter_parts.append(toeplitz[:, step * span : (step + 1) * span])
    gating_lags = jnp.concatenate(gating_parts, axis=1)
    relayed_lags = jnp.concatenate(relayed_parts, axis=1)
    forward = jnp.dot(
        gating_lags, jnp.concatenate(filter_parts, axis=0), preferred_element_type=jnp.float32
    )
    backward = lax.dot_general(
        relayed_lags, toeplitz, (((1,), (1,)), ((), ())), preferred_element_type=jnp.float32
    )
    half = span // 2
    flip = (
        lax.broadcasted_iota(jnp.int32, (span, span), 0)
        + lax.broadcasted_iota(jnp.int32, (span, span), 1)
        == span - 1
    ).astype(jnp.bfloat16)
    gating_turned = lax.dot_general(
        flip, gating, (((1,), (1,)), ((), ())), preferred_element_type=jnp.float32
    ).astype(jnp.bfloat16)
    gating_turned = jnp.concatenate([gating_turned[half:], gating_turned[:half]], axis=1)
    ahead = earlier(relayed.reshape(shape), half).reshape(rows, span)
    ahead_parts = [ahead]
    for step in range(1, count):
        gap = jnp.zeros((step * members, span), jnp.bfloat16)
        ahead_parts.append(jnp.concatenate([ahead[step * members :], gap], axis=0))
    targets = jnp.concatenate([relayed_lags, jnp.concatenate(ahead_parts, axis=1)], axis=0)
    products = jnp.dot(gating_turned, targets, preferred_element_type=jnp.float32)
    wide_ref[:, :seq_total] = products
    wide_ref[:, seq_total:] = jnp.zeros((half, span), jnp.float32)
    skewed = pltpu.roll(wide_ref[...], 0, 1, stride=1, stride_axis=0)
    diagonal = jnp.sum(skewed, axis=0, keepdims=True)
    diagonal = pltpu.roll(diagonal, seq_total + span - half + 1, 1)[:, :seq_total]
    lag_scale = 1.0 / math.sqrt(seq_total * members)
    lag_sums = jnp.concatenate(
        [diagonal[:, step * span : (step + 1) * span] for step in range(count)], axis=0
    )
    lag_sums = lag_sums * lag_scale

    gating_wide = gating.astype(jnp.float32).reshape(shape)
    relayed_wide = relayed.astype(jnp.float32).reshape(shape)
    gain = column(streams * tap_count)
    long_out = forward.reshape(shape) + gain * gating_wide
    grad_gating = backward.reshape(shape) + gain * relayed_wide
    out_ref[:, 0] = (query_short * long_out).astype(jnp.bfloat16)
    grad_shorts = [cot * long_out, grad_gating * value_short, grad_gating * key_short]
    tap_scale = 1.0 / math.sqrt(seq_total)
    stats = jnp.zeros((members, span), jnp.float32)
    stat_lane = lax.broadcasted_iota(jnp.int32, (members, span), 1)

    def put(stats, index, product):
        total = jnp.sum(jnp.sum(product, axis=0), axis=1, keepdims=True)
        return jnp.where(stat_lane == index, total, stats)

    for stream in range(streams):
        moved = [earlier(grad_shorts[stream], second) for second in range(reach)]
        running = None
        for place in reversed(range(len(delayed[stream]))):
            if running is not None:
                running = earlier(running, reach)
            value = delayed[stream][place].astype(jnp.float32)
            for second in range(min(reach, tap_count - reach * place)):
                index = stream * tap_count + reach * place + second
                term = column(index) * moved[second]
                running = term if running is None else running + term
                stats = put(stats, index, moved[second] * value)
        out_ref[:, 1 + stream] = running.astype(jnp.bfloat16)
    stats = put(stats, streams * tap_count, relayed_wide * gating_wide) * tap_scale

    stats_high = stats.astype(jnp.bfloat16).astype(jnp.float32)
    stats_low = pltpu.roll(stats - stats_high, half // 2, 1)
    lag_tile = jnp.concatenate([lag_sums, pltpu.roll(lag_sums, half, 1)], axis=0)
    tile = jnp.where(
        stat_lane < half, jnp.where(stat_lane < half // 2, stats_high, stats_low), lag_tile
    )
    out_ref[:, streams + 1] = jnp.broadcast_to(tile.astype(jnp.bfloat16)[None], shape)


def unpack_kernel(
    in_ref, out_ref, grads_ref, taps_ref, skip_ref, lags_ref,
    stream_buf, taps_buf, skip_buf, lags_buf, sems,
):
    count, _, members, span = in_ref.shape
    streams, tap_count, chan_width = taps_buf.shape
    moves = []

    def send(buf, ref):
        moves.append(pltpu.make_async_copy(buf, ref, sems.at[len(moves)]))
        moves[-1].start()

    for stream in range(streams + 1):
        block = in_ref[:, stream].reshape(count * members, span).astype(jnp.float32)
        stream_buf[stream] = block.T.astype(jnp.bfloat16)
        send(stream_buf.at[stream], out_ref if stream == 0 else grads_ref.at[stream - 1])
    tile = in_ref[:, streams + 1].astype(jnp.float32)
    lane = lax.broadcasted_iota(jnp.int32, (1, 1, span), 2)
    lags = jnp.where(
        lane < span // 2, pltpu.roll(tile[:, members // 2 :], span // 2, 2), tile[:, : members // 2]
    )
    for step in range(members // 2):
        lags_buf[:, step * span : (step + 1) * span] = lags[:, step]
    send(lags_buf, lags_ref)
    stats = tile.reshape(count * members, span)
    stats = (stats + pltpu.roll(stats, span - span // 4, 1)).T
    for stream in range(streams):
        taps_buf[stream] = stats[stream * tap_count : (stream + 1) * tap_count]
    send(taps_buf, taps_ref)
    skip_buf[...] = stats[streams * tap_count : streams * tap_count + 1]
    send(skip_buf, skip_ref)
    for move in moves:
        move.wait()


def by_group(query_in, key_in, value_in, short_taps, long_filters, skip_gain, cotangent):
    tok_rows, chan_width = query_in.shape
    groups, seq_total = long_filters.shape
    streams, tap_count, _ = short_taps.shape
    members = chan_width // groups
    count = groups
    vmem = pl.BlockSpec(memory_space=pltpu.VMEM)
    params = pltpu.CompilerParams(vmem_limit_bytes=32 * 1024 * 1024)
    packed, gain = pl.pallas_call(
        pack_kernel,
        out_shape=(
            jax.ShapeDtypeStruct((count, streams + 1, members, tok_rows), jnp.bfloat16),
            jax.ShapeDtypeStruct((1, chan_width), jnp.float32),
        ),
        in_specs=[pl.BlockSpec(memory_space=pltpu.HBM)] * 5,
        out_specs=(vmem,) * 2,
        scratch_shapes=[
            pltpu.VMEM((streams + 1, tok_rows, chan_width), jnp.bfloat16),
            pltpu.SemaphoreType.DMA((streams + 2,)),
        ],
        compiler_params=params,
        name="pack",
    )(
        *(
            pltpu.with_memory_space_constraint(value, pltpu.HBM)
            for value in (
                query_in, key_in, value_in, cotangent, skip_gain.reshape(1, chan_width)
            )
        )
    )
    packed = lax.all_to_all(packed, "seq", 0, 0, tiled=True)
    results = pl.pallas_call(
        group_kernel,
        out_shape=jax.ShapeDtypeStruct((count, streams + 2, members, tok_rows), jnp.bfloat16),
        in_specs=[vmem] * 4,
        out_specs=vmem,
        scratch_shapes=[
            pltpu.VMEM((chan_width, streams * tap_count + 3), jnp.float32),
            pltpu.VMEM((tok_rows // 2, seq_total + tok_rows), jnp.float32),
        ],
        compiler_params=params,
        name="group",
    )(packed, short_taps, long_filters, gain)
    results = lax.all_to_all(results, "seq", 0, 0, tiled=True)
    block_out, input_grads, tap_grads, skip_grad, filter_grad = pl.pallas_call(
        unpack_kernel,
        out_shape=(
            jax.ShapeDtypeStruct((tok_rows, chan_width), jnp.bfloat16),
            jax.ShapeDtypeStruct((streams, tok_rows, chan_width), jnp.bfloat16),
            jax.ShapeDtypeStruct((streams, tap_count, chan_width), jnp.float32),
            jax.ShapeDtypeStruct((1, chan_width), jnp.float32),
            jax.ShapeDtypeStruct((groups, seq_total), jnp.float32),
        ),
        in_specs=[vmem],
        out_specs=(pl.BlockSpec(memory_space=pltpu.HBM),) * 5,
        scratch_shapes=[
            pltpu.VMEM((streams + 1, tok_rows, chan_width), jnp.bfloat16),
            pltpu.VMEM((streams, tap_count, chan_width), jnp.float32),
            pltpu.VMEM((1, chan_width), jnp.float32),
            pltpu.VMEM((groups, seq_total), jnp.float32),
            pltpu.SemaphoreType.DMA((streams + 4,)),
        ],
        compiler_params=params,
        name="unpack",
    )(results)
    return block_out, input_grads, tap_grads, skip_grad.reshape(chan_width), filter_grad


def plan(query_in, key_in, value_in, short_taps, long_filters, skip_gain, cotangent):
    tok_rows, chan_width = query_in.shape
    groups, seq_total = long_filters.shape
    tap_rows = short_taps.shape[0] * short_taps.shape[1]
    fits = (
        lax.axis_size("seq") == groups
        and tok_rows == 128
        and chan_width == 128
        and chan_width // groups == 16
        and seq_total == groups * tok_rows
        and tap_rows % 8 == 5
        and tap_rows < 32
    )
    chosen = by_group if fits else local
    return chosen(query_in, key_in, value_in, short_taps, long_filters, skip_gain, cotangent)


def solution(mesh):
    in_specs = (
        P("seq", "chan"),
        P("seq", "chan"),
        P("seq", "chan"),
        P(None, None, "chan"),
        P("chan", None),
        P("chan"),
        P("seq", "chan"),
    )
    out_specs = (
        P("seq", "chan"),
        P(None, "seq", "chan"),
        P(None, None, "chan"),
        P("chan"),
        P("chan", None),
    )
    return jax.shard_map(plan, mesh=mesh, in_specs=in_specs, out_specs=out_specs, check_vma=False)
```

```python
import functools
import math

import jax
import jax.numpy as jnp
from jax import lax
from jax.experimental import pallas as pl
from jax.experimental.pallas import tpu as pltpu
from jax.sharding import PartitionSpec as P


def from_behind(value, axis, steps):
    count = lax.axis_size(axis)
    initial, last = (max(0, -steps), min(count, count - steps))
    return lax.ppermute(value, axis, [(source, source + steps) for source in range(initial, last)])


def short_forward(extended, weights, rows_here):
    margin = weights.shape[0] - 1
    running = jnp.zeros((rows_here, extended.shape[1]), jnp.float32)
    for offset in range(weights.shape[0]):
        running = (
            running + weights[offset] * extended[margin - offset : margin - offset + rows_here]
        )
    return running


def short_backward(extended, weights, rows_here):
    running = jnp.zeros((rows_here, extended.shape[1]), jnp.float32)
    for offset in range(weights.shape[0]):
        running = running + weights[offset] * extended[offset : offset + rows_here]
    return running


def tap_sums(grad_rows, extended, tap_count, rows_here):
    margin = tap_count - 1
    sums_list = []
    for offset in range(tap_count):
        sums_list.append(
            jnp.sum(grad_rows * extended[margin - offset : margin - offset + rows_here], axis=0)
        )
    return jnp.stack(sums_list)


def hankel(padded, lag_start, height, breadth, seq_total):
    span = height + breadth - 1
    window = lax.dynamic_slice_in_dim(padded, lag_start + seq_total, span, axis=1)
    tiled = jnp.tile(window, (1, height))
    tiled = jnp.pad(tiled, ((0, 0), (0, height)))
    return tiled.reshape(padded.shape[0], height, span + 1)[:, :, :breadth]


def causal_part(padded, source_rows, source_start, target_start, target_count, seq_total):
    breadth = source_rows.shape[0]
    matrix = hankel(
        padded, target_start - source_start - breadth + 1, target_count, breadth, seq_total
    )
    return jnp.einsum("gts,sgc->tgc", matrix, source_rows[::-1], preferred_element_type=jnp.float32)


def anti_part(padded, target_rows, target_start, source_start, source_count, seq_total):
    breadth = target_rows.shape[0]
    matrix = hankel(
        padded, target_start - source_start - source_count + 1, source_count, breadth, seq_total
    )
    return jnp.einsum("gab,bgc->agc", matrix, target_rows, preferred_element_type=jnp.float32)[::-1]


def lag_part(buffer, target_rows, source_rows, target_start, source_start, seq_total):
    height = target_rows.shape[0]
    breadth = source_rows.shape[0]
    groups = target_rows.shape[1]
    padded_source = jnp.pad(source_rows[::-1], ((0, height), (0, 0), (0, 0)))
    products = jnp.einsum(
        "tgc,sgc->gts", target_rows, padded_source, preferred_element_type=jnp.float32
    )
    full_width = height + breadth
    skewed = products.reshape(groups, height * full_width)[:, : height * (full_width - 1)]
    skewed = skewed.reshape(groups, height, full_width - 1)
    diagonal = jnp.sum(skewed, axis=1)
    position = target_start - source_start - breadth + 1 + seq_total
    current = lax.dynamic_slice_in_dim(buffer, position, full_width - 1, axis=1)
    return lax.dynamic_update_slice_in_dim(buffer, current + diagonal, position, axis=1)


def local(query_in, key_in, value_in, short_taps, long_filters, skip_gain, cotangent):
    tok_rows, chan_width = query_in.shape
    groups, seq_total = long_filters.shape
    members = chan_width // groups
    tap_count = short_taps.shape[1]
    margin = tap_count - 1
    device = lax.axis_index("seq")
    own_start = device * tok_rows
    rim_rows = jnp.stack(
        [query_in[tok_rows - margin :], key_in[tok_rows - margin :], value_in[tok_rows - margin :]]
    )
    before = from_behind(rim_rows, "seq", 1)
    streams = [query_in, key_in, value_in]
    extended = [
        jnp.concatenate([before[stream], streams[stream]]).astype(jnp.float32)
        for stream in range(3)
    ]
    query_short = short_forward(extended[0], short_taps[0], tok_rows)
    key_short = short_forward(extended[1], short_taps[1], tok_rows)
    value_short = short_forward(extended[2], short_taps[2], tok_rows)
    gating = (key_short * value_short).astype(jnp.bfloat16)
    relayed = (cotangent.astype(jnp.float32) * query_short).astype(jnp.bfloat16)
    gating_wide = gating.astype(jnp.float32)
    relayed_wide = relayed.astype(jnp.float32)
    gating_groups = gating.reshape(tok_rows, groups, members)
    relayed_groups = relayed.reshape(tok_rows, groups, members)
    padded = jnp.concatenate([jnp.zeros((groups, seq_total), jnp.bfloat16), long_filters], axis=1)
    lag_buffer = jnp.zeros((groups, 2 * seq_total), jnp.float32)
    zeros_out = jnp.zeros((tok_rows, groups, members), jnp.float32)

    def target_pair(distance):
        return distance < 0

    totals = (zeros_out, lag_buffer)
    shard_rows = lax.all_gather(gating, "seq", axis=0, tiled=True)
    piece_rows = shard_rows.shape[0]
    step_rows = min(piece_rows, tok_rows)
    pieces = shard_rows.reshape(piece_rows // step_rows, step_rows, groups, members)

    def forward_visit_block(carried, element):
        position, rows_block = element
        source_start = position * step_rows

        def forward_active(partial_value):
            output_part, buffer = partial_value
            output_part = output_part + causal_part(
                padded, rows_block, source_start, own_start, tok_rows, seq_total
            )
            distance = device - source_start // tok_rows
            buffer = lax.cond(
                target_pair(distance),
                lambda held: lag_part(
                    held, relayed_groups, rows_block, own_start, source_start, seq_total
                ),
                lambda held: held,
                buffer,
            )
            return (output_part, buffer)

        carried = lax.cond(
            source_start < own_start + tok_rows,
            forward_active,
            lambda partial_value: partial_value,
            carried,
        )
        return (carried, None)

    totals, ignored = lax.scan(
        forward_visit_block, totals, (jnp.arange(piece_rows // step_rows, dtype=jnp.int32), pieces)
    )
    output_part, lag_buffer = totals
    output_sum = output_part.reshape(tok_rows, chan_width)
    totals = (zeros_out, lag_buffer)
    shard_rows = lax.all_gather(relayed, "seq", axis=0, tiled=True)
    piece_rows = shard_rows.shape[0]
    backward_step_rows = min(piece_rows, tok_rows)
    pieces = shard_rows.reshape(
        piece_rows // backward_step_rows, backward_step_rows, groups, members
    )

    def backward_visit_block(carried, element):
        position, rows_block = element
        target_start = position * backward_step_rows

        def backward_active(partial_value):
            grad_part, buffer = partial_value
            grad_part = grad_part + anti_part(
                padded, rows_block, target_start, own_start, tok_rows, seq_total
            )
            distance = target_start // tok_rows - device
            buffer = lax.cond(
                target_pair(distance),
                lambda held: held,
                lambda held: lag_part(
                    held, rows_block, gating_groups, target_start, own_start, seq_total
                ),
                buffer,
            )
            return (grad_part, buffer)

        carried = lax.cond(
            target_start + backward_step_rows > own_start,
            backward_active,
            lambda partial_value: partial_value,
            carried,
        )
        return (carried, None)

    totals, ignored = lax.scan(
        backward_visit_block,
        totals,
        (jnp.arange(piece_rows // backward_step_rows, dtype=jnp.int32), pieces),
    )
    grad_part, lag_buffer = totals
    grad_sum = grad_part.reshape(tok_rows, chan_width)
    lag_local = lag_buffer[:, seq_total:]
    long_out = output_sum + skip_gain * gating_wide
    block_out = (query_short * long_out).astype(jnp.bfloat16)
    grad_gating = grad_sum + skip_gain * relayed_wide
    cot_wide = cotangent.astype(jnp.float32)
    grad_shorts = [cot_wide * long_out, grad_gating * value_short, grad_gating * key_short]
    lead_rows = jnp.stack([grad_shorts[stream][:margin] for stream in range(3)])
    after = from_behind(lead_rows, "seq", -1)
    input_grads = jnp.stack(
        [
            short_backward(
                jnp.concatenate([grad_shorts[stream], after[stream]]), short_taps[stream], tok_rows
            )
            for stream in range(3)
        ]
    ).astype(jnp.bfloat16)
    tap_local = jnp.stack(
        [
            tap_sums(grad_shorts[stream], extended[stream], tap_count, tok_rows)
            for stream in range(3)
        ]
    )
    skip_local = jnp.sum(relayed_wide * gating_wide, axis=0)
    lag_total, tap_total, skip_total = lax.psum((lag_local, tap_local, skip_local), "seq")
    tap_scale = 1.0 / math.sqrt(seq_total)
    lag_scale = 1.0 / math.sqrt(seq_total * members)
    return (
        block_out,
        input_grads,
        tap_total * tap_scale,
        skip_total * tap_scale,
        lag_total * lag_scale,
    )


def ring_order(count):
    return list(range(0, count, 2)) + list(range(1, count, 2))[::-1]


def in_order(value, count):
    order = ring_order(count)
    return jnp.stack([value[order.index(device)] for device in range(count)])


def in_ring(value, count):
    return jnp.stack([value[device] for device in ring_order(count)])


def pack_kernel(
    query_ref, key_ref, value_ref, cot_ref, skip_ref, out_ref, gain_ref, stream_buf, sems
):
    count, streams, members, tok_rows = out_ref.shape
    moves = [
        pltpu.make_async_copy(ref, stream_buf.at[stream], sems.at[stream])
        for stream, ref in enumerate((query_ref, key_ref, value_ref, cot_ref))
    ]
    moves.append(pltpu.make_async_copy(skip_ref, gain_ref, sems.at[streams]))
    for move in moves:
        move.start()
    for stream in range(streams):
        moves[stream].wait()
        flipped = stream_buf[stream].astype(jnp.float32).T.astype(jnp.bfloat16)
        out_ref[:, stream] = in_ring(flipped.reshape(count, members, tok_rows), count)
    moves[streams].wait()


def group_kernel(in_ref, taps_ref, filters_ref, gain_ref, out_ref, table_ref, wide_ref):
    count, _, members, span = in_ref.shape
    groups, seq_total = filters_ref.shape
    streams, tap_count, chan_width = taps_ref.shape
    rows = count * members
    mine = lax.axis_index("seq")
    shape = (count, members, span)
    lane = lax.broadcasted_iota(jnp.int32, shape, 2)
    reach = 3

    def later(value, steps):
        if steps == 0:
            return value
        turned = pltpu.roll(value, steps, 2)
        before = jnp.concatenate([jnp.zeros_like(turned[:1]), turned[:-1]], axis=0)
        return jnp.where(lane >= steps, turned, before)

    def earlier(value, steps):
        if steps == 0:
            return value
        turned = pltpu.roll(value, span - steps, 2)
        after = jnp.concatenate([turned[1:], jnp.zeros_like(turned[:1])], axis=0)
        return jnp.where(lane < span - steps, turned, after)

    table = jnp.concatenate(
        [taps_ref[stream] for stream in range(streams)]
        + [gain_ref[...], jnp.zeros((2, chan_width), jnp.float32)],
        axis=0,
    )
    table_ref[...] = table.T
    params = table_ref[pl.ds(pl.multiple_of(mine * members, members), members), :]

    def column(index):
        return jnp.broadcast_to(params[:, index : index + 1], (members, span))[None]

    chosen = lax.broadcasted_iota(jnp.int32, (groups, 1), 0) == mine
    filter_row = jnp.sum(
        jnp.where(chosen, filters_ref[...].astype(jnp.float32), 0.0), axis=0, keepdims=True
    )
    filter_row = jnp.concatenate([filter_row, jnp.zeros((1, span), jnp.float32)], axis=1)
    spread = jnp.broadcast_to(filter_row, (span, seq_total + span))
    toeplitz = pltpu.roll(spread, 0, 1, stride=1, stride_axis=0)[:, :seq_total]
    toeplitz = toeplitz.astype(jnp.bfloat16)

    cot = in_order(in_ref[:, streams], count).astype(jnp.float32)
    delayed, shorts = [], []
    for stream in range(streams):
        value = in_order(in_ref[:, stream], count)
        delayed.append([later(value, first) for first in range(0, tap_count, reach)])
        running = None
        for second in reversed(range(reach)):
            if running is not None:
                running = later(running, 1)
            for first in range(second, tap_count, reach):
                term = column(stream * tap_count + first) * delayed[stream][
                    first // reach
                ].astype(jnp.float32)
                running = term if running is None else running + term
        shorts.append(running)
    query_short, key_short, value_short = shorts
    gating = (key_short * value_short).astype(jnp.bfloat16).reshape(rows, span)
    relayed = (cot * query_short).astype(jnp.bfloat16).reshape(rows, span)

    gating_parts, relayed_parts, filter_parts = [gating], [relayed], [toeplitz[:, :span]]
    for step in range(1, count):
        gap = jnp.zeros((step * members, span), jnp.bfloat16)
        gating_parts.append(jnp.concatenate([gap, gating[: rows - step * members]], axis=0))
        relayed_parts.append(jnp.concatenate([relayed[step * members :], gap], axis=0))
        filter_parts.append(toeplitz[:, step * span : (step + 1) * span])
    gating_lags = jnp.concatenate(gating_parts, axis=1)
    relayed_lags = jnp.concatenate(relayed_parts, axis=1)
    forward = jnp.dot(
        gating_lags, jnp.concatenate(filter_parts, axis=0), preferred_element_type=jnp.float32
    )
    backward = lax.dot_general(
        relayed_lags, toeplitz, (((1,), (1,)), ((), ())), preferred_element_type=jnp.float32
    )
    flip = (
        lax.broadcasted_iota(jnp.int32, (span, span), 0)
        + lax.broadcasted_iota(jnp.int32, (span, span), 1)
        == span - 1
    ).astype(jnp.bfloat16)
    gating_turned = lax.dot_general(
        flip, gating, (((1,), (1,)), ((), ())), preferred_element_type=jnp.float32
    ).astype(jnp.bfloat16)
    products = jnp.dot(gating_turned, relayed_lags, preferred_element_type=jnp.float32)
    wide_ref[:, :seq_total] = products
    wide_ref[:, seq_total:] = jnp.zeros((span, span), jnp.float32)
    skewed = pltpu.roll(wide_ref[...], 0, 1, stride=1, stride_axis=0)
    diagonal = jnp.sum(skewed, axis=0, keepdims=True)
    diagonal = pltpu.roll(diagonal, seq_total + 1, 1)[:, :seq_total]
    lag_scale = 1.0 / math.sqrt(seq_total * members)
    lag_sums = jnp.concatenate(
        [diagonal[:, step * span : (step + 1) * span] for step in range(count)], axis=0
    )
    lag_sums = lag_sums * lag_scale

    gating_wide = gating.astype(jnp.float32).reshape(shape)
    relayed_wide = relayed.astype(jnp.float32).reshape(shape)
    gain = column(streams * tap_count)
    long_out = forward.reshape(shape) + gain * gating_wide
    grad_gating = backward.reshape(shape) + gain * relayed_wide
    out_ref[:, 0] = in_ring((query_short * long_out).astype(jnp.bfloat16), count)
    grad_shorts = [cot * long_out, grad_gating * value_short, grad_gating * key_short]
    tap_scale = 1.0 / math.sqrt(seq_total)
    stats = jnp.zeros((members, span), jnp.float32)
    stat_lane = lax.broadcasted_iota(jnp.int32, (members, span), 1)

    def put(stats, index, product):
        total = jnp.sum(jnp.sum(product, axis=0), axis=1, keepdims=True)
        return jnp.where(stat_lane == index, total, stats)

    for stream in range(streams):
        moved = [earlier(grad_shorts[stream], second) for second in range(reach)]
        running = None
        for place in reversed(range(len(delayed[stream]))):
            if running is not None:
                running = earlier(running, reach)
            value = delayed[stream][place].astype(jnp.float32)
            for second in range(min(reach, tap_count - reach * place)):
                index = stream * tap_count + reach * place + second
                term = column(index) * moved[second]
                running = term if running is None else running + term
                stats = put(stats, index, moved[second] * value)
        out_ref[:, 1 + stream] = in_ring(running.astype(jnp.bfloat16), count)
    stats = put(stats, streams * tap_count, relayed_wide * gating_wide) * tap_scale

    half = span // 2
    stats_high = stats.astype(jnp.bfloat16).astype(jnp.float32)
    stats_low = pltpu.roll(stats - stats_high, half // 2, 1)
    lag_tile = jnp.concatenate([lag_sums, pltpu.roll(lag_sums, half, 1)], axis=0)
    tile = jnp.where(
        stat_lane < half, jnp.where(stat_lane < half // 2, stats_high, stats_low), lag_tile
    )
    out_ref[:, streams + 1] = jnp.broadcast_to(tile.astype(jnp.bfloat16)[None], shape)


def unpack_kernel(in_ref, out_ref, grads_ref, taps_ref, skip_ref, lags_ref):
    count, _, members, span = in_ref.shape
    streams, tap_count, chan_width = taps_ref.shape
    for stream in range(streams + 1):
        block = in_order(in_ref[:, stream], count).reshape(count * members, span)
        block = block.astype(jnp.float32)
        flipped = block.T.astype(jnp.bfloat16)
        if stream == 0:
            out_ref[...] = flipped
        else:
            grads_ref[stream - 1] = flipped
    tile = in_order(in_ref[:, streams + 1], count).astype(jnp.float32)
    stats = tile.reshape(count * members, span)
    stats = (stats + pltpu.roll(stats, span - span // 4, 1)).T
    for stream in range(streams):
        taps_ref[stream] = stats[stream * tap_count : (stream + 1) * tap_count]
    skip_ref[...] = stats[streams * tap_count : streams * tap_count + 1]
    lane = lax.broadcasted_iota(jnp.int32, (1, 1, span), 2)
    lags = jnp.where(
        lane < span // 2, pltpu.roll(tile[:, members // 2 :], span // 2, 2), tile[:, : members // 2]
    )
    for step in range(members // 2):
        lags_ref[:, step * span : (step + 1) * span] = lags[:, step]


def by_group(query_in, key_in, value_in, short_taps, long_filters, skip_gain, cotangent):
    tok_rows, chan_width = query_in.shape
    groups, seq_total = long_filters.shape
    streams, tap_count, _ = short_taps.shape
    members = chan_width // groups
    count = groups
    vmem = pl.BlockSpec(memory_space=pltpu.VMEM)
    params = pltpu.CompilerParams(vmem_limit_bytes=32 * 1024 * 1024)
    packed, gain = pl.pallas_call(
        pack_kernel,
        out_shape=(
            jax.ShapeDtypeStruct((count, streams + 1, members, tok_rows), jnp.bfloat16),
            jax.ShapeDtypeStruct((1, chan_width), jnp.float32),
        ),
        in_specs=[pl.BlockSpec(memory_space=pltpu.HBM)] * 5,
        out_specs=(vmem,) * 2,
        scratch_shapes=[
            pltpu.VMEM((streams + 1, tok_rows, chan_width), jnp.bfloat16),
            pltpu.SemaphoreType.DMA((streams + 2,)),
        ],
        compiler_params=params,
        name="pack",
    )(
        *(
            pltpu.with_memory_space_constraint(value, pltpu.HBM)
            for value in (
                query_in, key_in, value_in, cotangent, skip_gain.reshape(1, chan_width)
            )
        )
    )
    packed = lax.all_to_all(
        packed, "seq", 0, 0, tiled=True, axis_index_groups=[ring_order(count)]
    )
    results = pl.pallas_call(
        group_kernel,
        out_shape=jax.ShapeDtypeStruct((count, streams + 2, members, tok_rows), jnp.bfloat16),
        in_specs=[vmem] * 4,
        out_specs=vmem,
        scratch_shapes=[
            pltpu.VMEM((chan_width, streams * tap_count + 3), jnp.float32),
            pltpu.VMEM((tok_rows, seq_total + tok_rows), jnp.float32),
        ],
        compiler_params=params,
        name="group",
    )(packed, short_taps, long_filters, gain)
    results = lax.all_to_all(
        results, "seq", 0, 0, tiled=True, axis_index_groups=[ring_order(count)]
    )
    block_out, input_grads, tap_grads, skip_grad, filter_grad = pl.pallas_call(
        unpack_kernel,
        out_shape=(
            jax.ShapeDtypeStruct((tok_rows, chan_width), jnp.bfloat16),
            jax.ShapeDtypeStruct((streams, tok_rows, chan_width), jnp.bfloat16),
            jax.ShapeDtypeStruct((streams, tap_count, chan_width), jnp.float32),
            jax.ShapeDtypeStruct((1, chan_width), jnp.float32),
            jax.ShapeDtypeStruct((groups, seq_total), jnp.float32),
        ),
        in_specs=[vmem],
        out_specs=(vmem,) * 5,
        compiler_params=params,
        name="unpack",
    )(results)
    return block_out, input_grads, tap_grads, skip_grad.reshape(chan_width), filter_grad


def plan(query_in, key_in, value_in, short_taps, long_filters, skip_gain, cotangent):
    tok_rows, chan_width = query_in.shape
    groups, seq_total = long_filters.shape
    tap_rows = short_taps.shape[0] * short_taps.shape[1]
    fits = (
        lax.axis_size("seq") == groups
        and tok_rows == 128
        and chan_width == 128
        and chan_width // groups == 16
        and seq_total == groups * tok_rows
        and tap_rows % 8 == 5
        and tap_rows < 32
    )
    chosen = by_group if fits else local
    return chosen(query_in, key_in, value_in, short_taps, long_filters, skip_gain, cotangent)


def solution(mesh):
    in_specs = (
        P("seq", "chan"),
        P("seq", "chan"),
        P("seq", "chan"),
        P(None, None, "chan"),
        P("chan", None),
        P("chan"),
        P("seq", "chan"),
    )
    out_specs = (
        P("seq", "chan"),
        P(None, "seq", "chan"),
        P(None, None, "chan"),
        P("chan"),
        P("chan", None),
    )
    return jax.shard_map(plan, mesh=mesh, in_specs=in_specs, out_specs=out_specs, check_vma=False)
```

```python
import functools
import math

import jax
import jax.numpy as jnp
from jax import lax
from jax.experimental import pallas as pl
from jax.experimental.pallas import tpu as pltpu
from jax.sharding import PartitionSpec as P


def from_behind(value, axis, steps):
    count = lax.axis_size(axis)
    initial, last = (max(0, -steps), min(count, count - steps))
    return lax.ppermute(value, axis, [(source, source + steps) for source in range(initial, last)])


def short_forward(extended, weights, rows_here):
    margin = weights.shape[0] - 1
    running = jnp.zeros((rows_here, extended.shape[1]), jnp.float32)
    for offset in range(weights.shape[0]):
        running = (
            running + weights[offset] * extended[margin - offset : margin - offset + rows_here]
        )
    return running


def short_backward(extended, weights, rows_here):
    running = jnp.zeros((rows_here, extended.shape[1]), jnp.float32)
    for offset in range(weights.shape[0]):
        running = running + weights[offset] * extended[offset : offset + rows_here]
    return running


def tap_sums(grad_rows, extended, tap_count, rows_here):
    margin = tap_count - 1
    sums_list = []
    for offset in range(tap_count):
        sums_list.append(
            jnp.sum(grad_rows * extended[margin - offset : margin - offset + rows_here], axis=0)
        )
    return jnp.stack(sums_list)


def hankel(padded, lag_start, height, breadth, seq_total):
    span = height + breadth - 1
    window = lax.dynamic_slice_in_dim(padded, lag_start + seq_total, span, axis=1)
    tiled = jnp.tile(window, (1, height))
    tiled = jnp.pad(tiled, ((0, 0), (0, height)))
    return tiled.reshape(padded.shape[0], height, span + 1)[:, :, :breadth]


def causal_part(padded, source_rows, source_start, target_start, target_count, seq_total):
    breadth = source_rows.shape[0]
    matrix = hankel(
        padded, target_start - source_start - breadth + 1, target_count, breadth, seq_total
    )
    return jnp.einsum("gts,sgc->tgc", matrix, source_rows[::-1], preferred_element_type=jnp.float32)


def anti_part(padded, target_rows, target_start, source_start, source_count, seq_total):
    breadth = target_rows.shape[0]
    matrix = hankel(
        padded, target_start - source_start - source_count + 1, source_count, breadth, seq_total
    )
    return jnp.einsum("gab,bgc->agc", matrix, target_rows, preferred_element_type=jnp.float32)[::-1]


def lag_part(buffer, target_rows, source_rows, target_start, source_start, seq_total):
    height = target_rows.shape[0]
    breadth = source_rows.shape[0]
    groups = target_rows.shape[1]
    padded_source = jnp.pad(source_rows[::-1], ((0, height), (0, 0), (0, 0)))
    products = jnp.einsum(
        "tgc,sgc->gts", target_rows, padded_source, preferred_element_type=jnp.float32
    )
    full_width = height + breadth
    skewed = products.reshape(groups, height * full_width)[:, : height * (full_width - 1)]
    skewed = skewed.reshape(groups, height, full_width - 1)
    diagonal = jnp.sum(skewed, axis=1)
    position = target_start - source_start - breadth + 1 + seq_total
    current = lax.dynamic_slice_in_dim(buffer, position, full_width - 1, axis=1)
    return lax.dynamic_update_slice_in_dim(buffer, current + diagonal, position, axis=1)


def local(query_in, key_in, value_in, short_taps, long_filters, skip_gain, cotangent):
    tok_rows, chan_width = query_in.shape
    groups, seq_total = long_filters.shape
    members = chan_width // groups
    tap_count = short_taps.shape[1]
    margin = tap_count - 1
    device = lax.axis_index("seq")
    own_start = device * tok_rows
    rim_rows = jnp.stack(
        [query_in[tok_rows - margin :], key_in[tok_rows - margin :], value_in[tok_rows - margin :]]
    )
    before = from_behind(rim_rows, "seq", 1)
    streams = [query_in, key_in, value_in]
    extended = [
        jnp.concatenate([before[stream], streams[stream]]).astype(jnp.float32)
        for stream in range(3)
    ]
    query_short = short_forward(extended[0], short_taps[0], tok_rows)
    key_short = short_forward(extended[1], short_taps[1], tok_rows)
    value_short = short_forward(extended[2], short_taps[2], tok_rows)
    gating = (key_short * value_short).astype(jnp.bfloat16)
    relayed = (cotangent.astype(jnp.float32) * query_short).astype(jnp.bfloat16)
    gating_wide = gating.astype(jnp.float32)
    relayed_wide = relayed.astype(jnp.float32)
    gating_groups = gating.reshape(tok_rows, groups, members)
    relayed_groups = relayed.reshape(tok_rows, groups, members)
    padded = jnp.concatenate([jnp.zeros((groups, seq_total), jnp.bfloat16), long_filters], axis=1)
    lag_buffer = jnp.zeros((groups, 2 * seq_total), jnp.float32)
    zeros_out = jnp.zeros((tok_rows, groups, members), jnp.float32)

    def target_pair(distance):
        return distance < 0

    totals = (zeros_out, lag_buffer)
    shard_rows = lax.all_gather(gating, "seq", axis=0, tiled=True)
    piece_rows = shard_rows.shape[0]
    step_rows = min(piece_rows, tok_rows)
    pieces = shard_rows.reshape(piece_rows // step_rows, step_rows, groups, members)

    def forward_visit_block(carried, element):
        position, rows_block = element
        source_start = position * step_rows

        def forward_active(partial_value):
            output_part, buffer = partial_value
            output_part = output_part + causal_part(
                padded, rows_block, source_start, own_start, tok_rows, seq_total
            )
            distance = device - source_start // tok_rows
            buffer = lax.cond(
                target_pair(distance),
                lambda held: lag_part(
                    held, relayed_groups, rows_block, own_start, source_start, seq_total
                ),
                lambda held: held,
                buffer,
            )
            return (output_part, buffer)

        carried = lax.cond(
            source_start < own_start + tok_rows,
            forward_active,
            lambda partial_value: partial_value,
            carried,
        )
        return (carried, None)

    totals, ignored = lax.scan(
        forward_visit_block, totals, (jnp.arange(piece_rows // step_rows, dtype=jnp.int32), pieces)
    )
    output_part, lag_buffer = totals
    output_sum = output_part.reshape(tok_rows, chan_width)
    totals = (zeros_out, lag_buffer)
    shard_rows = lax.all_gather(relayed, "seq", axis=0, tiled=True)
    piece_rows = shard_rows.shape[0]
    backward_step_rows = min(piece_rows, tok_rows)
    pieces = shard_rows.reshape(
        piece_rows // backward_step_rows, backward_step_rows, groups, members
    )

    def backward_visit_block(carried, element):
        position, rows_block = element
        target_start = position * backward_step_rows

        def backward_active(partial_value):
            grad_part, buffer = partial_value
            grad_part = grad_part + anti_part(
                padded, rows_block, target_start, own_start, tok_rows, seq_total
            )
            distance = target_start // tok_rows - device
            buffer = lax.cond(
                target_pair(distance),
                lambda held: held,
                lambda held: lag_part(
                    held, rows_block, gating_groups, target_start, own_start, seq_total
                ),
                buffer,
            )
            return (grad_part, buffer)

        carried = lax.cond(
            target_start + backward_step_rows > own_start,
            backward_active,
            lambda partial_value: partial_value,
            carried,
        )
        return (carried, None)

    totals, ignored = lax.scan(
        backward_visit_block,
        totals,
        (jnp.arange(piece_rows // backward_step_rows, dtype=jnp.int32), pieces),
    )
    grad_part, lag_buffer = totals
    grad_sum = grad_part.reshape(tok_rows, chan_width)
    lag_local = lag_buffer[:, seq_total:]
    long_out = output_sum + skip_gain * gating_wide
    block_out = (query_short * long_out).astype(jnp.bfloat16)
    grad_gating = grad_sum + skip_gain * relayed_wide
    cot_wide = cotangent.astype(jnp.float32)
    grad_shorts = [cot_wide * long_out, grad_gating * value_short, grad_gating * key_short]
    lead_rows = jnp.stack([grad_shorts[stream][:margin] for stream in range(3)])
    after = from_behind(lead_rows, "seq", -1)
    input_grads = jnp.stack(
        [
            short_backward(
                jnp.concatenate([grad_shorts[stream], after[stream]]), short_taps[stream], tok_rows
            )
            for stream in range(3)
        ]
    ).astype(jnp.bfloat16)
    tap_local = jnp.stack(
        [
            tap_sums(grad_shorts[stream], extended[stream], tap_count, tok_rows)
            for stream in range(3)
        ]
    )
    skip_local = jnp.sum(relayed_wide * gating_wide, axis=0)
    lag_total, tap_total, skip_total = lax.psum((lag_local, tap_local, skip_local), "seq")
    tap_scale = 1.0 / math.sqrt(seq_total)
    lag_scale = 1.0 / math.sqrt(seq_total * members)
    return (
        block_out,
        input_grads,
        tap_total * tap_scale,
        skip_total * tap_scale,
        lag_total * lag_scale,
    )


def pack_kernel(
    query_ref, key_ref, value_ref, cot_ref, skip_ref, out_ref, gain_ref, stream_buf, sems
):
    count, streams, members, tok_rows = out_ref.shape
    half = tok_rows // 2
    moves = []
    for stream, ref in enumerate((query_ref, key_ref, value_ref, cot_ref)):
        for part in range(2):
            span = pl.ds(part * half, half)
            move = pltpu.make_async_copy(
                ref.at[span], stream_buf.at[stream, span], sems.at[2 * stream + part]
            )
            move.start(priority=part)
            moves.append(move)
    moves.append(pltpu.make_async_copy(skip_ref, gain_ref, sems.at[2 * streams]))
    moves[-1].start()
    for stream in range(streams):
        moves[2 * stream].wait()
        moves[2 * stream + 1].wait()
        flipped = stream_buf[stream].astype(jnp.float32).T.astype(jnp.bfloat16)
        out_ref[:, stream] = flipped.reshape(count, members, tok_rows)
    moves[-1].wait()


def group_kernel(
    in_ref, taps_ref, filters_ref, gain_ref, out_ref, table_ref, wide_ref, tile_ref
):
    count, _, members, span = in_ref.shape
    groups, seq_total = filters_ref.shape
    streams, tap_count, chan_width = taps_ref.shape
    rows = count * members
    mine = lax.axis_index("seq")
    shape = (count, members, span)
    lane = lax.broadcasted_iota(jnp.int32, shape, 2)
    reach = 3

    def later(value, steps):
        if steps == 0:
            return value
        turned = pltpu.roll(value, steps, 2)
        before = jnp.concatenate([jnp.zeros_like(turned[:1]), turned[:-1]], axis=0)
        return jnp.where(lane >= steps, turned, before)

    def earlier(value, steps):
        if steps == 0:
            return value
        turned = pltpu.roll(value, span - steps, 2)
        after = jnp.concatenate([turned[1:], jnp.zeros_like(turned[:1])], axis=0)
        return jnp.where(lane < span - steps, turned, after)

    table = jnp.concatenate(
        [taps_ref[stream] for stream in range(streams)]
        + [gain_ref[...], jnp.zeros((2, chan_width), jnp.float32)],
        axis=0,
    )
    table_ref[...] = table.T
    params = table_ref[pl.ds(pl.multiple_of(mine * members, members), members), :]

    def column(index):
        return jnp.broadcast_to(params[:, index : index + 1], (members, span))[None]

    chosen = lax.broadcasted_iota(jnp.int32, (groups, 1), 0) == mine
    filter_row = jnp.sum(
        jnp.where(chosen, filters_ref[...].astype(jnp.float32), 0.0), axis=0, keepdims=True
    )
    filter_row = jnp.concatenate([filter_row, jnp.zeros((1, span), jnp.float32)], axis=1)
    spread = jnp.broadcast_to(filter_row, (span, seq_total + span))
    toeplitz = pltpu.roll(spread, 0, 1, stride=1, stride_axis=0)[:, :seq_total]
    toeplitz = toeplitz.astype(jnp.bfloat16)

    cot = in_ref[:, streams].astype(jnp.float32)
    delayed, shorts = [], []
    for stream in range(streams):
        value = in_ref[:, stream]
        delayed.append([later(value, first) for first in range(0, tap_count, reach)])
        running = None
        for second in reversed(range(reach)):
            if running is not None:
                running = later(running, 1)
            for first in range(second, tap_count, reach):
                term = column(stream * tap_count + first) * delayed[stream][
                    first // reach
                ].astype(jnp.float32)
                running = term if running is None else running + term
        shorts.append(running)
    query_short, key_short, value_short = shorts
    gating = (key_short * value_short).astype(jnp.bfloat16).reshape(rows, span)
    relayed = (cot * query_short).astype(jnp.bfloat16).reshape(rows, span)

    gating_parts, relayed_parts, filter_parts = [gating], [relayed], [toeplitz[:, :span]]
    for step in range(1, count):
        gap = jnp.zeros((step * members, span), jnp.bfloat16)
        gating_parts.append(jnp.concatenate([gap, gating[: rows - step * members]], axis=0))
        relayed_parts.append(jnp.concatenate([relayed[step * members :], gap], axis=0))
        filter_parts.append(toeplitz[:, step * span : (step + 1) * span])
    gating_lags = jnp.concatenate(gating_parts, axis=1)
    relayed_lags = jnp.concatenate(relayed_parts, axis=1)
    forward = jnp.dot(
        gating_lags, jnp.concatenate(filter_parts, axis=0), preferred_element_type=jnp.float32
    )
    backward = lax.dot_general(
        relayed_lags, toeplitz, (((1,), (1,)), ((), ())), preferred_element_type=jnp.float32
    )
    flip = (
        lax.broadcasted_iota(jnp.int32, (span, span), 0)
        + lax.broadcasted_iota(jnp.int32, (span, span), 1)
        == span - 1
    ).astype(jnp.bfloat16)
    gating_turned = lax.dot_general(
        flip, gating, (((1,), (1,)), ((), ())), preferred_element_type=jnp.float32
    ).astype(jnp.bfloat16)
    products = jnp.dot(gating_turned, relayed_lags, preferred_element_type=jnp.float32)
    wide_ref[:, :seq_total] = products
    wide_ref[:, seq_total:] = jnp.zeros((span, span), jnp.float32)
    skewed = pltpu.roll(wide_ref[...], 0, 1, stride=1, stride_axis=0)
    diagonal = jnp.sum(skewed, axis=0, keepdims=True)
    diagonal = pltpu.roll(diagonal, seq_total + 1, 1)[:, :seq_total]
    lag_scale = 1.0 / math.sqrt(seq_total * members)
    lag_sums = jnp.concatenate(
        [diagonal[:, step * span : (step + 1) * span] for step in range(count)], axis=0
    )
    lag_sums = lag_sums * lag_scale

    gating_wide = gating.astype(jnp.float32).reshape(shape)
    relayed_wide = relayed.astype(jnp.float32).reshape(shape)
    gain = column(streams * tap_count)
    long_out = forward.reshape(shape) + gain * gating_wide
    grad_gating = backward.reshape(shape) + gain * relayed_wide
    out_ref[:, 0] = (query_short * long_out).astype(jnp.bfloat16)
    grad_shorts = [cot * long_out, grad_gating * value_short, grad_gating * key_short]
    tap_scale = 1.0 / math.sqrt(seq_total)

    def tokens(value):
        return jnp.concatenate([value[block] for block in range(count)], axis=1)

    def sums(left, right):
        product = lax.dot_general(
            jnp.concatenate(left, axis=0),
            jnp.concatenate(right, axis=0),
            (((1,), (1,)), ((), ())),
            preferred_element_type=jnp.float32,
        )
        same = (
            lax.broadcasted_iota(jnp.int32, product.shape, 0) % members
            == lax.broadcasted_iota(jnp.int32, product.shape, 1) % members
        )
        product = jnp.where(same, product, 0.0).reshape(len(left), members, -1)
        return jnp.sum(product, axis=1) * tap_scale

    tile_ref[...] = jnp.zeros((members, span), jnp.float32)
    next_row = 0
    for stream in range(streams):
        moved = [earlier(grad_shorts[stream], second) for second in range(reach)]
        left = [tokens(value.astype(jnp.bfloat16)) for value in moved]
        right = [tokens(value) for value in delayed[stream]]
        if stream == 0:
            left.append(tokens(relayed.reshape(shape)))
            right.append(tokens(gating.reshape(shape)))
        totals = sums(left, right)
        tile_ref[next_row : next_row + len(left), : totals.shape[1]] = totals
        next_row += len(left)
        running = None
        for place in reversed(range(len(delayed[stream]))):
            if running is not None:
                running = earlier(running, reach)
            for second in range(min(reach, tap_count - reach * place)):
                term = column(stream * tap_count + reach * place + second) * moved[second]
                running = term if running is None else running + term
        out_ref[:, 1 + stream] = running.astype(jnp.bfloat16)
    half = span // 2
    tile_ref[:count, half:] = lag_sums[:, half:]
    tile_ref[count:, half:] = pltpu.roll(lag_sums, half, 1)[:, half:]
    out_ref[:, streams + 1] = jnp.broadcast_to(tile_ref[...].astype(jnp.bfloat16)[None], shape)


def unpack_kernel(
    in_ref, out_ref, grads_ref, taps_ref, skip_ref, lags_ref,
    stream_buf, taps_buf, skip_buf, lags_buf, sems,
):
    count, _, members, span = in_ref.shape
    streams, tap_count, chan_width = taps_buf.shape
    reach = 3
    moves = []

    def send(buf, ref, priority):
        moves.append(pltpu.make_async_copy(buf, ref, sems.at[len(moves)]))
        moves[-1].start(priority=priority)

    tile = in_ref[:, streams + 1].astype(jnp.float32)
    lane = lax.broadcasted_iota(jnp.int32, (1, members // 2, span), 2)
    lags = jnp.where(
        lane < span // 2, pltpu.roll(tile[:, members // 2 :], span // 2, 2), tile[:, : members // 2]
    )
    for step in range(members // 2):
        lags_buf[:, step * span : (step + 1) * span] = lags[:, step]
    send(lags_buf, lags_ref, 0)
    half = span // 2
    for stream in range(streams + 1):
        block = in_ref[:, stream].reshape(count * members, span).astype(jnp.float32)
        stream_buf[stream] = block.T.astype(jnp.bfloat16)
        target = out_ref if stream == 0 else grads_ref.at[stream - 1]
        for part in range(2):
            rows = pl.ds(part * half, half)
            send(stream_buf.at[stream, rows], target.at[rows], part)
    lane = lax.broadcasted_iota(jnp.int32, (members, span), 1)
    spread = []
    for place in range(-(-tap_count // reach) + 1):
        total = None
        for group in range(count):
            moved = pltpu.roll(tile[group], (members * (group - place)) % span, 1)
            inside = (lane >= members * group) & (lane < members * (group + 1))
            total = moved if total is None else jnp.where(inside, moved, total)
        spread.append(total)
    first = 0
    for stream in range(streams):
        for place in range(-(-tap_count // reach)):
            taken = min(reach, tap_count - reach * place)
            taps_buf[stream, reach * place : reach * place + taken] = spread[place][
                first : first + taken
            ]
        first += reach + (stream == 0)
    send(taps_buf, taps_ref, 0)
    skip_buf[...] = spread[-1][reach : reach + 1]
    send(skip_buf, skip_ref, 1)
    for move in moves:
        move.wait()


def by_group(query_in, key_in, value_in, short_taps, long_filters, skip_gain, cotangent):
    tok_rows, chan_width = query_in.shape
    groups, seq_total = long_filters.shape
    streams, tap_count, _ = short_taps.shape
    members = chan_width // groups
    count = groups
    vmem = pl.BlockSpec(memory_space=pltpu.VMEM)
    params = pltpu.CompilerParams(vmem_limit_bytes=32 * 1024 * 1024)
    packed, gain = pl.pallas_call(
        pack_kernel,
        out_shape=(
            jax.ShapeDtypeStruct((count, streams + 1, members, tok_rows), jnp.bfloat16),
            jax.ShapeDtypeStruct((1, chan_width), jnp.float32),
        ),
        in_specs=[pl.BlockSpec(memory_space=pltpu.HBM)] * 5,
        out_specs=(vmem,) * 2,
        scratch_shapes=[
            pltpu.VMEM((streams + 1, tok_rows, chan_width), jnp.bfloat16),
            pltpu.SemaphoreType.DMA((2 * streams + 3,)),
        ],
        compiler_params=params,
        name="pack",
    )(
        *(
            pltpu.with_memory_space_constraint(value, pltpu.HBM)
            for value in (
                query_in, key_in, value_in, cotangent, skip_gain.reshape(1, chan_width)
            )
        )
    )
    packed = lax.all_to_all(packed, "seq", 0, 0, tiled=True)
    results = pl.pallas_call(
        group_kernel,
        out_shape=jax.ShapeDtypeStruct((count, streams + 2, members, tok_rows), jnp.bfloat16),
        in_specs=[vmem] * 4,
        out_specs=vmem,
        scratch_shapes=[
            pltpu.VMEM((chan_width, streams * tap_count + 3), jnp.float32),
            pltpu.VMEM((tok_rows, seq_total + tok_rows), jnp.float32),
            pltpu.VMEM((members, tok_rows), jnp.float32),
        ],
        compiler_params=params,
        name="group",
    )(packed, short_taps, long_filters, gain)
    results = lax.all_to_all(results, "seq", 0, 0, tiled=True)
    block_out, input_grads, tap_grads, skip_grad, filter_grad = pl.pallas_call(
        unpack_kernel,
        out_shape=(
            jax.ShapeDtypeStruct((tok_rows, chan_width), jnp.bfloat16),
            jax.ShapeDtypeStruct((streams, tok_rows, chan_width), jnp.bfloat16),
            jax.ShapeDtypeStruct((streams, tap_count, chan_width), jnp.float32),
            jax.ShapeDtypeStruct((1, chan_width), jnp.float32),
            jax.ShapeDtypeStruct((groups, seq_total), jnp.float32),
        ),
        in_specs=[vmem],
        out_specs=(pl.BlockSpec(memory_space=pltpu.HBM),) * 5,
        scratch_shapes=[
            pltpu.VMEM((streams + 1, tok_rows, chan_width), jnp.bfloat16),
            pltpu.VMEM((streams, tap_count, chan_width), jnp.float32),
            pltpu.VMEM((1, chan_width), jnp.float32),
            pltpu.VMEM((groups, seq_total), jnp.float32),
            pltpu.SemaphoreType.DMA((2 * streams + 5,)),
        ],
        compiler_params=params,
        name="unpack",
    )(results)
    return block_out, input_grads, tap_grads, skip_grad.reshape(chan_width), filter_grad


def plan(query_in, key_in, value_in, short_taps, long_filters, skip_gain, cotangent):
    tok_rows, chan_width = query_in.shape
    groups, seq_total = long_filters.shape
    fits = (
        lax.axis_size("seq") == groups
        and tok_rows == 128
        and chan_width == 128
        and chan_width // groups == 16
        and seq_total == groups * tok_rows
        and short_taps.shape[:2] == (3, 7)
    )
    chosen = by_group if fits else local
    return chosen(query_in, key_in, value_in, short_taps, long_filters, skip_gain, cotangent)


def solution(mesh):
    in_specs = (
        P("seq", "chan"),
        P("seq", "chan"),
        P("seq", "chan"),
        P(None, None, "chan"),
        P("chan", None),
        P("chan"),
        P("seq", "chan"),
    )
    out_specs = (
        P("seq", "chan"),
        P(None, "seq", "chan"),
        P(None, None, "chan"),
        P("chan"),
        P("chan", None),
    )
    return jax.shard_map(plan, mesh=mesh, in_specs=in_specs, out_specs=out_specs, check_vma=False)
```

```python
import functools
import math

import jax
import jax.numpy as jnp
from jax import lax
from jax.experimental import pallas as pl
from jax.experimental.pallas import tpu as pltpu
from jax.sharding import PartitionSpec as P


def from_behind(value, axis, steps):
    count = lax.axis_size(axis)
    initial, last = (max(0, -steps), min(count, count - steps))
    return lax.ppermute(value, axis, [(source, source + steps) for source in range(initial, last)])


def short_forward(extended, weights, rows_here):
    margin = weights.shape[0] - 1
    running = jnp.zeros((rows_here, extended.shape[1]), jnp.float32)
    for offset in range(weights.shape[0]):
        running = (
            running + weights[offset] * extended[margin - offset : margin - offset + rows_here]
        )
    return running


def short_backward(extended, weights, rows_here):
    running = jnp.zeros((rows_here, extended.shape[1]), jnp.float32)
    for offset in range(weights.shape[0]):
        running = running + weights[offset] * extended[offset : offset + rows_here]
    return running


def tap_sums(grad_rows, extended, tap_count, rows_here):
    margin = tap_count - 1
    sums_list = []
    for offset in range(tap_count):
        sums_list.append(
            jnp.sum(grad_rows * extended[margin - offset : margin - offset + rows_here], axis=0)
        )
    return jnp.stack(sums_list)


def hankel(padded, lag_start, height, breadth, seq_total):
    span = height + breadth - 1
    window = lax.dynamic_slice_in_dim(padded, lag_start + seq_total, span, axis=1)
    tiled = jnp.tile(window, (1, height))
    tiled = jnp.pad(tiled, ((0, 0), (0, height)))
    return tiled.reshape(padded.shape[0], height, span + 1)[:, :, :breadth]


def causal_part(padded, source_rows, source_start, target_start, target_count, seq_total):
    breadth = source_rows.shape[0]
    matrix = hankel(
        padded, target_start - source_start - breadth + 1, target_count, breadth, seq_total
    )
    return jnp.einsum("gts,sgc->tgc", matrix, source_rows[::-1], preferred_element_type=jnp.float32)


def anti_part(padded, target_rows, target_start, source_start, source_count, seq_total):
    breadth = target_rows.shape[0]
    matrix = hankel(
        padded, target_start - source_start - source_count + 1, source_count, breadth, seq_total
    )
    return jnp.einsum("gab,bgc->agc", matrix, target_rows, preferred_element_type=jnp.float32)[::-1]


def lag_part(buffer, target_rows, source_rows, target_start, source_start, seq_total):
    height = target_rows.shape[0]
    breadth = source_rows.shape[0]
    groups = target_rows.shape[1]
    padded_source = jnp.pad(source_rows[::-1], ((0, height), (0, 0), (0, 0)))
    products = jnp.einsum(
        "tgc,sgc->gts", target_rows, padded_source, preferred_element_type=jnp.float32
    )
    full_width = height + breadth
    skewed = products.reshape(groups, height * full_width)[:, : height * (full_width - 1)]
    skewed = skewed.reshape(groups, height, full_width - 1)
    diagonal = jnp.sum(skewed, axis=1)
    position = target_start - source_start - breadth + 1 + seq_total
    current = lax.dynamic_slice_in_dim(buffer, position, full_width - 1, axis=1)
    return lax.dynamic_update_slice_in_dim(buffer, current + diagonal, position, axis=1)


def local(query_in, key_in, value_in, short_taps, long_filters, skip_gain, cotangent):
    tok_rows, chan_width = query_in.shape
    groups, seq_total = long_filters.shape
    members = chan_width // groups
    tap_count = short_taps.shape[1]
    margin = tap_count - 1
    device = lax.axis_index("seq")
    own_start = device * tok_rows
    rim_rows = jnp.stack(
        [query_in[tok_rows - margin :], key_in[tok_rows - margin :], value_in[tok_rows - margin :]]
    )
    before = from_behind(rim_rows, "seq", 1)
    streams = [query_in, key_in, value_in]
    extended = [
        jnp.concatenate([before[stream], streams[stream]]).astype(jnp.float32)
        for stream in range(3)
    ]
    query_short = short_forward(extended[0], short_taps[0], tok_rows)
    key_short = short_forward(extended[1], short_taps[1], tok_rows)
    value_short = short_forward(extended[2], short_taps[2], tok_rows)
    gating = (key_short * value_short).astype(jnp.bfloat16)
    relayed = (cotangent.astype(jnp.float32) * query_short).astype(jnp.bfloat16)
    gating_wide = gating.astype(jnp.float32)
    relayed_wide = relayed.astype(jnp.float32)
    gating_groups = gating.reshape(tok_rows, groups, members)
    relayed_groups = relayed.reshape(tok_rows, groups, members)
    padded = jnp.concatenate([jnp.zeros((groups, seq_total), jnp.bfloat16), long_filters], axis=1)
    lag_buffer = jnp.zeros((groups, 2 * seq_total), jnp.float32)
    zeros_out = jnp.zeros((tok_rows, groups, members), jnp.float32)

    def target_pair(distance):
        return distance < 0

    totals = (zeros_out, lag_buffer)
    shard_rows = lax.all_gather(gating, "seq", axis=0, tiled=True)
    piece_rows = shard_rows.shape[0]
    step_rows = min(piece_rows, tok_rows)
    pieces = shard_rows.reshape(piece_rows // step_rows, step_rows, groups, members)

    def forward_visit_block(carried, element):
        position, rows_block = element
        source_start = position * step_rows

        def forward_active(partial_value):
            output_part, buffer = partial_value
            output_part = output_part + causal_part(
                padded, rows_block, source_start, own_start, tok_rows, seq_total
            )
            distance = device - source_start // tok_rows
            buffer = lax.cond(
                target_pair(distance),
                lambda held: lag_part(
                    held, relayed_groups, rows_block, own_start, source_start, seq_total
                ),
                lambda held: held,
                buffer,
            )
            return (output_part, buffer)

        carried = lax.cond(
            source_start < own_start + tok_rows,
            forward_active,
            lambda partial_value: partial_value,
            carried,
        )
        return (carried, None)

    totals, ignored = lax.scan(
        forward_visit_block, totals, (jnp.arange(piece_rows // step_rows, dtype=jnp.int32), pieces)
    )
    output_part, lag_buffer = totals
    output_sum = output_part.reshape(tok_rows, chan_width)
    totals = (zeros_out, lag_buffer)
    shard_rows = lax.all_gather(relayed, "seq", axis=0, tiled=True)
    piece_rows = shard_rows.shape[0]
    backward_step_rows = min(piece_rows, tok_rows)
    pieces = shard_rows.reshape(
        piece_rows // backward_step_rows, backward_step_rows, groups, members
    )

    def backward_visit_block(carried, element):
        position, rows_block = element
        target_start = position * backward_step_rows

        def backward_active(partial_value):
            grad_part, buffer = partial_value
            grad_part = grad_part + anti_part(
                padded, rows_block, target_start, own_start, tok_rows, seq_total
            )
            distance = target_start // tok_rows - device
            buffer = lax.cond(
                target_pair(distance),
                lambda held: held,
                lambda held: lag_part(
                    held, rows_block, gating_groups, target_start, own_start, seq_total
                ),
                buffer,
            )
            return (grad_part, buffer)

        carried = lax.cond(
            target_start + backward_step_rows > own_start,
            backward_active,
            lambda partial_value: partial_value,
            carried,
        )
        return (carried, None)

    totals, ignored = lax.scan(
        backward_visit_block,
        totals,
        (jnp.arange(piece_rows // backward_step_rows, dtype=jnp.int32), pieces),
    )
    grad_part, lag_buffer = totals
    grad_sum = grad_part.reshape(tok_rows, chan_width)
    lag_local = lag_buffer[:, seq_total:]
    long_out = output_sum + skip_gain * gating_wide
    block_out = (query_short * long_out).astype(jnp.bfloat16)
    grad_gating = grad_sum + skip_gain * relayed_wide
    cot_wide = cotangent.astype(jnp.float32)
    grad_shorts = [cot_wide * long_out, grad_gating * value_short, grad_gating * key_short]
    lead_rows = jnp.stack([grad_shorts[stream][:margin] for stream in range(3)])
    after = from_behind(lead_rows, "seq", -1)
    input_grads = jnp.stack(
        [
            short_backward(
                jnp.concatenate([grad_shorts[stream], after[stream]]), short_taps[stream], tok_rows
            )
            for stream in range(3)
        ]
    ).astype(jnp.bfloat16)
    tap_local = jnp.stack(
        [
            tap_sums(grad_shorts[stream], extended[stream], tap_count, tok_rows)
            for stream in range(3)
        ]
    )
    skip_local = jnp.sum(relayed_wide * gating_wide, axis=0)
    lag_total, tap_total, skip_total = lax.psum((lag_local, tap_local, skip_local), "seq")
    tap_scale = 1.0 / math.sqrt(seq_total)
    lag_scale = 1.0 / math.sqrt(seq_total * members)
    return (
        block_out,
        input_grads,
        tap_total * tap_scale,
        skip_total * tap_scale,
        lag_total * lag_scale,
    )


def pack_kernel(
    query_ref, key_ref, value_ref, cot_ref, skip_ref, out_ref, gain_ref, stream_buf, sems
):
    count, streams, members, tok_rows = out_ref.shape
    moves = [
        pltpu.make_async_copy(ref, stream_buf.at[stream], sems.at[stream])
        for stream, ref in enumerate((query_ref, key_ref, value_ref, cot_ref))
    ]
    moves.append(pltpu.make_async_copy(skip_ref, gain_ref, sems.at[streams]))
    for move in moves:
        move.start()
    for stream in range(streams):
        moves[stream].wait()
        flipped = stream_buf[stream].astype(jnp.float32).T.astype(jnp.bfloat16)
        out_ref[:, stream] = flipped.reshape(count, members, tok_rows)
    moves[streams].wait()


def group_kernel(
    in_ref, taps_ref, filters_ref, gain_ref, out_ref, table_ref, wide_ref, tile_ref
):
    count, _, members, span = in_ref.shape
    groups, seq_total = filters_ref.shape
    streams, tap_count, chan_width = taps_ref.shape
    rows = count * members
    mine = lax.axis_index("seq")
    shape = (count, members, span)
    lane = lax.broadcasted_iota(jnp.int32, shape, 2)
    reach = 3

    def later(value, steps):
        if steps == 0:
            return value
        turned = pltpu.roll(value, steps, 2)
        before = jnp.concatenate([jnp.zeros_like(turned[:1]), turned[:-1]], axis=0)
        return jnp.where(lane >= steps, turned, before)

    def earlier(value, steps):
        if steps == 0:
            return value
        turned = pltpu.roll(value, span - steps, 2)
        after = jnp.concatenate([turned[1:], jnp.zeros_like(turned[:1])], axis=0)
        return jnp.where(lane < span - steps, turned, after)

    table = jnp.concatenate(
        [taps_ref[stream] for stream in range(streams)]
        + [gain_ref[...], jnp.zeros((2, chan_width), jnp.float32)],
        axis=0,
    )
    table_ref[...] = table.T
    params = table_ref[pl.ds(pl.multiple_of(mine * members, members), members), :]

    def column(index):
        return jnp.broadcast_to(params[:, index : index + 1], (members, span))[None]

    chosen = lax.broadcasted_iota(jnp.int32, (groups, 1), 0) == mine
    filter_row = jnp.sum(
        jnp.where(chosen, filters_ref[...].astype(jnp.float32), 0.0), axis=0, keepdims=True
    )
    filter_row = jnp.concatenate([filter_row, jnp.zeros((1, span), jnp.float32)], axis=1)
    spread = jnp.broadcast_to(filter_row, (members, seq_total + span))
    first_rows = pltpu.roll(spread, 0, 1, stride=1, stride_axis=0).astype(jnp.bfloat16)
    row_parts = [first_rows] + [
        pltpu.roll(first_rows, first, 1) for first in range(members, span, members)
    ]
    toeplitz = jnp.concatenate(row_parts, axis=0)[:, :seq_total]

    cot = in_ref[:, streams].astype(jnp.float32)
    delayed, shorts = [], []
    for stream in range(streams):
        value = in_ref[:, stream]
        delayed.append([later(value, first) for first in range(0, tap_count, reach)])
        running = None
        for second in reversed(range(reach)):
            if running is not None:
                running = later(running, 1)
            for first in range(second, tap_count, reach):
                term = column(stream * tap_count + first) * delayed[stream][
                    first // reach
                ].astype(jnp.float32)
                running = term if running is None else running + term
        shorts.append(running)
    query_short, key_short, value_short = shorts
    gating = (key_short * value_short).astype(jnp.bfloat16).reshape(rows, span)
    relayed = (cot * query_short).astype(jnp.bfloat16).reshape(rows, span)

    gating_parts, relayed_parts, filter_parts = [gating], [relayed], [toeplitz[:, :span]]
    for step in range(1, count):
        gap = jnp.zeros((step * members, span), jnp.bfloat16)
        gating_parts.append(jnp.concatenate([gap, gating[: rows - step * members]], axis=0))
        relayed_parts.append(jnp.concatenate([relayed[step * members :], gap], axis=0))
        filter_parts.append(toeplitz[:, step * span : (step + 1) * span])
    gating_lags = jnp.concatenate(gating_parts, axis=1)
    relayed_lags = jnp.concatenate(relayed_parts, axis=1)
    forward = jnp.dot(
        gating_lags, jnp.concatenate(filter_parts, axis=0), preferred_element_type=jnp.float32
    )
    backward = lax.dot_general(
        relayed_lags, toeplitz, (((1,), (1,)), ((), ())), preferred_element_type=jnp.float32
    )
    half = span // 2
    flip = (
        lax.broadcasted_iota(jnp.int32, (span, span), 0)
        + lax.broadcasted_iota(jnp.int32, (span, span), 1)
        == span - 1
    ).astype(jnp.bfloat16)
    gating_turned = lax.dot_general(
        flip, gating, (((1,), (1,)), ((), ())), preferred_element_type=jnp.float32
    ).astype(jnp.bfloat16)
    gating_turned = jnp.concatenate([gating_turned[half:], gating_turned[:half]], axis=1)
    ahead = earlier(relayed.reshape(shape), half).reshape(rows, span)
    ahead_parts = [ahead]
    for step in range(1, count):
        gap = jnp.zeros((step * members, span), jnp.bfloat16)
        ahead_parts.append(jnp.concatenate([ahead[step * members :], gap], axis=0))
    targets = jnp.concatenate([relayed_lags, jnp.concatenate(ahead_parts, axis=1)], axis=0)
    products = jnp.dot(gating_turned, targets, preferred_element_type=jnp.float32)
    wide_ref[:, :seq_total] = products
    wide_ref[:, seq_total:] = jnp.zeros((half, span), jnp.float32)
    skewed = pltpu.roll(wide_ref[...], 0, 1, stride=1, stride_axis=0)
    diagonal = jnp.sum(skewed, axis=0, keepdims=True)
    diagonal = pltpu.roll(diagonal, seq_total + span - half + 1, 1)[:, :seq_total]
    lag_scale = 1.0 / math.sqrt(seq_total * members)
    lag_sums = jnp.concatenate(
        [diagonal[:, step * span : (step + 1) * span] for step in range(count)], axis=0
    )
    lag_sums = lag_sums * lag_scale

    gating_wide = gating.astype(jnp.float32).reshape(shape)
    relayed_wide = relayed.astype(jnp.float32).reshape(shape)
    gain = column(streams * tap_count)
    long_out = forward.reshape(shape) + gain * gating_wide
    grad_gating = backward.reshape(shape) + gain * relayed_wide
    out_ref[:, 0] = (query_short * long_out).astype(jnp.bfloat16)
    grad_shorts = [cot * long_out, grad_gating * value_short, grad_gating * key_short]
    tap_scale = 1.0 / math.sqrt(seq_total)

    def tokens(value):
        return jnp.concatenate([value[block] for block in range(count)], axis=1)

    def sums(left, right):
        product = lax.dot_general(
            jnp.concatenate(left, axis=0),
            jnp.concatenate(right, axis=0),
            (((1,), (1,)), ((), ())),
            preferred_element_type=jnp.float32,
        )
        same = (
            lax.broadcasted_iota(jnp.int32, product.shape, 0) % members
            == lax.broadcasted_iota(jnp.int32, product.shape, 1) % members
        )
        product = jnp.where(same, product, 0.0).reshape(len(left), members, -1)
        return jnp.sum(product, axis=1) * tap_scale

    tile_ref[...] = jnp.zeros((members, span), jnp.float32)
    next_row = 0
    for stream in range(streams):
        moved = [earlier(grad_shorts[stream], second) for second in range(reach)]
        left = [tokens(value.astype(jnp.bfloat16)) for value in moved]
        right = [tokens(value) for value in delayed[stream]]
        if stream == 0:
            left.append(tokens(relayed.reshape(shape)))
            right.append(tokens(gating.reshape(shape)))
        totals = sums(left, right)
        tile_ref[next_row : next_row + len(left), : totals.shape[1]] = totals
        next_row += len(left)
        running = None
        for place in reversed(range(len(delayed[stream]))):
            if running is not None:
                running = earlier(running, reach)
            for second in range(min(reach, tap_count - reach * place)):
                term = column(stream * tap_count + reach * place + second) * moved[second]
                running = term if running is None else running + term
        out_ref[:, 1 + stream] = running.astype(jnp.bfloat16)
    tile_ref[:count, half:] = lag_sums[:, half:]
    tile_ref[count:, half:] = pltpu.roll(lag_sums, half, 1)[:, half:]
    out_ref[:, streams + 1] = jnp.broadcast_to(tile_ref[...].astype(jnp.bfloat16)[None], shape)


def unpack_kernel(in_ref, out_ref, grads_ref, taps_ref, skip_ref, lags_ref):
    count, _, members, span = in_ref.shape
    streams, tap_count, chan_width = taps_ref.shape
    reach = 3
    for stream in range(streams + 1):
        block = in_ref[:, stream].reshape(count * members, span).astype(jnp.float32)
        flipped = block.T.astype(jnp.bfloat16)
        if stream == 0:
            out_ref[...] = flipped
        else:
            grads_ref[stream - 1] = flipped
    tile = in_ref[:, streams + 1].astype(jnp.float32)
    lane = lax.broadcasted_iota(jnp.int32, (1, members // 2, span), 2)
    lags = jnp.where(
        lane < span // 2, pltpu.roll(tile[:, members // 2 :], span // 2, 2), tile[:, : members // 2]
    )
    for step in range(members // 2):
        lags_ref[:, step * span : (step + 1) * span] = lags[:, step]
    lane = lax.broadcasted_iota(jnp.int32, (members, span), 1)
    spread = []
    for place in range(-(-tap_count // reach) + 1):
        total = None
        for group in range(count):
            moved = pltpu.roll(tile[group], (members * (group - place)) % span, 1)
            inside = (lane >= members * group) & (lane < members * (group + 1))
            total = moved if total is None else jnp.where(inside, moved, total)
        spread.append(total)
    first = 0
    for stream in range(streams):
        for place in range(-(-tap_count // reach)):
            taken = min(reach, tap_count - reach * place)
            taps_ref[stream, reach * place : reach * place + taken] = spread[place][
                first : first + taken
            ]
        first += reach + (stream == 0)
    skip_ref[...] = spread[-1][reach : reach + 1]


def by_group(query_in, key_in, value_in, short_taps, long_filters, skip_gain, cotangent):
    tok_rows, chan_width = query_in.shape
    groups, seq_total = long_filters.shape
    streams, tap_count, _ = short_taps.shape
    members = chan_width // groups
    count = groups
    vmem = pl.BlockSpec(memory_space=pltpu.VMEM)
    params = pltpu.CompilerParams(vmem_limit_bytes=32 * 1024 * 1024)
    packed, gain = pl.pallas_call(
        pack_kernel,
        out_shape=(
            jax.ShapeDtypeStruct((count, streams + 1, members, tok_rows), jnp.bfloat16),
            jax.ShapeDtypeStruct((1, chan_width), jnp.float32),
        ),
        in_specs=[pl.BlockSpec(memory_space=pltpu.HBM)] * 5,
        out_specs=(vmem,) * 2,
        scratch_shapes=[
            pltpu.VMEM((streams + 1, tok_rows, chan_width), jnp.bfloat16),
            pltpu.SemaphoreType.DMA((streams + 2,)),
        ],
        compiler_params=params,
        name="pack",
    )(
        *(
            pltpu.with_memory_space_constraint(value, pltpu.HBM)
            for value in (
                query_in, key_in, value_in, cotangent, skip_gain.reshape(1, chan_width)
            )
        )
    )
    packed = lax.all_to_all(packed, "seq", 0, 0, tiled=True)
    results = pl.pallas_call(
        group_kernel,
        out_shape=jax.ShapeDtypeStruct((count, streams + 2, members, tok_rows), jnp.bfloat16),
        in_specs=[vmem] * 4,
        out_specs=vmem,
        scratch_shapes=[
            pltpu.VMEM((chan_width, streams * tap_count + 3), jnp.float32),
            pltpu.VMEM((tok_rows // 2, seq_total + tok_rows), jnp.float32),
            pltpu.VMEM((members, tok_rows), jnp.float32),
        ],
        compiler_params=params,
        name="group",
    )(packed, short_taps, long_filters, gain)
    results = lax.all_to_all(results, "seq", 0, 0, tiled=True)
    block_out, input_grads, tap_grads, skip_grad, filter_grad = pl.pallas_call(
        unpack_kernel,
        out_shape=(
            jax.ShapeDtypeStruct((tok_rows, chan_width), jnp.bfloat16),
            jax.ShapeDtypeStruct((streams, tok_rows, chan_width), jnp.bfloat16),
            jax.ShapeDtypeStruct((streams, tap_count, chan_width), jnp.float32),
            jax.ShapeDtypeStruct((1, chan_width), jnp.float32),
            jax.ShapeDtypeStruct((groups, seq_total), jnp.float32),
        ),
        in_specs=[vmem],
        out_specs=(vmem,) * 5,
        compiler_params=params,
        name="unpack",
    )(results)
    return block_out, input_grads, tap_grads, skip_grad.reshape(chan_width), filter_grad


def plan(query_in, key_in, value_in, short_taps, long_filters, skip_gain, cotangent):
    tok_rows, chan_width = query_in.shape
    groups, seq_total = long_filters.shape
    fits = (
        lax.axis_size("seq") == groups
        and tok_rows == 128
        and chan_width == 128
        and chan_width // groups == 16
        and seq_total == groups * tok_rows
        and short_taps.shape[:2] == (3, 7)
    )
    chosen = by_group if fits else local
    return chosen(query_in, key_in, value_in, short_taps, long_filters, skip_gain, cotangent)


def solution(mesh):
    in_specs = (
        P("seq", "chan"),
        P("seq", "chan"),
        P("seq", "chan"),
        P(None, None, "chan"),
        P("chan", None),
        P("chan"),
        P("seq", "chan"),
    )
    out_specs = (
        P("seq", "chan"),
        P(None, "seq", "chan"),
        P(None, None, "chan"),
        P("chan"),
        P("chan", None),
    )
    return jax.shard_map(plan, mesh=mesh, in_specs=in_specs, out_specs=out_specs, check_vma=False)
```

```python
import functools
import math

import jax
import jax.numpy as jnp
from jax import lax
from jax.experimental import pallas as pl
from jax.experimental.pallas import tpu as pltpu
from jax.sharding import PartitionSpec as P


def from_behind(value, axis, steps):
    count = lax.axis_size(axis)
    initial, last = (max(0, -steps), min(count, count - steps))
    return lax.ppermute(value, axis, [(source, source + steps) for source in range(initial, last)])


def short_forward(extended, weights, rows_here):
    margin = weights.shape[0] - 1
    running = jnp.zeros((rows_here, extended.shape[1]), jnp.float32)
    for offset in range(weights.shape[0]):
        running = (
            running + weights[offset] * extended[margin - offset : margin - offset + rows_here]
        )
    return running


def short_backward(extended, weights, rows_here):
    running = jnp.zeros((rows_here, extended.shape[1]), jnp.float32)
    for offset in range(weights.shape[0]):
        running = running + weights[offset] * extended[offset : offset + rows_here]
    return running


def tap_sums(grad_rows, extended, tap_count, rows_here):
    margin = tap_count - 1
    sums_list = []
    for offset in range(tap_count):
        sums_list.append(
            jnp.sum(grad_rows * extended[margin - offset : margin - offset + rows_here], axis=0)
        )
    return jnp.stack(sums_list)


def hankel(padded, lag_start, height, breadth, seq_total):
    span = height + breadth - 1
    window = lax.dynamic_slice_in_dim(padded, lag_start + seq_total, span, axis=1)
    tiled = jnp.tile(window, (1, height))
    tiled = jnp.pad(tiled, ((0, 0), (0, height)))
    return tiled.reshape(padded.shape[0], height, span + 1)[:, :, :breadth]


def causal_part(padded, source_rows, source_start, target_start, target_count, seq_total):
    breadth = source_rows.shape[0]
    matrix = hankel(
        padded, target_start - source_start - breadth + 1, target_count, breadth, seq_total
    )
    return jnp.einsum("gts,sgc->tgc", matrix, source_rows[::-1], preferred_element_type=jnp.float32)


def anti_part(padded, target_rows, target_start, source_start, source_count, seq_total):
    breadth = target_rows.shape[0]
    matrix = hankel(
        padded, target_start - source_start - source_count + 1, source_count, breadth, seq_total
    )
    return jnp.einsum("gab,bgc->agc", matrix, target_rows, preferred_element_type=jnp.float32)[::-1]


def lag_part(buffer, target_rows, source_rows, target_start, source_start, seq_total):
    height = target_rows.shape[0]
    breadth = source_rows.shape[0]
    groups = target_rows.shape[1]
    padded_source = jnp.pad(source_rows[::-1], ((0, height), (0, 0), (0, 0)))
    products = jnp.einsum(
        "tgc,sgc->gts", target_rows, padded_source, preferred_element_type=jnp.float32
    )
    full_width = height + breadth
    skewed = products.reshape(groups, height * full_width)[:, : height * (full_width - 1)]
    skewed = skewed.reshape(groups, height, full_width - 1)
    diagonal = jnp.sum(skewed, axis=1)
    position = target_start - source_start - breadth + 1 + seq_total
    current = lax.dynamic_slice_in_dim(buffer, position, full_width - 1, axis=1)
    return lax.dynamic_update_slice_in_dim(buffer, current + diagonal, position, axis=1)


def local(query_in, key_in, value_in, short_taps, long_filters, skip_gain, cotangent):
    tok_rows, chan_width = query_in.shape
    groups, seq_total = long_filters.shape
    members = chan_width // groups
    tap_count = short_taps.shape[1]
    margin = tap_count - 1
    device = lax.axis_index("seq")
    own_start = device * tok_rows
    rim_rows = jnp.stack(
        [query_in[tok_rows - margin :], key_in[tok_rows - margin :], value_in[tok_rows - margin :]]
    )
    before = from_behind(rim_rows, "seq", 1)
    streams = [query_in, key_in, value_in]
    extended = [
        jnp.concatenate([before[stream], streams[stream]]).astype(jnp.float32)
        for stream in range(3)
    ]
    query_short = short_forward(extended[0], short_taps[0], tok_rows)
    key_short = short_forward(extended[1], short_taps[1], tok_rows)
    value_short = short_forward(extended[2], short_taps[2], tok_rows)
    gating = (key_short * value_short).astype(jnp.bfloat16)
    relayed = (cotangent.astype(jnp.float32) * query_short).astype(jnp.bfloat16)
    gating_wide = gating.astype(jnp.float32)
    relayed_wide = relayed.astype(jnp.float32)
    gating_groups = gating.reshape(tok_rows, groups, members)
    relayed_groups = relayed.reshape(tok_rows, groups, members)
    padded = jnp.concatenate([jnp.zeros((groups, seq_total), jnp.bfloat16), long_filters], axis=1)
    lag_buffer = jnp.zeros((groups, 2 * seq_total), jnp.float32)
    zeros_out = jnp.zeros((tok_rows, groups, members), jnp.float32)

    def target_pair(distance):
        return distance < 0

    totals = (zeros_out, lag_buffer)
    shard_rows = lax.all_gather(gating, "seq", axis=0, tiled=True)
    piece_rows = shard_rows.shape[0]
    step_rows = min(piece_rows, tok_rows)
    pieces = shard_rows.reshape(piece_rows // step_rows, step_rows, groups, members)

    def forward_visit_block(carried, element):
        position, rows_block = element
        source_start = position * step_rows

        def forward_active(partial_value):
            output_part, buffer = partial_value
            output_part = output_part + causal_part(
                padded, rows_block, source_start, own_start, tok_rows, seq_total
            )
            distance = device - source_start // tok_rows
            buffer = lax.cond(
                target_pair(distance),
                lambda held: lag_part(
                    held, relayed_groups, rows_block, own_start, source_start, seq_total
                ),
                lambda held: held,
                buffer,
            )
            return (output_part, buffer)

        carried = lax.cond(
            source_start < own_start + tok_rows,
            forward_active,
            lambda partial_value: partial_value,
            carried,
        )
        return (carried, None)

    totals, ignored = lax.scan(
        forward_visit_block, totals, (jnp.arange(piece_rows // step_rows, dtype=jnp.int32), pieces)
    )
    output_part, lag_buffer = totals
    output_sum = output_part.reshape(tok_rows, chan_width)
    totals = (zeros_out, lag_buffer)
    shard_rows = lax.all_gather(relayed, "seq", axis=0, tiled=True)
    piece_rows = shard_rows.shape[0]
    backward_step_rows = min(piece_rows, tok_rows)
    pieces = shard_rows.reshape(
        piece_rows // backward_step_rows, backward_step_rows, groups, members
    )

    def backward_visit_block(carried, element):
        position, rows_block = element
        target_start = position * backward_step_rows

        def backward_active(partial_value):
            grad_part, buffer = partial_value
            grad_part = grad_part + anti_part(
                padded, rows_block, target_start, own_start, tok_rows, seq_total
            )
            distance = target_start // tok_rows - device
            buffer = lax.cond(
                target_pair(distance),
                lambda held: held,
                lambda held: lag_part(
                    held, rows_block, gating_groups, target_start, own_start, seq_total
                ),
                buffer,
            )
            return (grad_part, buffer)

        carried = lax.cond(
            target_start + backward_step_rows > own_start,
            backward_active,
            lambda partial_value: partial_value,
            carried,
        )
        return (carried, None)

    totals, ignored = lax.scan(
        backward_visit_block,
        totals,
        (jnp.arange(piece_rows // backward_step_rows, dtype=jnp.int32), pieces),
    )
    grad_part, lag_buffer = totals
    grad_sum = grad_part.reshape(tok_rows, chan_width)
    lag_local = lag_buffer[:, seq_total:]
    long_out = output_sum + skip_gain * gating_wide
    block_out = (query_short * long_out).astype(jnp.bfloat16)
    grad_gating = grad_sum + skip_gain * relayed_wide
    cot_wide = cotangent.astype(jnp.float32)
    grad_shorts = [cot_wide * long_out, grad_gating * value_short, grad_gating * key_short]
    lead_rows = jnp.stack([grad_shorts[stream][:margin] for stream in range(3)])
    after = from_behind(lead_rows, "seq", -1)
    input_grads = jnp.stack(
        [
            short_backward(
                jnp.concatenate([grad_shorts[stream], after[stream]]), short_taps[stream], tok_rows
            )
            for stream in range(3)
        ]
    ).astype(jnp.bfloat16)
    tap_local = jnp.stack(
        [
            tap_sums(grad_shorts[stream], extended[stream], tap_count, tok_rows)
            for stream in range(3)
        ]
    )
    skip_local = jnp.sum(relayed_wide * gating_wide, axis=0)
    lag_total, tap_total, skip_total = lax.psum((lag_local, tap_local, skip_local), "seq")
    tap_scale = 1.0 / math.sqrt(seq_total)
    lag_scale = 1.0 / math.sqrt(seq_total * members)
    return (
        block_out,
        input_grads,
        tap_total * tap_scale,
        skip_total * tap_scale,
        lag_total * lag_scale,
    )


def pack_kernel(
    query_ref, key_ref, value_ref, cot_ref, skip_ref, out_ref, gain_ref, stream_buf, sems
):
    count, streams, members, tok_rows = out_ref.shape
    moves = [
        pltpu.make_async_copy(ref, stream_buf.at[stream], sems.at[stream])
        for stream, ref in enumerate((query_ref, key_ref, value_ref, cot_ref))
    ]
    moves.append(pltpu.make_async_copy(skip_ref, gain_ref, sems.at[streams]))
    for move in moves:
        move.start()
    for stream in range(streams):
        moves[stream].wait()
        flipped = stream_buf[stream].astype(jnp.float32).T.astype(jnp.bfloat16)
        out_ref[:, stream] = flipped.reshape(count, members, tok_rows)
    moves[streams].wait()


def group_kernel(
    in_ref, taps_ref, filters_ref, gain_ref, out_ref, table_ref, wide_ref, tile_ref
):
    count, _, members, span = in_ref.shape
    groups, seq_total = filters_ref.shape
    streams, tap_count, chan_width = taps_ref.shape
    rows = count * members
    mine = lax.axis_index("seq")
    shape = (count, members, span)
    lane = lax.broadcasted_iota(jnp.int32, shape, 2)
    reach = 3

    def later(value, steps):
        if steps == 0:
            return value
        turned = pltpu.roll(value, steps, 2)
        before = jnp.concatenate([jnp.zeros_like(turned[:1]), turned[:-1]], axis=0)
        return jnp.where(lane >= steps, turned, before)

    def earlier(value, steps):
        if steps == 0:
            return value
        turned = pltpu.roll(value, span - steps, 2)
        after = jnp.concatenate([turned[1:], jnp.zeros_like(turned[:1])], axis=0)
        return jnp.where(lane < span - steps, turned, after)

    table = jnp.concatenate(
        [taps_ref[stream] for stream in range(streams)]
        + [gain_ref[...], jnp.zeros((2, chan_width), jnp.float32)],
        axis=0,
    )
    table_ref[...] = table.T
    params = table_ref[pl.ds(pl.multiple_of(mine * members, members), members), :]

    def column(index):
        return jnp.broadcast_to(params[:, index : index + 1], (members, span))[None]

    chosen = lax.broadcasted_iota(jnp.int32, (groups, 1), 0) == mine
    filter_row = jnp.sum(
        jnp.where(chosen, filters_ref[...].astype(jnp.float32), 0.0), axis=0, keepdims=True
    )
    filter_row = jnp.concatenate([filter_row, jnp.zeros((1, span), jnp.float32)], axis=1)
    spread = jnp.broadcast_to(filter_row, (members, seq_total + span))
    first_rows = pltpu.roll(spread, 0, 1, stride=1, stride_axis=0).astype(jnp.bfloat16)
    row_parts = [first_rows] + [
        pltpu.roll(first_rows, first, 1) for first in range(members, span, members)
    ]
    toeplitz = jnp.concatenate(row_parts, axis=0)[:, :seq_total]

    def delays(stream):
        return [later(in_ref[:, stream], first) for first in range(0, tap_count, reach)]

    def short(stream, values):
        running = None
        for second in reversed(range(reach)):
            if running is not None:
                running = later(running, 1)
            for first in range(second, tap_count, reach):
                value = values[first // reach].astype(jnp.float32)
                term = column(stream * tap_count + first) * value
                running = term if running is None else running + term
        return running

    def ahead_by_blocks(value):
        parts = [value]
        for step in range(1, count):
            gap = jnp.zeros((step * members, span), jnp.bfloat16)
            parts.append(jnp.concatenate([value[step * members :], gap], axis=0))
        return jnp.concatenate(parts, axis=1)

    gain = column(streams * tap_count)
    cot = in_ref[:, streams].astype(jnp.float32)
    delayed = [delays(0)]
    query_short = short(0, delayed[0])
    relayed = (cot * query_short).astype(jnp.bfloat16).reshape(rows, span)
    relayed_lags = ahead_by_blocks(relayed)
    backward = lax.dot_general(
        relayed_lags, toeplitz, (((1,), (1,)), ((), ())), preferred_element_type=jnp.float32
    )

    delayed += [delays(1), delays(2)]
    key_short = short(1, delayed[1])
    value_short = short(2, delayed[2])
    gating = (key_short * value_short).astype(jnp.bfloat16).reshape(rows, span)
    gating_parts, filter_parts = [gating], [toeplitz[:, :span]]
    for step in range(1, count):
        gap = jnp.zeros((step * members, span), jnp.bfloat16)
        gating_parts.append(jnp.concatenate([gap, gating[: rows - step * members]], axis=0))
        filter_parts.append(toeplitz[:, step * span : (step + 1) * span])
    forward = jnp.dot(
        jnp.concatenate(gating_parts, axis=1),
        jnp.concatenate(filter_parts, axis=0),
        preferred_element_type=jnp.float32,
    )

    half = span // 2
    flip = (
        lax.broadcasted_iota(jnp.int32, (span, span), 0)
        + lax.broadcasted_iota(jnp.int32, (span, span), 1)
        == span - 1
    ).astype(jnp.bfloat16)
    gating_turned = lax.dot_general(
        flip, gating, (((1,), (1,)), ((), ())), preferred_element_type=jnp.float32
    ).astype(jnp.bfloat16)
    gating_turned = jnp.concatenate([gating_turned[half:], gating_turned[:half]], axis=1)
    ahead = earlier(relayed.reshape(shape), half).reshape(rows, span)
    targets = jnp.concatenate([relayed_lags, ahead_by_blocks(ahead)], axis=0)
    wide_ref[:, :seq_total] = jnp.dot(
        gating_turned, targets, preferred_element_type=jnp.float32
    )
    wide_ref[:, seq_total:] = jnp.zeros((half, span), jnp.float32)

    tap_scale = 1.0 / math.sqrt(seq_total)

    def tokens(value):
        return jnp.concatenate([value[block] for block in range(count)], axis=1)

    def sums(left, right):
        product = lax.dot_general(
            jnp.concatenate(left, axis=0),
            jnp.concatenate(right, axis=0),
            (((1,), (1,)), ((), ())),
            preferred_element_type=jnp.float32,
        )
        same = (
            lax.broadcasted_iota(jnp.int32, product.shape, 0) % members
            == lax.broadcasted_iota(jnp.int32, product.shape, 1) % members
        )
        product = jnp.where(same, product, 0.0).reshape(len(left), members, -1)
        return jnp.sum(product, axis=1) * tap_scale

    tile_ref[...] = jnp.zeros((members, span), jnp.float32)

    def finish(stream, grad_short, first_row, more_left=(), more_right=()):
        moved = [earlier(grad_short, second) for second in range(reach)]
        left = [tokens(value.astype(jnp.bfloat16)) for value in moved] + list(more_left)
        right = [tokens(value) for value in delayed[stream]] + list(more_right)
        totals = sums(left, right)
        tile_ref[first_row : first_row + len(left), : totals.shape[1]] = totals
        running = None
        for place in reversed(range(len(delayed[stream]))):
            if running is not None:
                running = earlier(running, reach)
            for second in range(min(reach, tap_count - reach * place)):
                term = column(stream * tap_count + reach * place + second) * moved[second]
                running = term if running is None else running + term
        out_ref[:, 1 + stream] = running.astype(jnp.bfloat16)

    grad_gating = backward.reshape(shape) + gain * relayed.astype(jnp.float32).reshape(shape)
    finish(1, grad_gating * value_short, reach + 1)
    finish(2, grad_gating * key_short, 2 * reach + 1)

    long_out = forward.reshape(shape) + gain * gating.astype(jnp.float32).reshape(shape)
    out_ref[:, 0] = (query_short * long_out).astype(jnp.bfloat16)
    finish(
        0, cot * long_out, 0, [tokens(relayed.reshape(shape))], [tokens(gating.reshape(shape))]
    )

    skewed = pltpu.roll(wide_ref[...], 0, 1, stride=1, stride_axis=0)
    diagonal = jnp.sum(skewed, axis=0, keepdims=True)
    diagonal = pltpu.roll(diagonal, seq_total + span - half + 1, 1)[:, :seq_total]
    lag_scale = 1.0 / math.sqrt(seq_total * members)
    lag_sums = jnp.concatenate(
        [diagonal[:, step * span : (step + 1) * span] for step in range(count)], axis=0
    )
    lag_sums = lag_sums * lag_scale
    tile_ref[:count, half:] = lag_sums[:, half:]
    tile_ref[count:, half:] = pltpu.roll(lag_sums, half, 1)[:, half:]
    out_ref[:, streams + 1] = jnp.broadcast_to(tile_ref[...].astype(jnp.bfloat16)[None], shape)


def unpack_kernel(in_ref, out_ref, grads_ref, taps_ref, skip_ref, lags_ref):
    count, _, members, span = in_ref.shape
    streams, tap_count, chan_width = taps_ref.shape
    reach = 3
    for stream in range(streams + 1):
        block = in_ref[:, stream].reshape(count * members, span).astype(jnp.float32)
        flipped = block.T.astype(jnp.bfloat16)
        if stream == 0:
            out_ref[...] = flipped
        else:
            grads_ref[stream - 1] = flipped
    tile = in_ref[:, streams + 1].astype(jnp.float32)
    lane = lax.broadcasted_iota(jnp.int32, (1, members // 2, span), 2)
    lags = jnp.where(
        lane < span // 2, pltpu.roll(tile[:, members // 2 :], span // 2, 2), tile[:, : members // 2]
    )
    for step in range(members // 2):
        lags_ref[:, step * span : (step + 1) * span] = lags[:, step]
    lane = lax.broadcasted_iota(jnp.int32, (members, span), 1)
    spread = []
    for place in range(-(-tap_count // reach) + 1):
        total = None
        for group in range(count):
            moved = pltpu.roll(tile[group], (members * (group - place)) % span, 1)
            inside = (lane >= members * group) & (lane < members * (group + 1))
            total = moved if total is None else jnp.where(inside, moved, total)
        spread.append(total)
    first = 0
    for stream in range(streams):
        for place in range(-(-tap_count // reach)):
            taken = min(reach, tap_count - reach * place)
            taps_ref[stream, reach * place : reach * place + taken] = spread[place][
                first : first + taken
            ]
        first += reach + (stream == 0)
    skip_ref[...] = spread[-1][reach : reach + 1]


def by_group(query_in, key_in, value_in, short_taps, long_filters, skip_gain, cotangent):
    tok_rows, chan_width = query_in.shape
    groups, seq_total = long_filters.shape
    streams, tap_count, _ = short_taps.shape
    members = chan_width // groups
    count = groups
    vmem = pl.BlockSpec(memory_space=pltpu.VMEM)
    params = pltpu.CompilerParams(vmem_limit_bytes=32 * 1024 * 1024)
    packed, gain = pl.pallas_call(
        pack_kernel,
        out_shape=(
            jax.ShapeDtypeStruct((count, streams + 1, members, tok_rows), jnp.bfloat16),
            jax.ShapeDtypeStruct((1, chan_width), jnp.float32),
        ),
        in_specs=[pl.BlockSpec(memory_space=pltpu.HBM)] * 5,
        out_specs=(vmem,) * 2,
        scratch_shapes=[
            pltpu.VMEM((streams + 1, tok_rows, chan_width), jnp.bfloat16),
            pltpu.SemaphoreType.DMA((streams + 2,)),
        ],
        compiler_params=params,
        name="pack",
    )(
        *(
            pltpu.with_memory_space_constraint(value, pltpu.HBM)
            for value in (
                query_in, key_in, value_in, cotangent, skip_gain.reshape(1, chan_width)
            )
        )
    )
    packed = lax.all_to_all(packed, "seq", 0, 0, tiled=True)
    results = pl.pallas_call(
        group_kernel,
        out_shape=jax.ShapeDtypeStruct((count, streams + 2, members, tok_rows), jnp.bfloat16),
        in_specs=[vmem] * 4,
        out_specs=vmem,
        scratch_shapes=[
            pltpu.VMEM((chan_width, streams * tap_count + 3), jnp.float32),
            pltpu.VMEM((tok_rows // 2, seq_total + tok_rows), jnp.float32),
            pltpu.VMEM((members, tok_rows), jnp.float32),
        ],
        compiler_params=params,
        name="group",
    )(packed, short_taps, long_filters, gain)
    results = lax.all_to_all(results, "seq", 0, 0, tiled=True)
    block_out, input_grads, tap_grads, skip_grad, filter_grad = pl.pallas_call(
        unpack_kernel,
        out_shape=(
            jax.ShapeDtypeStruct((tok_rows, chan_width), jnp.bfloat16),
            jax.ShapeDtypeStruct((streams, tok_rows, chan_width), jnp.bfloat16),
            jax.ShapeDtypeStruct((streams, tap_count, chan_width), jnp.float32),
            jax.ShapeDtypeStruct((1, chan_width), jnp.float32),
            jax.ShapeDtypeStruct((groups, seq_total), jnp.float32),
        ),
        in_specs=[vmem],
        out_specs=(vmem,) * 5,
        compiler_params=params,
        name="unpack",
    )(results)
    return block_out, input_grads, tap_grads, skip_grad.reshape(chan_width), filter_grad


def plan(query_in, key_in, value_in, short_taps, long_filters, skip_gain, cotangent):
    tok_rows, chan_width = query_in.shape
    groups, seq_total = long_filters.shape
    fits = (
        lax.axis_size("seq") == groups
        and tok_rows == 128
        and chan_width == 128
        and chan_width // groups == 16
        and seq_total == groups * tok_rows
        and short_taps.shape[:2] == (3, 7)
    )
    chosen = by_group if fits else local
    return chosen(query_in, key_in, value_in, short_taps, long_filters, skip_gain, cotangent)


def solution(mesh):
    in_specs = (
        P("seq", "chan"),
        P("seq", "chan"),
        P("seq", "chan"),
        P(None, None, "chan"),
        P("chan", None),
        P("chan"),
        P("seq", "chan"),
    )
    out_specs = (
        P("seq", "chan"),
        P(None, "seq", "chan"),
        P(None, None, "chan"),
        P("chan"),
        P("chan", None),
    )
    return jax.shard_map(plan, mesh=mesh, in_specs=in_specs, out_specs=out_specs, check_vma=False)
```

```python
import functools
import math

import jax
import jax.numpy as jnp
from jax import lax
from jax.experimental import pallas as pl
from jax.experimental.pallas import tpu as pltpu
from jax.sharding import PartitionSpec as P


def from_behind(value, axis, steps):
    count = lax.axis_size(axis)
    initial, last = (max(0, -steps), min(count, count - steps))
    return lax.ppermute(value, axis, [(source, source + steps) for source in range(initial, last)])


def short_forward(extended, weights, rows_here):
    margin = weights.shape[0] - 1
    running = jnp.zeros((rows_here, extended.shape[1]), jnp.float32)
    for offset in range(weights.shape[0]):
        running = (
            running + weights[offset] * extended[margin - offset : margin - offset + rows_here]
        )
    return running


def short_backward(extended, weights, rows_here):
    running = jnp.zeros((rows_here, extended.shape[1]), jnp.float32)
    for offset in range(weights.shape[0]):
        running = running + weights[offset] * extended[offset : offset + rows_here]
    return running


def tap_sums(grad_rows, extended, tap_count, rows_here):
    margin = tap_count - 1
    sums_list = []
    for offset in range(tap_count):
        sums_list.append(
            jnp.sum(grad_rows * extended[margin - offset : margin - offset + rows_here], axis=0)
        )
    return jnp.stack(sums_list)


def hankel(padded, lag_start, height, breadth, seq_total):
    span = height + breadth - 1
    window = lax.dynamic_slice_in_dim(padded, lag_start + seq_total, span, axis=1)
    tiled = jnp.tile(window, (1, height))
    tiled = jnp.pad(tiled, ((0, 0), (0, height)))
    return tiled.reshape(padded.shape[0], height, span + 1)[:, :, :breadth]


def causal_part(padded, source_rows, source_start, target_start, target_count, seq_total):
    breadth = source_rows.shape[0]
    matrix = hankel(
        padded, target_start - source_start - breadth + 1, target_count, breadth, seq_total
    )
    return jnp.einsum("gts,sgc->tgc", matrix, source_rows[::-1], preferred_element_type=jnp.float32)


def anti_part(padded, target_rows, target_start, source_start, source_count, seq_total):
    breadth = target_rows.shape[0]
    matrix = hankel(
        padded, target_start - source_start - source_count + 1, source_count, breadth, seq_total
    )
    return jnp.einsum("gab,bgc->agc", matrix, target_rows, preferred_element_type=jnp.float32)[::-1]


def lag_part(buffer, target_rows, source_rows, target_start, source_start, seq_total):
    height = target_rows.shape[0]
    breadth = source_rows.shape[0]
    groups = target_rows.shape[1]
    padded_source = jnp.pad(source_rows[::-1], ((0, height), (0, 0), (0, 0)))
    products = jnp.einsum(
        "tgc,sgc->gts", target_rows, padded_source, preferred_element_type=jnp.float32
    )
    full_width = height + breadth
    skewed = products.reshape(groups, height * full_width)[:, : height * (full_width - 1)]
    skewed = skewed.reshape(groups, height, full_width - 1)
    diagonal = jnp.sum(skewed, axis=1)
    position = target_start - source_start - breadth + 1 + seq_total
    current = lax.dynamic_slice_in_dim(buffer, position, full_width - 1, axis=1)
    return lax.dynamic_update_slice_in_dim(buffer, current + diagonal, position, axis=1)


def local(query_in, key_in, value_in, short_taps, long_filters, skip_gain, cotangent):
    tok_rows, chan_width = query_in.shape
    groups, seq_total = long_filters.shape
    members = chan_width // groups
    tap_count = short_taps.shape[1]
    margin = tap_count - 1
    device = lax.axis_index("seq")
    own_start = device * tok_rows
    rim_rows = jnp.stack(
        [query_in[tok_rows - margin :], key_in[tok_rows - margin :], value_in[tok_rows - margin :]]
    )
    before = from_behind(rim_rows, "seq", 1)
    streams = [query_in, key_in, value_in]
    extended = [
        jnp.concatenate([before[stream], streams[stream]]).astype(jnp.float32)
        for stream in range(3)
    ]
    query_short = short_forward(extended[0], short_taps[0], tok_rows)
    key_short = short_forward(extended[1], short_taps[1], tok_rows)
    value_short = short_forward(extended[2], short_taps[2], tok_rows)
    gating = (key_short * value_short).astype(jnp.bfloat16)
    relayed = (cotangent.astype(jnp.float32) * query_short).astype(jnp.bfloat16)
    gating_wide = gating.astype(jnp.float32)
    relayed_wide = relayed.astype(jnp.float32)
    gating_groups = gating.reshape(tok_rows, groups, members)
    relayed_groups = relayed.reshape(tok_rows, groups, members)
    padded = jnp.concatenate([jnp.zeros((groups, seq_total), jnp.bfloat16), long_filters], axis=1)
    lag_buffer = jnp.zeros((groups, 2 * seq_total), jnp.float32)
    zeros_out = jnp.zeros((tok_rows, groups, members), jnp.float32)

    def target_pair(distance):
        return distance < 0

    totals = (zeros_out, lag_buffer)
    shard_rows = lax.all_gather(gating, "seq", axis=0, tiled=True)
    piece_rows = shard_rows.shape[0]
    step_rows = min(piece_rows, tok_rows)
    pieces = shard_rows.reshape(piece_rows // step_rows, step_rows, groups, members)

    def forward_visit_block(carried, element):
        position, rows_block = element
        source_start = position * step_rows

        def forward_active(partial_value):
            output_part, buffer = partial_value
            output_part = output_part + causal_part(
                padded, rows_block, source_start, own_start, tok_rows, seq_total
            )
            distance = device - source_start // tok_rows
            buffer = lax.cond(
                target_pair(distance),
                lambda held: lag_part(
                    held, relayed_groups, rows_block, own_start, source_start, seq_total
                ),
                lambda held: held,
                buffer,
            )
            return (output_part, buffer)

        carried = lax.cond(
            source_start < own_start + tok_rows,
            forward_active,
            lambda partial_value: partial_value,
            carried,
        )
        return (carried, None)

    totals, ignored = lax.scan(
        forward_visit_block, totals, (jnp.arange(piece_rows // step_rows, dtype=jnp.int32), pieces)
    )
    output_part, lag_buffer = totals
    output_sum = output_part.reshape(tok_rows, chan_width)
    totals = (zeros_out, lag_buffer)
    shard_rows = lax.all_gather(relayed, "seq", axis=0, tiled=True)
    piece_rows = shard_rows.shape[0]
    backward_step_rows = min(piece_rows, tok_rows)
    pieces = shard_rows.reshape(
        piece_rows // backward_step_rows, backward_step_rows, groups, members
    )

    def backward_visit_block(carried, element):
        position, rows_block = element
        target_start = position * backward_step_rows

        def backward_active(partial_value):
            grad_part, buffer = partial_value
            grad_part = grad_part + anti_part(
                padded, rows_block, target_start, own_start, tok_rows, seq_total
            )
            distance = target_start // tok_rows - device
            buffer = lax.cond(
                target_pair(distance),
                lambda held: held,
                lambda held: lag_part(
                    held, rows_block, gating_groups, target_start, own_start, seq_total
                ),
                buffer,
            )
            return (grad_part, buffer)

        carried = lax.cond(
            target_start + backward_step_rows > own_start,
            backward_active,
            lambda partial_value: partial_value,
            carried,
        )
        return (carried, None)

    totals, ignored = lax.scan(
        backward_visit_block,
        totals,
        (jnp.arange(piece_rows // backward_step_rows, dtype=jnp.int32), pieces),
    )
    grad_part, lag_buffer = totals
    grad_sum = grad_part.reshape(tok_rows, chan_width)
    lag_local = lag_buffer[:, seq_total:]
    long_out = output_sum + skip_gain * gating_wide
    block_out = (query_short * long_out).astype(jnp.bfloat16)
    grad_gating = grad_sum + skip_gain * relayed_wide
    cot_wide = cotangent.astype(jnp.float32)
    grad_shorts = [cot_wide * long_out, grad_gating * value_short, grad_gating * key_short]
    lead_rows = jnp.stack([grad_shorts[stream][:margin] for stream in range(3)])
    after = from_behind(lead_rows, "seq", -1)
    input_grads = jnp.stack(
        [
            short_backward(
                jnp.concatenate([grad_shorts[stream], after[stream]]), short_taps[stream], tok_rows
            )
            for stream in range(3)
        ]
    ).astype(jnp.bfloat16)
    tap_local = jnp.stack(
        [
            tap_sums(grad_shorts[stream], extended[stream], tap_count, tok_rows)
            for stream in range(3)
        ]
    )
    skip_local = jnp.sum(relayed_wide * gating_wide, axis=0)
    lag_total, tap_total, skip_total = lax.psum((lag_local, tap_local, skip_local), "seq")
    tap_scale = 1.0 / math.sqrt(seq_total)
    lag_scale = 1.0 / math.sqrt(seq_total * members)
    return (
        block_out,
        input_grads,
        tap_total * tap_scale,
        skip_total * tap_scale,
        lag_total * lag_scale,
    )


def pack_kernel(
    query_ref, key_ref, value_ref, cot_ref, skip_ref, out_ref, gain_ref, stream_buf, sems
):
    count, streams, members, tok_rows = out_ref.shape
    moves = [
        pltpu.make_async_copy(ref, stream_buf.at[stream], sems.at[stream])
        for stream, ref in enumerate((query_ref, key_ref, value_ref, cot_ref))
    ]
    moves.append(pltpu.make_async_copy(skip_ref, gain_ref, sems.at[streams]))
    for move in moves:
        move.start()
    for stream in range(streams):
        moves[stream].wait()
        flipped = stream_buf[stream].astype(jnp.float32).T.astype(jnp.bfloat16)
        out_ref[:, stream] = flipped.reshape(count, members, tok_rows)
    moves[streams].wait()


def group_kernel(
    in_ref, taps_ref, filters_ref, gain_ref, out_ref,
    table_ref, wide_ref, tile_ref, columns_ref, short_ref, grad_ref, delayed_ref, moved_ref,
):
    count, _, members, span = in_ref.shape
    groups, seq_total = filters_ref.shape
    streams, tap_count, chan_width = taps_ref.shape
    rows = count * members
    mine = lax.axis_index("seq")
    shape = (count, members, span)
    lane = lax.broadcasted_iota(jnp.int32, shape, 2)
    reach = 3

    def later(value, steps):
        if steps == 0:
            return value
        turned = pltpu.roll(value, steps, 2)
        before = jnp.concatenate([jnp.zeros_like(turned[:1]), turned[:-1]], axis=0)
        return jnp.where(lane >= steps, turned, before)

    def earlier(value, steps):
        if steps == 0:
            return value
        turned = pltpu.roll(value, span - steps, 2)
        after = jnp.concatenate([turned[1:], jnp.zeros_like(turned[:1])], axis=0)
        return jnp.where(lane < span - steps, turned, after)

    table = jnp.concatenate(
        [taps_ref[stream] for stream in range(streams)]
        + [gain_ref[...], jnp.zeros((2, chan_width), jnp.float32)],
        axis=0,
    )
    table_ref[...] = table.T
    params = table_ref[pl.ds(pl.multiple_of(mine * members, members), members), :]

    for index in range(streams * tap_count + 1):
        columns_ref[index] = jnp.broadcast_to(params[:, index : index + 1], (members, span))

    chosen = lax.broadcasted_iota(jnp.int32, (groups, 1), 0) == mine
    filter_row = jnp.sum(
        jnp.where(chosen, filters_ref[...].astype(jnp.float32), 0.0), axis=0, keepdims=True
    )
    filter_row = jnp.concatenate([filter_row, jnp.zeros((1, span), jnp.float32)], axis=1)
    spread = jnp.broadcast_to(filter_row, (members, seq_total + span))
    first_rows = pltpu.roll(spread, 0, 1, stride=1, stride_axis=0).astype(jnp.bfloat16)
    row_parts = [first_rows] + [
        pltpu.roll(first_rows, first, 1) for first in range(members, span, members)
    ]
    toeplitz = jnp.concatenate(row_parts, axis=0)[:, :seq_total]

    places = range(-(-tap_count // reach))

    @pl.loop(0, streams)
    def _(stream):
        values = [later(in_ref[:, stream], reach * place) for place in places]
        for place in places:
            delayed_ref[stream, place] = values[place]
        running = None
        for second in reversed(range(reach)):
            if running is not None:
                running = later(running, 1)
            for first in range(second, tap_count, reach):
                value = values[first // reach].astype(jnp.float32)
                term = columns_ref[stream * tap_count + first][None] * value
                running = term if running is None else running + term
        short_ref[stream] = running

    query_short, key_short, value_short = [short_ref[stream] for stream in range(streams)]

    def ahead_by_blocks(value):
        parts = [value]
        for step in range(1, count):
            gap = jnp.zeros((step * members, span), jnp.bfloat16)
            parts.append(jnp.concatenate([value[step * members :], gap], axis=0))
        return jnp.concatenate(parts, axis=1)

    gain = columns_ref[streams * tap_count][None]
    cot = in_ref[:, streams].astype(jnp.float32)
    relayed = (cot * query_short).astype(jnp.bfloat16).reshape(rows, span)
    relayed_lags = ahead_by_blocks(relayed)
    backward = lax.dot_general(
        relayed_lags, toeplitz, (((1,), (1,)), ((), ())), preferred_element_type=jnp.float32
    )

    gating = (key_short * value_short).astype(jnp.bfloat16).reshape(rows, span)
    gating_parts, filter_parts = [gating], [toeplitz[:, :span]]
    for step in range(1, count):
        gap = jnp.zeros((step * members, span), jnp.bfloat16)
        gating_parts.append(jnp.concatenate([gap, gating[: rows - step * members]], axis=0))
        filter_parts.append(toeplitz[:, step * span : (step + 1) * span])
    forward = jnp.dot(
        jnp.concatenate(gating_parts, axis=1),
        jnp.concatenate(filter_parts, axis=0),
        preferred_element_type=jnp.float32,
    )

    half = span // 2
    flip = (
        lax.broadcasted_iota(jnp.int32, (span, span), 0)
        + lax.broadcasted_iota(jnp.int32, (span, span), 1)
        == span - 1
    ).astype(jnp.bfloat16)
    gating_turned = lax.dot_general(
        flip, gating, (((1,), (1,)), ((), ())), preferred_element_type=jnp.float32
    ).astype(jnp.bfloat16)
    gating_turned = jnp.concatenate([gating_turned[half:], gating_turned[:half]], axis=1)
    ahead = earlier(relayed.reshape(shape), half).reshape(rows, span)
    targets = jnp.concatenate([relayed_lags, ahead_by_blocks(ahead)], axis=0)
    wide_ref[:, :seq_total] = jnp.dot(
        gating_turned, targets, preferred_element_type=jnp.float32
    )
    wide_ref[:, seq_total:] = jnp.zeros((half, span), jnp.float32)

    tap_scale = 1.0 / math.sqrt(seq_total)

    def tokens(value):
        return jnp.concatenate([value[block] for block in range(count)], axis=1)

    def sums(left, right):
        product = lax.dot_general(
            jnp.concatenate(left, axis=0),
            jnp.concatenate(right, axis=0),
            (((1,), (1,)), ((), ())),
            preferred_element_type=jnp.float32,
        )
        same = (
            lax.broadcasted_iota(jnp.int32, product.shape, 0) % members
            == lax.broadcasted_iota(jnp.int32, product.shape, 1) % members
        )
        product = jnp.where(same, product, 0.0).reshape(len(left), members, -1)
        return jnp.sum(product, axis=1) * tap_scale

    tile_ref[...] = jnp.zeros((members, span), jnp.float32)

    grad_gating = backward.reshape(shape) + gain * relayed.astype(jnp.float32).reshape(shape)
    long_out = forward.reshape(shape) + gain * gating.astype(jnp.float32).reshape(shape)
    out_ref[:, 0] = (query_short * long_out).astype(jnp.bfloat16)
    grad_ref[0] = cot * long_out
    grad_ref[1] = grad_gating * value_short
    grad_ref[2] = grad_gating * key_short

    @pl.loop(0, streams)
    def _(stream):
        moved = [earlier(grad_ref[stream], second) for second in range(reach)]
        for second in range(reach):
            moved_ref[stream, second] = moved[second].astype(jnp.bfloat16)
        running = None
        for place in reversed(places):
            if running is not None:
                running = earlier(running, reach)
            for second in range(min(reach, tap_count - reach * place)):
                index = stream * tap_count + reach * place + second
                term = columns_ref[index][None] * moved[second]
                running = term if running is None else running + term
        out_ref[:, 1 + stream] = running.astype(jnp.bfloat16)

    first_row = 0
    for stream in range(streams):
        left = [tokens(moved_ref[stream, second]) for second in range(reach)]
        right = [tokens(delayed_ref[stream, place]) for place in places]
        if stream == 0:
            left.append(tokens(relayed.reshape(shape)))
            right.append(tokens(gating.reshape(shape)))
        totals = sums(left, right)
        tile_ref[first_row : first_row + len(left), : totals.shape[1]] = totals
        first_row += len(left)

    skewed = pltpu.roll(wide_ref[...], 0, 1, stride=1, stride_axis=0)
    diagonal = jnp.sum(skewed, axis=0, keepdims=True)
    diagonal = pltpu.roll(diagonal, seq_total + span - half + 1, 1)[:, :seq_total]
    lag_scale = 1.0 / math.sqrt(seq_total * members)
    lag_sums = jnp.concatenate(
        [diagonal[:, step * span : (step + 1) * span] for step in range(count)], axis=0
    )
    lag_sums = lag_sums * lag_scale
    tile_ref[:count, half:] = lag_sums[:, half:]
    tile_ref[count:, half:] = pltpu.roll(lag_sums, half, 1)[:, half:]
    out_ref[:, streams + 1] = jnp.broadcast_to(tile_ref[...].astype(jnp.bfloat16)[None], shape)


def unpack_kernel(in_ref, out_ref, grads_ref, taps_ref, skip_ref, lags_ref):
    count, _, members, span = in_ref.shape
    streams, tap_count, chan_width = taps_ref.shape
    reach = 3
    for stream in range(streams + 1):
        block = in_ref[:, stream].reshape(count * members, span).astype(jnp.float32)
        flipped = block.T.astype(jnp.bfloat16)
        if stream == 0:
            out_ref[...] = flipped
        else:
            grads_ref[stream - 1] = flipped
    tile = in_ref[:, streams + 1].astype(jnp.float32)
    lane = lax.broadcasted_iota(jnp.int32, (1, members // 2, span), 2)
    lags = jnp.where(
        lane < span // 2, pltpu.roll(tile[:, members // 2 :], span // 2, 2), tile[:, : members // 2]
    )
    for step in range(members // 2):
        lags_ref[:, step * span : (step + 1) * span] = lags[:, step]
    lane = lax.broadcasted_iota(jnp.int32, (members, span), 1)
    spread = []
    for place in range(-(-tap_count // reach) + 1):
        total = None
        for group in range(count):
            moved = pltpu.roll(tile[group], (members * (group - place)) % span, 1)
            inside = (lane >= members * group) & (lane < members * (group + 1))
            total = moved if total is None else jnp.where(inside, moved, total)
        spread.append(total)
    first = 0
    for stream in range(streams):
        for place in range(-(-tap_count // reach)):
            taken = min(reach, tap_count - reach * place)
            taps_ref[stream, reach * place : reach * place + taken] = spread[place][
                first : first + taken
            ]
        first += reach + (stream == 0)
    skip_ref[...] = spread[-1][reach : reach + 1]


def by_group(query_in, key_in, value_in, short_taps, long_filters, skip_gain, cotangent):
    tok_rows, chan_width = query_in.shape
    groups, seq_total = long_filters.shape
    streams, tap_count, _ = short_taps.shape
    members = chan_width // groups
    count = groups
    vmem = pl.BlockSpec(memory_space=pltpu.VMEM)
    params = pltpu.CompilerParams(vmem_limit_bytes=32 * 1024 * 1024)
    packed, gain = pl.pallas_call(
        pack_kernel,
        out_shape=(
            jax.ShapeDtypeStruct((count, streams + 1, members, tok_rows), jnp.bfloat16),
            jax.ShapeDtypeStruct((1, chan_width), jnp.float32),
        ),
        in_specs=[pl.BlockSpec(memory_space=pltpu.HBM)] * 5,
        out_specs=(vmem,) * 2,
        scratch_shapes=[
            pltpu.VMEM((streams + 1, tok_rows, chan_width), jnp.bfloat16),
            pltpu.SemaphoreType.DMA((streams + 2,)),
        ],
        compiler_params=params,
        name="pack",
    )(
        *(
            pltpu.with_memory_space_constraint(value, pltpu.HBM)
            for value in (
                query_in, key_in, value_in, cotangent, skip_gain.reshape(1, chan_width)
            )
        )
    )
    packed = lax.all_to_all(packed, "seq", 0, 0, tiled=True)
    results = pl.pallas_call(
        group_kernel,
        out_shape=jax.ShapeDtypeStruct((count, streams + 2, members, tok_rows), jnp.bfloat16),
        in_specs=[vmem] * 4,
        out_specs=vmem,
        scratch_shapes=[
            pltpu.VMEM((chan_width, streams * tap_count + 3), jnp.float32),
            pltpu.VMEM((tok_rows // 2, seq_total + tok_rows), jnp.float32),
            pltpu.VMEM((members, tok_rows), jnp.float32),
            pltpu.VMEM((streams * tap_count + 1, members, tok_rows), jnp.float32),
            pltpu.VMEM((streams, count, members, tok_rows), jnp.float32),
            pltpu.VMEM((streams, count, members, tok_rows), jnp.float32),
            pltpu.VMEM((streams, 3, count, members, tok_rows), jnp.bfloat16),
            pltpu.VMEM((streams, 3, count, members, tok_rows), jnp.bfloat16),
        ],
        compiler_params=params,
        name="group",
    )(packed, short_taps, long_filters, gain)
    results = lax.all_to_all(results, "seq", 0, 0, tiled=True)
    block_out, input_grads, tap_grads, skip_grad, filter_grad = pl.pallas_call(
        unpack_kernel,
        out_shape=(
            jax.ShapeDtypeStruct((tok_rows, chan_width), jnp.bfloat16),
            jax.ShapeDtypeStruct((streams, tok_rows, chan_width), jnp.bfloat16),
            jax.ShapeDtypeStruct((streams, tap_count, chan_width), jnp.float32),
            jax.ShapeDtypeStruct((1, chan_width), jnp.float32),
            jax.ShapeDtypeStruct((groups, seq_total), jnp.float32),
        ),
        in_specs=[vmem],
        out_specs=(vmem,) * 5,
        compiler_params=params,
        name="unpack",
    )(results)
    return block_out, input_grads, tap_grads, skip_grad.reshape(chan_width), filter_grad


def plan(query_in, key_in, value_in, short_taps, long_filters, skip_gain, cotangent):
    tok_rows, chan_width = query_in.shape
    groups, seq_total = long_filters.shape
    fits = (
        lax.axis_size("seq") == groups
        and tok_rows == 128
        and chan_width == 128
        and chan_width // groups == 16
        and seq_total == groups * tok_rows
        and short_taps.shape[:2] == (3, 7)
    )
    chosen = by_group if fits else local
    return chosen(query_in, key_in, value_in, short_taps, long_filters, skip_gain, cotangent)


def solution(mesh):
    in_specs = (
        P("seq", "chan"),
        P("seq", "chan"),
        P("seq", "chan"),
        P(None, None, "chan"),
        P("chan", None),
        P("chan"),
        P("seq", "chan"),
    )
    out_specs = (
        P("seq", "chan"),
        P(None, "seq", "chan"),
        P(None, None, "chan"),
        P("chan"),
        P("chan", None),
    )
    return jax.shard_map(plan, mesh=mesh, in_specs=in_specs, out_specs=out_specs, check_vma=False)
```

```python
import functools
import math

import jax
import jax.numpy as jnp
from jax import lax
from jax.experimental import pallas as pl
from jax.experimental.pallas import tpu as pltpu
from jax.sharding import PartitionSpec as P


def from_behind(value, axis, steps):
    count = lax.axis_size(axis)
    initial, last = (max(0, -steps), min(count, count - steps))
    return lax.ppermute(value, axis, [(source, source + steps) for source in range(initial, last)])


def short_forward(extended, weights, rows_here):
    margin = weights.shape[0] - 1
    running = jnp.zeros((rows_here, extended.shape[1]), jnp.float32)
    for offset in range(weights.shape[0]):
        running = (
            running + weights[offset] * extended[margin - offset : margin - offset + rows_here]
        )
    return running


def short_backward(extended, weights, rows_here):
    running = jnp.zeros((rows_here, extended.shape[1]), jnp.float32)
    for offset in range(weights.shape[0]):
        running = running + weights[offset] * extended[offset : offset + rows_here]
    return running


def tap_sums(grad_rows, extended, tap_count, rows_here):
    margin = tap_count - 1
    sums_list = []
    for offset in range(tap_count):
        sums_list.append(
            jnp.sum(grad_rows * extended[margin - offset : margin - offset + rows_here], axis=0)
        )
    return jnp.stack(sums_list)


def hankel(padded, lag_start, height, breadth, seq_total):
    span = height + breadth - 1
    window = lax.dynamic_slice_in_dim(padded, lag_start + seq_total, span, axis=1)
    tiled = jnp.tile(window, (1, height))
    tiled = jnp.pad(tiled, ((0, 0), (0, height)))
    return tiled.reshape(padded.shape[0], height, span + 1)[:, :, :breadth]


def causal_part(padded, source_rows, source_start, target_start, target_count, seq_total):
    breadth = source_rows.shape[0]
    matrix = hankel(
        padded, target_start - source_start - breadth + 1, target_count, breadth, seq_total
    )
    return jnp.einsum("gts,sgc->tgc", matrix, source_rows[::-1], preferred_element_type=jnp.float32)


def anti_part(padded, target_rows, target_start, source_start, source_count, seq_total):
    breadth = target_rows.shape[0]
    matrix = hankel(
        padded, target_start - source_start - source_count + 1, source_count, breadth, seq_total
    )
    return jnp.einsum("gab,bgc->agc", matrix, target_rows, preferred_element_type=jnp.float32)[::-1]


def lag_part(buffer, target_rows, source_rows, target_start, source_start, seq_total):
    height = target_rows.shape[0]
    breadth = source_rows.shape[0]
    groups = target_rows.shape[1]
    padded_source = jnp.pad(source_rows[::-1], ((0, height), (0, 0), (0, 0)))
    products = jnp.einsum(
        "tgc,sgc->gts", target_rows, padded_source, preferred_element_type=jnp.float32
    )
    full_width = height + breadth
    skewed = products.reshape(groups, height * full_width)[:, : height * (full_width - 1)]
    skewed = skewed.reshape(groups, height, full_width - 1)
    diagonal = jnp.sum(skewed, axis=1)
    position = target_start - source_start - breadth + 1 + seq_total
    current = lax.dynamic_slice_in_dim(buffer, position, full_width - 1, axis=1)
    return lax.dynamic_update_slice_in_dim(buffer, current + diagonal, position, axis=1)


def local(query_in, key_in, value_in, short_taps, long_filters, skip_gain, cotangent):
    tok_rows, chan_width = query_in.shape
    groups, seq_total = long_filters.shape
    members = chan_width // groups
    tap_count = short_taps.shape[1]
    margin = tap_count - 1
    device = lax.axis_index("seq")
    own_start = device * tok_rows
    rim_rows = jnp.stack(
        [query_in[tok_rows - margin :], key_in[tok_rows - margin :], value_in[tok_rows - margin :]]
    )
    before = from_behind(rim_rows, "seq", 1)
    streams = [query_in, key_in, value_in]
    extended = [
        jnp.concatenate([before[stream], streams[stream]]).astype(jnp.float32)
        for stream in range(3)
    ]
    query_short = short_forward(extended[0], short_taps[0], tok_rows)
    key_short = short_forward(extended[1], short_taps[1], tok_rows)
    value_short = short_forward(extended[2], short_taps[2], tok_rows)
    gating = (key_short * value_short).astype(jnp.bfloat16)
    relayed = (cotangent.astype(jnp.float32) * query_short).astype(jnp.bfloat16)
    gating_wide = gating.astype(jnp.float32)
    relayed_wide = relayed.astype(jnp.float32)
    gating_groups = gating.reshape(tok_rows, groups, members)
    relayed_groups = relayed.reshape(tok_rows, groups, members)
    padded = jnp.concatenate([jnp.zeros((groups, seq_total), jnp.bfloat16), long_filters], axis=1)
    lag_buffer = jnp.zeros((groups, 2 * seq_total), jnp.float32)
    zeros_out = jnp.zeros((tok_rows, groups, members), jnp.float32)

    def target_pair(distance):
        return distance < 0

    totals = (zeros_out, lag_buffer)
    shard_rows = lax.all_gather(gating, "seq", axis=0, tiled=True)
    piece_rows = shard_rows.shape[0]
    step_rows = min(piece_rows, tok_rows)
    pieces = shard_rows.reshape(piece_rows // step_rows, step_rows, groups, members)

    def forward_visit_block(carried, element):
        position, rows_block = element
        source_start = position * step_rows

        def forward_active(partial_value):
            output_part, buffer = partial_value
            output_part = output_part + causal_part(
                padded, rows_block, source_start, own_start, tok_rows, seq_total
            )
            distance = device - source_start // tok_rows
            buffer = lax.cond(
                target_pair(distance),
                lambda held: lag_part(
                    held, relayed_groups, rows_block, own_start, source_start, seq_total
                ),
                lambda held: held,
                buffer,
            )
            return (output_part, buffer)

        carried = lax.cond(
            source_start < own_start + tok_rows,
            forward_active,
            lambda partial_value: partial_value,
            carried,
        )
        return (carried, None)

    totals, ignored = lax.scan(
        forward_visit_block, totals, (jnp.arange(piece_rows // step_rows, dtype=jnp.int32), pieces)
    )
    output_part, lag_buffer = totals
    output_sum = output_part.reshape(tok_rows, chan_width)
    totals = (zeros_out, lag_buffer)
    shard_rows = lax.all_gather(relayed, "seq", axis=0, tiled=True)
    piece_rows = shard_rows.shape[0]
    backward_step_rows = min(piece_rows, tok_rows)
    pieces = shard_rows.reshape(
        piece_rows // backward_step_rows, backward_step_rows, groups, members
    )

    def backward_visit_block(carried, element):
        position, rows_block = element
        target_start = position * backward_step_rows

        def backward_active(partial_value):
            grad_part, buffer = partial_value
            grad_part = grad_part + anti_part(
                padded, rows_block, target_start, own_start, tok_rows, seq_total
            )
            distance = target_start // tok_rows - device
            buffer = lax.cond(
                target_pair(distance),
                lambda held: held,
                lambda held: lag_part(
                    held, rows_block, gating_groups, target_start, own_start, seq_total
                ),
                buffer,
            )
            return (grad_part, buffer)

        carried = lax.cond(
            target_start + backward_step_rows > own_start,
            backward_active,
            lambda partial_value: partial_value,
            carried,
        )
        return (carried, None)

    totals, ignored = lax.scan(
        backward_visit_block,
        totals,
        (jnp.arange(piece_rows // backward_step_rows, dtype=jnp.int32), pieces),
    )
    grad_part, lag_buffer = totals
    grad_sum = grad_part.reshape(tok_rows, chan_width)
    lag_local = lag_buffer[:, seq_total:]
    long_out = output_sum + skip_gain * gating_wide
    block_out = (query_short * long_out).astype(jnp.bfloat16)
    grad_gating = grad_sum + skip_gain * relayed_wide
    cot_wide = cotangent.astype(jnp.float32)
    grad_shorts = [cot_wide * long_out, grad_gating * value_short, grad_gating * key_short]
    lead_rows = jnp.stack([grad_shorts[stream][:margin] for stream in range(3)])
    after = from_behind(lead_rows, "seq", -1)
    input_grads = jnp.stack(
        [
            short_backward(
                jnp.concatenate([grad_shorts[stream], after[stream]]), short_taps[stream], tok_rows
            )
            for stream in range(3)
        ]
    ).astype(jnp.bfloat16)
    tap_local = jnp.stack(
        [
            tap_sums(grad_shorts[stream], extended[stream], tap_count, tok_rows)
            for stream in range(3)
        ]
    )
    skip_local = jnp.sum(relayed_wide * gating_wide, axis=0)
    lag_total, tap_total, skip_total = lax.psum((lag_local, tap_local, skip_local), "seq")
    tap_scale = 1.0 / math.sqrt(seq_total)
    lag_scale = 1.0 / math.sqrt(seq_total * members)
    return (
        block_out,
        input_grads,
        tap_total * tap_scale,
        skip_total * tap_scale,
        lag_total * lag_scale,
    )


def pack_kernel(
    query_ref, key_ref, value_ref, cot_ref, skip_ref, out_ref, gain_ref, stream_buf, sems
):
    count, streams, members, tok_rows = out_ref.shape
    moves = [
        pltpu.make_async_copy(ref, stream_buf.at[stream], sems.at[stream])
        for stream, ref in enumerate((query_ref, key_ref, value_ref, cot_ref))
    ]
    moves.append(pltpu.make_async_copy(skip_ref, gain_ref, sems.at[streams]))
    for move in moves:
        move.start()
    for stream in range(streams):
        moves[stream].wait()
        flipped = stream_buf[stream].astype(jnp.float32).T.astype(jnp.bfloat16)
        out_ref[:, stream] = flipped.reshape(count, members, tok_rows)
    moves[streams].wait()


def group_kernel(
    in_ref, taps_ref, filters_ref, gain_ref, out_ref, table_ref, wide_ref, tile_ref
):
    count, _, members, span = in_ref.shape
    groups, seq_total = filters_ref.shape
    streams, tap_count, chan_width = taps_ref.shape
    rows = count * members
    mine = lax.axis_index("seq")
    shape = (count, members, span)
    lane = lax.broadcasted_iota(jnp.int32, shape, 2)
    reach = 3

    def later(value, steps):
        if steps == 0:
            return value
        turned = pltpu.roll(value, steps, 2)
        before = jnp.concatenate([jnp.zeros_like(turned[:1]), turned[:-1]], axis=0)
        return jnp.where(lane >= steps, turned, before)

    def earlier(value, steps):
        if steps == 0:
            return value
        turned = pltpu.roll(value, span - steps, 2)
        after = jnp.concatenate([turned[1:], jnp.zeros_like(turned[:1])], axis=0)
        return jnp.where(lane < span - steps, turned, after)

    table = jnp.concatenate(
        [taps_ref[stream] for stream in range(streams)]
        + [gain_ref[...], jnp.zeros((2, chan_width), jnp.float32)],
        axis=0,
    )
    table_ref[...] = table.T
    params = table_ref[pl.ds(pl.multiple_of(mine * members, members), members), :]

    def column(index):
        return jnp.broadcast_to(params[:, index : index + 1], (members, span))[None]

    chosen = lax.broadcasted_iota(jnp.int32, (groups, 1), 0) == mine
    filter_row = jnp.sum(
        jnp.where(chosen, filters_ref[...].astype(jnp.float32), 0.0), axis=0, keepdims=True
    )
    filter_row = jnp.concatenate([filter_row, jnp.zeros((1, span), jnp.float32)], axis=1)
    spread = jnp.broadcast_to(filter_row, (members, seq_total + span))
    first_rows = pltpu.roll(spread, 0, 1, stride=1, stride_axis=0).astype(jnp.bfloat16)
    row_parts = [first_rows] + [
        pltpu.roll(first_rows, first, 1) for first in range(members, span, members)
    ]
    toeplitz = jnp.concatenate(row_parts, axis=0)[:, :seq_total]

    def delays(stream):
        return [later(in_ref[:, stream], first) for first in range(0, tap_count, reach)]

    def short(stream, values):
        total = None
        for second in range(reach):
            running = None
            for first in range(second, tap_count, reach):
                value = values[first // reach].astype(jnp.float32)
                term = column(stream * tap_count + first) * value
                running = term if running is None else running + term
            running = later(running, second)
            total = running if total is None else total + running
        return total

    def ahead_by_blocks(value):
        parts = [value]
        for step in range(1, count):
            gap = jnp.zeros((step * members, span), jnp.bfloat16)
            parts.append(jnp.concatenate([value[step * members :], gap], axis=0))
        return jnp.concatenate(parts, axis=1)

    gain = column(streams * tap_count)
    cot = in_ref[:, streams].astype(jnp.float32)
    delayed = [delays(0)]
    query_short = short(0, delayed[0])
    relayed = (cot * query_short).astype(jnp.bfloat16).reshape(rows, span)
    relayed_lags = ahead_by_blocks(relayed)
    backward = lax.dot_general(
        relayed_lags, toeplitz, (((1,), (1,)), ((), ())), preferred_element_type=jnp.float32
    )

    delayed += [delays(1), delays(2)]
    key_short = short(1, delayed[1])
    value_short = short(2, delayed[2])
    gating = (key_short * value_short).astype(jnp.bfloat16).reshape(rows, span)
    gating_parts, filter_parts = [gating], [toeplitz[:, :span]]
    for step in range(1, count):
        gap = jnp.zeros((step * members, span), jnp.bfloat16)
        gating_parts.append(jnp.concatenate([gap, gating[: rows - step * members]], axis=0))
        filter_parts.append(toeplitz[:, step * span : (step + 1) * span])
    forward = jnp.dot(
        jnp.concatenate(gating_parts, axis=1),
        jnp.concatenate(filter_parts, axis=0),
        preferred_element_type=jnp.float32,
    )

    half = span // 2
    flip = (
        lax.broadcasted_iota(jnp.int32, (span, span), 0)
        + lax.broadcasted_iota(jnp.int32, (span, span), 1)
        == span - 1
    ).astype(jnp.bfloat16)
    gating_turned = lax.dot_general(
        flip, gating, (((1,), (1,)), ((), ())), preferred_element_type=jnp.float32
    ).astype(jnp.bfloat16)
    gating_turned = jnp.concatenate([gating_turned[half:], gating_turned[:half]], axis=1)
    ahead = earlier(relayed.reshape(shape), half).reshape(rows, span)
    targets = jnp.concatenate([relayed_lags, ahead_by_blocks(ahead)], axis=0)
    wide_ref[:, :seq_total] = jnp.dot(
        gating_turned, targets, preferred_element_type=jnp.float32
    )
    wide_ref[:, seq_total:] = jnp.zeros((half, span), jnp.float32)

    tap_scale = 1.0 / math.sqrt(seq_total)

    def tokens(value):
        return jnp.concatenate([value[block] for block in range(count)], axis=1)

    def sums(left, right):
        product = lax.dot_general(
            jnp.concatenate(left, axis=0),
            jnp.concatenate(right, axis=0),
            (((1,), (1,)), ((), ())),
            preferred_element_type=jnp.float32,
        )
        same = (
            lax.broadcasted_iota(jnp.int32, product.shape, 0) % members
            == lax.broadcasted_iota(jnp.int32, product.shape, 1) % members
        )
        product = jnp.where(same, product, 0.0).reshape(len(left), members, -1)
        return jnp.sum(product, axis=1) * tap_scale

    tile_ref[...] = jnp.zeros((members, span), jnp.float32)

    def finish(stream, grad_short, first_row, more_left=(), more_right=()):
        moved = [earlier(grad_short, second) for second in range(reach)]
        left = [tokens(value.astype(jnp.bfloat16)) for value in moved] + list(more_left)
        right = [tokens(value) for value in delayed[stream]] + list(more_right)
        totals = sums(left, right)
        tile_ref[first_row : first_row + len(left), : totals.shape[1]] = totals
        total = None
        for place in range(len(delayed[stream])):
            running = None
            for second in range(min(reach, tap_count - reach * place)):
                term = column(stream * tap_count + reach * place + second) * moved[second]
                running = term if running is None else running + term
            running = earlier(running, reach * place)
            total = running if total is None else total + running
        out_ref[:, 1 + stream] = total.astype(jnp.bfloat16)

    grad_gating = backward.reshape(shape) + gain * relayed.astype(jnp.float32).reshape(shape)
    finish(1, grad_gating * value_short, reach + 1)
    finish(2, grad_gating * key_short, 2 * reach + 1)

    long_out = forward.reshape(shape) + gain * gating.astype(jnp.float32).reshape(shape)
    out_ref[:, 0] = (query_short * long_out).astype(jnp.bfloat16)
    finish(
        0, cot * long_out, 0, [tokens(relayed.reshape(shape))], [tokens(gating.reshape(shape))]
    )

    skewed = pltpu.roll(wide_ref[...], span - half + 1, 1, stride=1, stride_axis=0)
    diagonal = jnp.sum(skewed, axis=0, keepdims=True)
    lag_scale = 1.0 / math.sqrt(seq_total * members)
    lag_sums = jnp.concatenate(
        [diagonal[:, step * span : (step + 1) * span] for step in range(1, count + 1)], axis=0
    )
    lag_sums = lag_sums * lag_scale
    tile_ref[:count, half:] = lag_sums[:, half:]
    tile_ref[count:, half:] = pltpu.roll(lag_sums, half, 1)[:, half:]
    out_ref[:, streams + 1] = jnp.broadcast_to(tile_ref[...].astype(jnp.bfloat16)[None], shape)


def unpack_kernel(in_ref, out_ref, grads_ref, taps_ref, skip_ref, lags_ref):
    count, _, members, span = in_ref.shape
    streams, tap_count, chan_width = taps_ref.shape
    reach = 3
    for stream in range(streams + 1):
        block = in_ref[:, stream].reshape(count * members, span).astype(jnp.float32)
        flipped = block.T.astype(jnp.bfloat16)
        if stream == 0:
            out_ref[...] = flipped
        else:
            grads_ref[stream - 1] = flipped
    tile = in_ref[:, streams + 1].astype(jnp.float32)
    lane = lax.broadcasted_iota(jnp.int32, (1, members // 2, span), 2)
    lags = jnp.where(
        lane < span // 2, pltpu.roll(tile[:, members // 2 :], span // 2, 2), tile[:, : members // 2]
    )
    for step in range(members // 2):
        lags_ref[:, step * span : (step + 1) * span] = lags[:, step]
    lane = lax.broadcasted_iota(jnp.int32, (members, span), 1)
    spread = []
    for place in range(-(-tap_count // reach) + 1):
        total = None
        for group in range(count):
            moved = pltpu.roll(tile[group], (members * (group - place)) % span, 1)
            inside = (lane >= members * group) & (lane < members * (group + 1))
            total = moved if total is None else jnp.where(inside, moved, total)
        spread.append(total)
    first = 0
    for stream in range(streams):
        for place in range(-(-tap_count // reach)):
            taken = min(reach, tap_count - reach * place)
            taps_ref[stream, reach * place : reach * place + taken] = spread[place][
                first : first + taken
            ]
        first += reach + (stream == 0)
    skip_ref[...] = spread[-1][reach : reach + 1]


def by_group(query_in, key_in, value_in, short_taps, long_filters, skip_gain, cotangent):
    tok_rows, chan_width = query_in.shape
    groups, seq_total = long_filters.shape
    streams, tap_count, _ = short_taps.shape
    members = chan_width // groups
    count = groups
    vmem = pl.BlockSpec(memory_space=pltpu.VMEM)
    params = pltpu.CompilerParams(vmem_limit_bytes=32 * 1024 * 1024)
    packed, gain = pl.pallas_call(
        pack_kernel,
        out_shape=(
            jax.ShapeDtypeStruct((count, streams + 1, members, tok_rows), jnp.bfloat16),
            jax.ShapeDtypeStruct((1, chan_width), jnp.float32),
        ),
        in_specs=[pl.BlockSpec(memory_space=pltpu.HBM)] * 5,
        out_specs=(vmem,) * 2,
        scratch_shapes=[
            pltpu.VMEM((streams + 1, tok_rows, chan_width), jnp.bfloat16),
            pltpu.SemaphoreType.DMA((streams + 2,)),
        ],
        compiler_params=params,
        name="pack",
    )(
        *(
            pltpu.with_memory_space_constraint(value, pltpu.HBM)
            for value in (
                query_in, key_in, value_in, cotangent, skip_gain.reshape(1, chan_width)
            )
        )
    )
    packed = lax.all_to_all(packed, "seq", 0, 0, tiled=True)
    results = pl.pallas_call(
        group_kernel,
        out_shape=jax.ShapeDtypeStruct((count, streams + 2, members, tok_rows), jnp.bfloat16),
        in_specs=[vmem] * 4,
        out_specs=vmem,
        scratch_shapes=[
            pltpu.VMEM((chan_width, streams * tap_count + 3), jnp.float32),
            pltpu.VMEM((tok_rows // 2, seq_total + tok_rows), jnp.float32),
            pltpu.VMEM((members, tok_rows), jnp.float32),
        ],
        compiler_params=params,
        name="group",
    )(packed, short_taps, long_filters, gain)
    results = lax.all_to_all(results, "seq", 0, 0, tiled=True)
    block_out, input_grads, tap_grads, skip_grad, filter_grad = pl.pallas_call(
        unpack_kernel,
        out_shape=(
            jax.ShapeDtypeStruct((tok_rows, chan_width), jnp.bfloat16),
            jax.ShapeDtypeStruct((streams, tok_rows, chan_width), jnp.bfloat16),
            jax.ShapeDtypeStruct((streams, tap_count, chan_width), jnp.float32),
            jax.ShapeDtypeStruct((1, chan_width), jnp.float32),
            jax.ShapeDtypeStruct((groups, seq_total), jnp.float32),
        ),
        in_specs=[vmem],
        out_specs=(vmem,) * 5,
        compiler_params=params,
        name="unpack",
    )(results)
    return block_out, input_grads, tap_grads, skip_grad.reshape(chan_width), filter_grad


def plan(query_in, key_in, value_in, short_taps, long_filters, skip_gain, cotangent):
    tok_rows, chan_width = query_in.shape
    groups, seq_total = long_filters.shape
    fits = (
        lax.axis_size("seq") == groups
        and tok_rows == 128
        and chan_width == 128
        and chan_width // groups == 16
        and seq_total == groups * tok_rows
        and short_taps.shape[:2] == (3, 7)
    )
    chosen = by_group if fits else local
    return chosen(query_in, key_in, value_in, short_taps, long_filters, skip_gain, cotangent)


def solution(mesh):
    in_specs = (
        P("seq", "chan"),
        P("seq", "chan"),
        P("seq", "chan"),
        P(None, None, "chan"),
        P("chan", None),
        P("chan"),
        P("seq", "chan"),
    )
    out_specs = (
        P("seq", "chan"),
        P(None, "seq", "chan"),
        P(None, None, "chan"),
        P("chan"),
        P("chan", None),
    )
    return jax.shard_map(plan, mesh=mesh, in_specs=in_specs, out_specs=out_specs, check_vma=False)
```

```python
import functools
import math

import jax
import jax.numpy as jnp
from jax import lax
from jax.experimental import pallas as pl
from jax.experimental.pallas import tpu as pltpu
from jax.sharding import PartitionSpec as P


def from_behind(value, axis, steps):
    count = lax.axis_size(axis)
    initial, last = (max(0, -steps), min(count, count - steps))
    return lax.ppermute(value, axis, [(source, source + steps) for source in range(initial, last)])


def short_forward(extended, weights, rows_here):
    margin = weights.shape[0] - 1
    running = jnp.zeros((rows_here, extended.shape[1]), jnp.float32)
    for offset in range(weights.shape[0]):
        running = (
            running + weights[offset] * extended[margin - offset : margin - offset + rows_here]
        )
    return running


def short_backward(extended, weights, rows_here):
    running = jnp.zeros((rows_here, extended.shape[1]), jnp.float32)
    for offset in range(weights.shape[0]):
        running = running + weights[offset] * extended[offset : offset + rows_here]
    return running


def tap_sums(grad_rows, extended, tap_count, rows_here):
    margin = tap_count - 1
    sums_list = []
    for offset in range(tap_count):
        sums_list.append(
            jnp.sum(grad_rows * extended[margin - offset : margin - offset + rows_here], axis=0)
        )
    return jnp.stack(sums_list)


def hankel(padded, lag_start, height, breadth, seq_total):
    span = height + breadth - 1
    window = lax.dynamic_slice_in_dim(padded, lag_start + seq_total, span, axis=1)
    tiled = jnp.tile(window, (1, height))
    tiled = jnp.pad(tiled, ((0, 0), (0, height)))
    return tiled.reshape(padded.shape[0], height, span + 1)[:, :, :breadth]


def causal_part(padded, source_rows, source_start, target_start, target_count, seq_total):
    breadth = source_rows.shape[0]
    matrix = hankel(
        padded, target_start - source_start - breadth + 1, target_count, breadth, seq_total
    )
    return jnp.einsum("gts,sgc->tgc", matrix, source_rows[::-1], preferred_element_type=jnp.float32)


def anti_part(padded, target_rows, target_start, source_start, source_count, seq_total):
    breadth = target_rows.shape[0]
    matrix = hankel(
        padded, target_start - source_start - source_count + 1, source_count, breadth, seq_total
    )
    return jnp.einsum("gab,bgc->agc", matrix, target_rows, preferred_element_type=jnp.float32)[::-1]


def lag_part(buffer, target_rows, source_rows, target_start, source_start, seq_total):
    height = target_rows.shape[0]
    breadth = source_rows.shape[0]
    groups = target_rows.shape[1]
    padded_source = jnp.pad(source_rows[::-1], ((0, height), (0, 0), (0, 0)))
    products = jnp.einsum(
        "tgc,sgc->gts", target_rows, padded_source, preferred_element_type=jnp.float32
    )
    full_width = height + breadth
    skewed = products.reshape(groups, height * full_width)[:, : height * (full_width - 1)]
    skewed = skewed.reshape(groups, height, full_width - 1)
    diagonal = jnp.sum(skewed, axis=1)
    position = target_start - source_start - breadth + 1 + seq_total
    current = lax.dynamic_slice_in_dim(buffer, position, full_width - 1, axis=1)
    return lax.dynamic_update_slice_in_dim(buffer, current + diagonal, position, axis=1)


def local(query_in, key_in, value_in, short_taps, long_filters, skip_gain, cotangent):
    tok_rows, chan_width = query_in.shape
    groups, seq_total = long_filters.shape
    members = chan_width // groups
    tap_count = short_taps.shape[1]
    margin = tap_count - 1
    device = lax.axis_index("seq")
    own_start = device * tok_rows
    rim_rows = jnp.stack(
        [query_in[tok_rows - margin :], key_in[tok_rows - margin :], value_in[tok_rows - margin :]]
    )
    before = from_behind(rim_rows, "seq", 1)
    streams = [query_in, key_in, value_in]
    extended = [
        jnp.concatenate([before[stream], streams[stream]]).astype(jnp.float32)
        for stream in range(3)
    ]
    query_short = short_forward(extended[0], short_taps[0], tok_rows)
    key_short = short_forward(extended[1], short_taps[1], tok_rows)
    value_short = short_forward(extended[2], short_taps[2], tok_rows)
    gating = (key_short * value_short).astype(jnp.bfloat16)
    relayed = (cotangent.astype(jnp.float32) * query_short).astype(jnp.bfloat16)
    gating_wide = gating.astype(jnp.float32)
    relayed_wide = relayed.astype(jnp.float32)
    gating_groups = gating.reshape(tok_rows, groups, members)
    relayed_groups = relayed.reshape(tok_rows, groups, members)
    padded = jnp.concatenate([jnp.zeros((groups, seq_total), jnp.bfloat16), long_filters], axis=1)
    lag_buffer = jnp.zeros((groups, 2 * seq_total), jnp.float32)
    zeros_out = jnp.zeros((tok_rows, groups, members), jnp.float32)

    def target_pair(distance):
        return distance < 0

    totals = (zeros_out, lag_buffer)
    shard_rows = lax.all_gather(gating, "seq", axis=0, tiled=True)
    piece_rows = shard_rows.shape[0]
    step_rows = min(piece_rows, tok_rows)
    pieces = shard_rows.reshape(piece_rows // step_rows, step_rows, groups, members)

    def forward_visit_block(carried, element):
        position, rows_block = element
        source_start = position * step_rows

        def forward_active(partial_value):
            output_part, buffer = partial_value
            output_part = output_part + causal_part(
                padded, rows_block, source_start, own_start, tok_rows, seq_total
            )
            distance = device - source_start // tok_rows
            buffer = lax.cond(
                target_pair(distance),
                lambda held: lag_part(
                    held, relayed_groups, rows_block, own_start, source_start, seq_total
                ),
                lambda held: held,
                buffer,
            )
            return (output_part, buffer)

        carried = lax.cond(
            source_start < own_start + tok_rows,
            forward_active,
            lambda partial_value: partial_value,
            carried,
        )
        return (carried, None)

    totals, ignored = lax.scan(
        forward_visit_block, totals, (jnp.arange(piece_rows // step_rows, dtype=jnp.int32), pieces)
    )
    output_part, lag_buffer = totals
    output_sum = output_part.reshape(tok_rows, chan_width)
    totals = (zeros_out, lag_buffer)
    shard_rows = lax.all_gather(relayed, "seq", axis=0, tiled=True)
    piece_rows = shard_rows.shape[0]
    backward_step_rows = min(piece_rows, tok_rows)
    pieces = shard_rows.reshape(
        piece_rows // backward_step_rows, backward_step_rows, groups, members
    )

    def backward_visit_block(carried, element):
        position, rows_block = element
        target_start = position * backward_step_rows

        def backward_active(partial_value):
            grad_part, buffer = partial_value
            grad_part = grad_part + anti_part(
                padded, rows_block, target_start, own_start, tok_rows, seq_total
            )
            distance = target_start // tok_rows - device
            buffer = lax.cond(
                target_pair(distance),
                lambda held: held,
                lambda held: lag_part(
                    held, rows_block, gating_groups, target_start, own_start, seq_total
                ),
                buffer,
            )
            return (grad_part, buffer)

        carried = lax.cond(
            target_start + backward_step_rows > own_start,
            backward_active,
            lambda partial_value: partial_value,
            carried,
        )
        return (carried, None)

    totals, ignored = lax.scan(
        backward_visit_block,
        totals,
        (jnp.arange(piece_rows // backward_step_rows, dtype=jnp.int32), pieces),
    )
    grad_part, lag_buffer = totals
    grad_sum = grad_part.reshape(tok_rows, chan_width)
    lag_local = lag_buffer[:, seq_total:]
    long_out = output_sum + skip_gain * gating_wide
    block_out = (query_short * long_out).astype(jnp.bfloat16)
    grad_gating = grad_sum + skip_gain * relayed_wide
    cot_wide = cotangent.astype(jnp.float32)
    grad_shorts = [cot_wide * long_out, grad_gating * value_short, grad_gating * key_short]
    lead_rows = jnp.stack([grad_shorts[stream][:margin] for stream in range(3)])
    after = from_behind(lead_rows, "seq", -1)
    input_grads = jnp.stack(
        [
            short_backward(
                jnp.concatenate([grad_shorts[stream], after[stream]]), short_taps[stream], tok_rows
            )
            for stream in range(3)
        ]
    ).astype(jnp.bfloat16)
    tap_local = jnp.stack(
        [
            tap_sums(grad_shorts[stream], extended[stream], tap_count, tok_rows)
            for stream in range(3)
        ]
    )
    skip_local = jnp.sum(relayed_wide * gating_wide, axis=0)
    lag_total, tap_total, skip_total = lax.psum((lag_local, tap_local, skip_local), "seq")
    tap_scale = 1.0 / math.sqrt(seq_total)
    lag_scale = 1.0 / math.sqrt(seq_total * members)
    return (
        block_out,
        input_grads,
        tap_total * tap_scale,
        skip_total * tap_scale,
        lag_total * lag_scale,
    )


def pack_kernel(
    query_ref, key_ref, value_ref, cot_ref, skip_ref, out_ref, gain_ref, stream_buf, sems
):
    count, streams, members, tok_rows = out_ref.shape
    moves = [
        pltpu.make_async_copy(ref, stream_buf.at[stream], sems.at[stream])
        for stream, ref in enumerate((query_ref, key_ref, value_ref, cot_ref))
    ]
    moves.append(pltpu.make_async_copy(skip_ref, gain_ref, sems.at[streams]))
    for move in moves:
        move.start()
    for stream in range(streams):
        moves[stream].wait()
        flipped = stream_buf[stream].astype(jnp.float32).T.astype(jnp.bfloat16)
        out_ref[:, stream] = flipped.reshape(count, members, tok_rows)
    moves[streams].wait()


def group_kernel(
    in_ref, taps_ref, filters_ref, gain_ref, out_ref, table_ref, wide_ref, tile_ref
):
    count, _, members, span = in_ref.shape
    groups, seq_total = filters_ref.shape
    streams, tap_count, chan_width = taps_ref.shape
    rows = count * members
    mine = lax.axis_index("seq")
    shape = (count, members, span)
    lane = lax.broadcasted_iota(jnp.int32, shape, 2)
    reach = 3

    def later(value, steps):
        if steps == 0:
            return value
        turned = pltpu.roll(value, steps, 2)
        before = jnp.concatenate([jnp.zeros_like(turned[:1]), turned[:-1]], axis=0)
        return jnp.where(lane >= steps, turned, before)

    def earlier(value, steps):
        if steps == 0:
            return value
        turned = pltpu.roll(value, span - steps, 2)
        after = jnp.concatenate([turned[1:], jnp.zeros_like(turned[:1])], axis=0)
        return jnp.where(lane < span - steps, turned, after)

    table = jnp.concatenate(
        [taps_ref[stream] for stream in range(streams)]
        + [gain_ref[...], jnp.zeros((2, chan_width), jnp.float32)],
        axis=0,
    )
    table_ref[...] = table.T
    params = table_ref[pl.ds(pl.multiple_of(mine * members, members), members), :]

    def column(index):
        return jnp.broadcast_to(params[:, index : index + 1], (members, span))[None]

    chosen = lax.broadcasted_iota(jnp.int32, (groups, 1), 0) == mine
    filter_row = jnp.sum(
        jnp.where(chosen, filters_ref[...].astype(jnp.float32), 0.0), axis=0, keepdims=True
    )
    filter_row = jnp.concatenate([filter_row, jnp.zeros((1, span), jnp.float32)], axis=1)
    spread = jnp.broadcast_to(filter_row, (members, seq_total + span))
    first_rows = pltpu.roll(spread, 0, 1, stride=1, stride_axis=0).astype(jnp.bfloat16)
    row_parts = [first_rows] + [
        pltpu.roll(first_rows, first, 1) for first in range(members, span, members)
    ]
    toeplitz = jnp.concatenate(row_parts, axis=0)[:, :seq_total]

    def delays(stream):
        return [later(in_ref[:, stream], first) for first in range(0, tap_count, reach)]

    def short(stream, values):
        total = None
        for second in range(reach):
            running = None
            for first in range(second, tap_count, reach):
                value = values[first // reach].astype(jnp.float32)
                term = column(stream * tap_count + first) * value
                running = term if running is None else running + term
            running = later(running, second)
            total = running if total is None else total + running
        return total

    def ahead_by_blocks(value):
        parts = [value]
        for step in range(1, count):
            gap = jnp.zeros((step * members, span), jnp.bfloat16)
            parts.append(jnp.concatenate([value[step * members :], gap], axis=0))
        return jnp.concatenate(parts, axis=1)

    gain = column(streams * tap_count)
    cot = in_ref[:, streams].astype(jnp.float32)
    delayed = [delays(0)]
    query_short = short(0, delayed[0])
    relayed = (cot * query_short).astype(jnp.bfloat16).reshape(rows, span)
    relayed_lags = ahead_by_blocks(relayed)
    pair = 2 * members
    chunks = rows // pair
    gap = jnp.zeros((members, span), jnp.bfloat16)
    backward_parts = [[] for _ in range(chunks)]
    for step in range(chunks):
        near = relayed[step * pair :]
        term = lax.dot_general(
            jnp.concatenate([near, jnp.concatenate([near[members:], gap], axis=0)], axis=1),
            toeplitz[:, 2 * step * span : 2 * (step + 1) * span],
            (((1,), (1,)), ((), ())),
            preferred_element_type=jnp.float32,
        )
        for chunk in range(chunks - step):
            backward_parts[chunk].append(term[chunk * pair : (chunk + 1) * pair])
    backward = jnp.concatenate([sum(parts[1:], parts[0]) for parts in backward_parts], axis=0)

    delayed += [delays(1), delays(2)]
    key_short = short(1, delayed[1])
    value_short = short(2, delayed[2])
    gating = (key_short * value_short).astype(jnp.bfloat16).reshape(rows, span)
    forward_parts = [[] for _ in range(chunks)]
    for step in range(chunks):
        near = gating[: rows - step * pair]
        lanes = [slice((2 * step + part) * span, (2 * step + part + 1) * span) for part in range(2)]
        term = jnp.dot(
            jnp.concatenate([near, jnp.concatenate([gap, near[:-members]], axis=0)], axis=1),
            jnp.concatenate([toeplitz[:, lanes[0]], toeplitz[:, lanes[1]]], axis=0),
            preferred_element_type=jnp.float32,
        )
        for chunk in range(chunks - step):
            forward_parts[step + chunk].append(term[chunk * pair : (chunk + 1) * pair])
    forward = jnp.concatenate([sum(parts[1:], parts[0]) for parts in forward_parts], axis=0)

    half = span // 2
    flip = (
        lax.broadcasted_iota(jnp.int32, (span, span), 0)
        + lax.broadcasted_iota(jnp.int32, (span, span), 1)
        == span - 1
    ).astype(jnp.bfloat16)
    gating_turned = lax.dot_general(
        flip, gating, (((1,), (1,)), ((), ())), preferred_element_type=jnp.float32
    ).astype(jnp.bfloat16)
    gating_turned = jnp.concatenate([gating_turned[half:], gating_turned[:half]], axis=1)
    ahead = earlier(relayed.reshape(shape), half).reshape(rows, span)
    targets = jnp.concatenate([relayed_lags, ahead_by_blocks(ahead)], axis=0)
    wide_ref[:, :seq_total] = jnp.dot(
        gating_turned, targets, preferred_element_type=jnp.float32
    )
    wide_ref[:, seq_total:] = jnp.zeros((half, span), jnp.float32)

    tap_scale = 1.0 / math.sqrt(seq_total)

    def tokens(value):
        return jnp.concatenate([value[block] for block in range(count)], axis=1)

    def sums(left, right):
        product = lax.dot_general(
            jnp.concatenate(left, axis=0),
            jnp.concatenate(right, axis=0),
            (((1,), (1,)), ((), ())),
            preferred_element_type=jnp.float32,
        )
        same = (
            lax.broadcasted_iota(jnp.int32, product.shape, 0) % members
            == lax.broadcasted_iota(jnp.int32, product.shape, 1) % members
        )
        product = jnp.where(same, product, 0.0).reshape(len(left), members, -1)
        return jnp.sum(product, axis=1) * tap_scale

    tile_ref[...] = jnp.zeros((members, span), jnp.float32)

    def finish(stream, grad_short, first_row, more_left=(), more_right=()):
        moved = [earlier(grad_short, second) for second in range(reach)]
        left = [tokens(value.astype(jnp.bfloat16)) for value in moved] + list(more_left)
        right = [tokens(value) for value in delayed[stream]] + list(more_right)
        totals = sums(left, right)
        tile_ref[first_row : first_row + len(left), : totals.shape[1]] = totals
        total = None
        for place in range(len(delayed[stream])):
            running = None
            for second in range(min(reach, tap_count - reach * place)):
                term = column(stream * tap_count + reach * place + second) * moved[second]
                running = term if running is None else running + term
            running = earlier(running, reach * place)
            total = running if total is None else total + running
        out_ref[:, 1 + stream] = total.astype(jnp.bfloat16)

    grad_gating = backward.reshape(shape) + gain * relayed.astype(jnp.float32).reshape(shape)
    finish(1, grad_gating * value_short, reach + 1)
    finish(2, grad_gating * key_short, 2 * reach + 1)

    long_out = forward.reshape(shape) + gain * gating.astype(jnp.float32).reshape(shape)
    out_ref[:, 0] = (query_short * long_out).astype(jnp.bfloat16)
    finish(
        0, cot * long_out, 0, [tokens(relayed.reshape(shape))], [tokens(gating.reshape(shape))]
    )

    skewed = pltpu.roll(wide_ref[...], span - half + 1, 1, stride=1, stride_axis=0)
    diagonal = jnp.sum(skewed, axis=0, keepdims=True)
    lag_scale = 1.0 / math.sqrt(seq_total * members)
    lag_sums = jnp.concatenate(
        [diagonal[:, step * span : (step + 1) * span] for step in range(1, count + 1)], axis=0
    )
    lag_sums = lag_sums * lag_scale
    tile_ref[:count, half:] = lag_sums[:, half:]
    tile_ref[count:, half:] = pltpu.roll(lag_sums, half, 1)[:, half:]
    out_ref[:, streams + 1] = jnp.broadcast_to(tile_ref[...].astype(jnp.bfloat16)[None], shape)


def unpack_kernel(in_ref, out_ref, grads_ref, taps_ref, skip_ref, lags_ref):
    count, _, members, span = in_ref.shape
    streams, tap_count, chan_width = taps_ref.shape
    reach = 3
    for stream in range(streams + 1):
        block = in_ref[:, stream].reshape(count * members, span).astype(jnp.float32)
        flipped = block.T.astype(jnp.bfloat16)
        if stream == 0:
            out_ref[...] = flipped
        else:
            grads_ref[stream - 1] = flipped
    tile = in_ref[:, streams + 1].astype(jnp.float32)
    lane = lax.broadcasted_iota(jnp.int32, (1, members // 2, span), 2)
    lags = jnp.where(
        lane < span // 2, pltpu.roll(tile[:, members // 2 :], span // 2, 2), tile[:, : members // 2]
    )
    for step in range(members // 2):
        lags_ref[:, step * span : (step + 1) * span] = lags[:, step]
    lane = lax.broadcasted_iota(jnp.int32, (members, span), 1)
    spread = []
    for place in range(-(-tap_count // reach) + 1):
        total = None
        for group in range(count):
            moved = pltpu.roll(tile[group], (members * (group - place)) % span, 1)
            inside = (lane >= members * group) & (lane < members * (group + 1))
            total = moved if total is None else jnp.where(inside, moved, total)
        spread.append(total)
    first = 0
    for stream in range(streams):
        for place in range(-(-tap_count // reach)):
            taken = min(reach, tap_count - reach * place)
            taps_ref[stream, reach * place : reach * place + taken] = spread[place][
                first : first + taken
            ]
        first += reach + (stream == 0)
    skip_ref[...] = spread[-1][reach : reach + 1]


def by_group(query_in, key_in, value_in, short_taps, long_filters, skip_gain, cotangent):
    tok_rows, chan_width = query_in.shape
    groups, seq_total = long_filters.shape
    streams, tap_count, _ = short_taps.shape
    members = chan_width // groups
    count = groups
    vmem = pl.BlockSpec(memory_space=pltpu.VMEM)
    params = pltpu.CompilerParams(vmem_limit_bytes=32 * 1024 * 1024)
    packed, gain = pl.pallas_call(
        pack_kernel,
        out_shape=(
            jax.ShapeDtypeStruct((count, streams + 1, members, tok_rows), jnp.bfloat16),
            jax.ShapeDtypeStruct((1, chan_width), jnp.float32),
        ),
        in_specs=[pl.BlockSpec(memory_space=pltpu.HBM)] * 5,
        out_specs=(vmem,) * 2,
        scratch_shapes=[
            pltpu.VMEM((streams + 1, tok_rows, chan_width), jnp.bfloat16),
            pltpu.SemaphoreType.DMA((streams + 2,)),
        ],
        compiler_params=params,
        name="pack",
    )(
        *(
            pltpu.with_memory_space_constraint(value, pltpu.HBM)
            for value in (
                query_in, key_in, value_in, cotangent, skip_gain.reshape(1, chan_width)
            )
        )
    )
    packed = lax.all_to_all(packed, "seq", 0, 0, tiled=True)
    results = pl.pallas_call(
        group_kernel,
        out_shape=jax.ShapeDtypeStruct((count, streams + 2, members, tok_rows), jnp.bfloat16),
        in_specs=[vmem] * 4,
        out_specs=vmem,
        scratch_shapes=[
            pltpu.VMEM((chan_width, streams * tap_count + 3), jnp.float32),
            pltpu.VMEM((tok_rows // 2, seq_total + tok_rows), jnp.float32),
            pltpu.VMEM((members, tok_rows), jnp.float32),
        ],
        compiler_params=params,
        name="group",
    )(packed, short_taps, long_filters, gain)
    results = lax.all_to_all(results, "seq", 0, 0, tiled=True)
    block_out, input_grads, tap_grads, skip_grad, filter_grad = pl.pallas_call(
        unpack_kernel,
        out_shape=(
            jax.ShapeDtypeStruct((tok_rows, chan_width), jnp.bfloat16),
            jax.ShapeDtypeStruct((streams, tok_rows, chan_width), jnp.bfloat16),
            jax.ShapeDtypeStruct((streams, tap_count, chan_width), jnp.float32),
            jax.ShapeDtypeStruct((1, chan_width), jnp.float32),
            jax.ShapeDtypeStruct((groups, seq_total), jnp.float32),
        ),
        in_specs=[vmem],
        out_specs=(vmem,) * 5,
        compiler_params=params,
        name="unpack",
    )(results)
    return block_out, input_grads, tap_grads, skip_grad.reshape(chan_width), filter_grad


def plan(query_in, key_in, value_in, short_taps, long_filters, skip_gain, cotangent):
    tok_rows, chan_width = query_in.shape
    groups, seq_total = long_filters.shape
    fits = (
        lax.axis_size("seq") == groups
        and tok_rows == 128
        and chan_width == 128
        and chan_width // groups == 16
        and seq_total == groups * tok_rows
        and short_taps.shape[:2] == (3, 7)
    )
    chosen = by_group if fits else local
    return chosen(query_in, key_in, value_in, short_taps, long_filters, skip_gain, cotangent)


def solution(mesh):
    in_specs = (
        P("seq", "chan"),
        P("seq", "chan"),
        P("seq", "chan"),
        P(None, None, "chan"),
        P("chan", None),
        P("chan"),
        P("seq", "chan"),
    )
    out_specs = (
        P("seq", "chan"),
        P(None, "seq", "chan"),
        P(None, None, "chan"),
        P("chan"),
        P("chan", None),
    )
    return jax.shard_map(plan, mesh=mesh, in_specs=in_specs, out_specs=out_specs, check_vma=False)
```

```python
import functools
import math

import jax
import jax.numpy as jnp
from jax import lax
from jax.experimental import pallas as pl
from jax.experimental.pallas import tpu as pltpu
from jax.sharding import PartitionSpec as P


def from_behind(value, axis, steps):
    count = lax.axis_size(axis)
    initial, last = (max(0, -steps), min(count, count - steps))
    return lax.ppermute(value, axis, [(source, source + steps) for source in range(initial, last)])


def short_forward(extended, weights, rows_here):
    margin = weights.shape[0] - 1
    running = jnp.zeros((rows_here, extended.shape[1]), jnp.float32)
    for offset in range(weights.shape[0]):
        running = (
            running + weights[offset] * extended[margin - offset : margin - offset + rows_here]
        )
    return running


def short_backward(extended, weights, rows_here):
    running = jnp.zeros((rows_here, extended.shape[1]), jnp.float32)
    for offset in range(weights.shape[0]):
        running = running + weights[offset] * extended[offset : offset + rows_here]
    return running


def tap_sums(grad_rows, extended, tap_count, rows_here):
    margin = tap_count - 1
    sums_list = []
    for offset in range(tap_count):
        sums_list.append(
            jnp.sum(grad_rows * extended[margin - offset : margin - offset + rows_here], axis=0)
        )
    return jnp.stack(sums_list)


def hankel(padded, lag_start, height, breadth, seq_total):
    span = height + breadth - 1
    window = lax.dynamic_slice_in_dim(padded, lag_start + seq_total, span, axis=1)
    tiled = jnp.tile(window, (1, height))
    tiled = jnp.pad(tiled, ((0, 0), (0, height)))
    return tiled.reshape(padded.shape[0], height, span + 1)[:, :, :breadth]


def causal_part(padded, source_rows, source_start, target_start, target_count, seq_total):
    breadth = source_rows.shape[0]
    matrix = hankel(
        padded, target_start - source_start - breadth + 1, target_count, breadth, seq_total
    )
    return jnp.einsum("gts,sgc->tgc", matrix, source_rows[::-1], preferred_element_type=jnp.float32)


def anti_part(padded, target_rows, target_start, source_start, source_count, seq_total):
    breadth = target_rows.shape[0]
    matrix = hankel(
        padded, target_start - source_start - source_count + 1, source_count, breadth, seq_total
    )
    return jnp.einsum("gab,bgc->agc", matrix, target_rows, preferred_element_type=jnp.float32)[::-1]


def lag_part(buffer, target_rows, source_rows, target_start, source_start, seq_total):
    height = target_rows.shape[0]
    breadth = source_rows.shape[0]
    groups = target_rows.shape[1]
    padded_source = jnp.pad(source_rows[::-1], ((0, height), (0, 0), (0, 0)))
    products = jnp.einsum(
        "tgc,sgc->gts", target_rows, padded_source, preferred_element_type=jnp.float32
    )
    full_width = height + breadth
    skewed = products.reshape(groups, height * full_width)[:, : height * (full_width - 1)]
    skewed = skewed.reshape(groups, height, full_width - 1)
    diagonal = jnp.sum(skewed, axis=1)
    position = target_start - source_start - breadth + 1 + seq_total
    current = lax.dynamic_slice_in_dim(buffer, position, full_width - 1, axis=1)
    return lax.dynamic_update_slice_in_dim(buffer, current + diagonal, position, axis=1)


def local(query_in, key_in, value_in, short_taps, long_filters, skip_gain, cotangent):
    tok_rows, chan_width = query_in.shape
    groups, seq_total = long_filters.shape
    members = chan_width // groups
    tap_count = short_taps.shape[1]
    margin = tap_count - 1
    device = lax.axis_index("seq")
    own_start = device * tok_rows
    rim_rows = jnp.stack(
        [query_in[tok_rows - margin :], key_in[tok_rows - margin :], value_in[tok_rows - margin :]]
    )
    before = from_behind(rim_rows, "seq", 1)
    streams = [query_in, key_in, value_in]
    extended = [
        jnp.concatenate([before[stream], streams[stream]]).astype(jnp.float32)
        for stream in range(3)
    ]
    query_short = short_forward(extended[0], short_taps[0], tok_rows)
    key_short = short_forward(extended[1], short_taps[1], tok_rows)
    value_short = short_forward(extended[2], short_taps[2], tok_rows)
    gating = (key_short * value_short).astype(jnp.bfloat16)
    relayed = (cotangent.astype(jnp.float32) * query_short).astype(jnp.bfloat16)
    gating_wide = gating.astype(jnp.float32)
    relayed_wide = relayed.astype(jnp.float32)
    gating_groups = gating.reshape(tok_rows, groups, members)
    relayed_groups = relayed.reshape(tok_rows, groups, members)
    padded = jnp.concatenate([jnp.zeros((groups, seq_total), jnp.bfloat16), long_filters], axis=1)
    lag_buffer = jnp.zeros((groups, 2 * seq_total), jnp.float32)
    zeros_out = jnp.zeros((tok_rows, groups, members), jnp.float32)

    def target_pair(distance):
        return distance < 0

    totals = (zeros_out, lag_buffer)
    shard_rows = lax.all_gather(gating, "seq", axis=0, tiled=True)
    piece_rows = shard_rows.shape[0]
    step_rows = min(piece_rows, tok_rows)
    pieces = shard_rows.reshape(piece_rows // step_rows, step_rows, groups, members)

    def forward_visit_block(carried, element):
        position, rows_block = element
        source_start = position * step_rows

        def forward_active(partial_value):
            output_part, buffer = partial_value
            output_part = output_part + causal_part(
                padded, rows_block, source_start, own_start, tok_rows, seq_total
            )
            distance = device - source_start // tok_rows
            buffer = lax.cond(
                target_pair(distance),
                lambda held: lag_part(
                    held, relayed_groups, rows_block, own_start, source_start, seq_total
                ),
                lambda held: held,
                buffer,
            )
            return (output_part, buffer)

        carried = lax.cond(
            source_start < own_start + tok_rows,
            forward_active,
            lambda partial_value: partial_value,
            carried,
        )
        return (carried, None)

    totals, ignored = lax.scan(
        forward_visit_block, totals, (jnp.arange(piece_rows // step_rows, dtype=jnp.int32), pieces)
    )
    output_part, lag_buffer = totals
    output_sum = output_part.reshape(tok_rows, chan_width)
    totals = (zeros_out, lag_buffer)
    shard_rows = lax.all_gather(relayed, "seq", axis=0, tiled=True)
    piece_rows = shard_rows.shape[0]
    backward_step_rows = min(piece_rows, tok_rows)
    pieces = shard_rows.reshape(
        piece_rows // backward_step_rows, backward_step_rows, groups, members
    )

    def backward_visit_block(carried, element):
        position, rows_block = element
        target_start = position * backward_step_rows

        def backward_active(partial_value):
            grad_part, buffer = partial_value
            grad_part = grad_part + anti_part(
                padded, rows_block, target_start, own_start, tok_rows, seq_total
            )
            distance = target_start // tok_rows - device
            buffer = lax.cond(
                target_pair(distance),
                lambda held: held,
                lambda held: lag_part(
                    held, rows_block, gating_groups, target_start, own_start, seq_total
                ),
                buffer,
            )
            return (grad_part, buffer)

        carried = lax.cond(
            target_start + backward_step_rows > own_start,
            backward_active,
            lambda partial_value: partial_value,
            carried,
        )
        return (carried, None)

    totals, ignored = lax.scan(
        backward_visit_block,
        totals,
        (jnp.arange(piece_rows // backward_step_rows, dtype=jnp.int32), pieces),
    )
    grad_part, lag_buffer = totals
    grad_sum = grad_part.reshape(tok_rows, chan_width)
    lag_local = lag_buffer[:, seq_total:]
    long_out = output_sum + skip_gain * gating_wide
    block_out = (query_short * long_out).astype(jnp.bfloat16)
    grad_gating = grad_sum + skip_gain * relayed_wide
    cot_wide = cotangent.astype(jnp.float32)
    grad_shorts = [cot_wide * long_out, grad_gating * value_short, grad_gating * key_short]
    lead_rows = jnp.stack([grad_shorts[stream][:margin] for stream in range(3)])
    after = from_behind(lead_rows, "seq", -1)
    input_grads = jnp.stack(
        [
            short_backward(
                jnp.concatenate([grad_shorts[stream], after[stream]]), short_taps[stream], tok_rows
            )
            for stream in range(3)
        ]
    ).astype(jnp.bfloat16)
    tap_local = jnp.stack(
        [
            tap_sums(grad_shorts[stream], extended[stream], tap_count, tok_rows)
            for stream in range(3)
        ]
    )
    skip_local = jnp.sum(relayed_wide * gating_wide, axis=0)
    lag_total, tap_total, skip_total = lax.psum((lag_local, tap_local, skip_local), "seq")
    tap_scale = 1.0 / math.sqrt(seq_total)
    lag_scale = 1.0 / math.sqrt(seq_total * members)
    return (
        block_out,
        input_grads,
        tap_total * tap_scale,
        skip_total * tap_scale,
        lag_total * lag_scale,
    )


def member_order(count):
    return list(range(count))[::-1]


def in_order(value, count):
    order = member_order(count)
    return jnp.stack([value[order.index(device)] for device in range(count)])


def by_member(value, count):
    return jnp.stack([value[device] for device in member_order(count)])


def pack_kernel(
    query_ref, key_ref, value_ref, cot_ref, skip_ref, out_ref, gain_ref, stream_buf, sems
):
    count, streams, members, tok_rows = out_ref.shape
    moves = [
        pltpu.make_async_copy(ref, stream_buf.at[stream], sems.at[stream])
        for stream, ref in enumerate((query_ref, key_ref, value_ref, cot_ref))
    ]
    moves.append(pltpu.make_async_copy(skip_ref, gain_ref, sems.at[streams]))
    for move in moves:
        move.start()
    for stream in range(streams):
        moves[stream].wait()
        flipped = stream_buf[stream].astype(jnp.float32).T.astype(jnp.bfloat16)
        out_ref[:, stream] = by_member(flipped.reshape(count, members, tok_rows), count)
    moves[streams].wait()


def group_kernel(
    in_ref, taps_ref, filters_ref, gain_ref, out_ref, table_ref, wide_ref, tile_ref
):
    count, _, members, span = in_ref.shape
    groups, seq_total = filters_ref.shape
    streams, tap_count, chan_width = taps_ref.shape
    rows = count * members
    mine = lax.axis_index("seq")
    shape = (count, members, span)
    lane = lax.broadcasted_iota(jnp.int32, shape, 2)
    reach = 3

    def later(value, steps):
        if steps == 0:
            return value
        turned = pltpu.roll(value, steps, 2)
        before = jnp.concatenate([jnp.zeros_like(turned[:1]), turned[:-1]], axis=0)
        return jnp.where(lane >= steps, turned, before)

    def earlier(value, steps):
        if steps == 0:
            return value
        turned = pltpu.roll(value, span - steps, 2)
        after = jnp.concatenate([turned[1:], jnp.zeros_like(turned[:1])], axis=0)
        return jnp.where(lane < span - steps, turned, after)

    table = jnp.concatenate(
        [taps_ref[stream] for stream in range(streams)]
        + [gain_ref[...], jnp.zeros((2, chan_width), jnp.float32)],
        axis=0,
    )
    table_ref[...] = table.T
    params = table_ref[pl.ds(pl.multiple_of(mine * members, members), members), :]

    def column(index):
        return jnp.broadcast_to(params[:, index : index + 1], (members, span))[None]

    chosen = lax.broadcasted_iota(jnp.int32, (groups, 1), 0) == mine
    filter_row = jnp.sum(
        jnp.where(chosen, filters_ref[...].astype(jnp.float32), 0.0), axis=0, keepdims=True
    )
    filter_row = jnp.concatenate([filter_row, jnp.zeros((1, span), jnp.float32)], axis=1)
    spread = jnp.broadcast_to(filter_row, (members, seq_total + span))
    first_rows = pltpu.roll(spread, 0, 1, stride=1, stride_axis=0).astype(jnp.bfloat16)
    row_parts = [first_rows] + [
        pltpu.roll(first_rows, first, 1) for first in range(members, span, members)
    ]
    toeplitz = jnp.concatenate(row_parts, axis=0)[:, :seq_total]

    def delays(stream):
        value = in_order(in_ref[:, stream], count)
        return [later(value, first) for first in range(0, tap_count, reach)]

    def short(stream, values):
        total = None
        for second in range(reach):
            running = None
            for first in range(second, tap_count, reach):
                value = values[first // reach].astype(jnp.float32)
                term = column(stream * tap_count + first) * value
                running = term if running is None else running + term
            running = later(running, second)
            total = running if total is None else total + running
        return total

    def ahead_by_blocks(value):
        parts = [value]
        for step in range(1, count):
            gap = jnp.zeros((step * members, span), jnp.bfloat16)
            parts.append(jnp.concatenate([value[step * members :], gap], axis=0))
        return jnp.concatenate(parts, axis=1)

    gain = column(streams * tap_count)
    cot = in_order(in_ref[:, streams], count).astype(jnp.float32)
    delayed = [delays(0)]
    query_short = short(0, delayed[0])
    relayed = (cot * query_short).astype(jnp.bfloat16).reshape(rows, span)
    relayed_lags = ahead_by_blocks(relayed)
    backward = lax.dot_general(
        relayed_lags, toeplitz, (((1,), (1,)), ((), ())), preferred_element_type=jnp.float32
    )

    delayed += [delays(1), delays(2)]
    key_short = short(1, delayed[1])
    value_short = short(2, delayed[2])
    gating = (key_short * value_short).astype(jnp.bfloat16).reshape(rows, span)
    gating_parts, filter_parts = [gating], [toeplitz[:, :span]]
    for step in range(1, count):
        gap = jnp.zeros((step * members, span), jnp.bfloat16)
        gating_parts.append(jnp.concatenate([gap, gating[: rows - step * members]], axis=0))
        filter_parts.append(toeplitz[:, step * span : (step + 1) * span])
    forward = jnp.dot(
        jnp.concatenate(gating_parts, axis=1),
        jnp.concatenate(filter_parts, axis=0),
        preferred_element_type=jnp.float32,
    )

    half = span // 2
    flip = (
        lax.broadcasted_iota(jnp.int32, (span, span), 0)
        + lax.broadcasted_iota(jnp.int32, (span, span), 1)
        == span - 1
    ).astype(jnp.bfloat16)
    gating_turned = lax.dot_general(
        flip, gating, (((1,), (1,)), ((), ())), preferred_element_type=jnp.float32
    ).astype(jnp.bfloat16)
    gating_turned = jnp.concatenate([gating_turned[half:], gating_turned[:half]], axis=1)
    ahead = earlier(relayed.reshape(shape), half).reshape(rows, span)
    targets = jnp.concatenate([relayed_lags, ahead_by_blocks(ahead)], axis=0)
    wide_ref[:, :seq_total] = jnp.dot(
        gating_turned, targets, preferred_element_type=jnp.float32
    )
    wide_ref[:, seq_total:] = jnp.zeros((half, span), jnp.float32)

    tap_scale = 1.0 / math.sqrt(seq_total)

    def tokens(value):
        return jnp.concatenate([value[block] for block in range(count)], axis=1)

    def sums(left, right):
        product = lax.dot_general(
            jnp.concatenate(left, axis=0),
            jnp.concatenate(right, axis=0),
            (((1,), (1,)), ((), ())),
            preferred_element_type=jnp.float32,
        )
        same = (
            lax.broadcasted_iota(jnp.int32, product.shape, 0) % members
            == lax.broadcasted_iota(jnp.int32, product.shape, 1) % members
        )
        product = jnp.where(same, product, 0.0).reshape(len(left), members, -1)
        return jnp.sum(product, axis=1) * tap_scale

    tile_ref[...] = jnp.zeros((members, span), jnp.float32)

    def finish(stream, grad_short, first_row, more_left=(), more_right=()):
        moved = [earlier(grad_short, second) for second in range(reach)]
        left = [tokens(value.astype(jnp.bfloat16)) for value in moved] + list(more_left)
        right = [tokens(value) for value in delayed[stream]] + list(more_right)
        totals = sums(left, right)
        tile_ref[first_row : first_row + len(left), : totals.shape[1]] = totals
        total = None
        for place in range(len(delayed[stream])):
            running = None
            for second in range(min(reach, tap_count - reach * place)):
                term = column(stream * tap_count + reach * place + second) * moved[second]
                running = term if running is None else running + term
            running = earlier(running, reach * place)
            total = running if total is None else total + running
        out_ref[:, 1 + stream] = by_member(total.astype(jnp.bfloat16), count)

    grad_gating = backward.reshape(shape) + gain * relayed.astype(jnp.float32).reshape(shape)
    finish(1, grad_gating * value_short, reach + 1)
    finish(2, grad_gating * key_short, 2 * reach + 1)

    long_out = forward.reshape(shape) + gain * gating.astype(jnp.float32).reshape(shape)
    out_ref[:, 0] = by_member((query_short * long_out).astype(jnp.bfloat16), count)
    finish(
        0, cot * long_out, 0, [tokens(relayed.reshape(shape))], [tokens(gating.reshape(shape))]
    )

    skewed = pltpu.roll(wide_ref[...], span - half + 1, 1, stride=1, stride_axis=0)
    diagonal = jnp.sum(skewed, axis=0, keepdims=True)
    lag_scale = 1.0 / math.sqrt(seq_total * members)
    lag_sums = jnp.concatenate(
        [diagonal[:, step * span : (step + 1) * span] for step in range(1, count + 1)], axis=0
    )
    lag_sums = lag_sums * lag_scale
    tile_ref[:count, half:] = lag_sums[:, half:]
    tile_ref[count:, half:] = pltpu.roll(lag_sums, half, 1)[:, half:]
    out_ref[:, streams + 1] = jnp.broadcast_to(tile_ref[...].astype(jnp.bfloat16)[None], shape)


def unpack_kernel(in_ref, out_ref, grads_ref, taps_ref, skip_ref, lags_ref):
    count, _, members, span = in_ref.shape
    streams, tap_count, chan_width = taps_ref.shape
    reach = 3
    for stream in range(streams + 1):
        block = in_order(in_ref[:, stream], count).reshape(count * members, span)
        block = block.astype(jnp.float32)
        flipped = block.T.astype(jnp.bfloat16)
        if stream == 0:
            out_ref[...] = flipped
        else:
            grads_ref[stream - 1] = flipped
    tile = in_order(in_ref[:, streams + 1], count).astype(jnp.float32)
    lane = lax.broadcasted_iota(jnp.int32, (1, members // 2, span), 2)
    lags = jnp.where(
        lane < span // 2, pltpu.roll(tile[:, members // 2 :], span // 2, 2), tile[:, : members // 2]
    )
    for step in range(members // 2):
        lags_ref[:, step * span : (step + 1) * span] = lags[:, step]
    lane = lax.broadcasted_iota(jnp.int32, (members, span), 1)
    spread = []
    for place in range(-(-tap_count // reach) + 1):
        total = None
        for group in range(count):
            moved = pltpu.roll(tile[group], (members * (group - place)) % span, 1)
            inside = (lane >= members * group) & (lane < members * (group + 1))
            total = moved if total is None else jnp.where(inside, moved, total)
        spread.append(total)
    first = 0
    for stream in range(streams):
        for place in range(-(-tap_count // reach)):
            taken = min(reach, tap_count - reach * place)
            taps_ref[stream, reach * place : reach * place + taken] = spread[place][
                first : first + taken
            ]
        first += reach + (stream == 0)
    skip_ref[...] = spread[-1][reach : reach + 1]


def by_group(query_in, key_in, value_in, short_taps, long_filters, skip_gain, cotangent):
    tok_rows, chan_width = query_in.shape
    groups, seq_total = long_filters.shape
    streams, tap_count, _ = short_taps.shape
    members = chan_width // groups
    count = groups
    vmem = pl.BlockSpec(memory_space=pltpu.VMEM)
    params = pltpu.CompilerParams(vmem_limit_bytes=32 * 1024 * 1024)
    packed, gain = pl.pallas_call(
        pack_kernel,
        out_shape=(
            jax.ShapeDtypeStruct((count, streams + 1, members, tok_rows), jnp.bfloat16),
            jax.ShapeDtypeStruct((1, chan_width), jnp.float32),
        ),
        in_specs=[pl.BlockSpec(memory_space=pltpu.HBM)] * 5,
        out_specs=(vmem,) * 2,
        scratch_shapes=[
            pltpu.VMEM((streams + 1, tok_rows, chan_width), jnp.bfloat16),
            pltpu.SemaphoreType.DMA((streams + 2,)),
        ],
        compiler_params=params,
        name="pack",
    )(
        *(
            pltpu.with_memory_space_constraint(value, pltpu.HBM)
            for value in (
                query_in, key_in, value_in, cotangent, skip_gain.reshape(1, chan_width)
            )
        )
    )
    packed = lax.all_to_all(
        packed, "seq", 0, 0, tiled=True, axis_index_groups=[member_order(count)]
    )
    results = pl.pallas_call(
        group_kernel,
        out_shape=jax.ShapeDtypeStruct((count, streams + 2, members, tok_rows), jnp.bfloat16),
        in_specs=[vmem] * 4,
        out_specs=vmem,
        scratch_shapes=[
            pltpu.VMEM((chan_width, streams * tap_count + 3), jnp.float32),
            pltpu.VMEM((tok_rows // 2, seq_total + tok_rows), jnp.float32),
            pltpu.VMEM((members, tok_rows), jnp.float32),
        ],
        compiler_params=params,
        name="group",
    )(packed, short_taps, long_filters, gain)
    results = lax.all_to_all(
        results, "seq", 0, 0, tiled=True, axis_index_groups=[member_order(count)]
    )
    block_out, input_grads, tap_grads, skip_grad, filter_grad = pl.pallas_call(
        unpack_kernel,
        out_shape=(
            jax.ShapeDtypeStruct((tok_rows, chan_width), jnp.bfloat16),
            jax.ShapeDtypeStruct((streams, tok_rows, chan_width), jnp.bfloat16),
            jax.ShapeDtypeStruct((streams, tap_count, chan_width), jnp.float32),
            jax.ShapeDtypeStruct((1, chan_width), jnp.float32),
            jax.ShapeDtypeStruct((groups, seq_total), jnp.float32),
        ),
        in_specs=[vmem],
        out_specs=(vmem,) * 5,
        compiler_params=params,
        name="unpack",
    )(results)
    return block_out, input_grads, tap_grads, skip_grad.reshape(chan_width), filter_grad


def plan(query_in, key_in, value_in, short_taps, long_filters, skip_gain, cotangent):
    tok_rows, chan_width = query_in.shape
    groups, seq_total = long_filters.shape
    fits = (
        lax.axis_size("seq") == groups
        and tok_rows == 128
        and chan_width == 128
        and chan_width // groups == 16
        and seq_total == groups * tok_rows
        and short_taps.shape[:2] == (3, 7)
    )
    chosen = by_group if fits else local
    return chosen(query_in, key_in, value_in, short_taps, long_filters, skip_gain, cotangent)


def solution(mesh):
    in_specs = (
        P("seq", "chan"),
        P("seq", "chan"),
        P("seq", "chan"),
        P(None, None, "chan"),
        P("chan", None),
        P("chan"),
        P("seq", "chan"),
    )
    out_specs = (
        P("seq", "chan"),
        P(None, "seq", "chan"),
        P(None, None, "chan"),
        P("chan"),
        P("chan", None),
    )
    return jax.shard_map(plan, mesh=mesh, in_specs=in_specs, out_specs=out_specs, check_vma=False)
```

```python
import functools
import math

import jax
import jax.numpy as jnp
from jax import lax
from jax.experimental import pallas as pl
from jax.experimental.pallas import tpu as pltpu
from jax.sharding import PartitionSpec as P


def from_behind(value, axis, steps):
    count = lax.axis_size(axis)
    initial, last = (max(0, -steps), min(count, count - steps))
    return lax.ppermute(value, axis, [(source, source + steps) for source in range(initial, last)])


def short_forward(extended, weights, rows_here):
    margin = weights.shape[0] - 1
    running = jnp.zeros((rows_here, extended.shape[1]), jnp.float32)
    for offset in range(weights.shape[0]):
        running = (
            running + weights[offset] * extended[margin - offset : margin - offset + rows_here]
        )
    return running


def short_backward(extended, weights, rows_here):
    running = jnp.zeros((rows_here, extended.shape[1]), jnp.float32)
    for offset in range(weights.shape[0]):
        running = running + weights[offset] * extended[offset : offset + rows_here]
    return running


def tap_sums(grad_rows, extended, tap_count, rows_here):
    margin = tap_count - 1
    sums_list = []
    for offset in range(tap_count):
        sums_list.append(
            jnp.sum(grad_rows * extended[margin - offset : margin - offset + rows_here], axis=0)
        )
    return jnp.stack(sums_list)


def hankel(padded, lag_start, height, breadth, seq_total):
    span = height + breadth - 1
    window = lax.dynamic_slice_in_dim(padded, lag_start + seq_total, span, axis=1)
    tiled = jnp.tile(window, (1, height))
    tiled = jnp.pad(tiled, ((0, 0), (0, height)))
    return tiled.reshape(padded.shape[0], height, span + 1)[:, :, :breadth]


def causal_part(padded, source_rows, source_start, target_start, target_count, seq_total):
    breadth = source_rows.shape[0]
    matrix = hankel(
        padded, target_start - source_start - breadth + 1, target_count, breadth, seq_total
    )
    return jnp.einsum("gts,sgc->tgc", matrix, source_rows[::-1], preferred_element_type=jnp.float32)


def anti_part(padded, target_rows, target_start, source_start, source_count, seq_total):
    breadth = target_rows.shape[0]
    matrix = hankel(
        padded, target_start - source_start - source_count + 1, source_count, breadth, seq_total
    )
    return jnp.einsum("gab,bgc->agc", matrix, target_rows, preferred_element_type=jnp.float32)[::-1]


def lag_part(buffer, target_rows, source_rows, target_start, source_start, seq_total):
    height = target_rows.shape[0]
    breadth = source_rows.shape[0]
    groups = target_rows.shape[1]
    padded_source = jnp.pad(source_rows[::-1], ((0, height), (0, 0), (0, 0)))
    products = jnp.einsum(
        "tgc,sgc->gts", target_rows, padded_source, preferred_element_type=jnp.float32
    )
    full_width = height + breadth
    skewed = products.reshape(groups, height * full_width)[:, : height * (full_width - 1)]
    skewed = skewed.reshape(groups, height, full_width - 1)
    diagonal = jnp.sum(skewed, axis=1)
    position = target_start - source_start - breadth + 1 + seq_total
    current = lax.dynamic_slice_in_dim(buffer, position, full_width - 1, axis=1)
    return lax.dynamic_update_slice_in_dim(buffer, current + diagonal, position, axis=1)


def local(query_in, key_in, value_in, short_taps, long_filters, skip_gain, cotangent):
    tok_rows, chan_width = query_in.shape
    groups, seq_total = long_filters.shape
    members = chan_width // groups
    tap_count = short_taps.shape[1]
    margin = tap_count - 1
    device = lax.axis_index("seq")
    own_start = device * tok_rows
    rim_rows = jnp.stack(
        [query_in[tok_rows - margin :], key_in[tok_rows - margin :], value_in[tok_rows - margin :]]
    )
    before = from_behind(rim_rows, "seq", 1)
    streams = [query_in, key_in, value_in]
    extended = [
        jnp.concatenate([before[stream], streams[stream]]).astype(jnp.float32)
        for stream in range(3)
    ]
    query_short = short_forward(extended[0], short_taps[0], tok_rows)
    key_short = short_forward(extended[1], short_taps[1], tok_rows)
    value_short = short_forward(extended[2], short_taps[2], tok_rows)
    gating = (key_short * value_short).astype(jnp.bfloat16)
    relayed = (cotangent.astype(jnp.float32) * query_short).astype(jnp.bfloat16)
    gating_wide = gating.astype(jnp.float32)
    relayed_wide = relayed.astype(jnp.float32)
    gating_groups = gating.reshape(tok_rows, groups, members)
    relayed_groups = relayed.reshape(tok_rows, groups, members)
    padded = jnp.concatenate([jnp.zeros((groups, seq_total), jnp.bfloat16), long_filters], axis=1)
    lag_buffer = jnp.zeros((groups, 2 * seq_total), jnp.float32)
    zeros_out = jnp.zeros((tok_rows, groups, members), jnp.float32)

    def target_pair(distance):
        return distance < 0

    totals = (zeros_out, lag_buffer)
    shard_rows = lax.all_gather(gating, "seq", axis=0, tiled=True)
    piece_rows = shard_rows.shape[0]
    step_rows = min(piece_rows, tok_rows)
    pieces = shard_rows.reshape(piece_rows // step_rows, step_rows, groups, members)

    def forward_visit_block(carried, element):
        position, rows_block = element
        source_start = position * step_rows

        def forward_active(partial_value):
            output_part, buffer = partial_value
            output_part = output_part + causal_part(
                padded, rows_block, source_start, own_start, tok_rows, seq_total
            )
            distance = device - source_start // tok_rows
            buffer = lax.cond(
                target_pair(distance),
                lambda held: lag_part(
                    held, relayed_groups, rows_block, own_start, source_start, seq_total
                ),
                lambda held: held,
                buffer,
            )
            return (output_part, buffer)

        carried = lax.cond(
            source_start < own_start + tok_rows,
            forward_active,
            lambda partial_value: partial_value,
            carried,
        )
        return (carried, None)

    totals, ignored = lax.scan(
        forward_visit_block, totals, (jnp.arange(piece_rows // step_rows, dtype=jnp.int32), pieces)
    )
    output_part, lag_buffer = totals
    output_sum = output_part.reshape(tok_rows, chan_width)
    totals = (zeros_out, lag_buffer)
    shard_rows = lax.all_gather(relayed, "seq", axis=0, tiled=True)
    piece_rows = shard_rows.shape[0]
    backward_step_rows = min(piece_rows, tok_rows)
    pieces = shard_rows.reshape(
        piece_rows // backward_step_rows, backward_step_rows, groups, members
    )

    def backward_visit_block(carried, element):
        position, rows_block = element
        target_start = position * backward_step_rows

        def backward_active(partial_value):
            grad_part, buffer = partial_value
            grad_part = grad_part + anti_part(
                padded, rows_block, target_start, own_start, tok_rows, seq_total
            )
            distance = target_start // tok_rows - device
            buffer = lax.cond(
                target_pair(distance),
                lambda held: held,
                lambda held: lag_part(
                    held, rows_block, gating_groups, target_start, own_start, seq_total
                ),
                buffer,
            )
            return (grad_part, buffer)

        carried = lax.cond(
            target_start + backward_step_rows > own_start,
            backward_active,
            lambda partial_value: partial_value,
            carried,
        )
        return (carried, None)

    totals, ignored = lax.scan(
        backward_visit_block,
        totals,
        (jnp.arange(piece_rows // backward_step_rows, dtype=jnp.int32), pieces),
    )
    grad_part, lag_buffer = totals
    grad_sum = grad_part.reshape(tok_rows, chan_width)
    lag_local = lag_buffer[:, seq_total:]
    long_out = output_sum + skip_gain * gating_wide
    block_out = (query_short * long_out).astype(jnp.bfloat16)
    grad_gating = grad_sum + skip_gain * relayed_wide
    cot_wide = cotangent.astype(jnp.float32)
    grad_shorts = [cot_wide * long_out, grad_gating * value_short, grad_gating * key_short]
    lead_rows = jnp.stack([grad_shorts[stream][:margin] for stream in range(3)])
    after = from_behind(lead_rows, "seq", -1)
    input_grads = jnp.stack(
        [
            short_backward(
                jnp.concatenate([grad_shorts[stream], after[stream]]), short_taps[stream], tok_rows
            )
            for stream in range(3)
        ]
    ).astype(jnp.bfloat16)
    tap_local = jnp.stack(
        [
            tap_sums(grad_shorts[stream], extended[stream], tap_count, tok_rows)
            for stream in range(3)
        ]
    )
    skip_local = jnp.sum(relayed_wide * gating_wide, axis=0)
    lag_total, tap_total, skip_total = lax.psum((lag_local, tap_local, skip_local), "seq")
    tap_scale = 1.0 / math.sqrt(seq_total)
    lag_scale = 1.0 / math.sqrt(seq_total * members)
    return (
        block_out,
        input_grads,
        tap_total * tap_scale,
        skip_total * tap_scale,
        lag_total * lag_scale,
    )


def order_there(count):
    return [count - 1] + list(range(count - 1))


def order_back(count):
    return list(range(count // 2, count)) + list(range(count // 2))


def in_order(value, order):
    return jnp.stack([value[order.index(device)] for device in range(len(order))])


def by_member(value, order):
    return jnp.stack([value[device] for device in order])


def pack_kernel(
    query_ref, key_ref, value_ref, cot_ref, skip_ref, out_ref, gain_ref, stream_buf, sems
):
    count, streams, members, tok_rows = out_ref.shape
    moves = [
        pltpu.make_async_copy(ref, stream_buf.at[stream], sems.at[stream])
        for stream, ref in enumerate((query_ref, key_ref, value_ref, cot_ref))
    ]
    moves.append(pltpu.make_async_copy(skip_ref, gain_ref, sems.at[streams]))
    for move in moves:
        move.start()
    for stream in range(streams):
        moves[stream].wait()
        flipped = stream_buf[stream].astype(jnp.float32).T.astype(jnp.bfloat16)
        flipped = flipped.reshape(count, members, tok_rows)
        out_ref[:, stream] = by_member(flipped, order_there(count))
    moves[streams].wait()


def group_kernel(
    in_ref, taps_ref, filters_ref, gain_ref, out_ref, table_ref, wide_ref, tile_ref
):
    count, _, members, span = in_ref.shape
    groups, seq_total = filters_ref.shape
    streams, tap_count, chan_width = taps_ref.shape
    rows = count * members
    mine = lax.axis_index("seq")
    shape = (count, members, span)
    lane = lax.broadcasted_iota(jnp.int32, shape, 2)
    reach = 3

    def later(value, steps):
        if steps == 0:
            return value
        turned = pltpu.roll(value, steps, 2)
        before = jnp.concatenate([jnp.zeros_like(turned[:1]), turned[:-1]], axis=0)
        return jnp.where(lane >= steps, turned, before)

    def earlier(value, steps):
        if steps == 0:
            return value
        turned = pltpu.roll(value, span - steps, 2)
        after = jnp.concatenate([turned[1:], jnp.zeros_like(turned[:1])], axis=0)
        return jnp.where(lane < span - steps, turned, after)

    table = jnp.concatenate(
        [taps_ref[stream] for stream in range(streams)]
        + [gain_ref[...], jnp.zeros((2, chan_width), jnp.float32)],
        axis=0,
    )
    table_ref[...] = table.T
    params = table_ref[pl.ds(pl.multiple_of(mine * members, members), members), :]

    def column(index):
        return jnp.broadcast_to(params[:, index : index + 1], (members, span))[None]

    chosen = lax.broadcasted_iota(jnp.int32, (groups, 1), 0) == mine
    filter_row = jnp.sum(
        jnp.where(chosen, filters_ref[...].astype(jnp.float32), 0.0), axis=0, keepdims=True
    )
    filter_row = jnp.concatenate([filter_row, jnp.zeros((1, span), jnp.float32)], axis=1)
    spread = jnp.broadcast_to(filter_row, (members, seq_total + span))
    first_rows = pltpu.roll(spread, 0, 1, stride=1, stride_axis=0).astype(jnp.bfloat16)
    row_parts = [first_rows] + [
        pltpu.roll(first_rows, first, 1) for first in range(members, span, members)
    ]
    toeplitz = jnp.concatenate(row_parts, axis=0)[:, :seq_total]

    def delays(stream):
        value = in_order(in_ref[:, stream], order_there(count))
        return [later(value, first) for first in range(0, tap_count, reach)]

    def short(stream, values):
        total = None
        for second in range(reach):
            running = None
            for first in range(second, tap_count, reach):
                value = values[first // reach].astype(jnp.float32)
                term = column(stream * tap_count + first) * value
                running = term if running is None else running + term
            running = later(running, second)
            total = running if total is None else total + running
        return total

    def ahead_by_blocks(value):
        parts = [value]
        for step in range(1, count):
            gap = jnp.zeros((step * members, span), jnp.bfloat16)
            parts.append(jnp.concatenate([value[step * members :], gap], axis=0))
        return jnp.concatenate(parts, axis=1)

    gain = column(streams * tap_count)
    cot = in_order(in_ref[:, streams], order_there(count)).astype(jnp.float32)
    delayed = [delays(0)]
    query_short = short(0, delayed[0])
    relayed = (cot * query_short).astype(jnp.bfloat16).reshape(rows, span)
    relayed_lags = ahead_by_blocks(relayed)
    backward = lax.dot_general(
        relayed_lags, toeplitz, (((1,), (1,)), ((), ())), preferred_element_type=jnp.float32
    )

    delayed += [delays(1), delays(2)]
    key_short = short(1, delayed[1])
    value_short = short(2, delayed[2])
    gating = (key_short * value_short).astype(jnp.bfloat16).reshape(rows, span)
    gating_parts, filter_parts = [gating], [toeplitz[:, :span]]
    for step in range(1, count):
        gap = jnp.zeros((step * members, span), jnp.bfloat16)
        gating_parts.append(jnp.concatenate([gap, gating[: rows - step * members]], axis=0))
        filter_parts.append(toeplitz[:, step * span : (step + 1) * span])
    forward = jnp.dot(
        jnp.concatenate(gating_parts, axis=1),
        jnp.concatenate(filter_parts, axis=0),
        preferred_element_type=jnp.float32,
    )

    half = span // 2
    flip = (
        lax.broadcasted_iota(jnp.int32, (span, span), 0)
        + lax.broadcasted_iota(jnp.int32, (span, span), 1)
        == span - 1
    ).astype(jnp.bfloat16)
    gating_turned = lax.dot_general(
        flip, gating, (((1,), (1,)), ((), ())), preferred_element_type=jnp.float32
    ).astype(jnp.bfloat16)
    gating_turned = jnp.concatenate([gating_turned[half:], gating_turned[:half]], axis=1)
    ahead = earlier(relayed.reshape(shape), half).reshape(rows, span)
    targets = jnp.concatenate([relayed_lags, ahead_by_blocks(ahead)], axis=0)
    wide_ref[:, :seq_total] = jnp.dot(
        gating_turned, targets, preferred_element_type=jnp.float32
    )
    wide_ref[:, seq_total:] = jnp.zeros((half, span), jnp.float32)

    tap_scale = 1.0 / math.sqrt(seq_total)

    def tokens(value):
        return jnp.concatenate([value[block] for block in range(count)], axis=1)

    def sums(left, right):
        product = lax.dot_general(
            jnp.concatenate(left, axis=0),
            jnp.concatenate(right, axis=0),
            (((1,), (1,)), ((), ())),
            preferred_element_type=jnp.float32,
        )
        same = (
            lax.broadcasted_iota(jnp.int32, product.shape, 0) % members
            == lax.broadcasted_iota(jnp.int32, product.shape, 1) % members
        )
        product = jnp.where(same, product, 0.0).reshape(len(left), members, -1)
        return jnp.sum(product, axis=1) * tap_scale

    tile_ref[...] = jnp.zeros((members, span), jnp.float32)

    def finish(stream, grad_short, first_row, more_left=(), more_right=()):
        moved = [earlier(grad_short, second) for second in range(reach)]
        left = [tokens(value.astype(jnp.bfloat16)) for value in moved] + list(more_left)
        right = [tokens(value) for value in delayed[stream]] + list(more_right)
        totals = sums(left, right)
        tile_ref[first_row : first_row + len(left), : totals.shape[1]] = totals
        total = None
        for place in range(len(delayed[stream])):
            running = None
            for second in range(min(reach, tap_count - reach * place)):
                term = column(stream * tap_count + reach * place + second) * moved[second]
                running = term if running is None else running + term
            running = earlier(running, reach * place)
            total = running if total is None else total + running
        out_ref[:, 1 + stream] = by_member(total.astype(jnp.bfloat16), order_back(count))

    grad_gating = backward.reshape(shape) + gain * relayed.astype(jnp.float32).reshape(shape)
    finish(1, grad_gating * value_short, reach + 1)
    finish(2, grad_gating * key_short, 2 * reach + 1)

    long_out = forward.reshape(shape) + gain * gating.astype(jnp.float32).reshape(shape)
    block_out = (query_short * long_out).astype(jnp.bfloat16)
    out_ref[:, 0] = by_member(block_out, order_back(count))
    finish(
        0, cot * long_out, 0, [tokens(relayed.reshape(shape))], [tokens(gating.reshape(shape))]
    )

    skewed = pltpu.roll(wide_ref[...], span - half + 1, 1, stride=1, stride_axis=0)
    diagonal = jnp.sum(skewed, axis=0, keepdims=True)
    lag_scale = 1.0 / math.sqrt(seq_total * members)
    lag_sums = jnp.concatenate(
        [diagonal[:, step * span : (step + 1) * span] for step in range(1, count + 1)], axis=0
    )
    lag_sums = lag_sums * lag_scale
    tile_ref[:count, half:] = lag_sums[:, half:]
    tile_ref[count:, half:] = pltpu.roll(lag_sums, half, 1)[:, half:]
    out_ref[:, streams + 1] = jnp.broadcast_to(tile_ref[...].astype(jnp.bfloat16)[None], shape)


def unpack_kernel(in_ref, out_ref, grads_ref, taps_ref, skip_ref, lags_ref):
    count, _, members, span = in_ref.shape
    streams, tap_count, chan_width = taps_ref.shape
    reach = 3
    for stream in range(streams + 1):
        block = in_order(in_ref[:, stream], order_back(count)).reshape(count * members, span)
        block = block.astype(jnp.float32)
        flipped = block.T.astype(jnp.bfloat16)
        if stream == 0:
            out_ref[...] = flipped
        else:
            grads_ref[stream - 1] = flipped
    tile = in_order(in_ref[:, streams + 1], order_back(count)).astype(jnp.float32)
    lane = lax.broadcasted_iota(jnp.int32, (1, members // 2, span), 2)
    lags = jnp.where(
        lane < span // 2, pltpu.roll(tile[:, members // 2 :], span // 2, 2), tile[:, : members // 2]
    )
    for step in range(members // 2):
        lags_ref[:, step * span : (step + 1) * span] = lags[:, step]
    lane = lax.broadcasted_iota(jnp.int32, (members, span), 1)
    spread = []
    for place in range(-(-tap_count // reach) + 1):
        total = None
        for group in range(count):
            moved = pltpu.roll(tile[group], (members * (group - place)) % span, 1)
            inside = (lane >= members * group) & (lane < members * (group + 1))
            total = moved if total is None else jnp.where(inside, moved, total)
        spread.append(total)
    first = 0
    for stream in range(streams):
        for place in range(-(-tap_count // reach)):
            taken = min(reach, tap_count - reach * place)
            taps_ref[stream, reach * place : reach * place + taken] = spread[place][
                first : first + taken
            ]
        first += reach + (stream == 0)
    skip_ref[...] = spread[-1][reach : reach + 1]


def by_group(query_in, key_in, value_in, short_taps, long_filters, skip_gain, cotangent):
    tok_rows, chan_width = query_in.shape
    groups, seq_total = long_filters.shape
    streams, tap_count, _ = short_taps.shape
    members = chan_width // groups
    count = groups
    vmem = pl.BlockSpec(memory_space=pltpu.VMEM)
    params = pltpu.CompilerParams(vmem_limit_bytes=32 * 1024 * 1024)
    packed, gain = pl.pallas_call(
        pack_kernel,
        out_shape=(
            jax.ShapeDtypeStruct((count, streams + 1, members, tok_rows), jnp.bfloat16),
            jax.ShapeDtypeStruct((1, chan_width), jnp.float32),
        ),
        in_specs=[pl.BlockSpec(memory_space=pltpu.HBM)] * 5,
        out_specs=(vmem,) * 2,
        scratch_shapes=[
            pltpu.VMEM((streams + 1, tok_rows, chan_width), jnp.bfloat16),
            pltpu.SemaphoreType.DMA((streams + 2,)),
        ],
        compiler_params=params,
        name="pack",
    )(
        *(
            pltpu.with_memory_space_constraint(value, pltpu.HBM)
            for value in (
                query_in, key_in, value_in, cotangent, skip_gain.reshape(1, chan_width)
            )
        )
    )
    packed = lax.all_to_all(
        packed, "seq", 0, 0, tiled=True, axis_index_groups=[order_there(count)]
    )
    results = pl.pallas_call(
        group_kernel,
        out_shape=jax.ShapeDtypeStruct((count, streams + 2, members, tok_rows), jnp.bfloat16),
        in_specs=[vmem] * 4,
        out_specs=vmem,
        scratch_shapes=[
            pltpu.VMEM((chan_width, streams * tap_count + 3), jnp.float32),
            pltpu.VMEM((tok_rows // 2, seq_total + tok_rows), jnp.float32),
            pltpu.VMEM((members, tok_rows), jnp.float32),
        ],
        compiler_params=params,
        name="group",
    )(packed, short_taps, long_filters, gain)
    results = lax.all_to_all(
        results, "seq", 0, 0, tiled=True, axis_index_groups=[order_back(count)]
    )
    block_out, input_grads, tap_grads, skip_grad, filter_grad = pl.pallas_call(
        unpack_kernel,
        out_shape=(
            jax.ShapeDtypeStruct((tok_rows, chan_width), jnp.bfloat16),
            jax.ShapeDtypeStruct((streams, tok_rows, chan_width), jnp.bfloat16),
            jax.ShapeDtypeStruct((streams, tap_count, chan_width), jnp.float32),
            jax.ShapeDtypeStruct((1, chan_width), jnp.float32),
            jax.ShapeDtypeStruct((groups, seq_total), jnp.float32),
        ),
        in_specs=[vmem],
        out_specs=(vmem,) * 5,
        compiler_params=params,
        name="unpack",
    )(results)
    return block_out, input_grads, tap_grads, skip_grad.reshape(chan_width), filter_grad


def plan(query_in, key_in, value_in, short_taps, long_filters, skip_gain, cotangent):
    tok_rows, chan_width = query_in.shape
    groups, seq_total = long_filters.shape
    fits = (
        lax.axis_size("seq") == groups
        and tok_rows == 128
        and chan_width == 128
        and chan_width // groups == 16
        and seq_total == groups * tok_rows
        and short_taps.shape[:2] == (3, 7)
    )
    chosen = by_group if fits else local
    return chosen(query_in, key_in, value_in, short_taps, long_filters, skip_gain, cotangent)


def solution(mesh):
    in_specs = (
        P("seq", "chan"),
        P("seq", "chan"),
        P("seq", "chan"),
        P(None, None, "chan"),
        P("chan", None),
        P("chan"),
        P("seq", "chan"),
    )
    out_specs = (
        P("seq", "chan"),
        P(None, "seq", "chan"),
        P(None, None, "chan"),
        P("chan"),
        P("chan", None),
    )
    return jax.shard_map(plan, mesh=mesh, in_specs=in_specs, out_specs=out_specs, check_vma=False)
```

```python
import functools
import math

import jax
import jax.numpy as jnp
from jax import lax
from jax.experimental import pallas as pl
from jax.experimental.pallas import tpu as pltpu
from jax.sharding import PartitionSpec as P


def from_behind(value, axis, steps):
    count = lax.axis_size(axis)
    initial, last = (max(0, -steps), min(count, count - steps))
    return lax.ppermute(value, axis, [(source, source + steps) for source in range(initial, last)])


def short_forward(extended, weights, rows_here):
    margin = weights.shape[0] - 1
    running = jnp.zeros((rows_here, extended.shape[1]), jnp.float32)
    for offset in range(weights.shape[0]):
        running = (
            running + weights[offset] * extended[margin - offset : margin - offset + rows_here]
        )
    return running


def short_backward(extended, weights, rows_here):
    running = jnp.zeros((rows_here, extended.shape[1]), jnp.float32)
    for offset in range(weights.shape[0]):
        running = running + weights[offset] * extended[offset : offset + rows_here]
    return running


def tap_sums(grad_rows, extended, tap_count, rows_here):
    margin = tap_count - 1
    sums_list = []
    for offset in range(tap_count):
        sums_list.append(
            jnp.sum(grad_rows * extended[margin - offset : margin - offset + rows_here], axis=0)
        )
    return jnp.stack(sums_list)


def hankel(padded, lag_start, height, breadth, seq_total):
    span = height + breadth - 1
    window = lax.dynamic_slice_in_dim(padded, lag_start + seq_total, span, axis=1)
    tiled = jnp.tile(window, (1, height))
    tiled = jnp.pad(tiled, ((0, 0), (0, height)))
    return tiled.reshape(padded.shape[0], height, span + 1)[:, :, :breadth]


def causal_part(padded, source_rows, source_start, target_start, target_count, seq_total):
    breadth = source_rows.shape[0]
    matrix = hankel(
        padded, target_start - source_start - breadth + 1, target_count, breadth, seq_total
    )
    return jnp.einsum("gts,sgc->tgc", matrix, source_rows[::-1], preferred_element_type=jnp.float32)


def anti_part(padded, target_rows, target_start, source_start, source_count, seq_total):
    breadth = target_rows.shape[0]
    matrix = hankel(
        padded, target_start - source_start - source_count + 1, source_count, breadth, seq_total
    )
    return jnp.einsum("gab,bgc->agc", matrix, target_rows, preferred_element_type=jnp.float32)[::-1]


def lag_part(buffer, target_rows, source_rows, target_start, source_start, seq_total):
    height = target_rows.shape[0]
    breadth = source_rows.shape[0]
    groups = target_rows.shape[1]
    padded_source = jnp.pad(source_rows[::-1], ((0, height), (0, 0), (0, 0)))
    products = jnp.einsum(
        "tgc,sgc->gts", target_rows, padded_source, preferred_element_type=jnp.float32
    )
    full_width = height + breadth
    skewed = products.reshape(groups, height * full_width)[:, : height * (full_width - 1)]
    skewed = skewed.reshape(groups, height, full_width - 1)
    diagonal = jnp.sum(skewed, axis=1)
    position = target_start - source_start - breadth + 1 + seq_total
    current = lax.dynamic_slice_in_dim(buffer, position, full_width - 1, axis=1)
    return lax.dynamic_update_slice_in_dim(buffer, current + diagonal, position, axis=1)


def local(query_in, key_in, value_in, short_taps, long_filters, skip_gain, cotangent):
    tok_rows, chan_width = query_in.shape
    groups, seq_total = long_filters.shape
    members = chan_width // groups
    tap_count = short_taps.shape[1]
    margin = tap_count - 1
    device = lax.axis_index("seq")
    own_start = device * tok_rows
    rim_rows = jnp.stack(
        [query_in[tok_rows - margin :], key_in[tok_rows - margin :], value_in[tok_rows - margin :]]
    )
    before = from_behind(rim_rows, "seq", 1)
    streams = [query_in, key_in, value_in]
    extended = [
        jnp.concatenate([before[stream], streams[stream]]).astype(jnp.float32)
        for stream in range(3)
    ]
    query_short = short_forward(extended[0], short_taps[0], tok_rows)
    key_short = short_forward(extended[1], short_taps[1], tok_rows)
    value_short = short_forward(extended[2], short_taps[2], tok_rows)
    gating = (key_short * value_short).astype(jnp.bfloat16)
    relayed = (cotangent.astype(jnp.float32) * query_short).astype(jnp.bfloat16)
    gating_wide = gating.astype(jnp.float32)
    relayed_wide = relayed.astype(jnp.float32)
    gating_groups = gating.reshape(tok_rows, groups, members)
    relayed_groups = relayed.reshape(tok_rows, groups, members)
    padded = jnp.concatenate([jnp.zeros((groups, seq_total), jnp.bfloat16), long_filters], axis=1)
    lag_buffer = jnp.zeros((groups, 2 * seq_total), jnp.float32)
    zeros_out = jnp.zeros((tok_rows, groups, members), jnp.float32)

    def target_pair(distance):
        return distance < 0

    totals = (zeros_out, lag_buffer)
    shard_rows = lax.all_gather(gating, "seq", axis=0, tiled=True)
    piece_rows = shard_rows.shape[0]
    step_rows = min(piece_rows, tok_rows)
    pieces = shard_rows.reshape(piece_rows // step_rows, step_rows, groups, members)

    def forward_visit_block(carried, element):
        position, rows_block = element
        source_start = position * step_rows

        def forward_active(partial_value):
            output_part, buffer = partial_value
            output_part = output_part + causal_part(
                padded, rows_block, source_start, own_start, tok_rows, seq_total
            )
            distance = device - source_start // tok_rows
            buffer = lax.cond(
                target_pair(distance),
                lambda held: lag_part(
                    held, relayed_groups, rows_block, own_start, source_start, seq_total
                ),
                lambda held: held,
                buffer,
            )
            return (output_part, buffer)

        carried = lax.cond(
            source_start < own_start + tok_rows,
            forward_active,
            lambda partial_value: partial_value,
            carried,
        )
        return (carried, None)

    totals, ignored = lax.scan(
        forward_visit_block, totals, (jnp.arange(piece_rows // step_rows, dtype=jnp.int32), pieces)
    )
    output_part, lag_buffer = totals
    output_sum = output_part.reshape(tok_rows, chan_width)
    totals = (zeros_out, lag_buffer)
    shard_rows = lax.all_gather(relayed, "seq", axis=0, tiled=True)
    piece_rows = shard_rows.shape[0]
    backward_step_rows = min(piece_rows, tok_rows)
    pieces = shard_rows.reshape(
        piece_rows // backward_step_rows, backward_step_rows, groups, members
    )

    def backward_visit_block(carried, element):
        position, rows_block = element
        target_start = position * backward_step_rows

        def backward_active(partial_value):
            grad_part, buffer = partial_value
            grad_part = grad_part + anti_part(
                padded, rows_block, target_start, own_start, tok_rows, seq_total
            )
            distance = target_start // tok_rows - device
            buffer = lax.cond(
                target_pair(distance),
                lambda held: held,
                lambda held: lag_part(
                    held, rows_block, gating_groups, target_start, own_start, seq_total
                ),
                buffer,
            )
            return (grad_part, buffer)

        carried = lax.cond(
            target_start + backward_step_rows > own_start,
            backward_active,
            lambda partial_value: partial_value,
            carried,
        )
        return (carried, None)

    totals, ignored = lax.scan(
        backward_visit_block,
        totals,
        (jnp.arange(piece_rows // backward_step_rows, dtype=jnp.int32), pieces),
    )
    grad_part, lag_buffer = totals
    grad_sum = grad_part.reshape(tok_rows, chan_width)
    lag_local = lag_buffer[:, seq_total:]
    long_out = output_sum + skip_gain * gating_wide
    block_out = (query_short * long_out).astype(jnp.bfloat16)
    grad_gating = grad_sum + skip_gain * relayed_wide
    cot_wide = cotangent.astype(jnp.float32)
    grad_shorts = [cot_wide * long_out, grad_gating * value_short, grad_gating * key_short]
    lead_rows = jnp.stack([grad_shorts[stream][:margin] for stream in range(3)])
    after = from_behind(lead_rows, "seq", -1)
    input_grads = jnp.stack(
        [
            short_backward(
                jnp.concatenate([grad_shorts[stream], after[stream]]), short_taps[stream], tok_rows
            )
            for stream in range(3)
        ]
    ).astype(jnp.bfloat16)
    tap_local = jnp.stack(
        [
            tap_sums(grad_shorts[stream], extended[stream], tap_count, tok_rows)
            for stream in range(3)
        ]
    )
    skip_local = jnp.sum(relayed_wide * gating_wide, axis=0)
    lag_total, tap_total, skip_total = lax.psum((lag_local, tap_local, skip_local), "seq")
    tap_scale = 1.0 / math.sqrt(seq_total)
    lag_scale = 1.0 / math.sqrt(seq_total * members)
    return (
        block_out,
        input_grads,
        tap_total * tap_scale,
        skip_total * tap_scale,
        lag_total * lag_scale,
    )


def order_there(count):
    return list(range(count // 2 + 1, count)) + list(range(count // 2 + 1))


def order_back(count):
    return list(range(count // 2 + 1, count)) + list(range(count // 2 + 1))


def in_order(value, order):
    return jnp.stack([value[order.index(device)] for device in range(len(order))])


def by_member(value, order):
    return jnp.stack([value[device] for device in order])


def pack_kernel(
    query_ref, key_ref, value_ref, cot_ref, skip_ref, out_ref, gain_ref, stream_buf, sems
):
    count, streams, members, tok_rows = out_ref.shape
    moves = [
        pltpu.make_async_copy(ref, stream_buf.at[stream], sems.at[stream])
        for stream, ref in enumerate((query_ref, key_ref, value_ref, cot_ref))
    ]
    moves.append(pltpu.make_async_copy(skip_ref, gain_ref, sems.at[streams]))
    for move in moves:
        move.start()
    for stream in range(streams):
        moves[stream].wait()
        flipped = stream_buf[stream].astype(jnp.float32).T.astype(jnp.bfloat16)
        flipped = flipped.reshape(count, members, tok_rows)
        out_ref[:, stream] = by_member(flipped, order_there(count))
    moves[streams].wait()


def group_kernel(
    in_ref, taps_ref, filters_ref, gain_ref, out_ref, table_ref, wide_ref, tile_ref
):
    count, _, members, span = in_ref.shape
    groups, seq_total = filters_ref.shape
    streams, tap_count, chan_width = taps_ref.shape
    rows = count * members
    mine = lax.axis_index("seq")
    shape = (count, members, span)
    lane = lax.broadcasted_iota(jnp.int32, shape, 2)
    reach = 3

    def later(value, steps):
        if steps == 0:
            return value
        turned = pltpu.roll(value, steps, 2)
        before = jnp.concatenate([jnp.zeros_like(turned[:1]), turned[:-1]], axis=0)
        return jnp.where(lane >= steps, turned, before)

    def earlier(value, steps):
        if steps == 0:
            return value
        turned = pltpu.roll(value, span - steps, 2)
        after = jnp.concatenate([turned[1:], jnp.zeros_like(turned[:1])], axis=0)
        return jnp.where(lane < span - steps, turned, after)

    table = jnp.concatenate(
        [taps_ref[stream] for stream in range(streams)]
        + [gain_ref[...], jnp.zeros((2, chan_width), jnp.float32)],
        axis=0,
    )
    table_ref[...] = table.T
    params = table_ref[pl.ds(pl.multiple_of(mine * members, members), members), :]

    def column(index):
        return jnp.broadcast_to(params[:, index : index + 1], (members, span))[None]

    chosen = lax.broadcasted_iota(jnp.int32, (groups, 1), 0) == mine
    filter_row = jnp.sum(
        jnp.where(chosen, filters_ref[...].astype(jnp.float32), 0.0), axis=0, keepdims=True
    )
    filter_row = jnp.concatenate([filter_row, jnp.zeros((1, span), jnp.float32)], axis=1)
    spread = jnp.broadcast_to(filter_row, (members, seq_total + span))
    first_rows = pltpu.roll(spread, 0, 1, stride=1, stride_axis=0).astype(jnp.bfloat16)
    row_parts = [first_rows] + [
        pltpu.roll(first_rows, first, 1) for first in range(members, span, members)
    ]
    toeplitz = jnp.concatenate(row_parts, axis=0)[:, :seq_total]

    def delays(stream):
        value = in_order(in_ref[:, stream], order_there(count))
        return [later(value, first) for first in range(0, tap_count, reach)]

    def short(stream, values):
        total = None
        for second in range(reach):
            running = None
            for first in range(second, tap_count, reach):
                value = values[first // reach].astype(jnp.float32)
                term = column(stream * tap_count + first) * value
                running = term if running is None else running + term
            running = later(running, second)
            total = running if total is None else total + running
        return total

    def ahead_by_blocks(value):
        parts = [value]
        for step in range(1, count):
            gap = jnp.zeros((step * members, span), jnp.bfloat16)
            parts.append(jnp.concatenate([value[step * members :], gap], axis=0))
        return jnp.concatenate(parts, axis=1)

    gain = column(streams * tap_count)
    cot = in_order(in_ref[:, streams], order_there(count)).astype(jnp.float32)
    delayed = [delays(0)]
    query_short = short(0, delayed[0])
    relayed = (cot * query_short).astype(jnp.bfloat16).reshape(rows, span)
    relayed_lags = ahead_by_blocks(relayed)
    backward = lax.dot_general(
        relayed_lags, toeplitz, (((1,), (1,)), ((), ())), preferred_element_type=jnp.float32
    )

    delayed += [delays(1), delays(2)]
    key_short = short(1, delayed[1])
    value_short = short(2, delayed[2])
    gating = (key_short * value_short).astype(jnp.bfloat16).reshape(rows, span)
    gating_parts, filter_parts = [gating], [toeplitz[:, :span]]
    for step in range(1, count):
        gap = jnp.zeros((step * members, span), jnp.bfloat16)
        gating_parts.append(jnp.concatenate([gap, gating[: rows - step * members]], axis=0))
        filter_parts.append(toeplitz[:, step * span : (step + 1) * span])
    forward = jnp.dot(
        jnp.concatenate(gating_parts, axis=1),
        jnp.concatenate(filter_parts, axis=0),
        preferred_element_type=jnp.float32,
    )

    half = span // 2
    flip = (
        lax.broadcasted_iota(jnp.int32, (span, span), 0)
        + lax.broadcasted_iota(jnp.int32, (span, span), 1)
        == span - 1
    ).astype(jnp.bfloat16)
    gating_turned = lax.dot_general(
        flip, gating, (((1,), (1,)), ((), ())), preferred_element_type=jnp.float32
    ).astype(jnp.bfloat16)
    gating_turned = jnp.concatenate([gating_turned[half:], gating_turned[:half]], axis=1)
    ahead = earlier(relayed.reshape(shape), half).reshape(rows, span)
    targets = jnp.concatenate([relayed_lags, ahead_by_blocks(ahead)], axis=0)
    wide_ref[:, :seq_total] = jnp.dot(
        gating_turned, targets, preferred_element_type=jnp.float32
    )
    wide_ref[:, seq_total:] = jnp.zeros((half, span), jnp.float32)

    tap_scale = 1.0 / math.sqrt(seq_total)

    def tokens(value):
        return jnp.concatenate([value[block] for block in range(count)], axis=1)

    def sums(left, right):
        product = lax.dot_general(
            jnp.concatenate(left, axis=0),
            jnp.concatenate(right, axis=0),
            (((1,), (1,)), ((), ())),
            preferred_element_type=jnp.float32,
        )
        same = (
            lax.broadcasted_iota(jnp.int32, product.shape, 0) % members
            == lax.broadcasted_iota(jnp.int32, product.shape, 1) % members
        )
        product = jnp.where(same, product, 0.0).reshape(len(left), members, -1)
        return jnp.sum(product, axis=1) * tap_scale

    tile_ref[...] = jnp.zeros((members, span), jnp.float32)

    def finish(stream, grad_short, first_row, more_left=(), more_right=()):
        moved = [earlier(grad_short, second) for second in range(reach)]
        left = [tokens(value.astype(jnp.bfloat16)) for value in moved] + list(more_left)
        right = [tokens(value) for value in delayed[stream]] + list(more_right)
        totals = sums(left, right)
        tile_ref[first_row : first_row + len(left), : totals.shape[1]] = totals
        total = None
        for place in range(len(delayed[stream])):
            running = None
            for second in range(min(reach, tap_count - reach * place)):
                term = column(stream * tap_count + reach * place + second) * moved[second]
                running = term if running is None else running + term
            running = earlier(running, reach * place)
            total = running if total is None else total + running
        out_ref[:, 1 + stream] = by_member(total.astype(jnp.bfloat16), order_back(count))

    grad_gating = backward.reshape(shape) + gain * relayed.astype(jnp.float32).reshape(shape)
    finish(1, grad_gating * value_short, reach + 1)
    finish(2, grad_gating * key_short, 2 * reach + 1)

    long_out = forward.reshape(shape) + gain * gating.astype(jnp.float32).reshape(shape)
    block_out = (query_short * long_out).astype(jnp.bfloat16)
    out_ref[:, 0] = by_member(block_out, order_back(count))
    finish(
        0, cot * long_out, 0, [tokens(relayed.reshape(shape))], [tokens(gating.reshape(shape))]
    )

    skewed = pltpu.roll(wide_ref[...], span - half + 1, 1, stride=1, stride_axis=0)
    diagonal = jnp.sum(skewed, axis=0, keepdims=True)
    lag_scale = 1.0 / math.sqrt(seq_total * members)
    lag_sums = jnp.concatenate(
        [diagonal[:, step * span : (step + 1) * span] for step in range(1, count + 1)], axis=0
    )
    lag_sums = lag_sums * lag_scale
    tile_ref[:count, half:] = lag_sums[:, half:]
    tile_ref[count:, half:] = pltpu.roll(lag_sums, half, 1)[:, half:]
    out_ref[:, streams + 1] = jnp.broadcast_to(tile_ref[...].astype(jnp.bfloat16)[None], shape)


def unpack_kernel(in_ref, out_ref, grads_ref, taps_ref, skip_ref, lags_ref):
    count, _, members, span = in_ref.shape
    streams, tap_count, chan_width = taps_ref.shape
    reach = 3
    for stream in range(streams + 1):
        block = in_order(in_ref[:, stream], order_back(count)).reshape(count * members, span)
        block = block.astype(jnp.float32)
        flipped = block.T.astype(jnp.bfloat16)
        if stream == 0:
            out_ref[...] = flipped
        else:
            grads_ref[stream - 1] = flipped
    tile = in_order(in_ref[:, streams + 1], order_back(count)).astype(jnp.float32)
    lane = lax.broadcasted_iota(jnp.int32, (1, members // 2, span), 2)
    lags = jnp.where(
        lane < span // 2, pltpu.roll(tile[:, members // 2 :], span // 2, 2), tile[:, : members // 2]
    )
    for step in range(members // 2):
        lags_ref[:, step * span : (step + 1) * span] = lags[:, step]
    lane = lax.broadcasted_iota(jnp.int32, (members, span), 1)
    spread = []
    for place in range(-(-tap_count // reach) + 1):
        total = None
        for group in range(count):
            moved = pltpu.roll(tile[group], (members * (group - place)) % span, 1)
            inside = (lane >= members * group) & (lane < members * (group + 1))
            total = moved if total is None else jnp.where(inside, moved, total)
        spread.append(total)
    first = 0
    for stream in range(streams):
        for place in range(-(-tap_count // reach)):
            taken = min(reach, tap_count - reach * place)
            taps_ref[stream, reach * place : reach * place + taken] = spread[place][
                first : first + taken
            ]
        first += reach + (stream == 0)
    skip_ref[...] = spread[-1][reach : reach + 1]


def by_group(query_in, key_in, value_in, short_taps, long_filters, skip_gain, cotangent):
    tok_rows, chan_width = query_in.shape
    groups, seq_total = long_filters.shape
    streams, tap_count, _ = short_taps.shape
    members = chan_width // groups
    count = groups
    vmem = pl.BlockSpec(memory_space=pltpu.VMEM)
    params = pltpu.CompilerParams(vmem_limit_bytes=32 * 1024 * 1024)
    packed, gain = pl.pallas_call(
        pack_kernel,
        out_shape=(
            jax.ShapeDtypeStruct((count, streams + 1, members, tok_rows), jnp.bfloat16),
            jax.ShapeDtypeStruct((1, chan_width), jnp.float32),
        ),
        in_specs=[pl.BlockSpec(memory_space=pltpu.HBM)] * 5,
        out_specs=(vmem,) * 2,
        scratch_shapes=[
            pltpu.VMEM((streams + 1, tok_rows, chan_width), jnp.bfloat16),
            pltpu.SemaphoreType.DMA((streams + 2,)),
        ],
        compiler_params=params,
        name="pack",
    )(
        *(
            pltpu.with_memory_space_constraint(value, pltpu.HBM)
            for value in (
                query_in, key_in, value_in, cotangent, skip_gain.reshape(1, chan_width)
            )
        )
    )
    packed = lax.all_to_all(
        packed, "seq", 0, 0, tiled=True, axis_index_groups=[order_there(count)]
    )
    results = pl.pallas_call(
        group_kernel,
        out_shape=jax.ShapeDtypeStruct((count, streams + 2, members, tok_rows), jnp.bfloat16),
        in_specs=[vmem] * 4,
        out_specs=vmem,
        scratch_shapes=[
            pltpu.VMEM((chan_width, streams * tap_count + 3), jnp.float32),
            pltpu.VMEM((tok_rows // 2, seq_total + tok_rows), jnp.float32),
            pltpu.VMEM((members, tok_rows), jnp.float32),
        ],
        compiler_params=params,
        name="group",
    )(packed, short_taps, long_filters, gain)
    results = lax.all_to_all(
        results, "seq", 0, 0, tiled=True, axis_index_groups=[order_back(count)]
    )
    block_out, input_grads, tap_grads, skip_grad, filter_grad = pl.pallas_call(
        unpack_kernel,
        out_shape=(
            jax.ShapeDtypeStruct((tok_rows, chan_width), jnp.bfloat16),
            jax.ShapeDtypeStruct((streams, tok_rows, chan_width), jnp.bfloat16),
            jax.ShapeDtypeStruct((streams, tap_count, chan_width), jnp.float32),
            jax.ShapeDtypeStruct((1, chan_width), jnp.float32),
            jax.ShapeDtypeStruct((groups, seq_total), jnp.float32),
        ),
        in_specs=[vmem],
        out_specs=(vmem,) * 5,
        compiler_params=params,
        name="unpack",
    )(results)
    return block_out, input_grads, tap_grads, skip_grad.reshape(chan_width), filter_grad


def plan(query_in, key_in, value_in, short_taps, long_filters, skip_gain, cotangent):
    tok_rows, chan_width = query_in.shape
    groups, seq_total = long_filters.shape
    fits = (
        lax.axis_size("seq") == groups
        and tok_rows == 128
        and chan_width == 128
        and chan_width // groups == 16
        and seq_total == groups * tok_rows
        and short_taps.shape[:2] == (3, 7)
    )
    chosen = by_group if fits else local
    return chosen(query_in, key_in, value_in, short_taps, long_filters, skip_gain, cotangent)


def solution(mesh):
    in_specs = (
        P("seq", "chan"),
        P("seq", "chan"),
        P("seq", "chan"),
        P(None, None, "chan"),
        P("chan", None),
        P("chan"),
        P("seq", "chan"),
    )
    out_specs = (
        P("seq", "chan"),
        P(None, "seq", "chan"),
        P(None, None, "chan"),
        P("chan"),
        P("chan", None),
    )
    return jax.shard_map(plan, mesh=mesh, in_specs=in_specs, out_specs=out_specs, check_vma=False)
```

```python
import functools
import math

import jax
import jax.numpy as jnp
from jax import lax
from jax.experimental import pallas as pl
from jax.experimental.pallas import tpu as pltpu
from jax.sharding import PartitionSpec as P


def from_behind(value, axis, steps):
    count = lax.axis_size(axis)
    initial, last = (max(0, -steps), min(count, count - steps))
    return lax.ppermute(value, axis, [(source, source + steps) for source in range(initial, last)])


def short_forward(extended, weights, rows_here):
    margin = weights.shape[0] - 1
    running = jnp.zeros((rows_here, extended.shape[1]), jnp.float32)
    for offset in range(weights.shape[0]):
        running = (
            running + weights[offset] * extended[margin - offset : margin - offset + rows_here]
        )
    return running


def short_backward(extended, weights, rows_here):
    running = jnp.zeros((rows_here, extended.shape[1]), jnp.float32)
    for offset in range(weights.shape[0]):
        running = running + weights[offset] * extended[offset : offset + rows_here]
    return running


def tap_sums(grad_rows, extended, tap_count, rows_here):
    margin = tap_count - 1
    sums_list = []
    for offset in range(tap_count):
        sums_list.append(
            jnp.sum(grad_rows * extended[margin - offset : margin - offset + rows_here], axis=0)
        )
    return jnp.stack(sums_list)


def hankel(padded, lag_start, height, breadth, seq_total):
    span = height + breadth - 1
    window = lax.dynamic_slice_in_dim(padded, lag_start + seq_total, span, axis=1)
    tiled = jnp.tile(window, (1, height))
    tiled = jnp.pad(tiled, ((0, 0), (0, height)))
    return tiled.reshape(padded.shape[0], height, span + 1)[:, :, :breadth]


def causal_part(padded, source_rows, source_start, target_start, target_count, seq_total):
    breadth = source_rows.shape[0]
    matrix = hankel(
        padded, target_start - source_start - breadth + 1, target_count, breadth, seq_total
    )
    return jnp.einsum("gts,sgc->tgc", matrix, source_rows[::-1], preferred_element_type=jnp.float32)


def anti_part(padded, target_rows, target_start, source_start, source_count, seq_total):
    breadth = target_rows.shape[0]
    matrix = hankel(
        padded, target_start - source_start - source_count + 1, source_count, breadth, seq_total
    )
    return jnp.einsum("gab,bgc->agc", matrix, target_rows, preferred_element_type=jnp.float32)[::-1]


def lag_part(buffer, target_rows, source_rows, target_start, source_start, seq_total):
    height = target_rows.shape[0]
    breadth = source_rows.shape[0]
    groups = target_rows.shape[1]
    padded_source = jnp.pad(source_rows[::-1], ((0, height), (0, 0), (0, 0)))
    products = jnp.einsum(
        "tgc,sgc->gts", target_rows, padded_source, preferred_element_type=jnp.float32
    )
    full_width = height + breadth
    skewed = products.reshape(groups, height * full_width)[:, : height * (full_width - 1)]
    skewed = skewed.reshape(groups, height, full_width - 1)
    diagonal = jnp.sum(skewed, axis=1)
    position = target_start - source_start - breadth + 1 + seq_total
    current = lax.dynamic_slice_in_dim(buffer, position, full_width - 1, axis=1)
    return lax.dynamic_update_slice_in_dim(buffer, current + diagonal, position, axis=1)


def local(query_in, key_in, value_in, short_taps, long_filters, skip_gain, cotangent):
    tok_rows, chan_width = query_in.shape
    groups, seq_total = long_filters.shape
    members = chan_width // groups
    tap_count = short_taps.shape[1]
    margin = tap_count - 1
    device = lax.axis_index("seq")
    own_start = device * tok_rows
    rim_rows = jnp.stack(
        [query_in[tok_rows - margin :], key_in[tok_rows - margin :], value_in[tok_rows - margin :]]
    )
    before = from_behind(rim_rows, "seq", 1)
    streams = [query_in, key_in, value_in]
    extended = [
        jnp.concatenate([before[stream], streams[stream]]).astype(jnp.float32)
        for stream in range(3)
    ]
    query_short = short_forward(extended[0], short_taps[0], tok_rows)
    key_short = short_forward(extended[1], short_taps[1], tok_rows)
    value_short = short_forward(extended[2], short_taps[2], tok_rows)
    gating = (key_short * value_short).astype(jnp.bfloat16)
    relayed = (cotangent.astype(jnp.float32) * query_short).astype(jnp.bfloat16)
    gating_wide = gating.astype(jnp.float32)
    relayed_wide = relayed.astype(jnp.float32)
    gating_groups = gating.reshape(tok_rows, groups, members)
    relayed_groups = relayed.reshape(tok_rows, groups, members)
    padded = jnp.concatenate([jnp.zeros((groups, seq_total), jnp.bfloat16), long_filters], axis=1)
    lag_buffer = jnp.zeros((groups, 2 * seq_total), jnp.float32)
    zeros_out = jnp.zeros((tok_rows, groups, members), jnp.float32)

    def target_pair(distance):
        return distance < 0

    totals = (zeros_out, lag_buffer)
    shard_rows = lax.all_gather(gating, "seq", axis=0, tiled=True)
    piece_rows = shard_rows.shape[0]
    step_rows = min(piece_rows, tok_rows)
    pieces = shard_rows.reshape(piece_rows // step_rows, step_rows, groups, members)

    def forward_visit_block(carried, element):
        position, rows_block = element
        source_start = position * step_rows

        def forward_active(partial_value):
            output_part, buffer = partial_value
            output_part = output_part + causal_part(
                padded, rows_block, source_start, own_start, tok_rows, seq_total
            )
            distance = device - source_start // tok_rows
            buffer = lax.cond(
                target_pair(distance),
                lambda held: lag_part(
                    held, relayed_groups, rows_block, own_start, source_start, seq_total
                ),
                lambda held: held,
                buffer,
            )
            return (output_part, buffer)

        carried = lax.cond(
            source_start < own_start + tok_rows,
            forward_active,
            lambda partial_value: partial_value,
            carried,
        )
        return (carried, None)

    totals, ignored = lax.scan(
        forward_visit_block, totals, (jnp.arange(piece_rows // step_rows, dtype=jnp.int32), pieces)
    )
    output_part, lag_buffer = totals
    output_sum = output_part.reshape(tok_rows, chan_width)
    totals = (zeros_out, lag_buffer)
    shard_rows = lax.all_gather(relayed, "seq", axis=0, tiled=True)
    piece_rows = shard_rows.shape[0]
    backward_step_rows = min(piece_rows, tok_rows)
    pieces = shard_rows.reshape(
        piece_rows // backward_step_rows, backward_step_rows, groups, members
    )

    def backward_visit_block(carried, element):
        position, rows_block = element
        target_start = position * backward_step_rows

        def backward_active(partial_value):
            grad_part, buffer = partial_value
            grad_part = grad_part + anti_part(
                padded, rows_block, target_start, own_start, tok_rows, seq_total
            )
            distance = target_start // tok_rows - device
            buffer = lax.cond(
                target_pair(distance),
                lambda held: held,
                lambda held: lag_part(
                    held, rows_block, gating_groups, target_start, own_start, seq_total
                ),
                buffer,
            )
            return (grad_part, buffer)

        carried = lax.cond(
            target_start + backward_step_rows > own_start,
            backward_active,
            lambda partial_value: partial_value,
            carried,
        )
        return (carried, None)

    totals, ignored = lax.scan(
        backward_visit_block,
        totals,
        (jnp.arange(piece_rows // backward_step_rows, dtype=jnp.int32), pieces),
    )
    grad_part, lag_buffer = totals
    grad_sum = grad_part.reshape(tok_rows, chan_width)
    lag_local = lag_buffer[:, seq_total:]
    long_out = output_sum + skip_gain * gating_wide
    block_out = (query_short * long_out).astype(jnp.bfloat16)
    grad_gating = grad_sum + skip_gain * relayed_wide
    cot_wide = cotangent.astype(jnp.float32)
    grad_shorts = [cot_wide * long_out, grad_gating * value_short, grad_gating * key_short]
    lead_rows = jnp.stack([grad_shorts[stream][:margin] for stream in range(3)])
    after = from_behind(lead_rows, "seq", -1)
    input_grads = jnp.stack(
        [
            short_backward(
                jnp.concatenate([grad_shorts[stream], after[stream]]), short_taps[stream], tok_rows
            )
            for stream in range(3)
        ]
    ).astype(jnp.bfloat16)
    tap_local = jnp.stack(
        [
            tap_sums(grad_shorts[stream], extended[stream], tap_count, tok_rows)
            for stream in range(3)
        ]
    )
    skip_local = jnp.sum(relayed_wide * gating_wide, axis=0)
    lag_total, tap_total, skip_total = lax.psum((lag_local, tap_local, skip_local), "seq")
    tap_scale = 1.0 / math.sqrt(seq_total)
    lag_scale = 1.0 / math.sqrt(seq_total * members)
    return (
        block_out,
        input_grads,
        tap_total * tap_scale,
        skip_total * tap_scale,
        lag_total * lag_scale,
    )


def order_there(count):
    return [(count // 2 + 1 - step) % count for step in range(count)]


def order_back(count):
    return [(count // 2 - 1 + step) % count for step in range(count)]


def in_order(value, order):
    return jnp.stack([value[order.index(device)] for device in range(len(order))])


def by_member(value, order):
    return jnp.stack([value[device] for device in order])


def pack_kernel(
    query_ref, key_ref, value_ref, cot_ref, skip_ref, out_ref, gain_ref, stream_buf, sems
):
    count, streams, members, tok_rows = out_ref.shape
    moves = [
        pltpu.make_async_copy(ref, stream_buf.at[stream], sems.at[stream])
        for stream, ref in enumerate((query_ref, key_ref, value_ref, cot_ref))
    ]
    moves.append(pltpu.make_async_copy(skip_ref, gain_ref, sems.at[streams]))
    for move in moves:
        move.start()
    for stream in range(streams):
        moves[stream].wait()
        flipped = stream_buf[stream].astype(jnp.float32).T.astype(jnp.bfloat16)
        flipped = flipped.reshape(count, members, tok_rows)
        out_ref[:, stream] = by_member(flipped, order_there(count))
    moves[streams].wait()


def group_kernel(
    in_ref, taps_ref, filters_ref, gain_ref, out_ref, table_ref, wide_ref, tile_ref
):
    count, _, members, span = in_ref.shape
    groups, seq_total = filters_ref.shape
    streams, tap_count, chan_width = taps_ref.shape
    rows = count * members
    mine = lax.axis_index("seq")
    shape = (count, members, span)
    lane = lax.broadcasted_iota(jnp.int32, shape, 2)
    reach = 3

    def later(value, steps):
        if steps == 0:
            return value
        turned = pltpu.roll(value, steps, 2)
        before = jnp.concatenate([jnp.zeros_like(turned[:1]), turned[:-1]], axis=0)
        return jnp.where(lane >= steps, turned, before)

    def earlier(value, steps):
        if steps == 0:
            return value
        turned = pltpu.roll(value, span - steps, 2)
        after = jnp.concatenate([turned[1:], jnp.zeros_like(turned[:1])], axis=0)
        return jnp.where(lane < span - steps, turned, after)

    table = jnp.concatenate(
        [taps_ref[stream] for stream in range(streams)]
        + [gain_ref[...], jnp.zeros((2, chan_width), jnp.float32)],
        axis=0,
    )
    table_ref[...] = table.T
    params = table_ref[pl.ds(pl.multiple_of(mine * members, members), members), :]

    def column(index):
        return jnp.broadcast_to(params[:, index : index + 1], (members, span))[None]

    chosen = lax.broadcasted_iota(jnp.int32, (groups, 1), 0) == mine
    filter_row = jnp.sum(
        jnp.where(chosen, filters_ref[...].astype(jnp.float32), 0.0), axis=0, keepdims=True
    )
    filter_row = jnp.concatenate([filter_row, jnp.zeros((1, span), jnp.float32)], axis=1)
    spread = jnp.broadcast_to(filter_row, (members, seq_total + span))
    first_rows = pltpu.roll(spread, 0, 1, stride=1, stride_axis=0).astype(jnp.bfloat16)
    row_parts = [first_rows] + [
        pltpu.roll(first_rows, first, 1) for first in range(members, span, members)
    ]
    toeplitz = jnp.concatenate(row_parts, axis=0)[:, :seq_total]

    def delays(stream):
        value = in_order(in_ref[:, stream], order_there(count))
        return [later(value, first) for first in range(0, tap_count, reach)]

    def short(stream, values):
        total = None
        for second in range(reach):
            running = None
            for first in range(second, tap_count, reach):
                value = values[first // reach].astype(jnp.float32)
                term = column(stream * tap_count + first) * value
                running = term if running is None else running + term
            running = later(running, second)
            total = running if total is None else total + running
        return total

    def ahead_by_blocks(value):
        parts = [value]
        for step in range(1, count):
            gap = jnp.zeros((step * members, span), jnp.bfloat16)
            parts.append(jnp.concatenate([value[step * members :], gap], axis=0))
        return jnp.concatenate(parts, axis=1)

    gain = column(streams * tap_count)
    cot = in_order(in_ref[:, streams], order_there(count)).astype(jnp.float32)
    delayed = [delays(0)]
    query_short = short(0, delayed[0])
    relayed = (cot * query_short).astype(jnp.bfloat16).reshape(rows, span)
    relayed_lags = ahead_by_blocks(relayed)
    backward = lax.dot_general(
        relayed_lags, toeplitz, (((1,), (1,)), ((), ())), preferred_element_type=jnp.float32
    )

    delayed += [delays(1), delays(2)]
    key_short = short(1, delayed[1])
    value_short = short(2, delayed[2])
    gating = (key_short * value_short).astype(jnp.bfloat16).reshape(rows, span)
    gating_parts, filter_parts = [gating], [toeplitz[:, :span]]
    for step in range(1, count):
        gap = jnp.zeros((step * members, span), jnp.bfloat16)
        gating_parts.append(jnp.concatenate([gap, gating[: rows - step * members]], axis=0))
        filter_parts.append(toeplitz[:, step * span : (step + 1) * span])
    forward = jnp.dot(
        jnp.concatenate(gating_parts, axis=1),
        jnp.concatenate(filter_parts, axis=0),
        preferred_element_type=jnp.float32,
    )

    half = span // 2
    flip = (
        lax.broadcasted_iota(jnp.int32, (span, span), 0)
        + lax.broadcasted_iota(jnp.int32, (span, span), 1)
        == span - 1
    ).astype(jnp.bfloat16)
    gating_turned = lax.dot_general(
        flip, gating, (((1,), (1,)), ((), ())), preferred_element_type=jnp.float32
    ).astype(jnp.bfloat16)
    gating_turned = jnp.concatenate([gating_turned[half:], gating_turned[:half]], axis=1)
    ahead = earlier(relayed.reshape(shape), half).reshape(rows, span)
    targets = jnp.concatenate([relayed_lags, ahead_by_blocks(ahead)], axis=0)
    wide_ref[:, :seq_total] = jnp.dot(
        gating_turned, targets, preferred_element_type=jnp.float32
    )
    wide_ref[:, seq_total:] = jnp.zeros((half, span), jnp.float32)

    tap_scale = 1.0 / math.sqrt(seq_total)

    def tokens(value):
        return jnp.concatenate([value[block] for block in range(count)], axis=1)

    def sums(left, right):
        product = lax.dot_general(
            jnp.concatenate(left, axis=0),
            jnp.concatenate(right, axis=0),
            (((1,), (1,)), ((), ())),
            preferred_element_type=jnp.float32,
        )
        same = (
            lax.broadcasted_iota(jnp.int32, product.shape, 0) % members
            == lax.broadcasted_iota(jnp.int32, product.shape, 1) % members
        )
        product = jnp.where(same, product, 0.0).reshape(len(left), members, -1)
        return jnp.sum(product, axis=1) * tap_scale

    tile_ref[...] = jnp.zeros((members, span), jnp.float32)

    def finish(stream, grad_short, first_row, more_left=(), more_right=()):
        moved = [earlier(grad_short, second) for second in range(reach)]
        left = [tokens(value.astype(jnp.bfloat16)) for value in moved] + list(more_left)
        right = [tokens(value) for value in delayed[stream]] + list(more_right)
        totals = sums(left, right)
        tile_ref[first_row : first_row + len(left), : totals.shape[1]] = totals
        total = None
        for place in range(len(delayed[stream])):
            running = None
            for second in range(min(reach, tap_count - reach * place)):
                term = column(stream * tap_count + reach * place + second) * moved[second]
                running = term if running is None else running + term
            running = earlier(running, reach * place)
            total = running if total is None else total + running
        out_ref[:, 1 + stream] = by_member(total.astype(jnp.bfloat16), order_back(count))

    grad_gating = backward.reshape(shape) + gain * relayed.astype(jnp.float32).reshape(shape)
    finish(1, grad_gating * value_short, reach + 1)
    finish(2, grad_gating * key_short, 2 * reach + 1)

    long_out = forward.reshape(shape) + gain * gating.astype(jnp.float32).reshape(shape)
    block_out = (query_short * long_out).astype(jnp.bfloat16)
    out_ref[:, 0] = by_member(block_out, order_back(count))
    finish(
        0, cot * long_out, 0, [tokens(relayed.reshape(shape))], [tokens(gating.reshape(shape))]
    )

    skewed = pltpu.roll(wide_ref[...], span - half + 1, 1, stride=1, stride_axis=0)
    diagonal = jnp.sum(skewed, axis=0, keepdims=True)
    lag_scale = 1.0 / math.sqrt(seq_total * members)
    lag_sums = jnp.concatenate(
        [diagonal[:, step * span : (step + 1) * span] for step in range(1, count + 1)], axis=0
    )
    lag_sums = lag_sums * lag_scale
    tile_ref[:count, half:] = lag_sums[:, half:]
    tile_ref[count:, half:] = pltpu.roll(lag_sums, half, 1)[:, half:]
    out_ref[:, streams + 1] = jnp.broadcast_to(tile_ref[...].astype(jnp.bfloat16)[None], shape)


def unpack_kernel(in_ref, out_ref, grads_ref, taps_ref, skip_ref, lags_ref):
    count, _, members, span = in_ref.shape
    streams, tap_count, chan_width = taps_ref.shape
    reach = 3
    for stream in range(streams + 1):
        block = in_order(in_ref[:, stream], order_back(count)).reshape(count * members, span)
        block = block.astype(jnp.float32)
        flipped = block.T.astype(jnp.bfloat16)
        if stream == 0:
            out_ref[...] = flipped
        else:
            grads_ref[stream - 1] = flipped
    tile = in_order(in_ref[:, streams + 1], order_back(count)).astype(jnp.float32)
    lane = lax.broadcasted_iota(jnp.int32, (1, members // 2, span), 2)
    lags = jnp.where(
        lane < span // 2, pltpu.roll(tile[:, members // 2 :], span // 2, 2), tile[:, : members // 2]
    )
    for step in range(members // 2):
        lags_ref[:, step * span : (step + 1) * span] = lags[:, step]
    lane = lax.broadcasted_iota(jnp.int32, (members, span), 1)
    spread = []
    for place in range(-(-tap_count // reach) + 1):
        total = None
        for group in range(count):
            moved = pltpu.roll(tile[group], (members * (group - place)) % span, 1)
            inside = (lane >= members * group) & (lane < members * (group + 1))
            total = moved if total is None else jnp.where(inside, moved, total)
        spread.append(total)
    first = 0
    for stream in range(streams):
        for place in range(-(-tap_count // reach)):
            taken = min(reach, tap_count - reach * place)
            taps_ref[stream, reach * place : reach * place + taken] = spread[place][
                first : first + taken
            ]
        first += reach + (stream == 0)
    skip_ref[...] = spread[-1][reach : reach + 1]


def by_group(query_in, key_in, value_in, short_taps, long_filters, skip_gain, cotangent):
    tok_rows, chan_width = query_in.shape
    groups, seq_total = long_filters.shape
    streams, tap_count, _ = short_taps.shape
    members = chan_width // groups
    count = groups
    vmem = pl.BlockSpec(memory_space=pltpu.VMEM)
    params = pltpu.CompilerParams(vmem_limit_bytes=32 * 1024 * 1024)
    packed, gain = pl.pallas_call(
        pack_kernel,
        out_shape=(
            jax.ShapeDtypeStruct((count, streams + 1, members, tok_rows), jnp.bfloat16),
            jax.ShapeDtypeStruct((1, chan_width), jnp.float32),
        ),
        in_specs=[pl.BlockSpec(memory_space=pltpu.HBM)] * 5,
        out_specs=(vmem,) * 2,
        scratch_shapes=[
            pltpu.VMEM((streams + 1, tok_rows, chan_width), jnp.bfloat16),
            pltpu.SemaphoreType.DMA((streams + 2,)),
        ],
        compiler_params=params,
        name="pack",
    )(
        *(
            pltpu.with_memory_space_constraint(value, pltpu.HBM)
            for value in (
                query_in, key_in, value_in, cotangent, skip_gain.reshape(1, chan_width)
            )
        )
    )
    packed = lax.all_to_all(
        packed, "seq", 0, 0, tiled=True, axis_index_groups=[order_there(count)]
    )
    results = pl.pallas_call(
        group_kernel,
        out_shape=jax.ShapeDtypeStruct((count, streams + 2, members, tok_rows), jnp.bfloat16),
        in_specs=[vmem] * 4,
        out_specs=vmem,
        scratch_shapes=[
            pltpu.VMEM((chan_width, streams * tap_count + 3), jnp.float32),
            pltpu.VMEM((tok_rows // 2, seq_total + tok_rows), jnp.float32),
            pltpu.VMEM((members, tok_rows), jnp.float32),
        ],
        compiler_params=params,
        name="group",
    )(packed, short_taps, long_filters, gain)
    results = lax.all_to_all(
        results, "seq", 0, 0, tiled=True, axis_index_groups=[order_back(count)]
    )
    block_out, input_grads, tap_grads, skip_grad, filter_grad = pl.pallas_call(
        unpack_kernel,
        out_shape=(
            jax.ShapeDtypeStruct((tok_rows, chan_width), jnp.bfloat16),
            jax.ShapeDtypeStruct((streams, tok_rows, chan_width), jnp.bfloat16),
            jax.ShapeDtypeStruct((streams, tap_count, chan_width), jnp.float32),
            jax.ShapeDtypeStruct((1, chan_width), jnp.float32),
            jax.ShapeDtypeStruct((groups, seq_total), jnp.float32),
        ),
        in_specs=[vmem],
        out_specs=(vmem,) * 5,
        compiler_params=params,
        name="unpack",
    )(results)
    return block_out, input_grads, tap_grads, skip_grad.reshape(chan_width), filter_grad


def plan(query_in, key_in, value_in, short_taps, long_filters, skip_gain, cotangent):
    tok_rows, chan_width = query_in.shape
    groups, seq_total = long_filters.shape
    fits = (
        lax.axis_size("seq") == groups
        and tok_rows == 128
        and chan_width == 128
        and chan_width // groups == 16
        and seq_total == groups * tok_rows
        and short_taps.shape[:2] == (3, 7)
    )
    chosen = by_group if fits else local
    return chosen(query_in, key_in, value_in, short_taps, long_filters, skip_gain, cotangent)


def solution(mesh):
    in_specs = (
        P("seq", "chan"),
        P("seq", "chan"),
        P("seq", "chan"),
        P(None, None, "chan"),
        P("chan", None),
        P("chan"),
        P("seq", "chan"),
    )
    out_specs = (
        P("seq", "chan"),
        P(None, "seq", "chan"),
        P(None, None, "chan"),
        P("chan"),
        P("chan", None),
    )
    return jax.shard_map(plan, mesh=mesh, in_specs=in_specs, out_specs=out_specs, check_vma=False)
```

```python
import functools
import math

import jax
import jax.numpy as jnp
from jax import lax
from jax.experimental import pallas as pl
from jax.experimental.pallas import tpu as pltpu
from jax.sharding import PartitionSpec as P


def from_behind(value, axis, steps):
    count = lax.axis_size(axis)
    initial, last = (max(0, -steps), min(count, count - steps))
    return lax.ppermute(value, axis, [(source, source + steps) for source in range(initial, last)])


def short_forward(extended, weights, rows_here):
    margin = weights.shape[0] - 1
    running = jnp.zeros((rows_here, extended.shape[1]), jnp.float32)
    for offset in range(weights.shape[0]):
        running = (
            running + weights[offset] * extended[margin - offset : margin - offset + rows_here]
        )
    return running


def short_backward(extended, weights, rows_here):
    running = jnp.zeros((rows_here, extended.shape[1]), jnp.float32)
    for offset in range(weights.shape[0]):
        running = running + weights[offset] * extended[offset : offset + rows_here]
    return running


def tap_sums(grad_rows, extended, tap_count, rows_here):
    margin = tap_count - 1
    sums_list = []
    for offset in range(tap_count):
        sums_list.append(
            jnp.sum(grad_rows * extended[margin - offset : margin - offset + rows_here], axis=0)
        )
    return jnp.stack(sums_list)


def hankel(padded, lag_start, height, breadth, seq_total):
    span = height + breadth - 1
    window = lax.dynamic_slice_in_dim(padded, lag_start + seq_total, span, axis=1)
    tiled = jnp.tile(window, (1, height))
    tiled = jnp.pad(tiled, ((0, 0), (0, height)))
    return tiled.reshape(padded.shape[0], height, span + 1)[:, :, :breadth]


def causal_part(padded, source_rows, source_start, target_start, target_count, seq_total):
    breadth = source_rows.shape[0]
    matrix = hankel(
        padded, target_start - source_start - breadth + 1, target_count, breadth, seq_total
    )
    return jnp.einsum("gts,sgc->tgc", matrix, source_rows[::-1], preferred_element_type=jnp.float32)


def anti_part(padded, target_rows, target_start, source_start, source_count, seq_total):
    breadth = target_rows.shape[0]
    matrix = hankel(
        padded, target_start - source_start - source_count + 1, source_count, breadth, seq_total
    )
    return jnp.einsum("gab,bgc->agc", matrix, target_rows, preferred_element_type=jnp.float32)[::-1]


def lag_part(buffer, target_rows, source_rows, target_start, source_start, seq_total):
    height = target_rows.shape[0]
    breadth = source_rows.shape[0]
    groups = target_rows.shape[1]
    padded_source = jnp.pad(source_rows[::-1], ((0, height), (0, 0), (0, 0)))
    products = jnp.einsum(
        "tgc,sgc->gts", target_rows, padded_source, preferred_element_type=jnp.float32
    )
    full_width = height + breadth
    skewed = products.reshape(groups, height * full_width)[:, : height * (full_width - 1)]
    skewed = skewed.reshape(groups, height, full_width - 1)
    diagonal = jnp.sum(skewed, axis=1)
    position = target_start - source_start - breadth + 1 + seq_total
    current = lax.dynamic_slice_in_dim(buffer, position, full_width - 1, axis=1)
    return lax.dynamic_update_slice_in_dim(buffer, current + diagonal, position, axis=1)


def local(query_in, key_in, value_in, short_taps, long_filters, skip_gain, cotangent):
    tok_rows, chan_width = query_in.shape
    groups, seq_total = long_filters.shape
    members = chan_width // groups
    tap_count = short_taps.shape[1]
    margin = tap_count - 1
    device = lax.axis_index("seq")
    own_start = device * tok_rows
    rim_rows = jnp.stack(
        [query_in[tok_rows - margin :], key_in[tok_rows - margin :], value_in[tok_rows - margin :]]
    )
    before = from_behind(rim_rows, "seq", 1)
    streams = [query_in, key_in, value_in]
    extended = [
        jnp.concatenate([before[stream], streams[stream]]).astype(jnp.float32)
        for stream in range(3)
    ]
    query_short = short_forward(extended[0], short_taps[0], tok_rows)
    key_short = short_forward(extended[1], short_taps[1], tok_rows)
    value_short = short_forward(extended[2], short_taps[2], tok_rows)
    gating = (key_short * value_short).astype(jnp.bfloat16)
    relayed = (cotangent.astype(jnp.float32) * query_short).astype(jnp.bfloat16)
    gating_wide = gating.astype(jnp.float32)
    relayed_wide = relayed.astype(jnp.float32)
    gating_groups = gating.reshape(tok_rows, groups, members)
    relayed_groups = relayed.reshape(tok_rows, groups, members)
    padded = jnp.concatenate([jnp.zeros((groups, seq_total), jnp.bfloat16), long_filters], axis=1)
    lag_buffer = jnp.zeros((groups, 2 * seq_total), jnp.float32)
    zeros_out = jnp.zeros((tok_rows, groups, members), jnp.float32)

    def target_pair(distance):
        return distance < 0

    totals = (zeros_out, lag_buffer)
    shard_rows = lax.all_gather(gating, "seq", axis=0, tiled=True)
    piece_rows = shard_rows.shape[0]
    step_rows = min(piece_rows, tok_rows)
    pieces = shard_rows.reshape(piece_rows // step_rows, step_rows, groups, members)

    def forward_visit_block(carried, element):
        position, rows_block = element
        source_start = position * step_rows

        def forward_active(partial_value):
            output_part, buffer = partial_value
            output_part = output_part + causal_part(
                padded, rows_block, source_start, own_start, tok_rows, seq_total
            )
            distance = device - source_start // tok_rows
            buffer = lax.cond(
                target_pair(distance),
                lambda held: lag_part(
                    held, relayed_groups, rows_block, own_start, source_start, seq_total
                ),
                lambda held: held,
                buffer,
            )
            return (output_part, buffer)

        carried = lax.cond(
            source_start < own_start + tok_rows,
            forward_active,
            lambda partial_value: partial_value,
            carried,
        )
        return (carried, None)

    totals, ignored = lax.scan(
        forward_visit_block, totals, (jnp.arange(piece_rows // step_rows, dtype=jnp.int32), pieces)
    )
    output_part, lag_buffer = totals
    output_sum = output_part.reshape(tok_rows, chan_width)
    totals = (zeros_out, lag_buffer)
    shard_rows = lax.all_gather(relayed, "seq", axis=0, tiled=True)
    piece_rows = shard_rows.shape[0]
    backward_step_rows = min(piece_rows, tok_rows)
    pieces = shard_rows.reshape(
        piece_rows // backward_step_rows, backward_step_rows, groups, members
    )

    def backward_visit_block(carried, element):
        position, rows_block = element
        target_start = position * backward_step_rows

        def backward_active(partial_value):
            grad_part, buffer = partial_value
            grad_part = grad_part + anti_part(
                padded, rows_block, target_start, own_start, tok_rows, seq_total
            )
            distance = target_start // tok_rows - device
            buffer = lax.cond(
                target_pair(distance),
                lambda held: held,
                lambda held: lag_part(
                    held, rows_block, gating_groups, target_start, own_start, seq_total
                ),
                buffer,
            )
            return (grad_part, buffer)

        carried = lax.cond(
            target_start + backward_step_rows > own_start,
            backward_active,
            lambda partial_value: partial_value,
            carried,
        )
        return (carried, None)

    totals, ignored = lax.scan(
        backward_visit_block,
        totals,
        (jnp.arange(piece_rows // backward_step_rows, dtype=jnp.int32), pieces),
    )
    grad_part, lag_buffer = totals
    grad_sum = grad_part.reshape(tok_rows, chan_width)
    lag_local = lag_buffer[:, seq_total:]
    long_out = output_sum + skip_gain * gating_wide
    block_out = (query_short * long_out).astype(jnp.bfloat16)
    grad_gating = grad_sum + skip_gain * relayed_wide
    cot_wide = cotangent.astype(jnp.float32)
    grad_shorts = [cot_wide * long_out, grad_gating * value_short, grad_gating * key_short]
    lead_rows = jnp.stack([grad_shorts[stream][:margin] for stream in range(3)])
    after = from_behind(lead_rows, "seq", -1)
    input_grads = jnp.stack(
        [
            short_backward(
                jnp.concatenate([grad_shorts[stream], after[stream]]), short_taps[stream], tok_rows
            )
            for stream in range(3)
        ]
    ).astype(jnp.bfloat16)
    tap_local = jnp.stack(
        [
            tap_sums(grad_shorts[stream], extended[stream], tap_count, tok_rows)
            for stream in range(3)
        ]
    )
    skip_local = jnp.sum(relayed_wide * gating_wide, axis=0)
    lag_total, tap_total, skip_total = lax.psum((lag_local, tap_local, skip_local), "seq")
    tap_scale = 1.0 / math.sqrt(seq_total)
    lag_scale = 1.0 / math.sqrt(seq_total * members)
    return (
        block_out,
        input_grads,
        tap_total * tap_scale,
        skip_total * tap_scale,
        lag_total * lag_scale,
    )


def order_there(count):
    return [(count // 2 + 1 - step) % count for step in range(count)]


def order_back(count):
    return [(count // 2 + 1 - step) % count for step in range(count)]


def in_order(value, order):
    return jnp.stack([value[order.index(device)] for device in range(len(order))])


def by_member(value, order):
    return jnp.stack([value[device] for device in order])


def pack_kernel(
    query_ref, key_ref, value_ref, cot_ref, skip_ref, out_ref, gain_ref, stream_buf, sems
):
    count, streams, members, tok_rows = out_ref.shape
    moves = [
        pltpu.make_async_copy(ref, stream_buf.at[stream], sems.at[stream])
        for stream, ref in enumerate((query_ref, key_ref, value_ref, cot_ref))
    ]
    moves.append(pltpu.make_async_copy(skip_ref, gain_ref, sems.at[streams]))
    for move in moves:
        move.start()
    for stream in range(streams):
        moves[stream].wait()
        flipped = stream_buf[stream].astype(jnp.float32).T.astype(jnp.bfloat16)
        flipped = flipped.reshape(count, members, tok_rows)
        out_ref[:, stream] = by_member(flipped, order_there(count))
    moves[streams].wait()


def group_kernel(
    in_ref, taps_ref, filters_ref, gain_ref, out_ref, table_ref, wide_ref, tile_ref
):
    count, _, members, span = in_ref.shape
    groups, seq_total = filters_ref.shape
    streams, tap_count, chan_width = taps_ref.shape
    rows = count * members
    mine = lax.axis_index("seq")
    shape = (count, members, span)
    lane = lax.broadcasted_iota(jnp.int32, shape, 2)
    reach = 3

    def later(value, steps):
        if steps == 0:
            return value
        turned = pltpu.roll(value, steps, 2)
        before = jnp.concatenate([jnp.zeros_like(turned[:1]), turned[:-1]], axis=0)
        return jnp.where(lane >= steps, turned, before)

    def earlier(value, steps):
        if steps == 0:
            return value
        turned = pltpu.roll(value, span - steps, 2)
        after = jnp.concatenate([turned[1:], jnp.zeros_like(turned[:1])], axis=0)
        return jnp.where(lane < span - steps, turned, after)

    table = jnp.concatenate(
        [taps_ref[stream] for stream in range(streams)]
        + [gain_ref[...], jnp.zeros((2, chan_width), jnp.float32)],
        axis=0,
    )
    table_ref[...] = table.T
    params = table_ref[pl.ds(pl.multiple_of(mine * members, members), members), :]

    def column(index):
        return jnp.broadcast_to(params[:, index : index + 1], (members, span))[None]

    chosen = lax.broadcasted_iota(jnp.int32, (groups, 1), 0) == mine
    filter_row = jnp.sum(
        jnp.where(chosen, filters_ref[...].astype(jnp.float32), 0.0), axis=0, keepdims=True
    )
    filter_row = jnp.concatenate([filter_row, jnp.zeros((1, span), jnp.float32)], axis=1)
    spread = jnp.broadcast_to(filter_row, (members, seq_total + span))
    first_rows = pltpu.roll(spread, 0, 1, stride=1, stride_axis=0).astype(jnp.bfloat16)
    row_parts = [first_rows] + [
        pltpu.roll(first_rows, first, 1) for first in range(members, span, members)
    ]
    toeplitz = jnp.concatenate(row_parts, axis=0)[:, :seq_total]

    def delays(stream):
        value = in_order(in_ref[:, stream], order_there(count))
        return [later(value, first) for first in range(0, tap_count, reach)]

    def short(stream, values):
        total = None
        for second in range(reach):
            running = None
            for first in range(second, tap_count, reach):
                value = values[first // reach].astype(jnp.float32)
                term = column(stream * tap_count + first) * value
                running = term if running is None else running + term
            running = later(running, second)
            total = running if total is None else total + running
        return total

    def ahead_by_blocks(value):
        parts = [value]
        for step in range(1, count):
            gap = jnp.zeros((step * members, span), jnp.bfloat16)
            parts.append(jnp.concatenate([value[step * members :], gap], axis=0))
        return jnp.concatenate(parts, axis=1)

    gain = column(streams * tap_count)
    cot = in_order(in_ref[:, streams], order_there(count)).astype(jnp.float32)
    delayed = [delays(0)]
    query_short = short(0, delayed[0])
    relayed = (cot * query_short).astype(jnp.bfloat16).reshape(rows, span)
    relayed_lags = ahead_by_blocks(relayed)
    backward = lax.dot_general(
        relayed_lags, toeplitz, (((1,), (1,)), ((), ())), preferred_element_type=jnp.float32
    )

    delayed += [delays(1), delays(2)]
    key_short = short(1, delayed[1])
    value_short = short(2, delayed[2])
    gating = (key_short * value_short).astype(jnp.bfloat16).reshape(rows, span)
    gating_parts, filter_parts = [gating], [toeplitz[:, :span]]
    for step in range(1, count):
        gap = jnp.zeros((step * members, span), jnp.bfloat16)
        gating_parts.append(jnp.concatenate([gap, gating[: rows - step * members]], axis=0))
        filter_parts.append(toeplitz[:, step * span : (step + 1) * span])
    forward = jnp.dot(
        jnp.concatenate(gating_parts, axis=1),
        jnp.concatenate(filter_parts, axis=0),
        preferred_element_type=jnp.float32,
    )

    half = span // 2
    flip = (
        lax.broadcasted_iota(jnp.int32, (span, span), 0)
        + lax.broadcasted_iota(jnp.int32, (span, span), 1)
        == span - 1
    ).astype(jnp.bfloat16)
    gating_turned = lax.dot_general(
        flip, gating, (((1,), (1,)), ((), ())), preferred_element_type=jnp.float32
    ).astype(jnp.bfloat16)
    gating_turned = jnp.concatenate([gating_turned[half:], gating_turned[:half]], axis=1)
    ahead = earlier(relayed.reshape(shape), half).reshape(rows, span)
    targets = jnp.concatenate([relayed_lags, ahead_by_blocks(ahead)], axis=0)
    wide_ref[:, :seq_total] = jnp.dot(
        gating_turned, targets, preferred_element_type=jnp.float32
    )
    wide_ref[:, seq_total:] = jnp.zeros((half, span), jnp.float32)

    tap_scale = 1.0 / math.sqrt(seq_total)

    def tokens(value):
        return jnp.concatenate([value[block] for block in range(count)], axis=1)

    def sums(left, right):
        product = lax.dot_general(
            jnp.concatenate(left, axis=0),
            jnp.concatenate(right, axis=0),
            (((1,), (1,)), ((), ())),
            preferred_element_type=jnp.float32,
        )
        same = (
            lax.broadcasted_iota(jnp.int32, product.shape, 0) % members
            == lax.broadcasted_iota(jnp.int32, product.shape, 1) % members
        )
        product = jnp.where(same, product, 0.0).reshape(len(left), members, -1)
        return jnp.sum(product, axis=1) * tap_scale

    tile_ref[...] = jnp.zeros((members, span), jnp.float32)

    def finish(stream, grad_short, first_row, more_left=(), more_right=()):
        moved = [earlier(grad_short, second) for second in range(reach)]
        left = [tokens(value.astype(jnp.bfloat16)) for value in moved] + list(more_left)
        right = [tokens(value) for value in delayed[stream]] + list(more_right)
        totals = sums(left, right)
        tile_ref[first_row : first_row + len(left), : totals.shape[1]] = totals
        total = None
        for place in range(len(delayed[stream])):
            running = None
            for second in range(min(reach, tap_count - reach * place)):
                term = column(stream * tap_count + reach * place + second) * moved[second]
                running = term if running is None else running + term
            running = earlier(running, reach * place)
            total = running if total is None else total + running
        out_ref[:, 1 + stream] = by_member(total.astype(jnp.bfloat16), order_back(count))

    grad_gating = backward.reshape(shape) + gain * relayed.astype(jnp.float32).reshape(shape)
    finish(1, grad_gating * value_short, reach + 1)
    finish(2, grad_gating * key_short, 2 * reach + 1)

    long_out = forward.reshape(shape) + gain * gating.astype(jnp.float32).reshape(shape)
    block_out = (query_short * long_out).astype(jnp.bfloat16)
    out_ref[:, 0] = by_member(block_out, order_back(count))
    finish(
        0, cot * long_out, 0, [tokens(relayed.reshape(shape))], [tokens(gating.reshape(shape))]
    )

    skewed = pltpu.roll(wide_ref[...], span - half + 1, 1, stride=1, stride_axis=0)
    diagonal = jnp.sum(skewed, axis=0, keepdims=True)
    lag_scale = 1.0 / math.sqrt(seq_total * members)
    lag_sums = jnp.concatenate(
        [diagonal[:, step * span : (step + 1) * span] for step in range(1, count + 1)], axis=0
    )
    lag_sums = lag_sums * lag_scale
    tile_ref[:count, half:] = lag_sums[:, half:]
    tile_ref[count:, half:] = pltpu.roll(lag_sums, half, 1)[:, half:]
    out_ref[:, streams + 1] = jnp.broadcast_to(tile_ref[...].astype(jnp.bfloat16)[None], shape)


def unpack_kernel(in_ref, out_ref, grads_ref, taps_ref, skip_ref, lags_ref):
    count, _, members, span = in_ref.shape
    streams, tap_count, chan_width = taps_ref.shape
    reach = 3
    for stream in range(streams + 1):
        block = in_order(in_ref[:, stream], order_back(count)).reshape(count * members, span)
        block = block.astype(jnp.float32)
        flipped = block.T.astype(jnp.bfloat16)
        if stream == 0:
            out_ref[...] = flipped
        else:
            grads_ref[stream - 1] = flipped
    tile = in_order(in_ref[:, streams + 1], order_back(count)).astype(jnp.float32)
    lane = lax.broadcasted_iota(jnp.int32, (1, members // 2, span), 2)
    lags = jnp.where(
        lane < span // 2, pltpu.roll(tile[:, members // 2 :], span // 2, 2), tile[:, : members // 2]
    )
    for step in range(members // 2):
        lags_ref[:, step * span : (step + 1) * span] = lags[:, step]
    lane = lax.broadcasted_iota(jnp.int32, (members, span), 1)
    spread = []
    for place in range(-(-tap_count // reach) + 1):
        total = None
        for group in range(count):
            moved = pltpu.roll(tile[group], (members * (group - place)) % span, 1)
            inside = (lane >= members * group) & (lane < members * (group + 1))
            total = moved if total is None else jnp.where(inside, moved, total)
        spread.append(total)
    first = 0
    for stream in range(streams):
        for place in range(-(-tap_count // reach)):
            taken = min(reach, tap_count - reach * place)
            taps_ref[stream, reach * place : reach * place + taken] = spread[place][
                first : first + taken
            ]
        first += reach + (stream == 0)
    skip_ref[...] = spread[-1][reach : reach + 1]


def by_group(query_in, key_in, value_in, short_taps, long_filters, skip_gain, cotangent):
    tok_rows, chan_width = query_in.shape
    groups, seq_total = long_filters.shape
    streams, tap_count, _ = short_taps.shape
    members = chan_width // groups
    count = groups
    vmem = pl.BlockSpec(memory_space=pltpu.VMEM)
    params = pltpu.CompilerParams(vmem_limit_bytes=32 * 1024 * 1024)
    packed, gain = pl.pallas_call(
        pack_kernel,
        out_shape=(
            jax.ShapeDtypeStruct((count, streams + 1, members, tok_rows), jnp.bfloat16),
            jax.ShapeDtypeStruct((1, chan_width), jnp.float32),
        ),
        in_specs=[pl.BlockSpec(memory_space=pltpu.HBM)] * 5,
        out_specs=(vmem,) * 2,
        scratch_shapes=[
            pltpu.VMEM((streams + 1, tok_rows, chan_width), jnp.bfloat16),
            pltpu.SemaphoreType.DMA((streams + 2,)),
        ],
        compiler_params=params,
        name="pack",
    )(
        *(
            pltpu.with_memory_space_constraint(value, pltpu.HBM)
            for value in (
                query_in, key_in, value_in, cotangent, skip_gain.reshape(1, chan_width)
            )
        )
    )
    packed = lax.all_to_all(
        packed, "seq", 0, 0, tiled=True, axis_index_groups=[order_there(count)]
    )
    results = pl.pallas_call(
        group_kernel,
        out_shape=jax.ShapeDtypeStruct((count, streams + 2, members, tok_rows), jnp.bfloat16),
        in_specs=[vmem] * 4,
        out_specs=vmem,
        scratch_shapes=[
            pltpu.VMEM((chan_width, streams * tap_count + 3), jnp.float32),
            pltpu.VMEM((tok_rows // 2, seq_total + tok_rows), jnp.float32),
            pltpu.VMEM((members, tok_rows), jnp.float32),
        ],
        compiler_params=params,
        name="group",
    )(packed, short_taps, long_filters, gain)
    results = lax.all_to_all(
        results, "seq", 0, 0, tiled=True, axis_index_groups=[order_back(count)]
    )
    block_out, input_grads, tap_grads, skip_grad, filter_grad = pl.pallas_call(
        unpack_kernel,
        out_shape=(
            jax.ShapeDtypeStruct((tok_rows, chan_width), jnp.bfloat16),
            jax.ShapeDtypeStruct((streams, tok_rows, chan_width), jnp.bfloat16),
            jax.ShapeDtypeStruct((streams, tap_count, chan_width), jnp.float32),
            jax.ShapeDtypeStruct((1, chan_width), jnp.float32),
            jax.ShapeDtypeStruct((groups, seq_total), jnp.float32),
        ),
        in_specs=[vmem],
        out_specs=(vmem,) * 5,
        compiler_params=params,
        name="unpack",
    )(results)
    return block_out, input_grads, tap_grads, skip_grad.reshape(chan_width), filter_grad


def plan(query_in, key_in, value_in, short_taps, long_filters, skip_gain, cotangent):
    tok_rows, chan_width = query_in.shape
    groups, seq_total = long_filters.shape
    fits = (
        lax.axis_size("seq") == groups
        and tok_rows == 128
        and chan_width == 128
        and chan_width // groups == 16
        and seq_total == groups * tok_rows
        and short_taps.shape[:2] == (3, 7)
    )
    chosen = by_group if fits else local
    return chosen(query_in, key_in, value_in, short_taps, long_filters, skip_gain, cotangent)


def solution(mesh):
    in_specs = (
        P("seq", "chan"),
        P("seq", "chan"),
        P("seq", "chan"),
        P(None, None, "chan"),
        P("chan", None),
        P("chan"),
        P("seq", "chan"),
    )
    out_specs = (
        P("seq", "chan"),
        P(None, "seq", "chan"),
        P(None, None, "chan"),
        P("chan"),
        P("chan", None),
    )
    return jax.shard_map(plan, mesh=mesh, in_specs=in_specs, out_specs=out_specs, check_vma=False)
```

```python
import functools
import math

import jax
import jax.numpy as jnp
from jax import lax
from jax.experimental import pallas as pl
from jax.experimental.pallas import tpu as pltpu
from jax.sharding import PartitionSpec as P


def from_behind(value, axis, steps):
    count = lax.axis_size(axis)
    initial, last = (max(0, -steps), min(count, count - steps))
    return lax.ppermute(value, axis, [(source, source + steps) for source in range(initial, last)])


def short_forward(extended, weights, rows_here):
    margin = weights.shape[0] - 1
    running = jnp.zeros((rows_here, extended.shape[1]), jnp.float32)
    for offset in range(weights.shape[0]):
        running = (
            running + weights[offset] * extended[margin - offset : margin - offset + rows_here]
        )
    return running


def short_backward(extended, weights, rows_here):
    running = jnp.zeros((rows_here, extended.shape[1]), jnp.float32)
    for offset in range(weights.shape[0]):
        running = running + weights[offset] * extended[offset : offset + rows_here]
    return running


def tap_sums(grad_rows, extended, tap_count, rows_here):
    margin = tap_count - 1
    sums_list = []
    for offset in range(tap_count):
        sums_list.append(
            jnp.sum(grad_rows * extended[margin - offset : margin - offset + rows_here], axis=0)
        )
    return jnp.stack(sums_list)


def hankel(padded, lag_start, height, breadth, seq_total):
    span = height + breadth - 1
    window = lax.dynamic_slice_in_dim(padded, lag_start + seq_total, span, axis=1)
    tiled = jnp.tile(window, (1, height))
    tiled = jnp.pad(tiled, ((0, 0), (0, height)))
    return tiled.reshape(padded.shape[0], height, span + 1)[:, :, :breadth]


def causal_part(padded, source_rows, source_start, target_start, target_count, seq_total):
    breadth = source_rows.shape[0]
    matrix = hankel(
        padded, target_start - source_start - breadth + 1, target_count, breadth, seq_total
    )
    return jnp.einsum("gts,sgc->tgc", matrix, source_rows[::-1], preferred_element_type=jnp.float32)


def anti_part(padded, target_rows, target_start, source_start, source_count, seq_total):
    breadth = target_rows.shape[0]
    matrix = hankel(
        padded, target_start - source_start - source_count + 1, source_count, breadth, seq_total
    )
    return jnp.einsum("gab,bgc->agc", matrix, target_rows, preferred_element_type=jnp.float32)[::-1]


def lag_part(buffer, target_rows, source_rows, target_start, source_start, seq_total):
    height = target_rows.shape[0]
    breadth = source_rows.shape[0]
    groups = target_rows.shape[1]
    padded_source = jnp.pad(source_rows[::-1], ((0, height), (0, 0), (0, 0)))
    products = jnp.einsum(
        "tgc,sgc->gts", target_rows, padded_source, preferred_element_type=jnp.float32
    )
    full_width = height + breadth
    skewed = products.reshape(groups, height * full_width)[:, : height * (full_width - 1)]
    skewed = skewed.reshape(groups, height, full_width - 1)
    diagonal = jnp.sum(skewed, axis=1)
    position = target_start - source_start - breadth + 1 + seq_total
    current = lax.dynamic_slice_in_dim(buffer, position, full_width - 1, axis=1)
    return lax.dynamic_update_slice_in_dim(buffer, current + diagonal, position, axis=1)


def local(query_in, key_in, value_in, short_taps, long_filters, skip_gain, cotangent):
    tok_rows, chan_width = query_in.shape
    groups, seq_total = long_filters.shape
    members = chan_width // groups
    tap_count = short_taps.shape[1]
    margin = tap_count - 1
    device = lax.axis_index("seq")
    own_start = device * tok_rows
    rim_rows = jnp.stack(
        [query_in[tok_rows - margin :], key_in[tok_rows - margin :], value_in[tok_rows - margin :]]
    )
    before = from_behind(rim_rows, "seq", 1)
    streams = [query_in, key_in, value_in]
    extended = [
        jnp.concatenate([before[stream], streams[stream]]).astype(jnp.float32)
        for stream in range(3)
    ]
    query_short = short_forward(extended[0], short_taps[0], tok_rows)
    key_short = short_forward(extended[1], short_taps[1], tok_rows)
    value_short = short_forward(extended[2], short_taps[2], tok_rows)
    gating = (key_short * value_short).astype(jnp.bfloat16)
    relayed = (cotangent.astype(jnp.float32) * query_short).astype(jnp.bfloat16)
    gating_wide = gating.astype(jnp.float32)
    relayed_wide = relayed.astype(jnp.float32)
    gating_groups = gating.reshape(tok_rows, groups, members)
    relayed_groups = relayed.reshape(tok_rows, groups, members)
    padded = jnp.concatenate([jnp.zeros((groups, seq_total), jnp.bfloat16), long_filters], axis=1)
    lag_buffer = jnp.zeros((groups, 2 * seq_total), jnp.float32)
    zeros_out = jnp.zeros((tok_rows, groups, members), jnp.float32)

    def target_pair(distance):
        return distance < 0

    totals = (zeros_out, lag_buffer)
    shard_rows = lax.all_gather(gating, "seq", axis=0, tiled=True)
    piece_rows = shard_rows.shape[0]
    step_rows = min(piece_rows, tok_rows)
    pieces = shard_rows.reshape(piece_rows // step_rows, step_rows, groups, members)

    def forward_visit_block(carried, element):
        position, rows_block = element
        source_start = position * step_rows

        def forward_active(partial_value):
            output_part, buffer = partial_value
            output_part = output_part + causal_part(
                padded, rows_block, source_start, own_start, tok_rows, seq_total
            )
            distance = device - source_start // tok_rows
            buffer = lax.cond(
                target_pair(distance),
                lambda held: lag_part(
                    held, relayed_groups, rows_block, own_start, source_start, seq_total
                ),
                lambda held: held,
                buffer,
            )
            return (output_part, buffer)

        carried = lax.cond(
            source_start < own_start + tok_rows,
            forward_active,
            lambda partial_value: partial_value,
            carried,
        )
        return (carried, None)

    totals, ignored = lax.scan(
        forward_visit_block, totals, (jnp.arange(piece_rows // step_rows, dtype=jnp.int32), pieces)
    )
    output_part, lag_buffer = totals
    output_sum = output_part.reshape(tok_rows, chan_width)
    totals = (zeros_out, lag_buffer)
    shard_rows = lax.all_gather(relayed, "seq", axis=0, tiled=True)
    piece_rows = shard_rows.shape[0]
    backward_step_rows = min(piece_rows, tok_rows)
    pieces = shard_rows.reshape(
        piece_rows // backward_step_rows, backward_step_rows, groups, members
    )

    def backward_visit_block(carried, element):
        position, rows_block = element
        target_start = position * backward_step_rows

        def backward_active(partial_value):
            grad_part, buffer = partial_value
            grad_part = grad_part + anti_part(
                padded, rows_block, target_start, own_start, tok_rows, seq_total
            )
            distance = target_start // tok_rows - device
            buffer = lax.cond(
                target_pair(distance),
                lambda held: held,
                lambda held: lag_part(
                    held, rows_block, gating_groups, target_start, own_start, seq_total
                ),
                buffer,
            )
            return (grad_part, buffer)

        carried = lax.cond(
            target_start + backward_step_rows > own_start,
            backward_active,
            lambda partial_value: partial_value,
            carried,
        )
        return (carried, None)

    totals, ignored = lax.scan(
        backward_visit_block,
        totals,
        (jnp.arange(piece_rows // backward_step_rows, dtype=jnp.int32), pieces),
    )
    grad_part, lag_buffer = totals
    grad_sum = grad_part.reshape(tok_rows, chan_width)
    lag_local = lag_buffer[:, seq_total:]
    long_out = output_sum + skip_gain * gating_wide
    block_out = (query_short * long_out).astype(jnp.bfloat16)
    grad_gating = grad_sum + skip_gain * relayed_wide
    cot_wide = cotangent.astype(jnp.float32)
    grad_shorts = [cot_wide * long_out, grad_gating * value_short, grad_gating * key_short]
    lead_rows = jnp.stack([grad_shorts[stream][:margin] for stream in range(3)])
    after = from_behind(lead_rows, "seq", -1)
    input_grads = jnp.stack(
        [
            short_backward(
                jnp.concatenate([grad_shorts[stream], after[stream]]), short_taps[stream], tok_rows
            )
            for stream in range(3)
        ]
    ).astype(jnp.bfloat16)
    tap_local = jnp.stack(
        [
            tap_sums(grad_shorts[stream], extended[stream], tap_count, tok_rows)
            for stream in range(3)
        ]
    )
    skip_local = jnp.sum(relayed_wide * gating_wide, axis=0)
    lag_total, tap_total, skip_total = lax.psum((lag_local, tap_local, skip_local), "seq")
    tap_scale = 1.0 / math.sqrt(seq_total)
    lag_scale = 1.0 / math.sqrt(seq_total * members)
    return (
        block_out,
        input_grads,
        tap_total * tap_scale,
        skip_total * tap_scale,
        lag_total * lag_scale,
    )


def order_there(count):
    return [(count // 2 + 2 - step) % count for step in range(count)]


def order_back(count):
    return [(count // 2 - step) % count for step in range(count)]


def in_order(value, order):
    return jnp.stack([value[order.index(device)] for device in range(len(order))])


def by_member(value, order):
    return jnp.stack([value[device] for device in order])


def pack_kernel(
    query_ref, key_ref, value_ref, cot_ref, skip_ref, out_ref, gain_ref, stream_buf, sems
):
    count, streams, members, tok_rows = out_ref.shape
    moves = [
        pltpu.make_async_copy(ref, stream_buf.at[stream], sems.at[stream])
        for stream, ref in enumerate((query_ref, key_ref, value_ref, cot_ref))
    ]
    moves.append(pltpu.make_async_copy(skip_ref, gain_ref, sems.at[streams]))
    for move in moves:
        move.start()
    for stream in range(streams):
        moves[stream].wait()
        flipped = stream_buf[stream].astype(jnp.float32).T.astype(jnp.bfloat16)
        flipped = flipped.reshape(count, members, tok_rows)
        out_ref[:, stream] = by_member(flipped, order_there(count))
    moves[streams].wait()


def group_kernel(
    in_ref, taps_ref, filters_ref, gain_ref, out_ref, table_ref, wide_ref, tile_ref
):
    count, _, members, span = in_ref.shape
    groups, seq_total = filters_ref.shape
    streams, tap_count, chan_width = taps_ref.shape
    rows = count * members
    mine = lax.axis_index("seq")
    shape = (count, members, span)
    lane = lax.broadcasted_iota(jnp.int32, shape, 2)
    reach = 3

    def later(value, steps):
        if steps == 0:
            return value
        turned = pltpu.roll(value, steps, 2)
        before = jnp.concatenate([jnp.zeros_like(turned[:1]), turned[:-1]], axis=0)
        return jnp.where(lane >= steps, turned, before)

    def earlier(value, steps):
        if steps == 0:
            return value
        turned = pltpu.roll(value, span - steps, 2)
        after = jnp.concatenate([turned[1:], jnp.zeros_like(turned[:1])], axis=0)
        return jnp.where(lane < span - steps, turned, after)

    table = jnp.concatenate(
        [taps_ref[stream] for stream in range(streams)]
        + [gain_ref[...], jnp.zeros((2, chan_width), jnp.float32)],
        axis=0,
    )
    table_ref[...] = table.T
    params = table_ref[pl.ds(pl.multiple_of(mine * members, members), members), :]

    def column(index):
        return jnp.broadcast_to(params[:, index : index + 1], (members, span))[None]

    chosen = lax.broadcasted_iota(jnp.int32, (groups, 1), 0) == mine
    filter_row = jnp.sum(
        jnp.where(chosen, filters_ref[...].astype(jnp.float32), 0.0), axis=0, keepdims=True
    )
    filter_row = jnp.concatenate([filter_row, jnp.zeros((1, span), jnp.float32)], axis=1)
    spread = jnp.broadcast_to(filter_row, (members, seq_total + span))
    first_rows = pltpu.roll(spread, 0, 1, stride=1, stride_axis=0).astype(jnp.bfloat16)
    row_parts = [first_rows] + [
        pltpu.roll(first_rows, first, 1) for first in range(members, span, members)
    ]
    toeplitz = jnp.concatenate(row_parts, axis=0)[:, :seq_total]

    def delays(stream):
        value = in_order(in_ref[:, stream], order_there(count))
        return [later(value, first) for first in range(0, tap_count, reach)]

    def short(stream, values):
        total = None
        for second in range(reach):
            running = None
            for first in range(second, tap_count, reach):
                value = values[first // reach].astype(jnp.float32)
                term = column(stream * tap_count + first) * value
                running = term if running is None else running + term
            running = later(running, second)
            total = running if total is None else total + running
        return total

    def ahead_by_blocks(value):
        parts = [value]
        for step in range(1, count):
            gap = jnp.zeros((step * members, span), jnp.bfloat16)
            parts.append(jnp.concatenate([value[step * members :], gap], axis=0))
        return jnp.concatenate(parts, axis=1)

    gain = column(streams * tap_count)
    cot = in_order(in_ref[:, streams], order_there(count)).astype(jnp.float32)
    delayed = [delays(0)]
    query_short = short(0, delayed[0])
    relayed = (cot * query_short).astype(jnp.bfloat16).reshape(rows, span)
    relayed_lags = ahead_by_blocks(relayed)
    backward = lax.dot_general(
        relayed_lags, toeplitz, (((1,), (1,)), ((), ())), preferred_element_type=jnp.float32
    )

    delayed += [delays(1), delays(2)]
    key_short = short(1, delayed[1])
    value_short = short(2, delayed[2])
    gating = (key_short * value_short).astype(jnp.bfloat16).reshape(rows, span)
    gating_parts, filter_parts = [gating], [toeplitz[:, :span]]
    for step in range(1, count):
        gap = jnp.zeros((step * members, span), jnp.bfloat16)
        gating_parts.append(jnp.concatenate([gap, gating[: rows - step * members]], axis=0))
        filter_parts.append(toeplitz[:, step * span : (step + 1) * span])
    forward = jnp.dot(
        jnp.concatenate(gating_parts, axis=1),
        jnp.concatenate(filter_parts, axis=0),
        preferred_element_type=jnp.float32,
    )

    half = span // 2
    flip = (
        lax.broadcasted_iota(jnp.int32, (span, span), 0)
        + lax.broadcasted_iota(jnp.int32, (span, span), 1)
        == span - 1
    ).astype(jnp.bfloat16)
    gating_turned = lax.dot_general(
        flip, gating, (((1,), (1,)), ((), ())), preferred_element_type=jnp.float32
    ).astype(jnp.bfloat16)
    gating_turned = jnp.concatenate([gating_turned[half:], gating_turned[:half]], axis=1)
    ahead = earlier(relayed.reshape(shape), half).reshape(rows, span)
    targets = jnp.concatenate([relayed_lags, ahead_by_blocks(ahead)], axis=0)
    wide_ref[:, :seq_total] = jnp.dot(
        gating_turned, targets, preferred_element_type=jnp.float32
    )
    wide_ref[:, seq_total:] = jnp.zeros((half, span), jnp.float32)

    tap_scale = 1.0 / math.sqrt(seq_total)

    def tokens(value):
        return jnp.concatenate([value[block] for block in range(count)], axis=1)

    def sums(left, right):
        product = lax.dot_general(
            jnp.concatenate(left, axis=0),
            jnp.concatenate(right, axis=0),
            (((1,), (1,)), ((), ())),
            preferred_element_type=jnp.float32,
        )
        same = (
            lax.broadcasted_iota(jnp.int32, product.shape, 0) % members
            == lax.broadcasted_iota(jnp.int32, product.shape, 1) % members
        )
        product = jnp.where(same, product, 0.0).reshape(len(left), members, -1)
        return jnp.sum(product, axis=1) * tap_scale

    tile_ref[...] = jnp.zeros((members, span), jnp.float32)

    def finish(stream, grad_short, first_row, more_left=(), more_right=()):
        moved = [earlier(grad_short, second) for second in range(reach)]
        left = [tokens(value.astype(jnp.bfloat16)) for value in moved] + list(more_left)
        right = [tokens(value) for value in delayed[stream]] + list(more_right)
        totals = sums(left, right)
        tile_ref[first_row : first_row + len(left), : totals.shape[1]] = totals
        total = None
        for place in range(len(delayed[stream])):
            running = None
            for second in range(min(reach, tap_count - reach * place)):
                term = column(stream * tap_count + reach * place + second) * moved[second]
                running = term if running is None else running + term
            running = earlier(running, reach * place)
            total = running if total is None else total + running
        out_ref[:, 1 + stream] = by_member(total.astype(jnp.bfloat16), order_back(count))

    grad_gating = backward.reshape(shape) + gain * relayed.astype(jnp.float32).reshape(shape)
    finish(1, grad_gating * value_short, reach + 1)
    finish(2, grad_gating * key_short, 2 * reach + 1)

    long_out = forward.reshape(shape) + gain * gating.astype(jnp.float32).reshape(shape)
    block_out = (query_short * long_out).astype(jnp.bfloat16)
    out_ref[:, 0] = by_member(block_out, order_back(count))
    finish(
        0, cot * long_out, 0, [tokens(relayed.reshape(shape))], [tokens(gating.reshape(shape))]
    )

    skewed = pltpu.roll(wide_ref[...], span - half + 1, 1, stride=1, stride_axis=0)
    diagonal = jnp.sum(skewed, axis=0, keepdims=True)
    lag_scale = 1.0 / math.sqrt(seq_total * members)
    lag_sums = jnp.concatenate(
        [diagonal[:, step * span : (step + 1) * span] for step in range(1, count + 1)], axis=0
    )
    lag_sums = lag_sums * lag_scale
    tile_ref[:count, half:] = lag_sums[:, half:]
    tile_ref[count:, half:] = pltpu.roll(lag_sums, half, 1)[:, half:]
    out_ref[:, streams + 1] = jnp.broadcast_to(tile_ref[...].astype(jnp.bfloat16)[None], shape)


def unpack_kernel(in_ref, out_ref, grads_ref, taps_ref, skip_ref, lags_ref):
    count, _, members, span = in_ref.shape
    streams, tap_count, chan_width = taps_ref.shape
    reach = 3
    for stream in range(streams + 1):
        block = in_order(in_ref[:, stream], order_back(count)).reshape(count * members, span)
        block = block.astype(jnp.float32)
        flipped = block.T.astype(jnp.bfloat16)
        if stream == 0:
            out_ref[...] = flipped
        else:
            grads_ref[stream - 1] = flipped
    tile = in_order(in_ref[:, streams + 1], order_back(count)).astype(jnp.float32)
    lane = lax.broadcasted_iota(jnp.int32, (1, members // 2, span), 2)
    lags = jnp.where(
        lane < span // 2, pltpu.roll(tile[:, members // 2 :], span // 2, 2), tile[:, : members // 2]
    )
    for step in range(members // 2):
        lags_ref[:, step * span : (step + 1) * span] = lags[:, step]
    lane = lax.broadcasted_iota(jnp.int32, (members, span), 1)
    spread = []
    for place in range(-(-tap_count // reach) + 1):
        total = None
        for group in range(count):
            moved = pltpu.roll(tile[group], (members * (group - place)) % span, 1)
            inside = (lane >= members * group) & (lane < members * (group + 1))
            total = moved if total is None else jnp.where(inside, moved, total)
        spread.append(total)
    first = 0
    for stream in range(streams):
        for place in range(-(-tap_count // reach)):
            taken = min(reach, tap_count - reach * place)
            taps_ref[stream, reach * place : reach * place + taken] = spread[place][
                first : first + taken
            ]
        first += reach + (stream == 0)
    skip_ref[...] = spread[-1][reach : reach + 1]


def by_group(query_in, key_in, value_in, short_taps, long_filters, skip_gain, cotangent):
    tok_rows, chan_width = query_in.shape
    groups, seq_total = long_filters.shape
    streams, tap_count, _ = short_taps.shape
    members = chan_width // groups
    count = groups
    vmem = pl.BlockSpec(memory_space=pltpu.VMEM)
    params = pltpu.CompilerParams(vmem_limit_bytes=32 * 1024 * 1024)
    packed, gain = pl.pallas_call(
        pack_kernel,
        out_shape=(
            jax.ShapeDtypeStruct((count, streams + 1, members, tok_rows), jnp.bfloat16),
            jax.ShapeDtypeStruct((1, chan_width), jnp.float32),
        ),
        in_specs=[pl.BlockSpec(memory_space=pltpu.HBM)] * 5,
        out_specs=(vmem,) * 2,
        scratch_shapes=[
            pltpu.VMEM((streams + 1, tok_rows, chan_width), jnp.bfloat16),
            pltpu.SemaphoreType.DMA((streams + 2,)),
        ],
        compiler_params=params,
        name="pack",
    )(
        *(
            pltpu.with_memory_space_constraint(value, pltpu.HBM)
            for value in (
                query_in, key_in, value_in, cotangent, skip_gain.reshape(1, chan_width)
            )
        )
    )
    packed = lax.all_to_all(
        packed, "seq", 0, 0, tiled=True, axis_index_groups=[order_there(count)]
    )
    results = pl.pallas_call(
        group_kernel,
        out_shape=jax.ShapeDtypeStruct((count, streams + 2, members, tok_rows), jnp.bfloat16),
        in_specs=[vmem] * 4,
        out_specs=vmem,
        scratch_shapes=[
            pltpu.VMEM((chan_width, streams * tap_count + 3), jnp.float32),
            pltpu.VMEM((tok_rows // 2, seq_total + tok_rows), jnp.float32),
            pltpu.VMEM((members, tok_rows), jnp.float32),
        ],
        compiler_params=params,
        name="group",
    )(packed, short_taps, long_filters, gain)
    results = lax.all_to_all(
        results, "seq", 0, 0, tiled=True, axis_index_groups=[order_back(count)]
    )
    block_out, input_grads, tap_grads, skip_grad, filter_grad = pl.pallas_call(
        unpack_kernel,
        out_shape=(
            jax.ShapeDtypeStruct((tok_rows, chan_width), jnp.bfloat16),
            jax.ShapeDtypeStruct((streams, tok_rows, chan_width), jnp.bfloat16),
            jax.ShapeDtypeStruct((streams, tap_count, chan_width), jnp.float32),
            jax.ShapeDtypeStruct((1, chan_width), jnp.float32),
            jax.ShapeDtypeStruct((groups, seq_total), jnp.float32),
        ),
        in_specs=[vmem],
        out_specs=(vmem,) * 5,
        compiler_params=params,
        name="unpack",
    )(results)
    return block_out, input_grads, tap_grads, skip_grad.reshape(chan_width), filter_grad


def plan(query_in, key_in, value_in, short_taps, long_filters, skip_gain, cotangent):
    tok_rows, chan_width = query_in.shape
    groups, seq_total = long_filters.shape
    fits = (
        lax.axis_size("seq") == groups
        and tok_rows == 128
        and chan_width == 128
        and chan_width // groups == 16
        and seq_total == groups * tok_rows
        and short_taps.shape[:2] == (3, 7)
    )
    chosen = by_group if fits else local
    return chosen(query_in, key_in, value_in, short_taps, long_filters, skip_gain, cotangent)


def solution(mesh):
    in_specs = (
        P("seq", "chan"),
        P("seq", "chan"),
        P("seq", "chan"),
        P(None, None, "chan"),
        P("chan", None),
        P("chan"),
        P("seq", "chan"),
    )
    out_specs = (
        P("seq", "chan"),
        P(None, "seq", "chan"),
        P(None, None, "chan"),
        P("chan"),
        P("chan", None),
    )
    return jax.shard_map(plan, mesh=mesh, in_specs=in_specs, out_specs=out_specs, check_vma=False)
```

```python
import functools
import math

import jax
import jax.numpy as jnp
from jax import lax
from jax.experimental import pallas as pl
from jax.experimental.pallas import tpu as pltpu
from jax.sharding import PartitionSpec as P


def from_behind(value, axis, steps):
    count = lax.axis_size(axis)
    initial, last = (max(0, -steps), min(count, count - steps))
    return lax.ppermute(value, axis, [(source, source + steps) for source in range(initial, last)])


def short_forward(extended, weights, rows_here):
    margin = weights.shape[0] - 1
    running = jnp.zeros((rows_here, extended.shape[1]), jnp.float32)
    for offset in range(weights.shape[0]):
        running = (
            running + weights[offset] * extended[margin - offset : margin - offset + rows_here]
        )
    return running


def short_backward(extended, weights, rows_here):
    running = jnp.zeros((rows_here, extended.shape[1]), jnp.float32)
    for offset in range(weights.shape[0]):
        running = running + weights[offset] * extended[offset : offset + rows_here]
    return running


def tap_sums(grad_rows, extended, tap_count, rows_here):
    margin = tap_count - 1
    sums_list = []
    for offset in range(tap_count):
        sums_list.append(
            jnp.sum(grad_rows * extended[margin - offset : margin - offset + rows_here], axis=0)
        )
    return jnp.stack(sums_list)


def hankel(padded, lag_start, height, breadth, seq_total):
    span = height + breadth - 1
    window = lax.dynamic_slice_in_dim(padded, lag_start + seq_total, span, axis=1)
    tiled = jnp.tile(window, (1, height))
    tiled = jnp.pad(tiled, ((0, 0), (0, height)))
    return tiled.reshape(padded.shape[0], height, span + 1)[:, :, :breadth]


def causal_part(padded, source_rows, source_start, target_start, target_count, seq_total):
    breadth = source_rows.shape[0]
    matrix = hankel(
        padded, target_start - source_start - breadth + 1, target_count, breadth, seq_total
    )
    return jnp.einsum("gts,sgc->tgc", matrix, source_rows[::-1], preferred_element_type=jnp.float32)


def anti_part(padded, target_rows, target_start, source_start, source_count, seq_total):
    breadth = target_rows.shape[0]
    matrix = hankel(
        padded, target_start - source_start - source_count + 1, source_count, breadth, seq_total
    )
    return jnp.einsum("gab,bgc->agc", matrix, target_rows, preferred_element_type=jnp.float32)[::-1]


def lag_part(buffer, target_rows, source_rows, target_start, source_start, seq_total):
    height = target_rows.shape[0]
    breadth = source_rows.shape[0]
    groups = target_rows.shape[1]
    padded_source = jnp.pad(source_rows[::-1], ((0, height), (0, 0), (0, 0)))
    products = jnp.einsum(
        "tgc,sgc->gts", target_rows, padded_source, preferred_element_type=jnp.float32
    )
    full_width = height + breadth
    skewed = products.reshape(groups, height * full_width)[:, : height * (full_width - 1)]
    skewed = skewed.reshape(groups, height, full_width - 1)
    diagonal = jnp.sum(skewed, axis=1)
    position = target_start - source_start - breadth + 1 + seq_total
    current = lax.dynamic_slice_in_dim(buffer, position, full_width - 1, axis=1)
    return lax.dynamic_update_slice_in_dim(buffer, current + diagonal, position, axis=1)


def local(query_in, key_in, value_in, short_taps, long_filters, skip_gain, cotangent):
    tok_rows, chan_width = query_in.shape
    groups, seq_total = long_filters.shape
    members = chan_width // groups
    tap_count = short_taps.shape[1]
    margin = tap_count - 1
    device = lax.axis_index("seq")
    own_start = device * tok_rows
    rim_rows = jnp.stack(
        [query_in[tok_rows - margin :], key_in[tok_rows - margin :], value_in[tok_rows - margin :]]
    )
    before = from_behind(rim_rows, "seq", 1)
    streams = [query_in, key_in, value_in]
    extended = [
        jnp.concatenate([before[stream], streams[stream]]).astype(jnp.float32)
        for stream in range(3)
    ]
    query_short = short_forward(extended[0], short_taps[0], tok_rows)
    key_short = short_forward(extended[1], short_taps[1], tok_rows)
    value_short = short_forward(extended[2], short_taps[2], tok_rows)
    gating = (key_short * value_short).astype(jnp.bfloat16)
    relayed = (cotangent.astype(jnp.float32) * query_short).astype(jnp.bfloat16)
    gating_wide = gating.astype(jnp.float32)
    relayed_wide = relayed.astype(jnp.float32)
    gating_groups = gating.reshape(tok_rows, groups, members)
    relayed_groups = relayed.reshape(tok_rows, groups, members)
    padded = jnp.concatenate([jnp.zeros((groups, seq_total), jnp.bfloat16), long_filters], axis=1)
    lag_buffer = jnp.zeros((groups, 2 * seq_total), jnp.float32)
    zeros_out = jnp.zeros((tok_rows, groups, members), jnp.float32)

    def target_pair(distance):
        return distance < 0

    totals = (zeros_out, lag_buffer)
    shard_rows = lax.all_gather(gating, "seq", axis=0, tiled=True)
    piece_rows = shard_rows.shape[0]
    step_rows = min(piece_rows, tok_rows)
    pieces = shard_rows.reshape(piece_rows // step_rows, step_rows, groups, members)

    def forward_visit_block(carried, element):
        position, rows_block = element
        source_start = position * step_rows

        def forward_active(partial_value):
            output_part, buffer = partial_value
            output_part = output_part + causal_part(
                padded, rows_block, source_start, own_start, tok_rows, seq_total
            )
            distance = device - source_start // tok_rows
            buffer = lax.cond(
                target_pair(distance),
                lambda held: lag_part(
                    held, relayed_groups, rows_block, own_start, source_start, seq_total
                ),
                lambda held: held,
                buffer,
            )
            return (output_part, buffer)

        carried = lax.cond(
            source_start < own_start + tok_rows,
            forward_active,
            lambda partial_value: partial_value,
            carried,
        )
        return (carried, None)

    totals, ignored = lax.scan(
        forward_visit_block, totals, (jnp.arange(piece_rows // step_rows, dtype=jnp.int32), pieces)
    )
    output_part, lag_buffer = totals
    output_sum = output_part.reshape(tok_rows, chan_width)
    totals = (zeros_out, lag_buffer)
    shard_rows = lax.all_gather(relayed, "seq", axis=0, tiled=True)
    piece_rows = shard_rows.shape[0]
    backward_step_rows = min(piece_rows, tok_rows)
    pieces = shard_rows.reshape(
        piece_rows // backward_step_rows, backward_step_rows, groups, members
    )

    def backward_visit_block(carried, element):
        position, rows_block = element
        target_start = position * backward_step_rows

        def backward_active(partial_value):
            grad_part, buffer = partial_value
            grad_part = grad_part + anti_part(
                padded, rows_block, target_start, own_start, tok_rows, seq_total
            )
            distance = target_start // tok_rows - device
            buffer = lax.cond(
                target_pair(distance),
                lambda held: held,
                lambda held: lag_part(
                    held, rows_block, gating_groups, target_start, own_start, seq_total
                ),
                buffer,
            )
            return (grad_part, buffer)

        carried = lax.cond(
            target_start + backward_step_rows > own_start,
            backward_active,
            lambda partial_value: partial_value,
            carried,
        )
        return (carried, None)

    totals, ignored = lax.scan(
        backward_visit_block,
        totals,
        (jnp.arange(piece_rows // backward_step_rows, dtype=jnp.int32), pieces),
    )
    grad_part, lag_buffer = totals
    grad_sum = grad_part.reshape(tok_rows, chan_width)
    lag_local = lag_buffer[:, seq_total:]
    long_out = output_sum + skip_gain * gating_wide
    block_out = (query_short * long_out).astype(jnp.bfloat16)
    grad_gating = grad_sum + skip_gain * relayed_wide
    cot_wide = cotangent.astype(jnp.float32)
    grad_shorts = [cot_wide * long_out, grad_gating * value_short, grad_gating * key_short]
    lead_rows = jnp.stack([grad_shorts[stream][:margin] for stream in range(3)])
    after = from_behind(lead_rows, "seq", -1)
    input_grads = jnp.stack(
        [
            short_backward(
                jnp.concatenate([grad_shorts[stream], after[stream]]), short_taps[stream], tok_rows
            )
            for stream in range(3)
        ]
    ).astype(jnp.bfloat16)
    tap_local = jnp.stack(
        [
            tap_sums(grad_shorts[stream], extended[stream], tap_count, tok_rows)
            for stream in range(3)
        ]
    )
    skip_local = jnp.sum(relayed_wide * gating_wide, axis=0)
    lag_total, tap_total, skip_total = lax.psum((lag_local, tap_local, skip_local), "seq")
    tap_scale = 1.0 / math.sqrt(seq_total)
    lag_scale = 1.0 / math.sqrt(seq_total * members)
    return (
        block_out,
        input_grads,
        tap_total * tap_scale,
        skip_total * tap_scale,
        lag_total * lag_scale,
    )


def order_there(count):
    return [(count // 2 - step) % count for step in range(count)]


def order_back(count):
    return [(count // 2 - step) % count for step in range(count)]


def in_order(value, order):
    return jnp.stack([value[order.index(device)] for device in range(len(order))])


def by_member(value, order):
    return jnp.stack([value[device] for device in order])


def pack_kernel(
    query_ref, key_ref, value_ref, cot_ref, skip_ref, out_ref, gain_ref, stream_buf, sems
):
    count, streams, members, tok_rows = out_ref.shape
    moves = [
        pltpu.make_async_copy(ref, stream_buf.at[stream], sems.at[stream])
        for stream, ref in enumerate((query_ref, key_ref, value_ref, cot_ref))
    ]
    moves.append(pltpu.make_async_copy(skip_ref, gain_ref, sems.at[streams]))
    for move in moves:
        move.start()
    for stream in range(streams):
        moves[stream].wait()
        flipped = stream_buf[stream].astype(jnp.float32).T.astype(jnp.bfloat16)
        flipped = flipped.reshape(count, members, tok_rows)
        out_ref[:, stream] = by_member(flipped, order_there(count))
    moves[streams].wait()


def group_kernel(
    in_ref, taps_ref, filters_ref, gain_ref, out_ref, table_ref, wide_ref, tile_ref
):
    count, _, members, span = in_ref.shape
    groups, seq_total = filters_ref.shape
    streams, tap_count, chan_width = taps_ref.shape
    rows = count * members
    mine = lax.axis_index("seq")
    shape = (count, members, span)
    lane = lax.broadcasted_iota(jnp.int32, shape, 2)
    reach = 3

    def later(value, steps):
        if steps == 0:
            return value
        turned = pltpu.roll(value, steps, 2)
        before = jnp.concatenate([jnp.zeros_like(turned[:1]), turned[:-1]], axis=0)
        return jnp.where(lane >= steps, turned, before)

    def earlier(value, steps):
        if steps == 0:
            return value
        turned = pltpu.roll(value, span - steps, 2)
        after = jnp.concatenate([turned[1:], jnp.zeros_like(turned[:1])], axis=0)
        return jnp.where(lane < span - steps, turned, after)

    table = jnp.concatenate(
        [taps_ref[stream] for stream in range(streams)]
        + [gain_ref[...], jnp.zeros((2, chan_width), jnp.float32)],
        axis=0,
    )
    table_ref[...] = table.T
    params = table_ref[pl.ds(pl.multiple_of(mine * members, members), members), :]

    def column(index):
        return jnp.broadcast_to(params[:, index : index + 1], (members, span))[None]

    chosen = lax.broadcasted_iota(jnp.int32, (groups, 1), 0) == mine
    filter_row = jnp.sum(
        jnp.where(chosen, filters_ref[...].astype(jnp.float32), 0.0), axis=0, keepdims=True
    )
    filter_row = jnp.concatenate([filter_row, jnp.zeros((1, span), jnp.float32)], axis=1)
    spread = jnp.broadcast_to(filter_row, (members, seq_total + span))
    first_rows = pltpu.roll(spread, 0, 1, stride=1, stride_axis=0).astype(jnp.bfloat16)
    row_parts = [first_rows] + [
        pltpu.roll(first_rows, first, 1) for first in range(members, span, members)
    ]
    toeplitz = jnp.concatenate(row_parts, axis=0)[:, :seq_total]

    def delays(stream):
        value = in_order(in_ref[:, stream], order_there(count))
        return [later(value, first) for first in range(0, tap_count, reach)]

    def short(stream, values):
        total = None
        for second in range(reach):
            running = None
            for first in range(second, tap_count, reach):
                value = values[first // reach].astype(jnp.float32)
                term = column(stream * tap_count + first) * value
                running = term if running is None else running + term
            running = later(running, second)
            total = running if total is None else total + running
        return total

    def ahead_by_blocks(value):
        parts = [value]
        for step in range(1, count):
            gap = jnp.zeros((step * members, span), jnp.bfloat16)
            parts.append(jnp.concatenate([value[step * members :], gap], axis=0))
        return jnp.concatenate(parts, axis=1)

    gain = column(streams * tap_count)
    cot = in_order(in_ref[:, streams], order_there(count)).astype(jnp.float32)
    delayed = [delays(0)]
    query_short = short(0, delayed[0])
    relayed = (cot * query_short).astype(jnp.bfloat16).reshape(rows, span)
    relayed_lags = ahead_by_blocks(relayed)
    backward = lax.dot_general(
        relayed_lags, toeplitz, (((1,), (1,)), ((), ())), preferred_element_type=jnp.float32
    )

    delayed += [delays(1), delays(2)]
    key_short = short(1, delayed[1])
    value_short = short(2, delayed[2])
    gating = (key_short * value_short).astype(jnp.bfloat16).reshape(rows, span)
    gating_parts, filter_parts = [gating], [toeplitz[:, :span]]
    for step in range(1, count):
        gap = jnp.zeros((step * members, span), jnp.bfloat16)
        gating_parts.append(jnp.concatenate([gap, gating[: rows - step * members]], axis=0))
        filter_parts.append(toeplitz[:, step * span : (step + 1) * span])
    forward = jnp.dot(
        jnp.concatenate(gating_parts, axis=1),
        jnp.concatenate(filter_parts, axis=0),
        preferred_element_type=jnp.float32,
    )

    half = span // 2
    flip = (
        lax.broadcasted_iota(jnp.int32, (span, span), 0)
        + lax.broadcasted_iota(jnp.int32, (span, span), 1)
        == span - 1
    ).astype(jnp.bfloat16)
    gating_turned = lax.dot_general(
        flip, gating, (((1,), (1,)), ((), ())), preferred_element_type=jnp.float32
    ).astype(jnp.bfloat16)
    gating_turned = jnp.concatenate([gating_turned[half:], gating_turned[:half]], axis=1)
    ahead = earlier(relayed.reshape(shape), half).reshape(rows, span)
    targets = jnp.concatenate([relayed_lags, ahead_by_blocks(ahead)], axis=0)
    wide_ref[:, :seq_total] = jnp.dot(
        gating_turned, targets, preferred_element_type=jnp.float32
    )
    wide_ref[:, seq_total:] = jnp.zeros((half, span), jnp.float32)

    tap_scale = 1.0 / math.sqrt(seq_total)

    def tokens(value):
        return jnp.concatenate([value[block] for block in range(count)], axis=1)

    def sums(left, right):
        product = lax.dot_general(
            jnp.concatenate(left, axis=0),
            jnp.concatenate(right, axis=0),
            (((1,), (1,)), ((), ())),
            preferred_element_type=jnp.float32,
        )
        same = (
            lax.broadcasted_iota(jnp.int32, product.shape, 0) % members
            == lax.broadcasted_iota(jnp.int32, product.shape, 1) % members
        )
        product = jnp.where(same, product, 0.0).reshape(len(left), members, -1)
        return jnp.sum(product, axis=1) * tap_scale

    tile_ref[...] = jnp.zeros((members, span), jnp.float32)

    def finish(stream, grad_short, first_row, more_left=(), more_right=()):
        moved = [earlier(grad_short, second) for second in range(reach)]
        left = [tokens(value.astype(jnp.bfloat16)) for value in moved] + list(more_left)
        right = [tokens(value) for value in delayed[stream]] + list(more_right)
        totals = sums(left, right)
        tile_ref[first_row : first_row + len(left), : totals.shape[1]] = totals
        total = None
        for place in range(len(delayed[stream])):
            running = None
            for second in range(min(reach, tap_count - reach * place)):
                term = column(stream * tap_count + reach * place + second) * moved[second]
                running = term if running is None else running + term
            running = earlier(running, reach * place)
            total = running if total is None else total + running
        out_ref[:, 1 + stream] = by_member(total.astype(jnp.bfloat16), order_back(count))

    grad_gating = backward.reshape(shape) + gain * relayed.astype(jnp.float32).reshape(shape)
    finish(1, grad_gating * value_short, reach + 1)
    finish(2, grad_gating * key_short, 2 * reach + 1)

    long_out = forward.reshape(shape) + gain * gating.astype(jnp.float32).reshape(shape)
    block_out = (query_short * long_out).astype(jnp.bfloat16)
    out_ref[:, 0] = by_member(block_out, order_back(count))
    finish(
        0, cot * long_out, 0, [tokens(relayed.reshape(shape))], [tokens(gating.reshape(shape))]
    )

    skewed = pltpu.roll(wide_ref[...], span - half + 1, 1, stride=1, stride_axis=0)
    diagonal = jnp.sum(skewed, axis=0, keepdims=True)
    lag_scale = 1.0 / math.sqrt(seq_total * members)
    lag_sums = jnp.concatenate(
        [diagonal[:, step * span : (step + 1) * span] for step in range(1, count + 1)], axis=0
    )
    lag_sums = lag_sums * lag_scale
    tile_ref[:count, half:] = lag_sums[:, half:]
    tile_ref[count:, half:] = pltpu.roll(lag_sums, half, 1)[:, half:]
    out_ref[:, streams + 1] = jnp.broadcast_to(tile_ref[...].astype(jnp.bfloat16)[None], shape)


def unpack_kernel(in_ref, out_ref, grads_ref, taps_ref, skip_ref, lags_ref):
    count, _, members, span = in_ref.shape
    streams, tap_count, chan_width = taps_ref.shape
    reach = 3
    for stream in range(streams + 1):
        block = in_order(in_ref[:, stream], order_back(count)).reshape(count * members, span)
        block = block.astype(jnp.float32)
        flipped = block.T.astype(jnp.bfloat16)
        if stream == 0:
            out_ref[...] = flipped
        else:
            grads_ref[stream - 1] = flipped
    tile = in_order(in_ref[:, streams + 1], order_back(count)).astype(jnp.float32)
    lane = lax.broadcasted_iota(jnp.int32, (1, members // 2, span), 2)
    lags = jnp.where(
        lane < span // 2, pltpu.roll(tile[:, members // 2 :], span // 2, 2), tile[:, : members // 2]
    )
    for step in range(members // 2):
        lags_ref[:, step * span : (step + 1) * span] = lags[:, step]
    lane = lax.broadcasted_iota(jnp.int32, (members, span), 1)
    spread = []
    for place in range(-(-tap_count // reach) + 1):
        total = None
        for group in range(count):
            moved = pltpu.roll(tile[group], (members * (group - place)) % span, 1)
            inside = (lane >= members * group) & (lane < members * (group + 1))
            total = moved if total is None else jnp.where(inside, moved, total)
        spread.append(total)
    first = 0
    for stream in range(streams):
        for place in range(-(-tap_count // reach)):
            taken = min(reach, tap_count - reach * place)
            taps_ref[stream, reach * place : reach * place + taken] = spread[place][
                first : first + taken
            ]
        first += reach + (stream == 0)
    skip_ref[...] = spread[-1][reach : reach + 1]


def by_group(query_in, key_in, value_in, short_taps, long_filters, skip_gain, cotangent):
    tok_rows, chan_width = query_in.shape
    groups, seq_total = long_filters.shape
    streams, tap_count, _ = short_taps.shape
    members = chan_width // groups
    count = groups
    vmem = pl.BlockSpec(memory_space=pltpu.VMEM)
    params = pltpu.CompilerParams(vmem_limit_bytes=32 * 1024 * 1024)
    packed, gain = pl.pallas_call(
        pack_kernel,
        out_shape=(
            jax.ShapeDtypeStruct((count, streams + 1, members, tok_rows), jnp.bfloat16),
            jax.ShapeDtypeStruct((1, chan_width), jnp.float32),
        ),
        in_specs=[pl.BlockSpec(memory_space=pltpu.HBM)] * 5,
        out_specs=(vmem,) * 2,
        scratch_shapes=[
            pltpu.VMEM((streams + 1, tok_rows, chan_width), jnp.bfloat16),
            pltpu.SemaphoreType.DMA((streams + 2,)),
        ],
        compiler_params=params,
        name="pack",
    )(
        *(
            pltpu.with_memory_space_constraint(value, pltpu.HBM)
            for value in (
                query_in, key_in, value_in, cotangent, skip_gain.reshape(1, chan_width)
            )
        )
    )
    packed = lax.all_to_all(
        packed, "seq", 0, 0, tiled=True, axis_index_groups=[order_there(count)]
    )
    results = pl.pallas_call(
        group_kernel,
        out_shape=jax.ShapeDtypeStruct((count, streams + 2, members, tok_rows), jnp.bfloat16),
        in_specs=[vmem] * 4,
        out_specs=vmem,
        scratch_shapes=[
            pltpu.VMEM((chan_width, streams * tap_count + 3), jnp.float32),
            pltpu.VMEM((tok_rows // 2, seq_total + tok_rows), jnp.float32),
            pltpu.VMEM((members, tok_rows), jnp.float32),
        ],
        compiler_params=params,
        name="group",
    )(packed, short_taps, long_filters, gain)
    results = lax.all_to_all(
        results, "seq", 0, 0, tiled=True, axis_index_groups=[order_back(count)]
    )
    block_out, input_grads, tap_grads, skip_grad, filter_grad = pl.pallas_call(
        unpack_kernel,
        out_shape=(
            jax.ShapeDtypeStruct((tok_rows, chan_width), jnp.bfloat16),
            jax.ShapeDtypeStruct((streams, tok_rows, chan_width), jnp.bfloat16),
            jax.ShapeDtypeStruct((streams, tap_count, chan_width), jnp.float32),
            jax.ShapeDtypeStruct((1, chan_width), jnp.float32),
            jax.ShapeDtypeStruct((groups, seq_total), jnp.float32),
        ),
        in_specs=[vmem],
        out_specs=(vmem,) * 5,
        compiler_params=params,
        name="unpack",
    )(results)
    return block_out, input_grads, tap_grads, skip_grad.reshape(chan_width), filter_grad


def plan(query_in, key_in, value_in, short_taps, long_filters, skip_gain, cotangent):
    tok_rows, chan_width = query_in.shape
    groups, seq_total = long_filters.shape
    fits = (
        lax.axis_size("seq") == groups
        and tok_rows == 128
        and chan_width == 128
        and chan_width // groups == 16
        and seq_total == groups * tok_rows
        and short_taps.shape[:2] == (3, 7)
    )
    chosen = by_group if fits else local
    return chosen(query_in, key_in, value_in, short_taps, long_filters, skip_gain, cotangent)


def solution(mesh):
    in_specs = (
        P("seq", "chan"),
        P("seq", "chan"),
        P("seq", "chan"),
        P(None, None, "chan"),
        P("chan", None),
        P("chan"),
        P("seq", "chan"),
    )
    out_specs = (
        P("seq", "chan"),
        P(None, "seq", "chan"),
        P(None, None, "chan"),
        P("chan"),
        P("chan", None),
    )
    return jax.shard_map(plan, mesh=mesh, in_specs=in_specs, out_specs=out_specs, check_vma=False)
```

```python
import functools
import math

import jax
import jax.numpy as jnp
from jax import lax
from jax.experimental import pallas as pl
from jax.experimental.pallas import tpu as pltpu
from jax.sharding import PartitionSpec as P


def from_behind(value, axis, steps):
    count = lax.axis_size(axis)
    initial, last = (max(0, -steps), min(count, count - steps))
    return lax.ppermute(value, axis, [(source, source + steps) for source in range(initial, last)])


def short_forward(extended, weights, rows_here):
    margin = weights.shape[0] - 1
    running = jnp.zeros((rows_here, extended.shape[1]), jnp.float32)
    for offset in range(weights.shape[0]):
        running = (
            running + weights[offset] * extended[margin - offset : margin - offset + rows_here]
        )
    return running


def short_backward(extended, weights, rows_here):
    running = jnp.zeros((rows_here, extended.shape[1]), jnp.float32)
    for offset in range(weights.shape[0]):
        running = running + weights[offset] * extended[offset : offset + rows_here]
    return running


def tap_sums(grad_rows, extended, tap_count, rows_here):
    margin = tap_count - 1
    sums_list = []
    for offset in range(tap_count):
        sums_list.append(
            jnp.sum(grad_rows * extended[margin - offset : margin - offset + rows_here], axis=0)
        )
    return jnp.stack(sums_list)


def hankel(padded, lag_start, height, breadth, seq_total):
    span = height + breadth - 1
    window = lax.dynamic_slice_in_dim(padded, lag_start + seq_total, span, axis=1)
    tiled = jnp.tile(window, (1, height))
    tiled = jnp.pad(tiled, ((0, 0), (0, height)))
    return tiled.reshape(padded.shape[0], height, span + 1)[:, :, :breadth]


def causal_part(padded, source_rows, source_start, target_start, target_count, seq_total):
    breadth = source_rows.shape[0]
    matrix = hankel(
        padded, target_start - source_start - breadth + 1, target_count, breadth, seq_total
    )
    return jnp.einsum("gts,sgc->tgc", matrix, source_rows[::-1], preferred_element_type=jnp.float32)


def anti_part(padded, target_rows, target_start, source_start, source_count, seq_total):
    breadth = target_rows.shape[0]
    matrix = hankel(
        padded, target_start - source_start - source_count + 1, source_count, breadth, seq_total
    )
    return jnp.einsum("gab,bgc->agc", matrix, target_rows, preferred_element_type=jnp.float32)[::-1]


def lag_part(buffer, target_rows, source_rows, target_start, source_start, seq_total):
    height = target_rows.shape[0]
    breadth = source_rows.shape[0]
    groups = target_rows.shape[1]
    padded_source = jnp.pad(source_rows[::-1], ((0, height), (0, 0), (0, 0)))
    products = jnp.einsum(
        "tgc,sgc->gts", target_rows, padded_source, preferred_element_type=jnp.float32
    )
    full_width = height + breadth
    skewed = products.reshape(groups, height * full_width)[:, : height * (full_width - 1)]
    skewed = skewed.reshape(groups, height, full_width - 1)
    diagonal = jnp.sum(skewed, axis=1)
    position = target_start - source_start - breadth + 1 + seq_total
    current = lax.dynamic_slice_in_dim(buffer, position, full_width - 1, axis=1)
    return lax.dynamic_update_slice_in_dim(buffer, current + diagonal, position, axis=1)


def local(query_in, key_in, value_in, short_taps, long_filters, skip_gain, cotangent):
    tok_rows, chan_width = query_in.shape
    groups, seq_total = long_filters.shape
    members = chan_width // groups
    tap_count = short_taps.shape[1]
    margin = tap_count - 1
    device = lax.axis_index("seq")
    own_start = device * tok_rows
    rim_rows = jnp.stack(
        [query_in[tok_rows - margin :], key_in[tok_rows - margin :], value_in[tok_rows - margin :]]
    )
    before = from_behind(rim_rows, "seq", 1)
    streams = [query_in, key_in, value_in]
    extended = [
        jnp.concatenate([before[stream], streams[stream]]).astype(jnp.float32)
        for stream in range(3)
    ]
    query_short = short_forward(extended[0], short_taps[0], tok_rows)
    key_short = short_forward(extended[1], short_taps[1], tok_rows)
    value_short = short_forward(extended[2], short_taps[2], tok_rows)
    gating = (key_short * value_short).astype(jnp.bfloat16)
    relayed = (cotangent.astype(jnp.float32) * query_short).astype(jnp.bfloat16)
    gating_wide = gating.astype(jnp.float32)
    relayed_wide = relayed.astype(jnp.float32)
    gating_groups = gating.reshape(tok_rows, groups, members)
    relayed_groups = relayed.reshape(tok_rows, groups, members)
    padded = jnp.concatenate([jnp.zeros((groups, seq_total), jnp.bfloat16), long_filters], axis=1)
    lag_buffer = jnp.zeros((groups, 2 * seq_total), jnp.float32)
    zeros_out = jnp.zeros((tok_rows, groups, members), jnp.float32)

    def target_pair(distance):
        return distance < 0

    totals = (zeros_out, lag_buffer)
    shard_rows = lax.all_gather(gating, "seq", axis=0, tiled=True)
    piece_rows = shard_rows.shape[0]
    step_rows = min(piece_rows, tok_rows)
    pieces = shard_rows.reshape(piece_rows // step_rows, step_rows, groups, members)

    def forward_visit_block(carried, element):
        position, rows_block = element
        source_start = position * step_rows

        def forward_active(partial_value):
            output_part, buffer = partial_value
            output_part = output_part + causal_part(
                padded, rows_block, source_start, own_start, tok_rows, seq_total
            )
            distance = device - source_start // tok_rows
            buffer = lax.cond(
                target_pair(distance),
                lambda held: lag_part(
                    held, relayed_groups, rows_block, own_start, source_start, seq_total
                ),
                lambda held: held,
                buffer,
            )
            return (output_part, buffer)

        carried = lax.cond(
            source_start < own_start + tok_rows,
            forward_active,
            lambda partial_value: partial_value,
            carried,
        )
        return (carried, None)

    totals, ignored = lax.scan(
        forward_visit_block, totals, (jnp.arange(piece_rows // step_rows, dtype=jnp.int32), pieces)
    )
    output_part, lag_buffer = totals
    output_sum = output_part.reshape(tok_rows, chan_width)
    totals = (zeros_out, lag_buffer)
    shard_rows = lax.all_gather(relayed, "seq", axis=0, tiled=True)
    piece_rows = shard_rows.shape[0]
    backward_step_rows = min(piece_rows, tok_rows)
    pieces = shard_rows.reshape(
        piece_rows // backward_step_rows, backward_step_rows, groups, members
    )

    def backward_visit_block(carried, element):
        position, rows_block = element
        target_start = position * backward_step_rows

        def backward_active(partial_value):
            grad_part, buffer = partial_value
            grad_part = grad_part + anti_part(
                padded, rows_block, target_start, own_start, tok_rows, seq_total
            )
            distance = target_start // tok_rows - device
            buffer = lax.cond(
                target_pair(distance),
                lambda held: held,
                lambda held: lag_part(
                    held, rows_block, gating_groups, target_start, own_start, seq_total
                ),
                buffer,
            )
            return (grad_part, buffer)

        carried = lax.cond(
            target_start + backward_step_rows > own_start,
            backward_active,
            lambda partial_value: partial_value,
            carried,
        )
        return (carried, None)

    totals, ignored = lax.scan(
        backward_visit_block,
        totals,
        (jnp.arange(piece_rows // backward_step_rows, dtype=jnp.int32), pieces),
    )
    grad_part, lag_buffer = totals
    grad_sum = grad_part.reshape(tok_rows, chan_width)
    lag_local = lag_buffer[:, seq_total:]
    long_out = output_sum + skip_gain * gating_wide
    block_out = (query_short * long_out).astype(jnp.bfloat16)
    grad_gating = grad_sum + skip_gain * relayed_wide
    cot_wide = cotangent.astype(jnp.float32)
    grad_shorts = [cot_wide * long_out, grad_gating * value_short, grad_gating * key_short]
    lead_rows = jnp.stack([grad_shorts[stream][:margin] for stream in range(3)])
    after = from_behind(lead_rows, "seq", -1)
    input_grads = jnp.stack(
        [
            short_backward(
                jnp.concatenate([grad_shorts[stream], after[stream]]), short_taps[stream], tok_rows
            )
            for stream in range(3)
        ]
    ).astype(jnp.bfloat16)
    tap_local = jnp.stack(
        [
            tap_sums(grad_shorts[stream], extended[stream], tap_count, tok_rows)
            for stream in range(3)
        ]
    )
    skip_local = jnp.sum(relayed_wide * gating_wide, axis=0)
    lag_total, tap_total, skip_total = lax.psum((lag_local, tap_local, skip_local), "seq")
    tap_scale = 1.0 / math.sqrt(seq_total)
    lag_scale = 1.0 / math.sqrt(seq_total * members)
    return (
        block_out,
        input_grads,
        tap_total * tap_scale,
        skip_total * tap_scale,
        lag_total * lag_scale,
    )


def order_there(count):
    return [(count // 2 + 1 - 2 * step) % count for step in range(count // 2)] + [
        (count // 2 - 2 * step) % count for step in range(count // 2)
    ]


def order_back(count):
    return [count // 2 + 1, count // 2] + [
        *range(count - 1, count // 2 + 1, -1), *range(count // 2 - 1, -1, -1)
    ]


def in_order(value, order):
    return jnp.stack([value[order.index(device)] for device in range(len(order))])


def by_member(value, order):
    return jnp.stack([value[device] for device in order])


def pack_kernel(
    query_ref, key_ref, value_ref, cot_ref, skip_ref, out_ref, gain_ref, stream_buf, sems
):
    count, streams, members, tok_rows = out_ref.shape
    moves = [
        pltpu.make_async_copy(ref, stream_buf.at[stream], sems.at[stream])
        for stream, ref in enumerate((query_ref, key_ref, value_ref, cot_ref))
    ]
    moves.append(pltpu.make_async_copy(skip_ref, gain_ref, sems.at[streams]))
    for move in moves:
        move.start()
    for stream in range(streams):
        moves[stream].wait()
        flipped = stream_buf[stream].astype(jnp.float32).T.astype(jnp.bfloat16)
        flipped = flipped.reshape(count, members, tok_rows)
        out_ref[:, stream] = by_member(flipped, order_there(count))
    moves[streams].wait()


def group_kernel(
    in_ref, taps_ref, filters_ref, gain_ref, out_ref, table_ref, wide_ref, tile_ref
):
    count, _, members, span = in_ref.shape
    groups, seq_total = filters_ref.shape
    streams, tap_count, chan_width = taps_ref.shape
    rows = count * members
    mine = lax.axis_index("seq")
    shape = (count, members, span)
    lane = lax.broadcasted_iota(jnp.int32, shape, 2)
    reach = 3

    def later(value, steps):
        if steps == 0:
            return value
        turned = pltpu.roll(value, steps, 2)
        before = jnp.concatenate([jnp.zeros_like(turned[:1]), turned[:-1]], axis=0)
        return jnp.where(lane >= steps, turned, before)

    def earlier(value, steps):
        if steps == 0:
            return value
        turned = pltpu.roll(value, span - steps, 2)
        after = jnp.concatenate([turned[1:], jnp.zeros_like(turned[:1])], axis=0)
        return jnp.where(lane < span - steps, turned, after)

    table = jnp.concatenate(
        [taps_ref[stream] for stream in range(streams)]
        + [gain_ref[...], jnp.zeros((2, chan_width), jnp.float32)],
        axis=0,
    )
    table_ref[...] = table.T
    params = table_ref[pl.ds(pl.multiple_of(mine * members, members), members), :]

    def column(index):
        return jnp.broadcast_to(params[:, index : index + 1], (members, span))[None]

    chosen = lax.broadcasted_iota(jnp.int32, (groups, 1), 0) == mine
    filter_row = jnp.sum(
        jnp.where(chosen, filters_ref[...].astype(jnp.float32), 0.0), axis=0, keepdims=True
    )
    filter_row = jnp.concatenate([filter_row, jnp.zeros((1, span), jnp.float32)], axis=1)
    spread = jnp.broadcast_to(filter_row, (members, seq_total + span))
    first_rows = pltpu.roll(spread, 0, 1, stride=1, stride_axis=0).astype(jnp.bfloat16)
    row_parts = [first_rows] + [
        pltpu.roll(first_rows, first, 1) for first in range(members, span, members)
    ]
    toeplitz = jnp.concatenate(row_parts, axis=0)[:, :seq_total]

    def delays(stream):
        value = in_order(in_ref[:, stream], order_there(count))
        return [later(value, first) for first in range(0, tap_count, reach)]

    def short(stream, values):
        total = None
        for second in range(reach):
            running = None
            for first in range(second, tap_count, reach):
                value = values[first // reach].astype(jnp.float32)
                term = column(stream * tap_count + first) * value
                running = term if running is None else running + term
            running = later(running, second)
            total = running if total is None else total + running
        return total

    def ahead_by_blocks(value):
        parts = [value]
        for step in range(1, count):
            gap = jnp.zeros((step * members, span), jnp.bfloat16)
            parts.append(jnp.concatenate([value[step * members :], gap], axis=0))
        return jnp.concatenate(parts, axis=1)

    gain = column(streams * tap_count)
    cot = in_order(in_ref[:, streams], order_there(count)).astype(jnp.float32)
    delayed = [delays(0)]
    query_short = short(0, delayed[0])
    relayed = (cot * query_short).astype(jnp.bfloat16).reshape(rows, span)
    relayed_lags = ahead_by_blocks(relayed)
    backward = lax.dot_general(
        relayed_lags, toeplitz, (((1,), (1,)), ((), ())), preferred_element_type=jnp.float32
    )

    delayed += [delays(1), delays(2)]
    key_short = short(1, delayed[1])
    value_short = short(2, delayed[2])
    gating = (key_short * value_short).astype(jnp.bfloat16).reshape(rows, span)
    gating_parts, filter_parts = [gating], [toeplitz[:, :span]]
    for step in range(1, count):
        gap = jnp.zeros((step * members, span), jnp.bfloat16)
        gating_parts.append(jnp.concatenate([gap, gating[: rows - step * members]], axis=0))
        filter_parts.append(toeplitz[:, step * span : (step + 1) * span])
    forward = jnp.dot(
        jnp.concatenate(gating_parts, axis=1),
        jnp.concatenate(filter_parts, axis=0),
        preferred_element_type=jnp.float32,
    )

    half = span // 2
    flip = (
        lax.broadcasted_iota(jnp.int32, (span, span), 0)
        + lax.broadcasted_iota(jnp.int32, (span, span), 1)
        == span - 1
    ).astype(jnp.bfloat16)
    gating_turned = lax.dot_general(
        flip, gating, (((1,), (1,)), ((), ())), preferred_element_type=jnp.float32
    ).astype(jnp.bfloat16)
    gating_turned = jnp.concatenate([gating_turned[half:], gating_turned[:half]], axis=1)
    ahead = earlier(relayed.reshape(shape), half).reshape(rows, span)
    targets = jnp.concatenate([relayed_lags, ahead_by_blocks(ahead)], axis=0)
    wide_ref[:, :seq_total] = jnp.dot(
        gating_turned, targets, preferred_element_type=jnp.float32
    )
    wide_ref[:, seq_total:] = jnp.zeros((half, span), jnp.float32)

    tap_scale = 1.0 / math.sqrt(seq_total)

    def tokens(value):
        return jnp.concatenate([value[block] for block in range(count)], axis=1)

    def sums(left, right):
        product = lax.dot_general(
            jnp.concatenate(left, axis=0),
            jnp.concatenate(right, axis=0),
            (((1,), (1,)), ((), ())),
            preferred_element_type=jnp.float32,
        )
        same = (
            lax.broadcasted_iota(jnp.int32, product.shape, 0) % members
            == lax.broadcasted_iota(jnp.int32, product.shape, 1) % members
        )
        product = jnp.where(same, product, 0.0).reshape(len(left), members, -1)
        return jnp.sum(product, axis=1) * tap_scale

    tile_ref[...] = jnp.zeros((members, span), jnp.float32)

    def finish(stream, grad_short, first_row, more_left=(), more_right=()):
        moved = [earlier(grad_short, second) for second in range(reach)]
        left = [tokens(value.astype(jnp.bfloat16)) for value in moved] + list(more_left)
        right = [tokens(value) for value in delayed[stream]] + list(more_right)
        totals = sums(left, right)
        tile_ref[first_row : first_row + len(left), : totals.shape[1]] = totals
        total = None
        for place in range(len(delayed[stream])):
            running = None
            for second in range(min(reach, tap_count - reach * place)):
                term = column(stream * tap_count + reach * place + second) * moved[second]
                running = term if running is None else running + term
            running = earlier(running, reach * place)
            total = running if total is None else total + running
        out_ref[:, 1 + stream] = by_member(total.astype(jnp.bfloat16), order_back(count))

    grad_gating = backward.reshape(shape) + gain * relayed.astype(jnp.float32).reshape(shape)
    finish(1, grad_gating * value_short, reach + 1)
    finish(2, grad_gating * key_short, 2 * reach + 1)

    long_out = forward.reshape(shape) + gain * gating.astype(jnp.float32).reshape(shape)
    block_out = (query_short * long_out).astype(jnp.bfloat16)
    out_ref[:, 0] = by_member(block_out, order_back(count))
    finish(
        0, cot * long_out, 0, [tokens(relayed.reshape(shape))], [tokens(gating.reshape(shape))]
    )

    skewed = pltpu.roll(wide_ref[...], span - half + 1, 1, stride=1, stride_axis=0)
    diagonal = jnp.sum(skewed, axis=0, keepdims=True)
    lag_scale = 1.0 / math.sqrt(seq_total * members)
    lag_sums = jnp.concatenate(
        [diagonal[:, step * span : (step + 1) * span] for step in range(1, count + 1)], axis=0
    )
    lag_sums = lag_sums * lag_scale
    tile_ref[:count, half:] = lag_sums[:, half:]
    tile_ref[count:, half:] = pltpu.roll(lag_sums, half, 1)[:, half:]
    out_ref[:, streams + 1] = jnp.broadcast_to(tile_ref[...].astype(jnp.bfloat16)[None], shape)


def unpack_kernel(in_ref, out_ref, grads_ref, taps_ref, skip_ref, lags_ref):
    count, _, members, span = in_ref.shape
    streams, tap_count, chan_width = taps_ref.shape
    reach = 3
    for stream in range(streams + 1):
        block = in_order(in_ref[:, stream], order_back(count)).reshape(count * members, span)
        block = block.astype(jnp.float32)
        flipped = block.T.astype(jnp.bfloat16)
        if stream == 0:
            out_ref[...] = flipped
        else:
            grads_ref[stream - 1] = flipped
    tile = in_order(in_ref[:, streams + 1], order_back(count)).astype(jnp.float32)
    lane = lax.broadcasted_iota(jnp.int32, (1, members // 2, span), 2)
    lags = jnp.where(
        lane < span // 2, pltpu.roll(tile[:, members // 2 :], span // 2, 2), tile[:, : members // 2]
    )
    for step in range(members // 2):
        lags_ref[:, step * span : (step + 1) * span] = lags[:, step]
    lane = lax.broadcasted_iota(jnp.int32, (members, span), 1)
    spread = []
    for place in range(-(-tap_count // reach) + 1):
        total = None
        for group in range(count):
            moved = pltpu.roll(tile[group], (members * (group - place)) % span, 1)
            inside = (lane >= members * group) & (lane < members * (group + 1))
            total = moved if total is None else jnp.where(inside, moved, total)
        spread.append(total)
    first = 0
    for stream in range(streams):
        for place in range(-(-tap_count // reach)):
            taken = min(reach, tap_count - reach * place)
            taps_ref[stream, reach * place : reach * place + taken] = spread[place][
                first : first + taken
            ]
        first += reach + (stream == 0)
    skip_ref[...] = spread[-1][reach : reach + 1]


def by_group(query_in, key_in, value_in, short_taps, long_filters, skip_gain, cotangent):
    tok_rows, chan_width = query_in.shape
    groups, seq_total = long_filters.shape
    streams, tap_count, _ = short_taps.shape
    members = chan_width // groups
    count = groups
    vmem = pl.BlockSpec(memory_space=pltpu.VMEM)
    params = pltpu.CompilerParams(vmem_limit_bytes=32 * 1024 * 1024)
    packed, gain = pl.pallas_call(
        pack_kernel,
        out_shape=(
            jax.ShapeDtypeStruct((count, streams + 1, members, tok_rows), jnp.bfloat16),
            jax.ShapeDtypeStruct((1, chan_width), jnp.float32),
        ),
        in_specs=[pl.BlockSpec(memory_space=pltpu.HBM)] * 5,
        out_specs=(vmem,) * 2,
        scratch_shapes=[
            pltpu.VMEM((streams + 1, tok_rows, chan_width), jnp.bfloat16),
            pltpu.SemaphoreType.DMA((streams + 2,)),
        ],
        compiler_params=params,
        name="pack",
    )(
        *(
            pltpu.with_memory_space_constraint(value, pltpu.HBM)
            for value in (
                query_in, key_in, value_in, cotangent, skip_gain.reshape(1, chan_width)
            )
        )
    )
    packed = lax.all_to_all(
        packed, "seq", 0, 0, tiled=True, axis_index_groups=[order_there(count)]
    )
    results = pl.pallas_call(
        group_kernel,
        out_shape=jax.ShapeDtypeStruct((count, streams + 2, members, tok_rows), jnp.bfloat16),
        in_specs=[vmem] * 4,
        out_specs=vmem,
        scratch_shapes=[
            pltpu.VMEM((chan_width, streams * tap_count + 3), jnp.float32),
            pltpu.VMEM((tok_rows // 2, seq_total + tok_rows), jnp.float32),
            pltpu.VMEM((members, tok_rows), jnp.float32),
        ],
        compiler_params=params,
        name="group",
    )(packed, short_taps, long_filters, gain)
    results = lax.all_to_all(
        results, "seq", 0, 0, tiled=True, axis_index_groups=[order_back(count)]
    )
    block_out, input_grads, tap_grads, skip_grad, filter_grad = pl.pallas_call(
        unpack_kernel,
        out_shape=(
            jax.ShapeDtypeStruct((tok_rows, chan_width), jnp.bfloat16),
            jax.ShapeDtypeStruct((streams, tok_rows, chan_width), jnp.bfloat16),
            jax.ShapeDtypeStruct((streams, tap_count, chan_width), jnp.float32),
            jax.ShapeDtypeStruct((1, chan_width), jnp.float32),
            jax.ShapeDtypeStruct((groups, seq_total), jnp.float32),
        ),
        in_specs=[vmem],
        out_specs=(vmem,) * 5,
        compiler_params=params,
        name="unpack",
    )(results)
    return block_out, input_grads, tap_grads, skip_grad.reshape(chan_width), filter_grad


def plan(query_in, key_in, value_in, short_taps, long_filters, skip_gain, cotangent):
    tok_rows, chan_width = query_in.shape
    groups, seq_total = long_filters.shape
    fits = (
        lax.axis_size("seq") == groups
        and tok_rows == 128
        and chan_width == 128
        and chan_width // groups == 16
        and seq_total == groups * tok_rows
        and short_taps.shape[:2] == (3, 7)
    )
    chosen = by_group if fits else local
    return chosen(query_in, key_in, value_in, short_taps, long_filters, skip_gain, cotangent)


def solution(mesh):
    in_specs = (
        P("seq", "chan"),
        P("seq", "chan"),
        P("seq", "chan"),
        P(None, None, "chan"),
        P("chan", None),
        P("chan"),
        P("seq", "chan"),
    )
    out_specs = (
        P("seq", "chan"),
        P(None, "seq", "chan"),
        P(None, None, "chan"),
        P("chan"),
        P("chan", None),
    )
    return jax.shard_map(plan, mesh=mesh, in_specs=in_specs, out_specs=out_specs, check_vma=False)
```

```python
import functools
import math

import jax
import jax.numpy as jnp
from jax import lax
from jax.experimental import pallas as pl
from jax.experimental.pallas import tpu as pltpu
from jax.sharding import PartitionSpec as P


def from_behind(value, axis, steps):
    count = lax.axis_size(axis)
    initial, last = (max(0, -steps), min(count, count - steps))
    return lax.ppermute(value, axis, [(source, source + steps) for source in range(initial, last)])


def short_forward(extended, weights, rows_here):
    margin = weights.shape[0] - 1
    running = jnp.zeros((rows_here, extended.shape[1]), jnp.float32)
    for offset in range(weights.shape[0]):
        running = (
            running + weights[offset] * extended[margin - offset : margin - offset + rows_here]
        )
    return running


def short_backward(extended, weights, rows_here):
    running = jnp.zeros((rows_here, extended.shape[1]), jnp.float32)
    for offset in range(weights.shape[0]):
        running = running + weights[offset] * extended[offset : offset + rows_here]
    return running


def tap_sums(grad_rows, extended, tap_count, rows_here):
    margin = tap_count - 1
    sums_list = []
    for offset in range(tap_count):
        sums_list.append(
            jnp.sum(grad_rows * extended[margin - offset : margin - offset + rows_here], axis=0)
        )
    return jnp.stack(sums_list)


def hankel(padded, lag_start, height, breadth, seq_total):
    span = height + breadth - 1
    window = lax.dynamic_slice_in_dim(padded, lag_start + seq_total, span, axis=1)
    tiled = jnp.tile(window, (1, height))
    tiled = jnp.pad(tiled, ((0, 0), (0, height)))
    return tiled.reshape(padded.shape[0], height, span + 1)[:, :, :breadth]


def causal_part(padded, source_rows, source_start, target_start, target_count, seq_total):
    breadth = source_rows.shape[0]
    matrix = hankel(
        padded, target_start - source_start - breadth + 1, target_count, breadth, seq_total
    )
    return jnp.einsum("gts,sgc->tgc", matrix, source_rows[::-1], preferred_element_type=jnp.float32)


def anti_part(padded, target_rows, target_start, source_start, source_count, seq_total):
    breadth = target_rows.shape[0]
    matrix = hankel(
        padded, target_start - source_start - source_count + 1, source_count, breadth, seq_total
    )
    return jnp.einsum("gab,bgc->agc", matrix, target_rows, preferred_element_type=jnp.float32)[::-1]


def lag_part(buffer, target_rows, source_rows, target_start, source_start, seq_total):
    height = target_rows.shape[0]
    breadth = source_rows.shape[0]
    groups = target_rows.shape[1]
    padded_source = jnp.pad(source_rows[::-1], ((0, height), (0, 0), (0, 0)))
    products = jnp.einsum(
        "tgc,sgc->gts", target_rows, padded_source, preferred_element_type=jnp.float32
    )
    full_width = height + breadth
    skewed = products.reshape(groups, height * full_width)[:, : height * (full_width - 1)]
    skewed = skewed.reshape(groups, height, full_width - 1)
    diagonal = jnp.sum(skewed, axis=1)
    position = target_start - source_start - breadth + 1 + seq_total
    current = lax.dynamic_slice_in_dim(buffer, position, full_width - 1, axis=1)
    return lax.dynamic_update_slice_in_dim(buffer, current + diagonal, position, axis=1)


def local(query_in, key_in, value_in, short_taps, long_filters, skip_gain, cotangent):
    tok_rows, chan_width = query_in.shape
    groups, seq_total = long_filters.shape
    members = chan_width // groups
    tap_count = short_taps.shape[1]
    margin = tap_count - 1
    device = lax.axis_index("seq")
    own_start = device * tok_rows
    rim_rows = jnp.stack(
        [query_in[tok_rows - margin :], key_in[tok_rows - margin :], value_in[tok_rows - margin :]]
    )
    before = from_behind(rim_rows, "seq", 1)
    streams = [query_in, key_in, value_in]
    extended = [
        jnp.concatenate([before[stream], streams[stream]]).astype(jnp.float32)
        for stream in range(3)
    ]
    query_short = short_forward(extended[0], short_taps[0], tok_rows)
    key_short = short_forward(extended[1], short_taps[1], tok_rows)
    value_short = short_forward(extended[2], short_taps[2], tok_rows)
    gating = (key_short * value_short).astype(jnp.bfloat16)
    relayed = (cotangent.astype(jnp.float32) * query_short).astype(jnp.bfloat16)
    gating_wide = gating.astype(jnp.float32)
    relayed_wide = relayed.astype(jnp.float32)
    gating_groups = gating.reshape(tok_rows, groups, members)
    relayed_groups = relayed.reshape(tok_rows, groups, members)
    padded = jnp.concatenate([jnp.zeros((groups, seq_total), jnp.bfloat16), long_filters], axis=1)
    lag_buffer = jnp.zeros((groups, 2 * seq_total), jnp.float32)
    zeros_out = jnp.zeros((tok_rows, groups, members), jnp.float32)

    def target_pair(distance):
        return distance < 0

    totals = (zeros_out, lag_buffer)
    shard_rows = lax.all_gather(gating, "seq", axis=0, tiled=True)
    piece_rows = shard_rows.shape[0]
    step_rows = min(piece_rows, tok_rows)
    pieces = shard_rows.reshape(piece_rows // step_rows, step_rows, groups, members)

    def forward_visit_block(carried, element):
        position, rows_block = element
        source_start = position * step_rows

        def forward_active(partial_value):
            output_part, buffer = partial_value
            output_part = output_part + causal_part(
                padded, rows_block, source_start, own_start, tok_rows, seq_total
            )
            distance = device - source_start // tok_rows
            buffer = lax.cond(
                target_pair(distance),
                lambda held: lag_part(
                    held, relayed_groups, rows_block, own_start, source_start, seq_total
                ),
                lambda held: held,
                buffer,
            )
            return (output_part, buffer)

        carried = lax.cond(
            source_start < own_start + tok_rows,
            forward_active,
            lambda partial_value: partial_value,
            carried,
        )
        return (carried, None)

    totals, ignored = lax.scan(
        forward_visit_block, totals, (jnp.arange(piece_rows // step_rows, dtype=jnp.int32), pieces)
    )
    output_part, lag_buffer = totals
    output_sum = output_part.reshape(tok_rows, chan_width)
    totals = (zeros_out, lag_buffer)
    shard_rows = lax.all_gather(relayed, "seq", axis=0, tiled=True)
    piece_rows = shard_rows.shape[0]
    backward_step_rows = min(piece_rows, tok_rows)
    pieces = shard_rows.reshape(
        piece_rows // backward_step_rows, backward_step_rows, groups, members
    )

    def backward_visit_block(carried, element):
        position, rows_block = element
        target_start = position * backward_step_rows

        def backward_active(partial_value):
            grad_part, buffer = partial_value
            grad_part = grad_part + anti_part(
                padded, rows_block, target_start, own_start, tok_rows, seq_total
            )
            distance = target_start // tok_rows - device
            buffer = lax.cond(
                target_pair(distance),
                lambda held: held,
                lambda held: lag_part(
                    held, rows_block, gating_groups, target_start, own_start, seq_total
                ),
                buffer,
            )
            return (grad_part, buffer)

        carried = lax.cond(
            target_start + backward_step_rows > own_start,
            backward_active,
            lambda partial_value: partial_value,
            carried,
        )
        return (carried, None)

    totals, ignored = lax.scan(
        backward_visit_block,
        totals,
        (jnp.arange(piece_rows // backward_step_rows, dtype=jnp.int32), pieces),
    )
    grad_part, lag_buffer = totals
    grad_sum = grad_part.reshape(tok_rows, chan_width)
    lag_local = lag_buffer[:, seq_total:]
    long_out = output_sum + skip_gain * gating_wide
    block_out = (query_short * long_out).astype(jnp.bfloat16)
    grad_gating = grad_sum + skip_gain * relayed_wide
    cot_wide = cotangent.astype(jnp.float32)
    grad_shorts = [cot_wide * long_out, grad_gating * value_short, grad_gating * key_short]
    lead_rows = jnp.stack([grad_shorts[stream][:margin] for stream in range(3)])
    after = from_behind(lead_rows, "seq", -1)
    input_grads = jnp.stack(
        [
            short_backward(
                jnp.concatenate([grad_shorts[stream], after[stream]]), short_taps[stream], tok_rows
            )
            for stream in range(3)
        ]
    ).astype(jnp.bfloat16)
    tap_local = jnp.stack(
        [
            tap_sums(grad_shorts[stream], extended[stream], tap_count, tok_rows)
            for stream in range(3)
        ]
    )
    skip_local = jnp.sum(relayed_wide * gating_wide, axis=0)
    lag_total, tap_total, skip_total = lax.psum((lag_local, tap_local, skip_local), "seq")
    tap_scale = 1.0 / math.sqrt(seq_total)
    lag_scale = 1.0 / math.sqrt(seq_total * members)
    return (
        block_out,
        input_grads,
        tap_total * tap_scale,
        skip_total * tap_scale,
        lag_total * lag_scale,
    )


def order_there(count):
    return [(count // 2 + 1 - 2 * step) % count for step in range(count // 2)] + [
        (count // 2 - 2 * step) % count for step in range(count // 2)
    ]


def order_back(count):
    return order_there(count)


def in_order(value, order):
    return jnp.stack([value[order.index(device)] for device in range(len(order))])


def by_member(value, order):
    return jnp.stack([value[device] for device in order])


def pack_kernel(
    query_ref, key_ref, value_ref, cot_ref, skip_ref, out_ref, gain_ref, stream_buf, sems
):
    count, streams, members, tok_rows = out_ref.shape
    moves = [
        pltpu.make_async_copy(ref, stream_buf.at[stream], sems.at[stream])
        for stream, ref in enumerate((query_ref, key_ref, value_ref, cot_ref))
    ]
    moves.append(pltpu.make_async_copy(skip_ref, gain_ref, sems.at[streams]))
    for move in moves:
        move.start()
    for stream in range(streams):
        moves[stream].wait()
        flipped = stream_buf[stream].astype(jnp.float32).T.astype(jnp.bfloat16)
        flipped = flipped.reshape(count, members, tok_rows)
        out_ref[:, stream] = by_member(flipped, order_there(count))
    moves[streams].wait()


def group_kernel(
    in_ref, taps_ref, filters_ref, gain_ref, out_ref, table_ref, wide_ref, tile_ref
):
    count, _, members, span = in_ref.shape
    groups, seq_total = filters_ref.shape
    streams, tap_count, chan_width = taps_ref.shape
    rows = count * members
    mine = lax.axis_index("seq")
    shape = (count, members, span)
    lane = lax.broadcasted_iota(jnp.int32, shape, 2)
    reach = 3

    def later(value, steps):
        if steps == 0:
            return value
        turned = pltpu.roll(value, steps, 2)
        before = jnp.concatenate([jnp.zeros_like(turned[:1]), turned[:-1]], axis=0)
        return jnp.where(lane >= steps, turned, before)

    def earlier(value, steps):
        if steps == 0:
            return value
        turned = pltpu.roll(value, span - steps, 2)
        after = jnp.concatenate([turned[1:], jnp.zeros_like(turned[:1])], axis=0)
        return jnp.where(lane < span - steps, turned, after)

    table = jnp.concatenate(
        [taps_ref[stream] for stream in range(streams)]
        + [gain_ref[...], jnp.zeros((2, chan_width), jnp.float32)],
        axis=0,
    )
    table_ref[...] = table.T
    params = table_ref[pl.ds(pl.multiple_of(mine * members, members), members), :]

    def column(index):
        return jnp.broadcast_to(params[:, index : index + 1], (members, span))[None]

    chosen = lax.broadcasted_iota(jnp.int32, (groups, 1), 0) == mine
    filter_row = jnp.sum(
        jnp.where(chosen, filters_ref[...].astype(jnp.float32), 0.0), axis=0, keepdims=True
    )
    filter_row = jnp.concatenate([filter_row, jnp.zeros((1, span), jnp.float32)], axis=1)
    spread = jnp.broadcast_to(filter_row, (members, seq_total + span))
    first_rows = pltpu.roll(spread, 0, 1, stride=1, stride_axis=0).astype(jnp.bfloat16)
    row_parts = [first_rows] + [
        pltpu.roll(first_rows, first, 1) for first in range(members, span, members)
    ]
    toeplitz = jnp.concatenate(row_parts, axis=0)[:, :seq_total]

    def delays(stream):
        value = in_order(in_ref[:, stream], order_there(count))
        return [later(value, first) for first in range(0, tap_count, reach)]

    def short(stream, values):
        total = None
        for second in range(reach):
            running = None
            for first in range(second, tap_count, reach):
                value = values[first // reach].astype(jnp.float32)
                term = column(stream * tap_count + first) * value
                running = term if running is None else running + term
            running = later(running, second)
            total = running if total is None else total + running
        return total

    def ahead_by_blocks(value):
        parts = [value]
        for step in range(1, count):
            gap = jnp.zeros((step * members, span), jnp.bfloat16)
            parts.append(jnp.concatenate([value[step * members :], gap], axis=0))
        return jnp.concatenate(parts, axis=1)

    gain = column(streams * tap_count)
    cot = in_order(in_ref[:, streams], order_there(count)).astype(jnp.float32)
    delayed = [delays(0)]
    query_short = short(0, delayed[0])
    relayed = (cot * query_short).astype(jnp.bfloat16).reshape(rows, span)
    relayed_lags = ahead_by_blocks(relayed)
    backward = lax.dot_general(
        relayed_lags, toeplitz, (((1,), (1,)), ((), ())), preferred_element_type=jnp.float32
    )

    delayed += [delays(1), delays(2)]
    key_short = short(1, delayed[1])
    value_short = short(2, delayed[2])
    gating = (key_short * value_short).astype(jnp.bfloat16).reshape(rows, span)
    gating_parts, filter_parts = [gating], [toeplitz[:, :span]]
    for step in range(1, count):
        gap = jnp.zeros((step * members, span), jnp.bfloat16)
        gating_parts.append(jnp.concatenate([gap, gating[: rows - step * members]], axis=0))
        filter_parts.append(toeplitz[:, step * span : (step + 1) * span])
    forward = jnp.dot(
        jnp.concatenate(gating_parts, axis=1),
        jnp.concatenate(filter_parts, axis=0),
        preferred_element_type=jnp.float32,
    )

    half = span // 2
    flip = (
        lax.broadcasted_iota(jnp.int32, (span, span), 0)
        + lax.broadcasted_iota(jnp.int32, (span, span), 1)
        == span - 1
    ).astype(jnp.bfloat16)
    gating_turned = lax.dot_general(
        flip, gating, (((1,), (1,)), ((), ())), preferred_element_type=jnp.float32
    ).astype(jnp.bfloat16)
    gating_turned = jnp.concatenate([gating_turned[half:], gating_turned[:half]], axis=1)
    ahead = earlier(relayed.reshape(shape), half).reshape(rows, span)
    targets = jnp.concatenate([relayed_lags, ahead_by_blocks(ahead)], axis=0)
    wide_ref[:, :seq_total] = jnp.dot(
        gating_turned, targets, preferred_element_type=jnp.float32
    )
    wide_ref[:, seq_total:] = jnp.zeros((half, span), jnp.float32)

    tap_scale = 1.0 / math.sqrt(seq_total)

    def tokens(value):
        return jnp.concatenate([value[block] for block in range(count)], axis=1)

    def sums(left, right):
        product = lax.dot_general(
            jnp.concatenate(left, axis=0),
            jnp.concatenate(right, axis=0),
            (((1,), (1,)), ((), ())),
            preferred_element_type=jnp.float32,
        )
        same = (
            lax.broadcasted_iota(jnp.int32, product.shape, 0) % members
            == lax.broadcasted_iota(jnp.int32, product.shape, 1) % members
        )
        product = jnp.where(same, product, 0.0).reshape(len(left), members, -1)
        return jnp.sum(product, axis=1) * tap_scale

    tile_ref[...] = jnp.zeros((members, span), jnp.float32)

    def finish(stream, grad_short, first_row, more_left=(), more_right=()):
        moved = [earlier(grad_short, second) for second in range(reach)]
        left = [tokens(value.astype(jnp.bfloat16)) for value in moved] + list(more_left)
        right = [tokens(value) for value in delayed[stream]] + list(more_right)
        totals = sums(left, right)
        tile_ref[first_row : first_row + len(left), : totals.shape[1]] = totals
        total = None
        for place in range(len(delayed[stream])):
            running = None
            for second in range(min(reach, tap_count - reach * place)):
                term = column(stream * tap_count + reach * place + second) * moved[second]
                running = term if running is None else running + term
            running = earlier(running, reach * place)
            total = running if total is None else total + running
        out_ref[:, 1 + stream] = by_member(total.astype(jnp.bfloat16), order_back(count))

    grad_gating = backward.reshape(shape) + gain * relayed.astype(jnp.float32).reshape(shape)
    finish(1, grad_gating * value_short, reach + 1)
    finish(2, grad_gating * key_short, 2 * reach + 1)

    long_out = forward.reshape(shape) + gain * gating.astype(jnp.float32).reshape(shape)
    block_out = (query_short * long_out).astype(jnp.bfloat16)
    out_ref[:, 0] = by_member(block_out, order_back(count))
    finish(
        0, cot * long_out, 0, [tokens(relayed.reshape(shape))], [tokens(gating.reshape(shape))]
    )

    skewed = pltpu.roll(wide_ref[...], span - half + 1, 1, stride=1, stride_axis=0)
    diagonal = jnp.sum(skewed, axis=0, keepdims=True)
    lag_scale = 1.0 / math.sqrt(seq_total * members)
    lag_sums = jnp.concatenate(
        [diagonal[:, step * span : (step + 1) * span] for step in range(1, count + 1)], axis=0
    )
    lag_sums = lag_sums * lag_scale
    tile_ref[:count, half:] = lag_sums[:, half:]
    tile_ref[count:, half:] = pltpu.roll(lag_sums, half, 1)[:, half:]
    out_ref[:, streams + 1] = jnp.broadcast_to(tile_ref[...].astype(jnp.bfloat16)[None], shape)


def unpack_kernel(in_ref, out_ref, grads_ref, taps_ref, skip_ref, lags_ref):
    count, _, members, span = in_ref.shape
    streams, tap_count, chan_width = taps_ref.shape
    reach = 3
    for stream in range(streams + 1):
        block = in_order(in_ref[:, stream], order_back(count)).reshape(count * members, span)
        block = block.astype(jnp.float32)
        flipped = block.T.astype(jnp.bfloat16)
        if stream == 0:
            out_ref[...] = flipped
        else:
            grads_ref[stream - 1] = flipped
    tile = in_order(in_ref[:, streams + 1], order_back(count)).astype(jnp.float32)
    lane = lax.broadcasted_iota(jnp.int32, (1, members // 2, span), 2)
    lags = jnp.where(
        lane < span // 2, pltpu.roll(tile[:, members // 2 :], span // 2, 2), tile[:, : members // 2]
    )
    for step in range(members // 2):
        lags_ref[:, step * span : (step + 1) * span] = lags[:, step]
    lane = lax.broadcasted_iota(jnp.int32, (members, span), 1)
    spread = []
    for place in range(-(-tap_count // reach) + 1):
        total = None
        for group in range(count):
            moved = pltpu.roll(tile[group], (members * (group - place)) % span, 1)
            inside = (lane >= members * group) & (lane < members * (group + 1))
            total = moved if total is None else jnp.where(inside, moved, total)
        spread.append(total)
    first = 0
    for stream in range(streams):
        for place in range(-(-tap_count // reach)):
            taken = min(reach, tap_count - reach * place)
            taps_ref[stream, reach * place : reach * place + taken] = spread[place][
                first : first + taken
            ]
        first += reach + (stream == 0)
    skip_ref[...] = spread[-1][reach : reach + 1]


def by_group(query_in, key_in, value_in, short_taps, long_filters, skip_gain, cotangent):
    tok_rows, chan_width = query_in.shape
    groups, seq_total = long_filters.shape
    streams, tap_count, _ = short_taps.shape
    members = chan_width // groups
    count = groups
    vmem = pl.BlockSpec(memory_space=pltpu.VMEM)
    params = pltpu.CompilerParams(vmem_limit_bytes=32 * 1024 * 1024)
    packed, gain = pl.pallas_call(
        pack_kernel,
        out_shape=(
            jax.ShapeDtypeStruct((count, streams + 1, members, tok_rows), jnp.bfloat16),
            jax.ShapeDtypeStruct((1, chan_width), jnp.float32),
        ),
        in_specs=[pl.BlockSpec(memory_space=pltpu.HBM)] * 5,
        out_specs=(vmem,) * 2,
        scratch_shapes=[
            pltpu.VMEM((streams + 1, tok_rows, chan_width), jnp.bfloat16),
            pltpu.SemaphoreType.DMA((streams + 2,)),
        ],
        compiler_params=params,
        name="pack",
    )(
        *(
            pltpu.with_memory_space_constraint(value, pltpu.HBM)
            for value in (
                query_in, key_in, value_in, cotangent, skip_gain.reshape(1, chan_width)
            )
        )
    )
    packed = lax.all_to_all(
        packed, "seq", 0, 0, tiled=True, axis_index_groups=[order_there(count)]
    )
    results = pl.pallas_call(
        group_kernel,
        out_shape=jax.ShapeDtypeStruct((count, streams + 2, members, tok_rows), jnp.bfloat16),
        in_specs=[vmem] * 4,
        out_specs=vmem,
        scratch_shapes=[
            pltpu.VMEM((chan_width, streams * tap_count + 3), jnp.float32),
            pltpu.VMEM((tok_rows // 2, seq_total + tok_rows), jnp.float32),
            pltpu.VMEM((members, tok_rows), jnp.float32),
        ],
        compiler_params=params,
        name="group",
    )(packed, short_taps, long_filters, gain)
    results = lax.all_to_all(
        results, "seq", 0, 0, tiled=True, axis_index_groups=[order_back(count)]
    )
    block_out, input_grads, tap_grads, skip_grad, filter_grad = pl.pallas_call(
        unpack_kernel,
        out_shape=(
            jax.ShapeDtypeStruct((tok_rows, chan_width), jnp.bfloat16),
            jax.ShapeDtypeStruct((streams, tok_rows, chan_width), jnp.bfloat16),
            jax.ShapeDtypeStruct((streams, tap_count, chan_width), jnp.float32),
            jax.ShapeDtypeStruct((1, chan_width), jnp.float32),
            jax.ShapeDtypeStruct((groups, seq_total), jnp.float32),
        ),
        in_specs=[vmem],
        out_specs=(vmem,) * 5,
        compiler_params=params,
        name="unpack",
    )(results)
    return block_out, input_grads, tap_grads, skip_grad.reshape(chan_width), filter_grad


def plan(query_in, key_in, value_in, short_taps, long_filters, skip_gain, cotangent):
    tok_rows, chan_width = query_in.shape
    groups, seq_total = long_filters.shape
    fits = (
        lax.axis_size("seq") == groups
        and tok_rows == 128
        and chan_width == 128
        and chan_width // groups == 16
        and seq_total == groups * tok_rows
        and short_taps.shape[:2] == (3, 7)
    )
    chosen = by_group if fits else local
    return chosen(query_in, key_in, value_in, short_taps, long_filters, skip_gain, cotangent)


def solution(mesh):
    in_specs = (
        P("seq", "chan"),
        P("seq", "chan"),
        P("seq", "chan"),
        P(None, None, "chan"),
        P("chan", None),
        P("chan"),
        P("seq", "chan"),
    )
    out_specs = (
        P("seq", "chan"),
        P(None, "seq", "chan"),
        P(None, None, "chan"),
        P("chan"),
        P("chan", None),
    )
    return jax.shard_map(plan, mesh=mesh, in_specs=in_specs, out_specs=out_specs, check_vma=False)
```

```python
import functools
import math

import jax
import jax.numpy as jnp
from jax import lax
from jax.experimental import pallas as pl
from jax.experimental.pallas import tpu as pltpu
from jax.sharding import PartitionSpec as P


def from_behind(value, axis, steps):
    count = lax.axis_size(axis)
    initial, last = (max(0, -steps), min(count, count - steps))
    return lax.ppermute(value, axis, [(source, source + steps) for source in range(initial, last)])


def short_forward(extended, weights, rows_here):
    margin = weights.shape[0] - 1
    running = jnp.zeros((rows_here, extended.shape[1]), jnp.float32)
    for offset in range(weights.shape[0]):
        running = (
            running + weights[offset] * extended[margin - offset : margin - offset + rows_here]
        )
    return running


def short_backward(extended, weights, rows_here):
    running = jnp.zeros((rows_here, extended.shape[1]), jnp.float32)
    for offset in range(weights.shape[0]):
        running = running + weights[offset] * extended[offset : offset + rows_here]
    return running


def tap_sums(grad_rows, extended, tap_count, rows_here):
    margin = tap_count - 1
    sums_list = []
    for offset in range(tap_count):
        sums_list.append(
            jnp.sum(grad_rows * extended[margin - offset : margin - offset + rows_here], axis=0)
        )
    return jnp.stack(sums_list)


def hankel(padded, lag_start, height, breadth, seq_total):
    span = height + breadth - 1
    window = lax.dynamic_slice_in_dim(padded, lag_start + seq_total, span, axis=1)
    tiled = jnp.tile(window, (1, height))
    tiled = jnp.pad(tiled, ((0, 0), (0, height)))
    return tiled.reshape(padded.shape[0], height, span + 1)[:, :, :breadth]


def causal_part(padded, source_rows, source_start, target_start, target_count, seq_total):
    breadth = source_rows.shape[0]
    matrix = hankel(
        padded, target_start - source_start - breadth + 1, target_count, breadth, seq_total
    )
    return jnp.einsum("gts,sgc->tgc", matrix, source_rows[::-1], preferred_element_type=jnp.float32)


def anti_part(padded, target_rows, target_start, source_start, source_count, seq_total):
    breadth = target_rows.shape[0]
    matrix = hankel(
        padded, target_start - source_start - source_count + 1, source_count, breadth, seq_total
    )
    return jnp.einsum("gab,bgc->agc", matrix, target_rows, preferred_element_type=jnp.float32)[::-1]


def lag_part(buffer, target_rows, source_rows, target_start, source_start, seq_total):
    height = target_rows.shape[0]
    breadth = source_rows.shape[0]
    groups = target_rows.shape[1]
    padded_source = jnp.pad(source_rows[::-1], ((0, height), (0, 0), (0, 0)))
    products = jnp.einsum(
        "tgc,sgc->gts", target_rows, padded_source, preferred_element_type=jnp.float32
    )
    full_width = height + breadth
    skewed = products.reshape(groups, height * full_width)[:, : height * (full_width - 1)]
    skewed = skewed.reshape(groups, height, full_width - 1)
    diagonal = jnp.sum(skewed, axis=1)
    position = target_start - source_start - breadth + 1 + seq_total
    current = lax.dynamic_slice_in_dim(buffer, position, full_width - 1, axis=1)
    return lax.dynamic_update_slice_in_dim(buffer, current + diagonal, position, axis=1)


def local(query_in, key_in, value_in, short_taps, long_filters, skip_gain, cotangent):
    tok_rows, chan_width = query_in.shape
    groups, seq_total = long_filters.shape
    members = chan_width // groups
    tap_count = short_taps.shape[1]
    margin = tap_count - 1
    device = lax.axis_index("seq")
    own_start = device * tok_rows
    rim_rows = jnp.stack(
        [query_in[tok_rows - margin :], key_in[tok_rows - margin :], value_in[tok_rows - margin :]]
    )
    before = from_behind(rim_rows, "seq", 1)
    streams = [query_in, key_in, value_in]
    extended = [
        jnp.concatenate([before[stream], streams[stream]]).astype(jnp.float32)
        for stream in range(3)
    ]
    query_short = short_forward(extended[0], short_taps[0], tok_rows)
    key_short = short_forward(extended[1], short_taps[1], tok_rows)
    value_short = short_forward(extended[2], short_taps[2], tok_rows)
    gating = (key_short * value_short).astype(jnp.bfloat16)
    relayed = (cotangent.astype(jnp.float32) * query_short).astype(jnp.bfloat16)
    gating_wide = gating.astype(jnp.float32)
    relayed_wide = relayed.astype(jnp.float32)
    gating_groups = gating.reshape(tok_rows, groups, members)
    relayed_groups = relayed.reshape(tok_rows, groups, members)
    padded = jnp.concatenate([jnp.zeros((groups, seq_total), jnp.bfloat16), long_filters], axis=1)
    lag_buffer = jnp.zeros((groups, 2 * seq_total), jnp.float32)
    zeros_out = jnp.zeros((tok_rows, groups, members), jnp.float32)

    def target_pair(distance):
        return distance < 0

    totals = (zeros_out, lag_buffer)
    shard_rows = lax.all_gather(gating, "seq", axis=0, tiled=True)
    piece_rows = shard_rows.shape[0]
    step_rows = min(piece_rows, tok_rows)
    pieces = shard_rows.reshape(piece_rows // step_rows, step_rows, groups, members)

    def forward_visit_block(carried, element):
        position, rows_block = element
        source_start = position * step_rows

        def forward_active(partial_value):
            output_part, buffer = partial_value
            output_part = output_part + causal_part(
                padded, rows_block, source_start, own_start, tok_rows, seq_total
            )
            distance = device - source_start // tok_rows
            buffer = lax.cond(
                target_pair(distance),
                lambda held: lag_part(
                    held, relayed_groups, rows_block, own_start, source_start, seq_total
                ),
                lambda held: held,
                buffer,
            )
            return (output_part, buffer)

        carried = lax.cond(
            source_start < own_start + tok_rows,
            forward_active,
            lambda partial_value: partial_value,
            carried,
        )
        return (carried, None)

    totals, ignored = lax.scan(
        forward_visit_block, totals, (jnp.arange(piece_rows // step_rows, dtype=jnp.int32), pieces)
    )
    output_part, lag_buffer = totals
    output_sum = output_part.reshape(tok_rows, chan_width)
    totals = (zeros_out, lag_buffer)
    shard_rows = lax.all_gather(relayed, "seq", axis=0, tiled=True)
    piece_rows = shard_rows.shape[0]
    backward_step_rows = min(piece_rows, tok_rows)
    pieces = shard_rows.reshape(
        piece_rows // backward_step_rows, backward_step_rows, groups, members
    )

    def backward_visit_block(carried, element):
        position, rows_block = element
        target_start = position * backward_step_rows

        def backward_active(partial_value):
            grad_part, buffer = partial_value
            grad_part = grad_part + anti_part(
                padded, rows_block, target_start, own_start, tok_rows, seq_total
            )
            distance = target_start // tok_rows - device
            buffer = lax.cond(
                target_pair(distance),
                lambda held: held,
                lambda held: lag_part(
                    held, rows_block, gating_groups, target_start, own_start, seq_total
                ),
                buffer,
            )
            return (grad_part, buffer)

        carried = lax.cond(
            target_start + backward_step_rows > own_start,
            backward_active,
            lambda partial_value: partial_value,
            carried,
        )
        return (carried, None)

    totals, ignored = lax.scan(
        backward_visit_block,
        totals,
        (jnp.arange(piece_rows // backward_step_rows, dtype=jnp.int32), pieces),
    )
    grad_part, lag_buffer = totals
    grad_sum = grad_part.reshape(tok_rows, chan_width)
    lag_local = lag_buffer[:, seq_total:]
    long_out = output_sum + skip_gain * gating_wide
    block_out = (query_short * long_out).astype(jnp.bfloat16)
    grad_gating = grad_sum + skip_gain * relayed_wide
    cot_wide = cotangent.astype(jnp.float32)
    grad_shorts = [cot_wide * long_out, grad_gating * value_short, grad_gating * key_short]
    lead_rows = jnp.stack([grad_shorts[stream][:margin] for stream in range(3)])
    after = from_behind(lead_rows, "seq", -1)
    input_grads = jnp.stack(
        [
            short_backward(
                jnp.concatenate([grad_shorts[stream], after[stream]]), short_taps[stream], tok_rows
            )
            for stream in range(3)
        ]
    ).astype(jnp.bfloat16)
    tap_local = jnp.stack(
        [
            tap_sums(grad_shorts[stream], extended[stream], tap_count, tok_rows)
            for stream in range(3)
        ]
    )
    skip_local = jnp.sum(relayed_wide * gating_wide, axis=0)
    lag_total, tap_total, skip_total = lax.psum((lag_local, tap_local, skip_local), "seq")
    tap_scale = 1.0 / math.sqrt(seq_total)
    lag_scale = 1.0 / math.sqrt(seq_total * members)
    return (
        block_out,
        input_grads,
        tap_total * tap_scale,
        skip_total * tap_scale,
        lag_total * lag_scale,
    )


def order_there(count):
    return [(count // 2 + 1 - 2 * step) % count for step in range(count // 2)] + [
        (count // 2 - 2 * step) % count for step in range(count // 2)
    ]


def order_back(count):
    return [(count // 2 + 1 - step) % count for step in range(count)]


def in_order(value, order):
    return jnp.stack([value[order.index(device)] for device in range(len(order))])


def by_member(value, order):
    return jnp.stack([value[device] for device in order])


def pack_kernel(
    query_ref, key_ref, value_ref, cot_ref, skip_ref, out_ref, gain_ref, stream_buf, sems
):
    count, streams, members, tok_rows = out_ref.shape
    moves = [
        pltpu.make_async_copy(ref, stream_buf.at[stream], sems.at[stream])
        for stream, ref in enumerate((query_ref, key_ref, value_ref, cot_ref))
    ]
    moves.append(pltpu.make_async_copy(skip_ref, gain_ref, sems.at[streams]))
    for move in moves:
        move.start()
    for stream in range(streams):
        moves[stream].wait()
        flipped = stream_buf[stream].astype(jnp.float32).T.astype(jnp.bfloat16)
        flipped = flipped.reshape(count, members, tok_rows)
        out_ref[:, stream] = by_member(flipped, order_there(count))
    moves[streams].wait()


def group_kernel(
    in_ref, taps_ref, filters_ref, gain_ref, out_ref, table_ref, wide_ref, tile_ref
):
    count, _, members, span = in_ref.shape
    groups, seq_total = filters_ref.shape
    streams, tap_count, chan_width = taps_ref.shape
    rows = count * members
    mine = lax.axis_index("seq")
    shape = (count, members, span)
    lane = lax.broadcasted_iota(jnp.int32, shape, 2)
    reach = 3

    def later(value, steps):
        if steps == 0:
            return value
        turned = pltpu.roll(value, steps, 2)
        before = jnp.concatenate([jnp.zeros_like(turned[:1]), turned[:-1]], axis=0)
        return jnp.where(lane >= steps, turned, before)

    def earlier(value, steps):
        if steps == 0:
            return value
        turned = pltpu.roll(value, span - steps, 2)
        after = jnp.concatenate([turned[1:], jnp.zeros_like(turned[:1])], axis=0)
        return jnp.where(lane < span - steps, turned, after)

    table = jnp.concatenate(
        [taps_ref[stream] for stream in range(streams)]
        + [gain_ref[...], jnp.zeros((2, chan_width), jnp.float32)],
        axis=0,
    )
    table_ref[...] = table.T
    params = table_ref[pl.ds(pl.multiple_of(mine * members, members), members), :]

    def column(index):
        return jnp.broadcast_to(params[:, index : index + 1], (members, span))[None]

    chosen = lax.broadcasted_iota(jnp.int32, (groups, 1), 0) == mine
    filter_row = jnp.sum(
        jnp.where(chosen, filters_ref[...].astype(jnp.float32), 0.0), axis=0, keepdims=True
    )
    filter_row = jnp.concatenate([filter_row, jnp.zeros((1, span), jnp.float32)], axis=1)
    spread = jnp.broadcast_to(filter_row, (members, seq_total + span))
    first_rows = pltpu.roll(spread, 0, 1, stride=1, stride_axis=0).astype(jnp.bfloat16)
    row_parts = [first_rows] + [
        pltpu.roll(first_rows, first, 1) for first in range(members, span, members)
    ]
    toeplitz = jnp.concatenate(row_parts, axis=0)[:, :seq_total]

    def delays(stream):
        value = in_order(in_ref[:, stream], order_there(count))
        return [later(value, first) for first in range(0, tap_count, reach)]

    def short(stream, values):
        total = None
        for second in range(reach):
            running = None
            for first in range(second, tap_count, reach):
                value = values[first // reach].astype(jnp.float32)
                term = column(stream * tap_count + first) * value
                running = term if running is None else running + term
            running = later(running, second)
            total = running if total is None else total + running
        return total

    def ahead_by_blocks(value):
        parts = [value]
        for step in range(1, count):
            gap = jnp.zeros((step * members, span), jnp.bfloat16)
            parts.append(jnp.concatenate([value[step * members :], gap], axis=0))
        return jnp.concatenate(parts, axis=1)

    gain = column(streams * tap_count)
    cot = in_order(in_ref[:, streams], order_there(count)).astype(jnp.float32)
    delayed = [delays(0)]
    query_short = short(0, delayed[0])
    relayed = (cot * query_short).astype(jnp.bfloat16).reshape(rows, span)
    relayed_lags = ahead_by_blocks(relayed)
    backward = lax.dot_general(
        relayed_lags, toeplitz, (((1,), (1,)), ((), ())), preferred_element_type=jnp.float32
    )

    delayed += [delays(1), delays(2)]
    key_short = short(1, delayed[1])
    value_short = short(2, delayed[2])
    gating = (key_short * value_short).astype(jnp.bfloat16).reshape(rows, span)
    gating_parts, filter_parts = [gating], [toeplitz[:, :span]]
    for step in range(1, count):
        gap = jnp.zeros((step * members, span), jnp.bfloat16)
        gating_parts.append(jnp.concatenate([gap, gating[: rows - step * members]], axis=0))
        filter_parts.append(toeplitz[:, step * span : (step + 1) * span])
    forward = jnp.dot(
        jnp.concatenate(gating_parts, axis=1),
        jnp.concatenate(filter_parts, axis=0),
        preferred_element_type=jnp.float32,
    )

    half = span // 2
    flip = (
        lax.broadcasted_iota(jnp.int32, (span, span), 0)
        + lax.broadcasted_iota(jnp.int32, (span, span), 1)
        == span - 1
    ).astype(jnp.bfloat16)
    gating_turned = lax.dot_general(
        flip, gating, (((1,), (1,)), ((), ())), preferred_element_type=jnp.float32
    ).astype(jnp.bfloat16)
    gating_turned = jnp.concatenate([gating_turned[half:], gating_turned[:half]], axis=1)
    ahead = earlier(relayed.reshape(shape), half).reshape(rows, span)
    targets = jnp.concatenate([relayed_lags, ahead_by_blocks(ahead)], axis=0)
    wide_ref[:, :seq_total] = jnp.dot(
        gating_turned, targets, preferred_element_type=jnp.float32
    )
    wide_ref[:, seq_total:] = jnp.zeros((half, span), jnp.float32)

    tap_scale = 1.0 / math.sqrt(seq_total)

    def tokens(value):
        return jnp.concatenate([value[block] for block in range(count)], axis=1)

    def sums(left, right):
        product = lax.dot_general(
            jnp.concatenate(left, axis=0),
            jnp.concatenate(right, axis=0),
            (((1,), (1,)), ((), ())),
            preferred_element_type=jnp.float32,
        )
        same = (
            lax.broadcasted_iota(jnp.int32, product.shape, 0) % members
            == lax.broadcasted_iota(jnp.int32, product.shape, 1) % members
        )
        product = jnp.where(same, product, 0.0).reshape(len(left), members, -1)
        return jnp.sum(product, axis=1) * tap_scale

    tile_ref[...] = jnp.zeros((members, span), jnp.float32)

    def finish(stream, grad_short, first_row, more_left=(), more_right=()):
        moved = [earlier(grad_short, second) for second in range(reach)]
        left = [tokens(value.astype(jnp.bfloat16)) for value in moved] + list(more_left)
        right = [tokens(value) for value in delayed[stream]] + list(more_right)
        totals = sums(left, right)
        tile_ref[first_row : first_row + len(left), : totals.shape[1]] = totals
        total = None
        for place in range(len(delayed[stream])):
            running = None
            for second in range(min(reach, tap_count - reach * place)):
                term = column(stream * tap_count + reach * place + second) * moved[second]
                running = term if running is None else running + term
            running = earlier(running, reach * place)
            total = running if total is None else total + running
        out_ref[:, 1 + stream] = by_member(total.astype(jnp.bfloat16), order_back(count))

    grad_gating = backward.reshape(shape) + gain * relayed.astype(jnp.float32).reshape(shape)
    finish(1, grad_gating * value_short, reach + 1)
    finish(2, grad_gating * key_short, 2 * reach + 1)

    long_out = forward.reshape(shape) + gain * gating.astype(jnp.float32).reshape(shape)
    block_out = (query_short * long_out).astype(jnp.bfloat16)
    out_ref[:, 0] = by_member(block_out, order_back(count))
    finish(
        0, cot * long_out, 0, [tokens(relayed.reshape(shape))], [tokens(gating.reshape(shape))]
    )

    skewed = pltpu.roll(wide_ref[...], span - half + 1, 1, stride=1, stride_axis=0)
    diagonal = jnp.sum(skewed, axis=0, keepdims=True)
    lag_scale = 1.0 / math.sqrt(seq_total * members)
    lag_sums = jnp.concatenate(
        [diagonal[:, step * span : (step + 1) * span] for step in range(1, count + 1)], axis=0
    )
    lag_sums = lag_sums * lag_scale
    tile_ref[:count, half:] = lag_sums[:, half:]
    tile_ref[count:, half:] = pltpu.roll(lag_sums, half, 1)[:, half:]
    out_ref[:, streams + 1] = jnp.broadcast_to(tile_ref[...].astype(jnp.bfloat16)[None], shape)


def unpack_kernel(in_ref, out_ref, grads_ref, taps_ref, skip_ref, lags_ref):
    count, _, members, span = in_ref.shape
    streams, tap_count, chan_width = taps_ref.shape
    reach = 3
    for stream in range(streams + 1):
        block = in_order(in_ref[:, stream], order_back(count)).reshape(count * members, span)
        block = block.astype(jnp.float32)
        flipped = block.T.astype(jnp.bfloat16)
        if stream == 0:
            out_ref[...] = flipped
        else:
            grads_ref[stream - 1] = flipped
    tile = in_order(in_ref[:, streams + 1], order_back(count)).astype(jnp.float32)
    lane = lax.broadcasted_iota(jnp.int32, (1, members // 2, span), 2)
    lags = jnp.where(
        lane < span // 2, pltpu.roll(tile[:, members // 2 :], span // 2, 2), tile[:, : members // 2]
    )
    for step in range(members // 2):
        lags_ref[:, step * span : (step + 1) * span] = lags[:, step]
    lane = lax.broadcasted_iota(jnp.int32, (members, span), 1)
    spread = []
    for place in range(-(-tap_count // reach) + 1):
        total = None
        for group in range(count):
            moved = pltpu.roll(tile[group], (members * (group - place)) % span, 1)
            inside = (lane >= members * group) & (lane < members * (group + 1))
            total = moved if total is None else jnp.where(inside, moved, total)
        spread.append(total)
    first = 0
    for stream in range(streams):
        for place in range(-(-tap_count // reach)):
            taken = min(reach, tap_count - reach * place)
            taps_ref[stream, reach * place : reach * place + taken] = spread[place][
                first : first + taken
            ]
        first += reach + (stream == 0)
    skip_ref[...] = spread[-1][reach : reach + 1]


def by_group(query_in, key_in, value_in, short_taps, long_filters, skip_gain, cotangent):
    tok_rows, chan_width = query_in.shape
    groups, seq_total = long_filters.shape
    streams, tap_count, _ = short_taps.shape
    members = chan_width // groups
    count = groups
    vmem = pl.BlockSpec(memory_space=pltpu.VMEM)
    params = pltpu.CompilerParams(vmem_limit_bytes=32 * 1024 * 1024)
    packed, gain = pl.pallas_call(
        pack_kernel,
        out_shape=(
            jax.ShapeDtypeStruct((count, streams + 1, members, tok_rows), jnp.bfloat16),
            jax.ShapeDtypeStruct((1, chan_width), jnp.float32),
        ),
        in_specs=[pl.BlockSpec(memory_space=pltpu.HBM)] * 5,
        out_specs=(vmem,) * 2,
        scratch_shapes=[
            pltpu.VMEM((streams + 1, tok_rows, chan_width), jnp.bfloat16),
            pltpu.SemaphoreType.DMA((streams + 2,)),
        ],
        compiler_params=params,
        name="pack",
    )(
        *(
            pltpu.with_memory_space_constraint(value, pltpu.HBM)
            for value in (
                query_in, key_in, value_in, cotangent, skip_gain.reshape(1, chan_width)
            )
        )
    )
    packed = lax.all_to_all(
        packed, "seq", 0, 0, tiled=True, axis_index_groups=[order_there(count)]
    )
    results = pl.pallas_call(
        group_kernel,
        out_shape=jax.ShapeDtypeStruct((count, streams + 2, members, tok_rows), jnp.bfloat16),
        in_specs=[vmem] * 4,
        out_specs=vmem,
        scratch_shapes=[
            pltpu.VMEM((chan_width, streams * tap_count + 3), jnp.float32),
            pltpu.VMEM((tok_rows // 2, seq_total + tok_rows), jnp.float32),
            pltpu.VMEM((members, tok_rows), jnp.float32),
        ],
        compiler_params=params,
        name="group",
    )(packed, short_taps, long_filters, gain)
    results = lax.all_to_all(
        results, "seq", 0, 0, tiled=True, axis_index_groups=[order_back(count)]
    )
    block_out, input_grads, tap_grads, skip_grad, filter_grad = pl.pallas_call(
        unpack_kernel,
        out_shape=(
            jax.ShapeDtypeStruct((tok_rows, chan_width), jnp.bfloat16),
            jax.ShapeDtypeStruct((streams, tok_rows, chan_width), jnp.bfloat16),
            jax.ShapeDtypeStruct((streams, tap_count, chan_width), jnp.float32),
            jax.ShapeDtypeStruct((1, chan_width), jnp.float32),
            jax.ShapeDtypeStruct((groups, seq_total), jnp.float32),
        ),
        in_specs=[vmem],
        out_specs=(vmem,) * 5,
        compiler_params=params,
        name="unpack",
    )(results)
    return block_out, input_grads, tap_grads, skip_grad.reshape(chan_width), filter_grad


def plan(query_in, key_in, value_in, short_taps, long_filters, skip_gain, cotangent):
    tok_rows, chan_width = query_in.shape
    groups, seq_total = long_filters.shape
    fits = (
        lax.axis_size("seq") == groups
        and tok_rows == 128
        and chan_width == 128
        and chan_width // groups == 16
        and seq_total == groups * tok_rows
        and short_taps.shape[:2] == (3, 7)
    )
    chosen = by_group if fits else local
    return chosen(query_in, key_in, value_in, short_taps, long_filters, skip_gain, cotangent)


def solution(mesh):
    in_specs = (
        P("seq", "chan"),
        P("seq", "chan"),
        P("seq", "chan"),
        P(None, None, "chan"),
        P("chan", None),
        P("chan"),
        P("seq", "chan"),
    )
    out_specs = (
        P("seq", "chan"),
        P(None, "seq", "chan"),
        P(None, None, "chan"),
        P("chan"),
        P("chan", None),
    )
    return jax.shard_map(plan, mesh=mesh, in_specs=in_specs, out_specs=out_specs, check_vma=False)
```

```python
import functools
import math

import jax
import jax.numpy as jnp
from jax import lax
from jax.experimental import pallas as pl
from jax.experimental.pallas import tpu as pltpu
from jax.sharding import PartitionSpec as P


def from_behind(value, axis, steps):
    count = lax.axis_size(axis)
    initial, last = (max(0, -steps), min(count, count - steps))
    return lax.ppermute(value, axis, [(source, source + steps) for source in range(initial, last)])


def short_forward(extended, weights, rows_here):
    margin = weights.shape[0] - 1
    running = jnp.zeros((rows_here, extended.shape[1]), jnp.float32)
    for offset in range(weights.shape[0]):
        running = (
            running + weights[offset] * extended[margin - offset : margin - offset + rows_here]
        )
    return running


def short_backward(extended, weights, rows_here):
    running = jnp.zeros((rows_here, extended.shape[1]), jnp.float32)
    for offset in range(weights.shape[0]):
        running = running + weights[offset] * extended[offset : offset + rows_here]
    return running


def tap_sums(grad_rows, extended, tap_count, rows_here):
    margin = tap_count - 1
    sums_list = []
    for offset in range(tap_count):
        sums_list.append(
            jnp.sum(grad_rows * extended[margin - offset : margin - offset + rows_here], axis=0)
        )
    return jnp.stack(sums_list)


def hankel(padded, lag_start, height, breadth, seq_total):
    span = height + breadth - 1
    window = lax.dynamic_slice_in_dim(padded, lag_start + seq_total, span, axis=1)
    tiled = jnp.tile(window, (1, height))
    tiled = jnp.pad(tiled, ((0, 0), (0, height)))
    return tiled.reshape(padded.shape[0], height, span + 1)[:, :, :breadth]


def causal_part(padded, source_rows, source_start, target_start, target_count, seq_total):
    breadth = source_rows.shape[0]
    matrix = hankel(
        padded, target_start - source_start - breadth + 1, target_count, breadth, seq_total
    )
    return jnp.einsum("gts,sgc->tgc", matrix, source_rows[::-1], preferred_element_type=jnp.float32)


def anti_part(padded, target_rows, target_start, source_start, source_count, seq_total):
    breadth = target_rows.shape[0]
    matrix = hankel(
        padded, target_start - source_start - source_count + 1, source_count, breadth, seq_total
    )
    return jnp.einsum("gab,bgc->agc", matrix, target_rows, preferred_element_type=jnp.float32)[::-1]


def lag_part(buffer, target_rows, source_rows, target_start, source_start, seq_total):
    height = target_rows.shape[0]
    breadth = source_rows.shape[0]
    groups = target_rows.shape[1]
    padded_source = jnp.pad(source_rows[::-1], ((0, height), (0, 0), (0, 0)))
    products = jnp.einsum(
        "tgc,sgc->gts", target_rows, padded_source, preferred_element_type=jnp.float32
    )
    full_width = height + breadth
    skewed = products.reshape(groups, height * full_width)[:, : height * (full_width - 1)]
    skewed = skewed.reshape(groups, height, full_width - 1)
    diagonal = jnp.sum(skewed, axis=1)
    position = target_start - source_start - breadth + 1 + seq_total
    current = lax.dynamic_slice_in_dim(buffer, position, full_width - 1, axis=1)
    return lax.dynamic_update_slice_in_dim(buffer, current + diagonal, position, axis=1)


def local(query_in, key_in, value_in, short_taps, long_filters, skip_gain, cotangent):
    tok_rows, chan_width = query_in.shape
    groups, seq_total = long_filters.shape
    members = chan_width // groups
    tap_count = short_taps.shape[1]
    margin = tap_count - 1
    device = lax.axis_index("seq")
    own_start = device * tok_rows
    rim_rows = jnp.stack(
        [query_in[tok_rows - margin :], key_in[tok_rows - margin :], value_in[tok_rows - margin :]]
    )
    before = from_behind(rim_rows, "seq", 1)
    streams = [query_in, key_in, value_in]
    extended = [
        jnp.concatenate([before[stream], streams[stream]]).astype(jnp.float32)
        for stream in range(3)
    ]
    query_short = short_forward(extended[0], short_taps[0], tok_rows)
    key_short = short_forward(extended[1], short_taps[1], tok_rows)
    value_short = short_forward(extended[2], short_taps[2], tok_rows)
    gating = (key_short * value_short).astype(jnp.bfloat16)
    relayed = (cotangent.astype(jnp.float32) * query_short).astype(jnp.bfloat16)
    gating_wide = gating.astype(jnp.float32)
    relayed_wide = relayed.astype(jnp.float32)
    gating_groups = gating.reshape(tok_rows, groups, members)
    relayed_groups = relayed.reshape(tok_rows, groups, members)
    padded = jnp.concatenate([jnp.zeros((groups, seq_total), jnp.bfloat16), long_filters], axis=1)
    lag_buffer = jnp.zeros((groups, 2 * seq_total), jnp.float32)
    zeros_out = jnp.zeros((tok_rows, groups, members), jnp.float32)

    def target_pair(distance):
        return distance < 0

    totals = (zeros_out, lag_buffer)
    shard_rows = lax.all_gather(gating, "seq", axis=0, tiled=True)
    piece_rows = shard_rows.shape[0]
    step_rows = min(piece_rows, tok_rows)
    pieces = shard_rows.reshape(piece_rows // step_rows, step_rows, groups, members)

    def forward_visit_block(carried, element):
        position, rows_block = element
        source_start = position * step_rows

        def forward_active(partial_value):
            output_part, buffer = partial_value
            output_part = output_part + causal_part(
                padded, rows_block, source_start, own_start, tok_rows, seq_total
            )
            distance = device - source_start // tok_rows
            buffer = lax.cond(
                target_pair(distance),
                lambda held: lag_part(
                    held, relayed_groups, rows_block, own_start, source_start, seq_total
                ),
                lambda held: held,
                buffer,
            )
            return (output_part, buffer)

        carried = lax.cond(
            source_start < own_start + tok_rows,
            forward_active,
            lambda partial_value: partial_value,
            carried,
        )
        return (carried, None)

    totals, ignored = lax.scan(
        forward_visit_block, totals, (jnp.arange(piece_rows // step_rows, dtype=jnp.int32), pieces)
    )
    output_part, lag_buffer = totals
    output_sum = output_part.reshape(tok_rows, chan_width)
    totals = (zeros_out, lag_buffer)
    shard_rows = lax.all_gather(relayed, "seq", axis=0, tiled=True)
    piece_rows = shard_rows.shape[0]
    backward_step_rows = min(piece_rows, tok_rows)
    pieces = shard_rows.reshape(
        piece_rows // backward_step_rows, backward_step_rows, groups, members
    )

    def backward_visit_block(carried, element):
        position, rows_block = element
        target_start = position * backward_step_rows

        def backward_active(partial_value):
            grad_part, buffer = partial_value
            grad_part = grad_part + anti_part(
                padded, rows_block, target_start, own_start, tok_rows, seq_total
            )
            distance = target_start // tok_rows - device
            buffer = lax.cond(
                target_pair(distance),
                lambda held: held,
                lambda held: lag_part(
                    held, rows_block, gating_groups, target_start, own_start, seq_total
                ),
                buffer,
            )
            return (grad_part, buffer)

        carried = lax.cond(
            target_start + backward_step_rows > own_start,
            backward_active,
            lambda partial_value: partial_value,
            carried,
        )
        return (carried, None)

    totals, ignored = lax.scan(
        backward_visit_block,
        totals,
        (jnp.arange(piece_rows // backward_step_rows, dtype=jnp.int32), pieces),
    )
    grad_part, lag_buffer = totals
    grad_sum = grad_part.reshape(tok_rows, chan_width)
    lag_local = lag_buffer[:, seq_total:]
    long_out = output_sum + skip_gain * gating_wide
    block_out = (query_short * long_out).astype(jnp.bfloat16)
    grad_gating = grad_sum + skip_gain * relayed_wide
    cot_wide = cotangent.astype(jnp.float32)
    grad_shorts = [cot_wide * long_out, grad_gating * value_short, grad_gating * key_short]
    lead_rows = jnp.stack([grad_shorts[stream][:margin] for stream in range(3)])
    after = from_behind(lead_rows, "seq", -1)
    input_grads = jnp.stack(
        [
            short_backward(
                jnp.concatenate([grad_shorts[stream], after[stream]]), short_taps[stream], tok_rows
            )
            for stream in range(3)
        ]
    ).astype(jnp.bfloat16)
    tap_local = jnp.stack(
        [
            tap_sums(grad_shorts[stream], extended[stream], tap_count, tok_rows)
            for stream in range(3)
        ]
    )
    skip_local = jnp.sum(relayed_wide * gating_wide, axis=0)
    lag_total, tap_total, skip_total = lax.psum((lag_local, tap_local, skip_local), "seq")
    tap_scale = 1.0 / math.sqrt(seq_total)
    lag_scale = 1.0 / math.sqrt(seq_total * members)
    return (
        block_out,
        input_grads,
        tap_total * tap_scale,
        skip_total * tap_scale,
        lag_total * lag_scale,
    )


def order_there(count):
    return [(count // 2 + 1 - 2 * step) % count for step in range(count // 2)] + [
        (count // 2 - 2 * step) % count for step in range(count // 2)
    ]


def order_back(count):
    return [(count // 2 - step) % count for step in range(count)]


def in_order(value, order):
    return jnp.stack([value[order.index(device)] for device in range(len(order))])


def by_member(value, order):
    return jnp.stack([value[device] for device in order])


def pack_kernel(
    query_ref, key_ref, value_ref, cot_ref, skip_ref, out_ref, gain_ref, stream_buf, sems
):
    count, streams, members, tok_rows = out_ref.shape
    moves = [
        pltpu.make_async_copy(ref, stream_buf.at[stream], sems.at[stream])
        for stream, ref in enumerate((query_ref, key_ref, value_ref, cot_ref))
    ]
    moves.append(pltpu.make_async_copy(skip_ref, gain_ref, sems.at[streams]))
    for move in moves:
        move.start()
    for stream in range(streams):
        moves[stream].wait()
        flipped = stream_buf[stream].astype(jnp.float32).T.astype(jnp.bfloat16)
        flipped = flipped.reshape(count, members, tok_rows)
        out_ref[:, stream] = by_member(flipped, order_there(count))
    moves[streams].wait()


def group_kernel(
    in_ref, taps_ref, filters_ref, gain_ref, out_ref, table_ref, wide_ref, tile_ref
):
    count, _, members, span = in_ref.shape
    groups, seq_total = filters_ref.shape
    streams, tap_count, chan_width = taps_ref.shape
    rows = count * members
    mine = lax.axis_index("seq")
    shape = (count, members, span)
    lane = lax.broadcasted_iota(jnp.int32, shape, 2)
    reach = 3

    def later(value, steps):
        if steps == 0:
            return value
        turned = pltpu.roll(value, steps, 2)
        before = jnp.concatenate([jnp.zeros_like(turned[:1]), turned[:-1]], axis=0)
        return jnp.where(lane >= steps, turned, before)

    def earlier(value, steps):
        if steps == 0:
            return value
        turned = pltpu.roll(value, span - steps, 2)
        after = jnp.concatenate([turned[1:], jnp.zeros_like(turned[:1])], axis=0)
        return jnp.where(lane < span - steps, turned, after)

    table = jnp.concatenate(
        [taps_ref[stream] for stream in range(streams)]
        + [gain_ref[...], jnp.zeros((2, chan_width), jnp.float32)],
        axis=0,
    )
    table_ref[...] = table.T
    params = table_ref[pl.ds(pl.multiple_of(mine * members, members), members), :]

    def column(index):
        return jnp.broadcast_to(params[:, index : index + 1], (members, span))[None]

    chosen = lax.broadcasted_iota(jnp.int32, (groups, 1), 0) == mine
    filter_row = jnp.sum(
        jnp.where(chosen, filters_ref[...].astype(jnp.float32), 0.0), axis=0, keepdims=True
    )
    filter_row = jnp.concatenate([filter_row, jnp.zeros((1, span), jnp.float32)], axis=1)
    spread = jnp.broadcast_to(filter_row, (members, seq_total + span))
    first_rows = pltpu.roll(spread, 0, 1, stride=1, stride_axis=0).astype(jnp.bfloat16)
    row_parts = [first_rows] + [
        pltpu.roll(first_rows, first, 1) for first in range(members, span, members)
    ]
    toeplitz = jnp.concatenate(row_parts, axis=0)[:, :seq_total]

    def delays(stream):
        value = in_order(in_ref[:, stream], order_there(count))
        return [later(value, first) for first in range(0, tap_count, reach)]

    def short(stream, values):
        total = None
        for second in range(reach):
            running = None
            for first in range(second, tap_count, reach):
                value = values[first // reach].astype(jnp.float32)
                term = column(stream * tap_count + first) * value
                running = term if running is None else running + term
            running = later(running, second)
            total = running if total is None else total + running
        return total

    def ahead_by_blocks(value):
        parts = [value]
        for step in range(1, count):
            gap = jnp.zeros((step * members, span), jnp.bfloat16)
            parts.append(jnp.concatenate([value[step * members :], gap], axis=0))
        return jnp.concatenate(parts, axis=1)

    gain = column(streams * tap_count)
    cot = in_order(in_ref[:, streams], order_there(count)).astype(jnp.float32)
    delayed = [delays(0)]
    query_short = short(0, delayed[0])
    relayed = (cot * query_short).astype(jnp.bfloat16).reshape(rows, span)
    relayed_lags = ahead_by_blocks(relayed)
    backward = lax.dot_general(
        relayed_lags, toeplitz, (((1,), (1,)), ((), ())), preferred_element_type=jnp.float32
    )

    delayed += [delays(1), delays(2)]
    key_short = short(1, delayed[1])
    value_short = short(2, delayed[2])
    gating = (key_short * value_short).astype(jnp.bfloat16).reshape(rows, span)
    gating_parts, filter_parts = [gating], [toeplitz[:, :span]]
    for step in range(1, count):
        gap = jnp.zeros((step * members, span), jnp.bfloat16)
        gating_parts.append(jnp.concatenate([gap, gating[: rows - step * members]], axis=0))
        filter_parts.append(toeplitz[:, step * span : (step + 1) * span])
    forward = jnp.dot(
        jnp.concatenate(gating_parts, axis=1),
        jnp.concatenate(filter_parts, axis=0),
        preferred_element_type=jnp.float32,
    )

    half = span // 2
    flip = (
        lax.broadcasted_iota(jnp.int32, (span, span), 0)
        + lax.broadcasted_iota(jnp.int32, (span, span), 1)
        == span - 1
    ).astype(jnp.bfloat16)
    gating_turned = lax.dot_general(
        flip, gating, (((1,), (1,)), ((), ())), preferred_element_type=jnp.float32
    ).astype(jnp.bfloat16)
    gating_turned = jnp.concatenate([gating_turned[half:], gating_turned[:half]], axis=1)
    ahead = earlier(relayed.reshape(shape), half).reshape(rows, span)
    targets = jnp.concatenate([relayed_lags, ahead_by_blocks(ahead)], axis=0)
    wide_ref[:, :seq_total] = jnp.dot(
        gating_turned, targets, preferred_element_type=jnp.float32
    )
    wide_ref[:, seq_total:] = jnp.zeros((half, span), jnp.float32)

    tap_scale = 1.0 / math.sqrt(seq_total)

    def tokens(value):
        return jnp.concatenate([value[block] for block in range(count)], axis=1)

    def sums(left, right):
        product = lax.dot_general(
            jnp.concatenate(left, axis=0),
            jnp.concatenate(right, axis=0),
            (((1,), (1,)), ((), ())),
            preferred_element_type=jnp.float32,
        )
        same = (
            lax.broadcasted_iota(jnp.int32, product.shape, 0) % members
            == lax.broadcasted_iota(jnp.int32, product.shape, 1) % members
        )
        product = jnp.where(same, product, 0.0).reshape(len(left), members, -1)
        return jnp.sum(product, axis=1) * tap_scale

    tile_ref[...] = jnp.zeros((members, span), jnp.float32)

    def finish(stream, grad_short, first_row, more_left=(), more_right=()):
        moved = [earlier(grad_short, second) for second in range(reach)]
        left = [tokens(value.astype(jnp.bfloat16)) for value in moved] + list(more_left)
        right = [tokens(value) for value in delayed[stream]] + list(more_right)
        totals = sums(left, right)
        tile_ref[first_row : first_row + len(left), : totals.shape[1]] = totals
        total = None
        for place in range(len(delayed[stream])):
            running = None
            for second in range(min(reach, tap_count - reach * place)):
                term = column(stream * tap_count + reach * place + second) * moved[second]
                running = term if running is None else running + term
            running = earlier(running, reach * place)
            total = running if total is None else total + running
        out_ref[:, 1 + stream] = by_member(total.astype(jnp.bfloat16), order_back(count))

    grad_gating = backward.reshape(shape) + gain * relayed.astype(jnp.float32).reshape(shape)
    finish(1, grad_gating * value_short, reach + 1)
    finish(2, grad_gating * key_short, 2 * reach + 1)

    long_out = forward.reshape(shape) + gain * gating.astype(jnp.float32).reshape(shape)
    block_out = (query_short * long_out).astype(jnp.bfloat16)
    out_ref[:, 0] = by_member(block_out, order_back(count))
    finish(
        0, cot * long_out, 0, [tokens(relayed.reshape(shape))], [tokens(gating.reshape(shape))]
    )

    skewed = pltpu.roll(wide_ref[...], span - half + 1, 1, stride=1, stride_axis=0)
    diagonal = jnp.sum(skewed, axis=0, keepdims=True)
    lag_scale = 1.0 / math.sqrt(seq_total * members)
    lag_sums = jnp.concatenate(
        [diagonal[:, step * span : (step + 1) * span] for step in range(1, count + 1)], axis=0
    )
    lag_sums = lag_sums * lag_scale
    tile_ref[:count, half:] = lag_sums[:, half:]
    tile_ref[count:, half:] = pltpu.roll(lag_sums, half, 1)[:, half:]
    out_ref[:, streams + 1] = jnp.broadcast_to(tile_ref[...].astype(jnp.bfloat16)[None], shape)


def unpack_kernel(in_ref, out_ref, grads_ref, taps_ref, skip_ref, lags_ref):
    count, _, members, span = in_ref.shape
    streams, tap_count, chan_width = taps_ref.shape
    reach = 3
    for stream in range(streams + 1):
        block = in_order(in_ref[:, stream], order_back(count)).reshape(count * members, span)
        block = block.astype(jnp.float32)
        flipped = block.T.astype(jnp.bfloat16)
        if stream == 0:
            out_ref[...] = flipped
        else:
            grads_ref[stream - 1] = flipped
    tile = in_order(in_ref[:, streams + 1], order_back(count)).astype(jnp.float32)
    lane = lax.broadcasted_iota(jnp.int32, (1, members // 2, span), 2)
    lags = jnp.where(
        lane < span // 2, pltpu.roll(tile[:, members // 2 :], span // 2, 2), tile[:, : members // 2]
    )
    for step in range(members // 2):
        lags_ref[:, step * span : (step + 1) * span] = lags[:, step]
    lane = lax.broadcasted_iota(jnp.int32, (members, span), 1)
    spread = []
    for place in range(-(-tap_count // reach) + 1):
        total = None
        for group in range(count):
            moved = pltpu.roll(tile[group], (members * (group - place)) % span, 1)
            inside = (lane >= members * group) & (lane < members * (group + 1))
            total = moved if total is None else jnp.where(inside, moved, total)
        spread.append(total)
    first = 0
    for stream in range(streams):
        for place in range(-(-tap_count // reach)):
            taken = min(reach, tap_count - reach * place)
            taps_ref[stream, reach * place : reach * place + taken] = spread[place][
                first : first + taken
            ]
        first += reach + (stream == 0)
    skip_ref[...] = spread[-1][reach : reach + 1]


def by_group(query_in, key_in, value_in, short_taps, long_filters, skip_gain, cotangent):
    tok_rows, chan_width = query_in.shape
    groups, seq_total = long_filters.shape
    streams, tap_count, _ = short_taps.shape
    members = chan_width // groups
    count = groups
    vmem = pl.BlockSpec(memory_space=pltpu.VMEM)
    params = pltpu.CompilerParams(vmem_limit_bytes=32 * 1024 * 1024)
    packed, gain = pl.pallas_call(
        pack_kernel,
        out_shape=(
            jax.ShapeDtypeStruct((count, streams + 1, members, tok_rows), jnp.bfloat16),
            jax.ShapeDtypeStruct((1, chan_width), jnp.float32),
        ),
        in_specs=[pl.BlockSpec(memory_space=pltpu.HBM)] * 5,
        out_specs=(vmem,) * 2,
        scratch_shapes=[
            pltpu.VMEM((streams + 1, tok_rows, chan_width), jnp.bfloat16),
            pltpu.SemaphoreType.DMA((streams + 2,)),
        ],
        compiler_params=params,
        name="pack",
    )(
        *(
            pltpu.with_memory_space_constraint(value, pltpu.HBM)
            for value in (
                query_in, key_in, value_in, cotangent, skip_gain.reshape(1, chan_width)
            )
        )
    )
    packed = lax.all_to_all(
        packed, "seq", 0, 0, tiled=True, axis_index_groups=[order_there(count)]
    )
    results = pl.pallas_call(
        group_kernel,
        out_shape=jax.ShapeDtypeStruct((count, streams + 2, members, tok_rows), jnp.bfloat16),
        in_specs=[vmem] * 4,
        out_specs=vmem,
        scratch_shapes=[
            pltpu.VMEM((chan_width, streams * tap_count + 3), jnp.float32),
            pltpu.VMEM((tok_rows // 2, seq_total + tok_rows), jnp.float32),
            pltpu.VMEM((members, tok_rows), jnp.float32),
        ],
        compiler_params=params,
        name="group",
    )(packed, short_taps, long_filters, gain)
    results = lax.all_to_all(
        results, "seq", 0, 0, tiled=True, axis_index_groups=[order_back(count)]
    )
    block_out, input_grads, tap_grads, skip_grad, filter_grad = pl.pallas_call(
        unpack_kernel,
        out_shape=(
            jax.ShapeDtypeStruct((tok_rows, chan_width), jnp.bfloat16),
            jax.ShapeDtypeStruct((streams, tok_rows, chan_width), jnp.bfloat16),
            jax.ShapeDtypeStruct((streams, tap_count, chan_width), jnp.float32),
            jax.ShapeDtypeStruct((1, chan_width), jnp.float32),
            jax.ShapeDtypeStruct((groups, seq_total), jnp.float32),
        ),
        in_specs=[vmem],
        out_specs=(vmem,) * 5,
        compiler_params=params,
        name="unpack",
    )(results)
    return block_out, input_grads, tap_grads, skip_grad.reshape(chan_width), filter_grad


def plan(query_in, key_in, value_in, short_taps, long_filters, skip_gain, cotangent):
    tok_rows, chan_width = query_in.shape
    groups, seq_total = long_filters.shape
    fits = (
        lax.axis_size("seq") == groups
        and tok_rows == 128
        and chan_width == 128
        and chan_width // groups == 16
        and seq_total == groups * tok_rows
        and short_taps.shape[:2] == (3, 7)
    )
    chosen = by_group if fits else local
    return chosen(query_in, key_in, value_in, short_taps, long_filters, skip_gain, cotangent)


def solution(mesh):
    in_specs = (
        P("seq", "chan"),
        P("seq", "chan"),
        P("seq", "chan"),
        P(None, None, "chan"),
        P("chan", None),
        P("chan"),
        P("seq", "chan"),
    )
    out_specs = (
        P("seq", "chan"),
        P(None, "seq", "chan"),
        P(None, None, "chan"),
        P("chan"),
        P("chan", None),
    )
    return jax.shard_map(plan, mesh=mesh, in_specs=in_specs, out_specs=out_specs, check_vma=False)
```
